32 devices in a mesh: rep: 2 (over y), pool: 16 (over z, x, core).
Axes of the slice: x: 2, y: 2, z: 4, core: 2. Of those that a mesh axis runs over, the one named last changes fastest.
Arguments:
- pool_kv: bfloat16 [128, 8, 16, 256], P(('rep', 'pool')), parts along dimension 0, may hold values from -6 to 6
- prefix_table: int32 [4, 32], P('rep'), parts along dimension 0, may hold values from 0 to 63, as said below
- prefix_count: int32 [4], P('rep'), parts along dimension 0, may hold values from 17 to 32, as said below
- prefill_q: bfloat16 [32, 512, 1024], P(('rep', 'pool')), parts along dimension 0, may hold values from -25 to 25
- prefill_new_kv: bfloat16 [32, 512, 256], P(('rep', 'pool')), parts along dimension 0, may hold values from -6 to 6
- decode_q: bfloat16 [512, 8192], P(('rep', 'pool')), parts along dimension 0, may hold values from -25 to 25
- decode_new: bfloat16 [512, 2048], P(('rep', 'pool')), parts along dimension 0, may hold values from -6 to 6
- decode_cache: bfloat16 [32, 128, 2, 64, 256], P(('rep', 'pool')), parts along dimension 0, may hold values from -6 to 6
- decode_group: int32 [512, 1], P('rep'), parts along dimension 0, may hold values from 0 to 3; in each aligned block of 16 rows (0 to 15, 16 to 31, ...) at most 8 rows name the same one
- cached_len: int32 [512], P('rep'), parts along dimension 0, may hold values from 1 to 64, 8192 in all
Outputs:
- prefill_out: bfloat16 [32, 512, 1024], P(('rep', 'pool')), parts along dimension 0
- decode_out: bfloat16 [512, 8192], P(('rep', 'pool')), parts along dimension 0
The draws below stay inside these ranges and needn't reach their ends.
There are 2 independent parts, one for each index of `rep`. The reference program is written for one: setup_inputs(seed, part) draws one part's arguments, and reference() takes and returns one part's arrays. A program takes and returns all parts, laid end to end along the dimension named above; each array names one. Nothing has to cross between parts.
Inputs may be any that keep to these rules, and one draw needn't show every extreme that they name: prefix_table[g, j] = o * 4 + b names block b of owner o. No block appears twice in the table. Among the first prefix_count[g] entries of a row, every owner holds at most 2; entries from prefix_count[g] on are not read. `prefix_count`: at least one request has 32 blocks. `decode_group`: among the rows of one home device, no group is named by more than 8 rows.
All inputs are finite; a program needn't handle non-finite values.
Results may differ from the reference program's by a relative error of at most 0.0055.
Values may be sent and summed in bfloat16 or wider, within the bound.
No kernel may reach another device: no remote copies, remote signals or barrier semaphores. Data moves between devices by JAX's collectives and lax.ppermute only.
A program may use at most 128 MiB of HBM per device.

```python
import math
import jax
import jax.numpy as jnp
import numpy as np
from jax import lax

HD = 128
KVH = 8
QPK = 8
PGRP = 8
DGRP = 4
BLK = 16
PCAP = 2
QT = 512
RDD = 16
LMAX = 64
HQ = 64
KVD = 2
NPG = 2
NDG = 4
MAXB = 32
NB_DEV = 4
DCAP = 8
DSLOT = 128
DR = 256
N_POOL = 16


def draw_prefix_table(key, part):
    key = jax.random.fold_in(key, 1)
    order_keys = jax.random.split(jax.random.fold_in(key, 5), NPG)
    slot_keys = jax.random.split(jax.random.fold_in(key, 6), NPG * PGRP)
    orders = jax.vmap(lambda single: jax.random.permutation(single, MAXB))(order_keys)
    owner_ids = orders // PCAP
    copy_index = orders % PCAP
    scramble = jax.vmap(lambda single: jax.random.permutation(single, NB_DEV))(slot_keys)
    local_slot = jnp.arange(NPG, dtype=jnp.int32)[:, None] * PCAP + copy_index
    chosen_slot = scramble[owner_ids, local_slot]
    return (owner_ids * NB_DEV + chosen_slot).astype(jnp.int32)


def draw_prefix_count(key, part):
    key = jax.random.fold_in(key, 2)
    counts = jax.random.randint(jax.random.fold_in(key, 1), (NPG,), MAXB // 2 + 1, MAXB + 1)
    fullest = jax.random.randint(jax.random.fold_in(key, 2), (), 0, NPG)
    second = (fullest + 1) % NPG
    short_value = jax.random.randint(jax.random.fold_in(key, 3), (), MAXB // 2 + 1, MAXB // 2 + MAXB // 4 + 1)
    counts = counts.at[second].set(short_value)
    return counts.at[fullest].set(MAXB).astype(jnp.int32)


def draw_prefill_q(key, part):
    key = jax.random.fold_in(key, 3)
    drawn = jnp.clip(2.0 * jax.random.normal(key, (NPG * PGRP, QT, QPK * HD), jnp.float32), -12.0, 12.0)
    return drawn.astype(jnp.bfloat16)


def draw_prefill_new_kv(key, part):
    key = jax.random.fold_in(key, 4)
    drawn = jnp.clip(jax.random.normal(key, (NPG * PGRP, QT, 2 * HD), jnp.float32), -6.0, 6.0)
    return drawn.astype(jnp.bfloat16)


def draw_decode_q(key, part):
    key = jax.random.fold_in(key, 7)
    drawn = jnp.clip(2.0 * jax.random.normal(key, (DR, KVH * QPK * HD), jnp.float32), -12.0, 12.0)
    return drawn.astype(jnp.bfloat16)


def draw_decode_new(key, part):
    key = jax.random.fold_in(key, 8)
    drawn = jnp.clip(jax.random.normal(key, (DR, KVH, 2 * HD), jnp.float32), -6.0, 6.0)
    return drawn.reshape(DR, KVH * 2 * HD).astype(jnp.bfloat16)


def draw_decode_cache(key, part):
    key = jax.random.fold_in(key, 9)
    drawn = jnp.clip(jax.random.normal(key, (NDG * DGRP, DSLOT, KVD, LMAX, 2 * HD), jnp.float32), -6.0, 6.0)
    return drawn.astype(jnp.bfloat16)


def block_scale(stream_key, extent, cuts, least, top_value):
    level = 1.0
    for dim, blocks in cuts:
        steps = jax.random.uniform(jax.random.fold_in(jax.random.fold_in(stream_key, 6), dim), (blocks,), jnp.float32, least / len(cuts), top_value / len(cuts))
        level = level * jnp.repeat(jnp.exp(steps), extent[dim] // blocks).reshape((-1,) + (1,) * (len(extent) - 1 - dim))
    return level


def split_up(amount, total, reach, slope):
    weights = [(1 << 20) // math.isqrt(standing ** slope) + 1 for standing in range(2, amount + 1)]
    spare, given = total - reach - (amount - 1), [1] * (amount - 1)
    while spare > 0:
        free = [i for i in range(amount - 1) if given[i] < reach]
        whole, remaining = sum([weights[i] for i in free]), spare
        for i in free:
            extra = min(reach - given[i], max(1, remaining * weights[i] // whole), spare)
            given[i] = given[i] + extra
            spare = spare - extra
    return np.array([reach] + given)


def uneven_parts(key, number_of, total, bound, slope):
    if number_of == 2:
        one = jax.random.randint(key, (), max(1, total - bound), min(bound, total - 1) + 1)
        return jnp.stack([one, total - one])
    sizes = jnp.asarray(split_up(number_of, total, bound, slope), jnp.int32)
    pairs = (number_of - 1) // 2
    donor, taker = sizes[1:1 + 2 * pairs:2], sizes[2:2 + 2 * pairs:2]
    room = jnp.minimum(donor - 1, bound - taker)
    moved = jax.random.randint(jax.random.fold_in(key, 1), (pairs,), 0, 1 << 20) % (room + 1)
    sizes = sizes.at[1:1 + 2 * pairs:2].set(donor - moved).at[2:2 + 2 * pairs:2].set(taker + moved)
    return sizes[jax.random.permutation(jax.random.fold_in(key, 2), number_of)]


def assign_block(stream_key, own, number, rows, amount, top, reach, lean):
    sequence = jax.random.permutation(stream_key, amount)
    heavy_load, usual = portions_of(amount, rows * top, reach, lean, True), portions_of(amount, rows * top, reach, lean, False)
    places = jnp.arange(amount)

    def named(tallies, offset_by):
        used = int((tallies > 0).sum())
        fixed = max(1, used // 4)
        moved = fixed + (places - fixed + offset_by * (used - fixed)) % max(1, amount - fixed)
        return jnp.zeros((amount,), jnp.int32).at[sequence[jnp.where(places < fixed, places, moved)]].set(jnp.asarray(tallies, jnp.int32))

    tallies = jnp.where(number % 4 == 0, named(heavy_load, number // 4), named(usual, number - number // 4 - 1))
    mixed = jax.random.permutation(jax.random.fold_in(own, 3), amount)
    giver, taker = mixed[0:amount // 2 * 2:2], mixed[1:amount // 2 * 2:2]
    margin = jnp.minimum(tallies[giver] - 1, reach - tallies[taker]) // 2
    margin = jnp.where((giver == sequence[0]) | (taker == sequence[0]) | (tallies[taker] == 0), 0, jnp.maximum(margin, 0))
    moved = jax.random.randint(jax.random.fold_in(own, 4), (amount // 2,), 0, 1 << 20) % (margin + 1)
    tallies = tallies.at[giver].add(-moved).at[taker].add(moved)
    items = jnp.searchsorted(jnp.cumsum(tallies), jnp.arange(rows * top), side="right").astype(jnp.int32)
    listing = items.reshape(top, rows).T
    listing = listing[jax.random.permutation(jax.random.fold_in(own, 1), rows)]
    offset_by = jax.random.randint(jax.random.fold_in(own, 2), (rows, 1), 0, top)
    return jnp.take_along_axis(listing, (jnp.arange(top)[None, :] + offset_by) % top, axis=1)


def portions_of(number_of, total, reach, slope, full):
    weights = [(1 << 20) // math.isqrt(rank ** slope) + 1 for rank in range(1, number_of + 1)]
    largest = reach if full else min(reach, max(-(-total // number_of), total * weights[0] // sum(weights)))
    least = 1 if total - largest >= number_of - 1 else 0
    given, rest = [largest] + [least] * (number_of - 1), total - largest - least * (number_of - 1)
    while rest > 0:
        movable = [i for i in range(1, number_of) if given[i] < largest] or [i for i in range(1, number_of) if given[i] < reach]
        whole, budget = sum([weights[i] for i in movable]), rest
        for i in movable:
            more = min(reach - given[i], max(1, budget * weights[i] // whole), rest)
            given[i] = given[i] + more
            rest = rest - more
    return np.array(given)


def gaussian(rng, shape, deviation, reach, shards=(), held_as=jnp.bfloat16):
    level = block_scale(rng, shape, shards, -0.22, 0.18) if shards else 1.0
    entries = jax.random.normal(rng, shape, jnp.float32) * deviation * level
    return jnp.minimum(jnp.maximum(entries, -reach), reach).astype(held_as)


def setup_inputs(seed: int = 0, part: int = 0) -> dict:
    streams_of = jax.random.split(jax.random.key(seed), 11)
    own_keys = jax.random.split(jax.random.fold_in(streams_of[10], part), 11)
    pool_kv = gaussian(own_keys[0], (N_POOL * NB_DEV, KVH, BLK, 2 * HD), 1.0, 6.0, ((0, 16),))
    prefix_table = draw_prefix_table(jax.random.fold_in(jax.random.fold_in(streams_of[10], part), 71), part)
    prefix_count = draw_prefix_count(jax.random.fold_in(jax.random.fold_in(streams_of[10], part), 71), part)
    prefill_q = draw_prefill_q(jax.random.fold_in(jax.random.fold_in(streams_of[10], part), 71), part)
    prefill_new_kv = draw_prefill_new_kv(jax.random.fold_in(jax.random.fold_in(streams_of[10], part), 71), part)
    decode_q = draw_decode_q(jax.random.fold_in(jax.random.fold_in(streams_of[10], part), 71), part)
    decode_new = draw_decode_new(jax.random.fold_in(jax.random.fold_in(streams_of[10], part), 71), part)
    decode_cache = draw_decode_cache(jax.random.fold_in(jax.random.fold_in(streams_of[10], part), 71), part)
    decode_group_keys = jax.random.split(jax.random.fold_in(own_keys[8], 1), DR // RDD)
    decode_group_turns = jax.random.permutation(jax.random.fold_in(own_keys[8], 3), DR // RDD)
    decode_group = jax.vmap(lambda own, number: assign_block(jax.random.fold_in(own_keys[8], 2), own, number, RDD, NDG, 1, DCAP, 2))(decode_group_keys, decode_group_turns).reshape((DR, 1))
    cached_len = uneven_parts(own_keys[9], DR, DR * LMAX // 2, LMAX, 2).astype(jnp.int32)
    return {"pool_kv": pool_kv, "prefix_table": prefix_table, "prefix_count": prefix_count, "prefill_q": prefill_q, "prefill_new_kv": prefill_new_kv, "decode_q": decode_q, "decode_new": decode_new, "decode_cache": decode_cache, "decode_group": decode_group, "cached_len": cached_len}


MASKED = -1.0e30


def softmax_mix(scores, key_live, values):
    scores = jnp.where(key_live, scores, MASKED)
    highest = jnp.max(scores, axis=-1, keepdims=True)
    expd = jnp.where(key_live, jnp.exp(scores - highest), 0.0)
    weights = (expd / jnp.sum(expd, axis=-1, keepdims=True)).astype(jnp.bfloat16)
    weights = lax.optimization_barrier(weights).astype(jnp.float32)
    return weights, values


def prefill_slot(slot_index, pool_kv, prefix_table, prefix_count, prefill_q, prefill_new_kv):
    group_id = slot_index // PGRP
    head_id = slot_index % PGRP
    block_ids = prefix_table[group_id].astype(jnp.int32)
    blocks = pool_kv[block_ids, head_id].astype(jnp.float32).reshape(MAXB * BLK, 2 * HD)
    fresh_kv = prefill_new_kv[slot_index].astype(jnp.float32)
    key_rows = jnp.concatenate([blocks[:, :HD], fresh_kv[:, :HD]], axis=0)
    value_rows = jnp.concatenate([blocks[:, HD:], fresh_kv[:, HD:]], axis=0)
    block_live = jnp.repeat(jnp.arange(MAXB, dtype=jnp.int32) < prefix_count[group_id], BLK)
    token_pos = jnp.arange(QT, dtype=jnp.int32)
    causal = token_pos[None, :] <= token_pos[:, None]
    key_live = jnp.concatenate([jnp.broadcast_to(block_live[None, :], (QT, MAXB * BLK)), causal], axis=1)
    queries = prefill_q[slot_index].astype(jnp.float32).reshape(QT, QPK, HD)
    scores = jnp.einsum("thd,kd->htk", queries, key_rows) * (HD ** -0.5)
    weights, value_rows = softmax_mix(scores, key_live[None, :, :], value_rows)
    mixed = jnp.einsum("htk,kd->thd", weights, value_rows)
    return mixed.reshape(QT, QPK * HD).astype(jnp.bfloat16)


def decode_one(packed, decode_cache):
    query_row, own_row, group_id, slot_id, length = packed
    members = group_id * DGRP + jnp.arange(DGRP, dtype=jnp.int32)
    cache_rows = decode_cache[members, slot_id].astype(jnp.float32).reshape(KVH, LMAX, 2 * HD)
    own_kv = own_row.astype(jnp.float32).reshape(KVH, 1, 2 * HD)
    key_rows = jnp.concatenate([cache_rows[:, :, :HD], own_kv[:, :, :HD]], axis=1)
    value_rows = jnp.concatenate([cache_rows[:, :, HD:], own_kv[:, :, HD:]], axis=1)
    key_live = jnp.concatenate([jnp.arange(LMAX, dtype=jnp.int32) < length, jnp.ones((1,), dtype=bool)])
    queries = query_row.astype(jnp.float32).reshape(KVH, QPK, HD)
    scores = jnp.einsum("kqd,ktd->kqt", queries, key_rows) * (HD ** -0.5)
    weights, value_rows = softmax_mix(scores, key_live[None, None, :], value_rows)
    mixed = jnp.einsum("kqt,ktd->kqd", weights, value_rows)
    return mixed.reshape(HQ * HD).astype(jnp.bfloat16)


def reference(pool_kv, prefix_table, prefix_count, prefill_q, prefill_new_kv, decode_q, decode_new, decode_cache, decode_group, cached_len):
    prefill_out = lax.map(lambda slot_index: prefill_slot(slot_index, pool_kv, prefix_table, prefix_count, prefill_q, prefill_new_kv), jnp.arange(NPG * PGRP, dtype=jnp.int32))
    group_ids = decode_group[:, 0].astype(jnp.int32)
    table_groups = group_ids.reshape(DR // RDD, RDD)
    same_group = table_groups[:, :, None] == table_groups[:, None, :]
    earlier = jnp.arange(RDD)[None, :] < jnp.arange(RDD)[:, None]
    row_rank = jnp.sum(same_group & earlier[None, :, :], axis=2).astype(jnp.int32).reshape(DR)
    slot_ids = (jnp.arange(DR, dtype=jnp.int32) // RDD) * DCAP + row_rank
    decode_out = lax.map(lambda packed: decode_one(packed, decode_cache), (decode_q, decode_new, group_ids, slot_ids, cached_len.astype(jnp.int32)))
    return prefill_out, decode_out
```

```python
import functools

import jax
import jax.numpy as jnp
from jax import lax
from jax.experimental import pallas as pl
from jax.experimental.pallas import tpu as pltpu
from jax.sharding import PartitionSpec as P

PGRP = 8
DGRP = 4
PCAP = 2
LANES = 128
MASKED = -1e30
LOG2E = 1.4426950408889634


def up16(n):
    return -(-n // 16) * 16


def any_spec():
    return pl.BlockSpec(memory_space=pl.ANY)


def smem_spec():
    return pl.BlockSpec(memory_space=pltpu.SMEM)


def vmem_spec():
    return pl.BlockSpec(memory_space=pltpu.VMEM)


def pack_kernel(
    layout, table, count, groups, pool, q, kv, out, rows_scr, group_fill, sems
):
    blk, cap, head_rows, own_rows, q_start, own_start = layout
    blocks_here = pool.shape[0]
    group_count, most_blocks = table.shape
    decode_groups = out.shape[0] // DGRP
    row_count = q.shape[0]
    head_total = q.shape[1] // LANES
    device = lax.axis_index("pool")
    first_block = device * blocks_here
    copies = []
    for g in range(group_count):

        def scan_table(j, carry):
            seen, chosen = carry
            entry = table[g, j]
            mine = (entry >= first_block) & (entry < first_block + blocks_here) & (j < count[g])
            chosen = tuple(
                jnp.where(mine & (seen == k), entry - first_block, chosen[k]) for k in range(PCAP)
            )
            return seen + mine.astype(jnp.int32), chosen

        start = (jnp.int32(0), tuple(jnp.int32(0) for _ in range(PCAP)))
        _, chosen = lax.fori_loop(0, most_blocks, scan_table, start, unroll=8)
        for k in range(PCAP):
            for part in range(2):
                copy = pltpu.make_async_copy(
                    pool.at[chosen[k], :, :, pl.ds(part * LANES, LANES)],
                    out.at[pl.ds(g * PGRP, PGRP), pl.ds((k * 2 + part) * blk, blk), :],
                    sems.at[(g * PCAP + k) * 2 + part],
                )
                copy.start()
                copies.append(copy)
    for a in range(decode_groups):
        group_fill[a] = 0
    for h in range(head_total):
        rows_scr[pl.ds(h, row_count, stride=head_total), :] = q[
            :, h * LANES : (h + 1) * LANES
        ].astype(jnp.float32)
    slot_axis = lax.broadcasted_iota(jnp.int32, (decode_groups * cap, row_count), 0)
    row_axis = lax.broadcasted_iota(jnp.int32, (decode_groups * cap, row_count), 1)
    slot_of_row = jnp.full((decode_groups * cap, row_count), -1, jnp.int32)
    for i in range(row_count):
        a = groups[device * row_count + i]
        c = group_fill[a]
        group_fill[a] = c + 1
        slot_of_row = jnp.where(row_axis == i, a * cap + c, slot_of_row)
        for m in range(DGRP):
            first = i * head_total + m * head_rows
            out[a * DGRP + m, pl.ds(q_start + pl.multiple_of(c * head_rows, 16), head_rows), :] = (
                rows_scr[first : first + head_rows, :].astype(out.dtype)
            )
    pick = (slot_of_row == slot_axis).astype(jnp.bfloat16)
    own = jnp.dot(pick, kv[...], preferred_element_type=jnp.float32)
    pair_count = kv.shape[1] // (2 * LANES * DGRP)
    blank = jnp.zeros((own_rows - pair_count * cap, LANES), jnp.float32)
    for a in range(decode_groups):
        for m in range(DGRP):
            for part in range(2):
                pieces = [
                    own[
                        a * cap : (a + 1) * cap,
                        ((m * pair_count + k) * 2 + part) * LANES : ((m * pair_count + k) * 2 + part + 1) * LANES,
                    ]
                    for k in range(pair_count)
                ]
                if blank.shape[0]:
                    pieces.append(blank)
                out[
                    a * DGRP + m,
                    own_start + part * own_rows : own_start + (part + 1) * own_rows,
                    :,
                ] = jnp.concatenate(pieces, axis=0).astype(out.dtype)
    for copy in copies:
        copy.wait()


def plan_kernel(cap, step, owners, table, count, groups, lengths, slot_len, listed, prefix_held):
    device = lax.axis_index("pool")
    home_count = owners
    row_count = groups.shape[0] // home_count
    group_id = device // DGRP
    prefill_id = device // PGRP
    blocks_here = listed.shape[0]
    most_blocks = table.shape[1]
    chunk = min(cap, step)

    def one_owner(o, carry):
        prefix_held[o] = 0
        return carry

    lax.fori_loop(0, owners, one_owner, 0)
    pool_blocks = prefix_held.shape[0] // owners

    def one_entry(j, carry):
        o = table[prefill_id, j] // pool_blocks
        prefix_held[o] = prefix_held[o] + 1
        return carry

    lax.fori_loop(0, jnp.minimum(count[prefill_id], most_blocks), one_entry, 0)

    def one_home(s, filled):
        for c in range(cap):
            slot_len[s * cap + c] = 0
        here = jnp.int32(0)
        for i in range(row_count):
            row = s * row_count + i
            mine = groups[row] == group_id
            place = s * cap + jnp.minimum(here, cap - 1)
            slot_len[place] = jnp.where(mine, lengths[row], slot_len[place])
            here = here + mine.astype(jnp.int32)
        for b in range(cap // chunk):
            listed[1 + jnp.minimum(filled, blocks_here - 2)] = s * (cap // chunk) + b
            filled = filled + (here > b * chunk).astype(jnp.int32)
        return filled

    listed[0] = lax.fori_loop(0, home_count, one_home, jnp.int32(0))


def decode_kernel(layout, chunk, width, listed, slot_len, recv, cache, out, held, sems):
    blk, cap, head_rows, own_rows, q_start, own_start = layout
    pair_count, positions = cache.shape[1], cache.shape[2]
    per_home = cap // chunk
    key_count = pair_count * positions
    query_heads = head_rows // pair_count
    live = listed[0]
    scale = LANES ** (-0.5)

    def fetch(i):
        return pltpu.make_async_copy(
            cache.at[pl.ds(listed[1 + i] * chunk, chunk)], held.at[i], sems.at[i]
        )

    def begin(i, carry):
        fetch(i).start()
        return carry

    lax.fori_loop(0, live, begin, 0)
    rows = chunk * head_rows
    row_pair = (
        lax.broadcasted_iota(jnp.int32, (chunk, head_rows, key_count), 1) // query_heads
    )
    key_axis = lax.broadcasted_iota(jnp.int32, (chunk, head_rows, key_count), 2)
    key_slot = lax.broadcasted_iota(jnp.int32, (chunk, head_rows, key_count), 0)
    pos = jnp.where(key_axis // positions == row_pair, key_axis % positions, positions)
    own_axis = lax.broadcasted_iota(jnp.int32, (rows, own_rows), 1)
    own_row = lax.broadcasted_iota(jnp.int32, (rows, own_rows), 0)
    own_want = ((own_row % head_rows) // query_heads) * cap + own_row // head_rows

    def one(i):
        block = listed[1 + i]
        home = block // per_home
        first = (block % per_home) * chunk
        kv = held[i]
        keys = kv[..., :LANES].reshape(chunk, key_count, LANES)
        values = kv[..., LANES:].reshape(chunk, key_count, LANES)
        place = pl.multiple_of(first * head_rows, 16)
        q = recv[home, pl.ds(q_start + place, rows), :]
        own_keys = recv[home, own_start : own_start + own_rows, :]
        own_values = recv[home, own_start + own_rows : own_start + 2 * own_rows, :]
        scores = jnp.einsum(
            "jqd,jkd->jqk",
            q.reshape(chunk, head_rows, LANES),
            keys,
            preferred_element_type=jnp.float32,
        )
        length = jnp.zeros_like(pos)
        for j in range(chunk):
            length = jnp.where(key_slot == j, slot_len[block * chunk + j], length)
        scores = jnp.where(pos < length, scores, MASKED)
        own_scores = lax.dot_general(
            q, own_keys, (((1,), (1,)), ((), ())), preferred_element_type=jnp.float32
        )
        own_hit = own_axis == own_want + first
        own_score = jnp.sum(jnp.where(own_hit, own_scores, 0.0), axis=1, keepdims=True)
        own_score3 = own_score.reshape(chunk, head_rows, 1)
        top = jnp.maximum(jnp.max(scores, axis=2, keepdims=True), own_score3)
        weights = jnp.exp2((scores - top) * (scale * LOG2E))
        own_weight = jnp.exp2((own_score3 - top) * (scale * LOG2E))
        total = jnp.sum(weights, axis=2, keepdims=True) + own_weight
        mixed = jnp.einsum(
            "jqk,jkd->jqd",
            weights.astype(jnp.bfloat16),
            values,
            preferred_element_type=jnp.float32,
        )
        own_part = jnp.where(own_hit, own_weight.reshape(rows, 1), 0.0).astype(jnp.bfloat16)
        mixed = mixed.reshape(rows, LANES) + jnp.dot(
            own_part, own_values, preferred_element_type=jnp.float32
        )
        answer = mixed / total.reshape(rows, 1)
        out[home, pl.ds(place, rows), :] = answer.astype(out.dtype)

    def several(t, carry):
        ids = [jnp.minimum(t * width + w, live - 1) for w in range(width)]
        for w in range(width):

            @pl.when(t * width + w < live)
            def _():
                fetch(t * width + w).wait()

        for i in ids:
            one(i)
        return carry

    lax.fori_loop(0, (live + width - 1) // width, several, 0)


def prefill_kernel(layout, tile, prefix_held, recv, q, new_kv, out, keys, values, bias):
    blk = layout[0]
    owners = recv.shape[0]
    prefix = owners * PCAP * blk
    token_count = new_kv.shape[0]
    scale = LANES ** (-0.5) * LOG2E

    @pl.when(pl.program_id(0) == 0)
    def _():
        lane_block = lax.broadcasted_iota(jnp.int32, (8, prefix), 1) // blk
        hide = jnp.zeros((8, prefix), jnp.float32)
        for o in range(owners):
            for k in range(PCAP):
                place = (o * PCAP + k) * blk
                keys[place : place + blk, :] = recv[o, (k * 2) * blk : (k * 2 + 1) * blk, :]
                values[place : place + blk, :] = recv[o, (k * 2 + 1) * blk : (k * 2 + 2) * blk, :]
                gone = jnp.where(prefix_held[o] > k, 0.0, MASKED)
                hide = jnp.where(lane_block == o * PCAP + k, gone, hide)
        bias[...] = hide
        keys[prefix:, :] = new_kv[:, :LANES]
        values[prefix:, :] = new_kv[:, LANES:]

    for t in range(token_count // tile):
        width = prefix + (t + 1) * tile
        block = q[t * tile : (t + 1) * tile, :]
        scores = lax.dot_general(
            block, keys[:width, :], (((1,), (1,)), ((), ())), preferred_element_type=jnp.float32
        )
        causal = lax.broadcasted_iota(jnp.int32, (tile, tile), 0) >= lax.broadcasted_iota(
            jnp.int32, (tile, tile), 1
        )
        pieces = [scores[:, :prefix] + bias[0:1, :]]
        if t:
            pieces.append(scores[:, prefix : width - tile])
        pieces.append(jnp.where(causal, scores[:, width - tile :], MASKED))
        scores = jnp.concatenate(pieces, axis=1)
        top = jnp.max(scores, axis=1, keepdims=True)
        weights = jnp.exp2((scores - top) * scale)
        total = jnp.sum(weights, axis=1, keepdims=True)
        mixed = jnp.dot(
            weights.astype(jnp.bfloat16), values[:width, :], preferred_element_type=jnp.float32
        )
        out[t * tile : (t + 1) * tile, :] = (mixed / total).astype(out.dtype)


def unpack_kernel(cap, head_rows, groups, back, out, rows_scr, group_fill):
    device = lax.axis_index("pool")
    row_count = out.shape[0]
    head_total = out.shape[1] // LANES
    for a in range(back.shape[0] // DGRP):
        group_fill[a] = 0
    for i in range(row_count):
        a = groups[device * row_count + i]
        c = group_fill[a]
        group_fill[a] = c + 1
        for m in range(DGRP):
            first = i * head_total + m * head_rows
            rows_scr[first : first + head_rows, :] = back[
                a * DGRP + m, pl.ds(pl.multiple_of(c * head_rows, 16), head_rows), :
            ].astype(jnp.float32)
    for h in range(head_total):
        out[:, h * LANES : (h + 1) * LANES] = rows_scr[
            pl.ds(h, row_count, stride=head_total), :
        ].astype(out.dtype)


def shards(
    pool_kv,
    prefix_table,
    prefix_count,
    prefill_q,
    prefill_new_kv,
    decode_q,
    decode_new,
    decode_cache,
    decode_group,
    cached_len,
):
    devices = lax.axis_size("pool")
    blk = pool_kv.shape[2]
    row_count, q_width = decode_q.shape
    cap = decode_cache.shape[1] // devices
    decode_groups = devices // DGRP
    pair_count = decode_cache.shape[2]
    head_rows = q_width // LANES // DGRP
    own_rows = up16(pair_count * cap)
    q_start = PCAP * 2 * blk
    own_start = q_start + cap * head_rows
    message_rows = own_start + 2 * own_rows
    layout = (blk, cap, head_rows, own_rows, q_start, own_start)
    groups = decode_group.reshape(-1)
    prefill_groups = prefix_table.shape[0]
    big = pltpu.CompilerParams(vmem_limit_bytes=40 * 2**20)

    sending = pl.pallas_call(
        functools.partial(pack_kernel, layout),
        out_shape=jax.ShapeDtypeStruct((devices, message_rows, LANES), jnp.bfloat16),
        in_specs=[smem_spec(), smem_spec(), smem_spec(), any_spec(), vmem_spec(), vmem_spec()],
        out_specs=vmem_spec(),
        scratch_shapes=[
            pltpu.VMEM((row_count * q_width // LANES, LANES), jnp.float32),
            pltpu.SMEM((decode_groups,), jnp.int32),
            pltpu.SemaphoreType.DMA((prefill_groups * PCAP * 2,)),
        ],
        compiler_params=big,
        name="pack",
    )(prefix_table, prefix_count, groups, pool_kv, decode_q, decode_new)

    received = lax.all_to_all(sending, "pool", split_axis=0, concat_axis=0, tiled=True)

    chunk = min(cap, 4)
    width = 4
    block_count = devices * cap // chunk
    slot_len, listed, prefix_held = pl.pallas_call(
        functools.partial(plan_kernel, cap, chunk, devices),
        out_shape=(
            jax.ShapeDtypeStruct((devices * cap,), jnp.int32),
            jax.ShapeDtypeStruct((block_count + 2,), jnp.int32),
            jax.ShapeDtypeStruct((devices * pool_kv.shape[0],), jnp.int32),
        ),
        in_specs=[smem_spec()] * 4,
        out_specs=(smem_spec(),) * 3,
        cost_estimate=pl.CostEstimate(flops=1000000, bytes_accessed=4000000, transcendentals=0),
        name="plan",
    )(prefix_table, prefix_count, groups, cached_len)

    answers = pl.pallas_call(
        functools.partial(decode_kernel, layout, chunk, width),
        out_shape=jax.ShapeDtypeStruct((devices, cap * head_rows, LANES), jnp.bfloat16),
        in_specs=[smem_spec(), smem_spec(), vmem_spec(), any_spec()],
        out_specs=vmem_spec(),
        scratch_shapes=[
            pltpu.VMEM((block_count, chunk) + decode_cache.shape[2:], jnp.bfloat16),
            pltpu.SemaphoreType.DMA((block_count,)),
        ],
        compiler_params=big,
        cost_estimate=pl.CostEstimate(
            flops=500000000, bytes_accessed=8000000, transcendentals=1000000
        ),
        name="decode",
    )(listed, slot_len, received, decode_cache[0])

    back = lax.all_to_all(answers, "pool", split_axis=0, concat_axis=0, tiled=True)

    token_count, fill_width = prefill_q.shape[1:]
    prefix = devices * PCAP * blk
    head_count = fill_width // LANES
    prefix_held, received, _ = lax.optimization_barrier((prefix_held, received, answers))
    prefill_out = pl.pallas_call(
        functools.partial(prefill_kernel, layout, min(256, token_count)),
        grid=(head_count,),
        out_shape=jax.ShapeDtypeStruct((token_count, fill_width), jnp.bfloat16),
        in_specs=[
            smem_spec(),
            pl.BlockSpec((devices, PCAP * 2 * blk, LANES), lambda u: (0, 0, 0)),
            pl.BlockSpec((token_count, LANES), lambda u: (0, u)),
            pl.BlockSpec(prefill_new_kv.shape[1:], lambda u: (0, 0)),
        ],
        out_specs=pl.BlockSpec((token_count, LANES), lambda u: (0, u)),
        scratch_shapes=[
            pltpu.VMEM((prefix + token_count, LANES), jnp.bfloat16),
            pltpu.VMEM((prefix + token_count, LANES), jnp.bfloat16),
            pltpu.VMEM((8, prefix), jnp.float32),
        ],
        compiler_params=big,
        cost_estimate=pl.CostEstimate(
            flops=2 * 2 * token_count * fill_width * (prefix + token_count // 2),
            bytes_accessed=3000000,
            transcendentals=token_count * head_count * (prefix + token_count // 2),
        ),
        name="prefill",
    )(prefix_held, received, prefill_q[0], prefill_new_kv[0])

    decode_out = pl.pallas_call(
        functools.partial(unpack_kernel, cap, head_rows),
        out_shape=jax.ShapeDtypeStruct((row_count, q_width), jnp.bfloat16),
        in_specs=[smem_spec(), vmem_spec()],
        out_specs=vmem_spec(),
        scratch_shapes=[
            pltpu.VMEM((row_count * q_width // LANES, LANES), jnp.float32),
            pltpu.SMEM((decode_groups,), jnp.int32),
        ],
        name="unpack",
    )(groups, back)
    return (prefill_out[None], decode_out)


def solution(mesh):
    in_specs = (
        P(("rep", "pool"), None, None, None),
        P("rep", None),
        P("rep"),
        P(("rep", "pool"), None, None),
        P(("rep", "pool"), None, None),
        P(("rep", "pool"), None),
        P(("rep", "pool"), None),
        P(("rep", "pool"), None, None, None, None),
        P("rep", None),
        P("rep"),
    )
    out_specs = (P(("rep", "pool"), None, None), P(("rep", "pool"), None))
    return jax.shard_map(shards, mesh=mesh, in_specs=in_specs, out_specs=out_specs, check_vma=False)
```

```python
import functools

import jax
import jax.numpy as jnp
from jax import lax
from jax.experimental import pallas as pl
from jax.experimental.pallas import tpu as pltpu
from jax.sharding import PartitionSpec as P

PGRP = 8
DGRP = 4
PCAP = 2
LANES = 128
MASKED = -1e30
LOG2E = 1.4426950408889634


def up16(n):
    return -(-n // 16) * 16


def any_spec():
    return pl.BlockSpec(memory_space=pl.ANY)


def smem_spec():
    return pl.BlockSpec(memory_space=pltpu.SMEM)


def vmem_spec():
    return pl.BlockSpec(memory_space=pltpu.VMEM)


def pack_kernel(
    layout, table, count, groups, pool, q, kv, out, rows_scr, group_fill, sems
):
    blk, cap, head_rows, own_rows, q_start, own_start = layout
    blocks_here = pool.shape[0]
    group_count, most_blocks = table.shape
    decode_groups = out.shape[0] // DGRP
    row_count = q.shape[0]
    head_total = q.shape[1] // LANES
    device = lax.axis_index("pool")
    first_block = device * blocks_here
    copies = []
    for g in range(group_count):

        def scan_table(j, carry):
            seen, chosen = carry
            entry = table[g, j]
            mine = (entry >= first_block) & (entry < first_block + blocks_here) & (j < count[g])
            chosen = tuple(
                jnp.where(mine & (seen == k), entry - first_block, chosen[k]) for k in range(PCAP)
            )
            return seen + mine.astype(jnp.int32), chosen

        start = (jnp.int32(0), tuple(jnp.int32(0) for _ in range(PCAP)))
        _, chosen = lax.fori_loop(0, most_blocks, scan_table, start, unroll=8)
        for k in range(PCAP):
            for part in range(2):
                copy = pltpu.make_async_copy(
                    pool.at[chosen[k], :, :, pl.ds(part * LANES, LANES)],
                    out.at[pl.ds(g * PGRP, PGRP), pl.ds((k * 2 + part) * blk, blk), :],
                    sems.at[(g * PCAP + k) * 2 + part],
                )
                copy.start()
                copies.append(copy)
    for a in range(decode_groups):
        group_fill[a] = 0
    for h in range(head_total):
        rows_scr[pl.ds(h, row_count, stride=head_total), :] = q[
            :, h * LANES : (h + 1) * LANES
        ].astype(jnp.float32)
    slot_axis = lax.broadcasted_iota(jnp.int32, (decode_groups * cap, row_count), 0)
    row_axis = lax.broadcasted_iota(jnp.int32, (decode_groups * cap, row_count), 1)
    slot_of_row = jnp.full((decode_groups * cap, row_count), -1, jnp.int32)
    for i in range(row_count):
        a = groups[device * row_count + i]
        c = group_fill[a]
        group_fill[a] = c + 1
        slot_of_row = jnp.where(row_axis == i, a * cap + c, slot_of_row)
        for m in range(DGRP):
            first = i * head_total + m * head_rows
            out[a * DGRP + m, pl.ds(q_start + pl.multiple_of(c * head_rows, 16), head_rows), :] = (
                rows_scr[first : first + head_rows, :].astype(out.dtype)
            )
    pick = (slot_of_row == slot_axis).astype(jnp.bfloat16)
    own = jnp.dot(pick, kv[...], preferred_element_type=jnp.float32)
    pair_count = kv.shape[1] // (2 * LANES * DGRP)
    blank = jnp.zeros((own_rows - pair_count * cap, LANES), jnp.float32)
    for a in range(decode_groups):
        for m in range(DGRP):
            for part in range(2):
                pieces = [
                    own[
                        a * cap : (a + 1) * cap,
                        ((m * pair_count + k) * 2 + part) * LANES : ((m * pair_count + k) * 2 + part + 1) * LANES,
                    ]
                    for k in range(pair_count)
                ]
                if blank.shape[0]:
                    pieces.append(blank)
                out[
                    a * DGRP + m,
                    own_start + part * own_rows : own_start + (part + 1) * own_rows,
                    :,
                ] = jnp.concatenate(pieces, axis=0).astype(out.dtype)
    for copy in copies:
        copy.wait()


def plan_kernel(cap, step, owners, table, count, groups, lengths, slot_len, listed, prefix_held):
    device = lax.axis_index("pool")
    home_count = owners
    row_count = groups.shape[0] // home_count
    group_id = device // DGRP
    prefill_id = device // PGRP
    blocks_here = listed.shape[0]
    most_blocks = table.shape[1]
    chunk = min(cap, step)

    def one_owner(o, carry):
        prefix_held[o] = 0
        return carry

    lax.fori_loop(0, owners, one_owner, 0)
    pool_blocks = prefix_held.shape[0] // owners

    def one_entry(j, carry):
        o = table[prefill_id, j] // pool_blocks
        prefix_held[o] = prefix_held[o] + 1
        return carry

    lax.fori_loop(0, jnp.minimum(count[prefill_id], most_blocks), one_entry, 0)

    def one_home(s, filled):
        for c in range(cap):
            slot_len[s * cap + c] = 0
        here = jnp.int32(0)
        for i in range(row_count):
            row = s * row_count + i
            mine = groups[row] == group_id
            place = s * cap + jnp.minimum(here, cap - 1)
            slot_len[place] = jnp.where(mine, lengths[row], slot_len[place])
            here = here + mine.astype(jnp.int32)
        for b in range(cap // chunk):
            listed[1 + jnp.minimum(filled, blocks_here - 2)] = s * (cap // chunk) + b
            filled = filled + (here > b * chunk).astype(jnp.int32)
        return filled

    listed[0] = lax.fori_loop(0, home_count, one_home, jnp.int32(0))


def decode_kernel(layout, chunk, width, listed, slot_len, recv, cache, out, held, sems):
    blk, cap, head_rows, own_rows, q_start, own_start = layout
    pair_count, positions = cache.shape[1], cache.shape[2]
    per_home = cap // chunk
    key_count = pair_count * positions
    query_heads = head_rows // pair_count
    live = listed[0]
    scale = LANES ** (-0.5) * LOG2E
    rows = chunk * head_rows
    slots = width * chunk

    def fetch(i):
        return pltpu.make_async_copy(
            cache.at[pl.ds(listed[1 + i] * chunk, chunk)],
            held.at[pl.ds(i * chunk, chunk)],
            sems.at[i],
        )

    def begin(i, carry):
        fetch(i).start()
        return carry

    lax.fori_loop(0, live, begin, 0)
    row_pair = lax.broadcasted_iota(jnp.int32, (head_rows, key_count), 0) // query_heads
    key_axis = lax.broadcasted_iota(jnp.int32, (head_rows, key_count), 1)
    pos = jnp.where(key_axis // positions == row_pair, key_axis % positions, positions)
    own_axis = lax.broadcasted_iota(jnp.int32, (rows, own_rows), 1)
    own_row = lax.broadcasted_iota(jnp.int32, (rows, own_rows), 0)
    own_want = ((own_row % head_rows) // query_heads) * cap + own_row // head_rows

    def several(t, carry):
        ids = [jnp.minimum(t * width + w, live - 1) for w in range(width)]
        for w in range(width):

            @pl.when(t * width + w < live)
            def _():
                fetch(t * width + w).wait()

        blocks = [listed[1 + i] for i in ids]
        homes = [b // per_home for b in blocks]
        firsts = [(b % per_home) * chunk for b in blocks]
        places = [pl.multiple_of(f * head_rows, 16) for f in firsts]
        q = jnp.concatenate(
            [recv[h, pl.ds(q_start + p, rows), :] for h, p in zip(homes, places)], axis=0
        )
        own_keys = jnp.stack([recv[h, own_start : own_start + own_rows, :] for h in homes])
        own_values = jnp.stack(
            [recv[h, own_start + own_rows : own_start + 2 * own_rows, :] for h in homes]
        )
        kv = held[pl.ds(t * slots, slots)]
        keys = kv[..., :LANES].reshape(slots, key_count, LANES)
        values = kv[..., LANES:].reshape(slots, key_count, LANES)
        scores = jnp.einsum(
            "jqd,jkd->jqk",
            q.reshape(slots, head_rows, LANES),
            keys,
            preferred_element_type=jnp.float32,
        )
        kept = jnp.stack(
            [pos < slot_len[blocks[w] * chunk + j] for w in range(width) for j in range(chunk)]
        )
        scores = jnp.where(kept, scores, MASKED)
        own_scores = jnp.einsum(
            "jqd,jkd->jqk",
            q.reshape(width, rows, LANES),
            own_keys,
            preferred_element_type=jnp.float32,
        )
        own_hit = jnp.stack([own_axis == own_want + f for f in firsts])
        own_score = jnp.sum(jnp.where(own_hit, own_scores, 0.0), axis=2, keepdims=True)
        own_score = own_score.reshape(slots, head_rows, 1)
        top = jnp.maximum(jnp.max(scores, axis=2, keepdims=True), own_score)
        weights = jnp.exp2((scores - top) * scale)
        own_weight = jnp.exp2((own_score - top) * scale)
        total = jnp.sum(weights, axis=2, keepdims=True) + own_weight
        mixed = jnp.einsum(
            "jqk,jkd->jqd",
            weights.astype(jnp.bfloat16),
            values,
            preferred_element_type=jnp.float32,
        )
        own_part = jnp.where(own_hit, own_weight.reshape(width, rows, 1), 0.0)
        mixed = mixed.reshape(width, rows, LANES) + jnp.einsum(
            "jqk,jkd->jqd",
            own_part.astype(jnp.bfloat16),
            own_values,
            preferred_element_type=jnp.float32,
        )
        mixed = mixed / total.reshape(width, rows, 1)
        for w in reversed(range(width)):
            out[homes[w], pl.ds(places[w], rows), :] = mixed[w].astype(out.dtype)
        return carry

    lax.fori_loop(0, (live + width - 1) // width, several, 0)


def prefill_kernel(layout, tile, prefix_held, recv, q, new_kv, out, keys, values, bias):
    blk = layout[0]
    owners = recv.shape[0]
    prefix = owners * PCAP * blk
    token_count = new_kv.shape[0]
    scale = LANES ** (-0.5) * LOG2E

    @pl.when(pl.program_id(0) == 0)
    def _():
        lane_block = lax.broadcasted_iota(jnp.int32, (8, prefix), 1) // blk
        hide = jnp.zeros((8, prefix), jnp.float32)
        for o in range(owners):
            for k in range(PCAP):
                place = (o * PCAP + k) * blk
                keys[place : place + blk, :] = recv[o, (k * 2) * blk : (k * 2 + 1) * blk, :]
                values[place : place + blk, :] = recv[o, (k * 2 + 1) * blk : (k * 2 + 2) * blk, :]
                gone = jnp.where(prefix_held[o] > k, 0.0, MASKED)
                hide = jnp.where(lane_block == o * PCAP + k, gone, hide)
        bias[...] = hide
        keys[prefix:, :] = new_kv[:, :LANES]
        values[prefix:, :] = new_kv[:, LANES:]

    for t in range(token_count // tile):
        width = prefix + (t + 1) * tile
        block = q[t * tile : (t + 1) * tile, :]
        scores = lax.dot_general(
            block, keys[:width, :], (((1,), (1,)), ((), ())), preferred_element_type=jnp.float32
        )
        causal = lax.broadcasted_iota(jnp.int32, (tile, tile), 0) >= lax.broadcasted_iota(
            jnp.int32, (tile, tile), 1
        )
        pieces = [scores[:, :prefix] + bias[0:1, :]]
        if t:
            pieces.append(scores[:, prefix : width - tile])
        pieces.append(jnp.where(causal, scores[:, width - tile :], MASKED))
        scores = jnp.concatenate(pieces, axis=1)
        top = jnp.max(scores, axis=1, keepdims=True)
        weights = jnp.exp2((scores - top) * scale)
        total = jnp.sum(weights, axis=1, keepdims=True)
        mixed = jnp.dot(
            weights.astype(jnp.bfloat16), values[:width, :], preferred_element_type=jnp.float32
        )
        out[t * tile : (t + 1) * tile, :] = (mixed / total).astype(out.dtype)


def unpack_kernel(cap, head_rows, groups, back, out, rows_scr, group_fill):
    device = lax.axis_index("pool")
    row_count = out.shape[0]
    head_total = out.shape[1] // LANES
    for a in range(back.shape[0] // DGRP):
        group_fill[a] = 0
    for i in range(row_count):
        a = groups[device * row_count + i]
        c = group_fill[a]
        group_fill[a] = c + 1
        for m in range(DGRP):
            first = i * head_total + m * head_rows
            rows_scr[first : first + head_rows, :] = back[
                a * DGRP + m, pl.ds(pl.multiple_of(c * head_rows, 16), head_rows), :
            ].astype(jnp.float32)
    for h in range(head_total):
        out[:, h * LANES : (h + 1) * LANES] = rows_scr[
            pl.ds(h, row_count, stride=head_total), :
        ].astype(out.dtype)


def shards(
    pool_kv,
    prefix_table,
    prefix_count,
    prefill_q,
    prefill_new_kv,
    decode_q,
    decode_new,
    decode_cache,
    decode_group,
    cached_len,
):
    devices = lax.axis_size("pool")
    blk = pool_kv.shape[2]
    row_count, q_width = decode_q.shape
    cap = decode_cache.shape[1] // devices
    decode_groups = devices // DGRP
    pair_count = decode_cache.shape[2]
    head_rows = q_width // LANES // DGRP
    own_rows = up16(pair_count * cap)
    q_start = PCAP * 2 * blk
    own_start = q_start + cap * head_rows
    message_rows = own_start + 2 * own_rows
    layout = (blk, cap, head_rows, own_rows, q_start, own_start)
    groups = decode_group.reshape(-1)
    prefill_groups = prefix_table.shape[0]
    big = pltpu.CompilerParams(vmem_limit_bytes=60 * 2**20)

    sending = pl.pallas_call(
        functools.partial(pack_kernel, layout),
        out_shape=jax.ShapeDtypeStruct((devices, message_rows, LANES), jnp.bfloat16),
        in_specs=[smem_spec(), smem_spec(), smem_spec(), any_spec(), vmem_spec(), vmem_spec()],
        out_specs=vmem_spec(),
        scratch_shapes=[
            pltpu.VMEM((row_count * q_width // LANES, LANES), jnp.float32),
            pltpu.SMEM((decode_groups,), jnp.int32),
            pltpu.SemaphoreType.DMA((prefill_groups * PCAP * 2,)),
        ],
        compiler_params=big,
        name="pack",
    )(prefix_table, prefix_count, groups, pool_kv, decode_q, decode_new)

    received = lax.all_to_all(sending, "pool", split_axis=0, concat_axis=0, tiled=True)

    chunk = min(cap, 4)
    width = 8
    block_count = devices * cap // chunk
    slot_len, listed, prefix_held = pl.pallas_call(
        functools.partial(plan_kernel, cap, chunk, devices),
        out_shape=(
            jax.ShapeDtypeStruct((devices * cap,), jnp.int32),
            jax.ShapeDtypeStruct((block_count + 2,), jnp.int32),
            jax.ShapeDtypeStruct((devices * pool_kv.shape[0],), jnp.int32),
        ),
        in_specs=[smem_spec()] * 4,
        out_specs=(smem_spec(),) * 3,
        compiler_params=big,
        cost_estimate=pl.CostEstimate(flops=1000000, bytes_accessed=4000000, transcendentals=0),
        name="plan",
    )(prefix_table, prefix_count, groups, cached_len)

    answers = pl.pallas_call(
        functools.partial(decode_kernel, layout, chunk, width),
        out_shape=jax.ShapeDtypeStruct((devices, cap * head_rows, LANES), jnp.bfloat16),
        in_specs=[smem_spec(), smem_spec(), vmem_spec(), any_spec()],
        out_specs=vmem_spec(),
        scratch_shapes=[
            pltpu.VMEM((block_count * chunk,) + decode_cache.shape[2:], jnp.bfloat16),
            pltpu.SemaphoreType.DMA((block_count,)),
        ],
        compiler_params=big,
        cost_estimate=pl.CostEstimate(
            flops=500000000, bytes_accessed=8000000, transcendentals=1000000
        ),
        name="decode",
    )(listed, slot_len, received, decode_cache[0])

    back = lax.all_to_all(answers, "pool", split_axis=0, concat_axis=0, tiled=True)

    token_count, fill_width = prefill_q.shape[1:]
    prefix = devices * PCAP * blk
    head_count = fill_width // LANES
    prefix_held, received, _ = lax.optimization_barrier((prefix_held, received, answers))
    prefill_out = pl.pallas_call(
        functools.partial(prefill_kernel, layout, min(256, token_count)),
        grid=(head_count,),
        out_shape=jax.ShapeDtypeStruct((token_count, fill_width), jnp.bfloat16),
        in_specs=[
            smem_spec(),
            pl.BlockSpec((devices, PCAP * 2 * blk, LANES), lambda u: (0, 0, 0)),
            pl.BlockSpec((token_count, LANES), lambda u: (0, u)),
            pl.BlockSpec(prefill_new_kv.shape[1:], lambda u: (0, 0)),
        ],
        out_specs=pl.BlockSpec((token_count, LANES), lambda u: (0, u)),
        scratch_shapes=[
            pltpu.VMEM((prefix + token_count, LANES), jnp.bfloat16),
            pltpu.VMEM((prefix + token_count, LANES), jnp.bfloat16),
            pltpu.VMEM((8, prefix), jnp.float32),
        ],
        compiler_params=big,
        cost_estimate=pl.CostEstimate(
            flops=2 * 2 * token_count * fill_width * (prefix + token_count // 2),
            bytes_accessed=3000000,
            transcendentals=token_count * head_count * (prefix + token_count // 2),
        ),
        name="prefill",
    )(prefix_held, received, prefill_q[0], prefill_new_kv[0])

    decode_out = pl.pallas_call(
        functools.partial(unpack_kernel, cap, head_rows),
        out_shape=jax.ShapeDtypeStruct((row_count, q_width), jnp.bfloat16),
        in_specs=[smem_spec(), vmem_spec()],
        out_specs=vmem_spec(),
        scratch_shapes=[
            pltpu.VMEM((row_count * q_width // LANES, LANES), jnp.float32),
            pltpu.SMEM((decode_groups,), jnp.int32),
        ],
        compiler_params=big,
        name="unpack",
    )(groups, back)
    return (prefill_out[None], decode_out)


def solution(mesh):
    in_specs = (
        P(("rep", "pool"), None, None, None),
        P("rep", None),
        P("rep"),
        P(("rep", "pool"), None, None),
        P(("rep", "pool"), None, None),
        P(("rep", "pool"), None),
        P(("rep", "pool"), None),
        P(("rep", "pool"), None, None, None, None),
        P("rep", None),
        P("rep"),
    )
    out_specs = (P(("rep", "pool"), None, None), P(("rep", "pool"), None))
    return jax.shard_map(shards, mesh=mesh, in_specs=in_specs, out_specs=out_specs, check_vma=False)
```

```python
import functools

import jax
import jax.numpy as jnp
from jax import lax
from jax.experimental import pallas as pl
from jax.experimental.pallas import tpu as pltpu
from jax.sharding import PartitionSpec as P

PGRP = 8
DGRP = 4
PCAP = 2
LANES = 128
MASKED = -1e30
LOG2E = 1.4426950408889634


def up16(n):
    return -(-n // 16) * 16


def any_spec():
    return pl.BlockSpec(memory_space=pl.ANY)


def smem_spec():
    return pl.BlockSpec(memory_space=pltpu.SMEM)


def vmem_spec():
    return pl.BlockSpec(memory_space=pltpu.VMEM)


def pack_kernel(
    layout, table, count, groups, pool, q, kv, out, rows_scr, group_fill, sems
):
    blk, cap, head_rows, own_rows, q_start, own_start = layout
    blocks_here = pool.shape[0]
    group_count, most_blocks = table.shape
    decode_groups = out.shape[0] // DGRP
    row_count = q.shape[0]
    head_total = q.shape[1] // LANES
    device = lax.axis_index("pool")
    first_block = device * blocks_here
    copies = []
    for g in range(group_count):

        def scan_table(j, carry):
            seen, chosen = carry
            entry = table[g, j]
            mine = (entry >= first_block) & (entry < first_block + blocks_here) & (j < count[g])
            chosen = tuple(
                jnp.where(mine & (seen == k), entry - first_block, chosen[k]) for k in range(PCAP)
            )
            return seen + mine.astype(jnp.int32), chosen

        start = (jnp.int32(0), tuple(jnp.int32(0) for _ in range(PCAP)))
        _, chosen = lax.fori_loop(0, most_blocks, scan_table, start, unroll=8)
        for k in range(PCAP):
            for part in range(2):
                copy = pltpu.make_async_copy(
                    pool.at[chosen[k], :, :, pl.ds(part * LANES, LANES)],
                    out.at[pl.ds(g * PGRP, PGRP), pl.ds((k * 2 + part) * blk, blk), :],
                    sems.at[(g * PCAP + k) * 2 + part],
                )
                copy.start()
                copies.append(copy)
    for a in range(decode_groups):
        group_fill[a] = 0
    for h in range(head_total):
        rows_scr[pl.ds(h, row_count, stride=head_total), :] = q[
            :, h * LANES : (h + 1) * LANES
        ].astype(jnp.float32)
    slot_axis = lax.broadcasted_iota(jnp.int32, (decode_groups * cap, row_count), 0)
    row_axis = lax.broadcasted_iota(jnp.int32, (decode_groups * cap, row_count), 1)
    slot_of_row = jnp.full((decode_groups * cap, row_count), -1, jnp.int32)
    for i in range(row_count):
        a = groups[device * row_count + i]
        c = group_fill[a]
        group_fill[a] = c + 1
        slot_of_row = jnp.where(row_axis == i, a * cap + c, slot_of_row)
        for m in range(DGRP):
            first = i * head_total + m * head_rows
            out[a * DGRP + m, pl.ds(q_start + pl.multiple_of(c * head_rows, 16), head_rows), :] = (
                rows_scr[first : first + head_rows, :].astype(out.dtype)
            )
    pick = (slot_of_row == slot_axis).astype(jnp.bfloat16)
    own = jnp.dot(pick, kv[...], preferred_element_type=jnp.float32)
    pair_count = kv.shape[1] // (2 * LANES * DGRP)
    blank = jnp.zeros((own_rows - pair_count * cap, LANES), jnp.float32)
    for a in range(decode_groups):
        for m in range(DGRP):
            for part in range(2):
                pieces = [
                    own[
                        a * cap : (a + 1) * cap,
                        ((m * pair_count + k) * 2 + part) * LANES : ((m * pair_count + k) * 2 + part + 1) * LANES,
                    ]
                    for k in range(pair_count)
                ]
                if blank.shape[0]:
                    pieces.append(blank)
                out[
                    a * DGRP + m,
                    own_start + part * own_rows : own_start + (part + 1) * own_rows,
                    :,
                ] = jnp.concatenate(pieces, axis=0).astype(out.dtype)
    for copy in copies:
        copy.wait()


def plan_kernel(cap, step, owners, table, count, groups, lengths, slot_len, listed, prefix_held):
    device = lax.axis_index("pool")
    home_count = owners
    row_count = groups.shape[0] // home_count
    group_id = device // DGRP
    prefill_id = device // PGRP
    blocks_here = listed.shape[0]
    most_blocks = table.shape[1]
    chunk = min(cap, step)

    def one_owner(o, carry):
        prefix_held[o] = 0
        return carry

    lax.fori_loop(0, owners, one_owner, 0)
    pool_blocks = prefix_held.shape[0] // owners

    def one_entry(j, carry):
        o = table[prefill_id, j] // pool_blocks
        prefix_held[o] = prefix_held[o] + 1
        return carry

    lax.fori_loop(0, jnp.minimum(count[prefill_id], most_blocks), one_entry, 0)

    def one_home(s, filled):
        for c in range(cap):
            slot_len[s * cap + c] = 0
        here = jnp.int32(0)
        for i in range(row_count):
            row = s * row_count + i
            mine = groups[row] == group_id
            place = s * cap + jnp.minimum(here, cap - 1)
            slot_len[place] = jnp.where(mine, lengths[row], slot_len[place])
            here = here + mine.astype(jnp.int32)
        for b in range(cap // chunk):
            listed[1 + jnp.minimum(filled, blocks_here - 2)] = s * (cap // chunk) + b
            filled = filled + (here > b * chunk).astype(jnp.int32)
        return filled

    listed[0] = lax.fori_loop(0, home_count, one_home, jnp.int32(0))


def decode_kernel(layout, chunk, width, listed, slot_len, recv, cache, out, held, sems):
    blk, cap, head_rows, own_rows, q_start, own_start = layout
    pair_count, positions = cache.shape[1], cache.shape[2]
    per_home = cap // chunk
    key_count = pair_count * positions
    query_heads = head_rows // pair_count
    live = listed[0]
    scale = LANES ** (-0.5) * LOG2E
    rows = chunk * head_rows
    slots = width * chunk

    def fetch(i):
        return pltpu.make_async_copy(
            cache.at[pl.ds(listed[1 + i] * chunk, chunk)],
            held.at[pl.ds(i * chunk, chunk)],
            sems.at[i],
        )

    def begin(i, carry):
        fetch(i).start()
        return carry

    lax.fori_loop(0, live, begin, 0)
    row_pair = lax.broadcasted_iota(jnp.int32, (head_rows, key_count), 0) // query_heads
    key_axis = lax.broadcasted_iota(jnp.int32, (head_rows, key_count), 1)
    pos = jnp.where(key_axis // positions == row_pair, key_axis % positions, positions)
    own_axis = lax.broadcasted_iota(jnp.int32, (rows, own_rows), 1)
    own_row = lax.broadcasted_iota(jnp.int32, (rows, own_rows), 0)
    own_want = ((own_row % head_rows) // query_heads) * cap + own_row // head_rows

    def several(t, carry):
        ids = [jnp.minimum(t * width + w, live - 1) for w in range(width)]
        for w in range(width):

            @pl.when(t * width + w < live)
            def _():
                fetch(t * width + w).wait()

        blocks = [listed[1 + i] for i in ids]
        homes = [b // per_home for b in blocks]
        firsts = [(b % per_home) * chunk for b in blocks]
        places = [pl.multiple_of(f * head_rows, 16) for f in firsts]
        q = jnp.concatenate(
            [recv[h, pl.ds(q_start + p, rows), :] for h, p in zip(homes, places)], axis=0
        )
        own_keys = jnp.stack([recv[h, own_start : own_start + own_rows, :] for h in homes])
        own_values = jnp.stack(
            [recv[h, own_start + own_rows : own_start + 2 * own_rows, :] for h in homes]
        )
        kv = held[pl.ds(t * slots, slots)]
        keys = kv[..., :LANES].reshape(slots, key_count, LANES)
        values = kv[..., LANES:].reshape(slots, key_count, LANES)
        scores = jnp.einsum(
            "jqd,jkd->jqk",
            q.reshape(slots, head_rows, LANES),
            keys,
            preferred_element_type=jnp.float32,
        )
        kept = jnp.stack(
            [pos < slot_len[blocks[w] * chunk + j] for w in range(width) for j in range(chunk)]
        )
        scores = jnp.where(kept, scores, MASKED)
        own_scores = jnp.einsum(
            "jqd,jkd->jqk",
            q.reshape(width, rows, LANES),
            own_keys,
            preferred_element_type=jnp.float32,
        )
        own_hit = jnp.stack([own_axis == own_want + f for f in firsts])
        own_score = jnp.sum(jnp.where(own_hit, own_scores, 0.0), axis=2, keepdims=True)
        own_score = own_score.reshape(slots, head_rows, 1)
        top = jnp.maximum(jnp.max(scores, axis=2, keepdims=True), own_score)
        weights = jnp.exp2((scores - top) * scale)
        own_weight = jnp.exp2((own_score - top) * scale)
        total = jnp.sum(weights, axis=2, keepdims=True) + own_weight
        mixed = jnp.einsum(
            "jqk,jkd->jqd",
            weights.astype(jnp.bfloat16),
            values,
            preferred_element_type=jnp.float32,
        )
        own_part = jnp.where(own_hit, own_weight.reshape(width, rows, 1), 0.0)
        mixed = mixed.reshape(width, rows, LANES) + jnp.einsum(
            "jqk,jkd->jqd",
            own_part.astype(jnp.bfloat16),
            own_values,
            preferred_element_type=jnp.float32,
        )
        mixed = mixed / total.reshape(width, rows, 1)
        for w in reversed(range(width)):
            out[homes[w], pl.ds(places[w], rows), :] = mixed[w].astype(out.dtype)
        return carry

    lax.fori_loop(0, (live + width - 1) // width, several, 0)


def prefill_kernel(layout, tile, prefix_held, recv, q, new_kv, out, keys, values, bias):
    blk = layout[0]
    owners = recv.shape[0]
    prefix = owners * PCAP * blk
    token_count = new_kv.shape[0]
    scale = LANES ** (-0.5) * LOG2E

    @pl.when(pl.program_id(0) == 0)
    def _():
        lane_block = lax.broadcasted_iota(jnp.int32, (8, prefix), 1) // blk
        hide = jnp.zeros((8, prefix), jnp.float32)
        for o in range(owners):
            for k in range(PCAP):
                place = (o * PCAP + k) * blk
                keys[place : place + blk, :] = recv[o, (k * 2) * blk : (k * 2 + 1) * blk, :]
                values[place : place + blk, :] = recv[o, (k * 2 + 1) * blk : (k * 2 + 2) * blk, :]
                gone = jnp.where(prefix_held[o] > k, 0.0, MASKED)
                hide = jnp.where(lane_block == o * PCAP + k, gone, hide)
        bias[...] = hide
        keys[prefix:, :] = new_kv[:, :LANES]
        values[prefix:, :] = new_kv[:, LANES:]

    for t in range(token_count // tile):
        width = prefix + (t + 1) * tile
        block = q[t * tile : (t + 1) * tile, :]
        scores = lax.dot_general(
            block, keys[:width, :], (((1,), (1,)), ((), ())), preferred_element_type=jnp.float32
        )
        causal = lax.broadcasted_iota(jnp.int32, (tile, tile), 0) >= lax.broadcasted_iota(
            jnp.int32, (tile, tile), 1
        )
        pieces = [scores[:, :prefix] + bias[0:1, :]]
        if t:
            pieces.append(scores[:, prefix : width - tile])
        pieces.append(jnp.where(causal, scores[:, width - tile :], MASKED))
        scores = jnp.concatenate(pieces, axis=1)
        top = jnp.max(scores, axis=1, keepdims=True)
        weights = jnp.exp2((scores - top) * scale)
        total = jnp.sum(weights, axis=1, keepdims=True)
        mixed = jnp.dot(
            weights.astype(jnp.bfloat16), values[:width, :], preferred_element_type=jnp.float32
        )
        out[t * tile : (t + 1) * tile, :] = (mixed / total).astype(out.dtype)


def unpack_kernel(cap, head_rows, groups, back, out, rows_scr, group_fill):
    device = lax.axis_index("pool")
    row_count = out.shape[0]
    head_total = out.shape[1] // LANES
    for a in range(back.shape[0] // DGRP):
        group_fill[a] = 0
    for i in range(row_count):
        a = groups[device * row_count + i]
        c = group_fill[a]
        group_fill[a] = c + 1
        for m in range(DGRP):
            first = i * head_total + m * head_rows
            rows_scr[first : first + head_rows, :] = back[
                a * DGRP + m, pl.ds(pl.multiple_of(c * head_rows, 16), head_rows), :
            ].astype(jnp.float32)
    for h in range(head_total):
        out[:, h * LANES : (h + 1) * LANES] = rows_scr[
            pl.ds(h, row_count, stride=head_total), :
        ].astype(out.dtype)


def shards(
    pool_kv,
    prefix_table,
    prefix_count,
    prefill_q,
    prefill_new_kv,
    decode_q,
    decode_new,
    decode_cache,
    decode_group,
    cached_len,
):
    devices = lax.axis_size("pool")
    blk = pool_kv.shape[2]
    row_count, q_width = decode_q.shape
    cap = decode_cache.shape[1] // devices
    decode_groups = devices // DGRP
    pair_count = decode_cache.shape[2]
    head_rows = q_width // LANES // DGRP
    own_rows = up16(pair_count * cap)
    q_start = PCAP * 2 * blk
    own_start = q_start + cap * head_rows
    message_rows = own_start + 2 * own_rows
    layout = (blk, cap, head_rows, own_rows, q_start, own_start)
    groups = decode_group.reshape(-1)
    prefill_groups = prefix_table.shape[0]
    big = pltpu.CompilerParams(vmem_limit_bytes=60 * 2**20)
    part = pltpu.CompilerParams(vmem_limit_bytes=52 * 2**20)
    small = pltpu.CompilerParams(vmem_limit_bytes=8 * 2**20)

    sending = pl.pallas_call(
        functools.partial(pack_kernel, layout),
        out_shape=jax.ShapeDtypeStruct((devices, message_rows, LANES), jnp.bfloat16),
        in_specs=[smem_spec(), smem_spec(), smem_spec(), any_spec(), vmem_spec(), vmem_spec()],
        out_specs=vmem_spec(),
        scratch_shapes=[
            pltpu.VMEM((row_count * q_width // LANES, LANES), jnp.float32),
            pltpu.SMEM((decode_groups,), jnp.int32),
            pltpu.SemaphoreType.DMA((prefill_groups * PCAP * 2,)),
        ],
        compiler_params=big,
        name="pack",
    )(prefix_table, prefix_count, groups, pool_kv, decode_q, decode_new)

    received = lax.all_to_all(sending, "pool", split_axis=0, concat_axis=0, tiled=True)

    chunk = min(cap, 4)
    width = 8
    block_count = devices * cap // chunk
    slot_len, listed, prefix_held = pl.pallas_call(
        functools.partial(plan_kernel, cap, chunk, devices),
        out_shape=(
            jax.ShapeDtypeStruct((devices * cap,), jnp.int32),
            jax.ShapeDtypeStruct((block_count + 2,), jnp.int32),
            jax.ShapeDtypeStruct((devices * pool_kv.shape[0],), jnp.int32),
        ),
        in_specs=[smem_spec()] * 4,
        out_specs=(smem_spec(),) * 3,
        compiler_params=big,
        cost_estimate=pl.CostEstimate(flops=1000000, bytes_accessed=4000000, transcendentals=0),
        name="plan",
    )(prefix_table, prefix_count, groups, cached_len)

    answers = pl.pallas_call(
        functools.partial(decode_kernel, layout, chunk, width),
        out_shape=jax.ShapeDtypeStruct((devices, cap * head_rows, LANES), jnp.bfloat16),
        in_specs=[smem_spec(), smem_spec(), vmem_spec(), any_spec()],
        out_specs=vmem_spec(),
        scratch_shapes=[
            pltpu.VMEM((block_count * chunk,) + decode_cache.shape[2:], jnp.bfloat16),
            pltpu.SemaphoreType.DMA((block_count,)),
        ],
        compiler_params=part,
        cost_estimate=pl.CostEstimate(
            flops=500000000, bytes_accessed=8000000, transcendentals=1000000
        ),
        name="decode",
    )(listed, slot_len, received, decode_cache[0])

    back = lax.all_to_all(answers, "pool", split_axis=0, concat_axis=0, tiled=True)

    token_count, fill_width = prefill_q.shape[1:]
    prefix = devices * PCAP * blk
    head_count = fill_width // LANES
    prefix_held, received, _ = lax.optimization_barrier((prefix_held, received, answers))
    prefill_out = pl.pallas_call(
        functools.partial(prefill_kernel, layout, min(256, token_count)),
        grid=(head_count,),
        out_shape=jax.ShapeDtypeStruct((token_count, fill_width), jnp.bfloat16),
        in_specs=[
            smem_spec(),
            pl.BlockSpec((devices, PCAP * 2 * blk, LANES), lambda u: (0, 0, 0)),
            pl.BlockSpec((token_count, LANES), lambda u: (0, u)),
            pl.BlockSpec(prefill_new_kv.shape[1:], lambda u: (0, 0)),
        ],
        out_specs=pl.BlockSpec((token_count, LANES), lambda u: (0, u)),
        scratch_shapes=[
            pltpu.VMEM((prefix + token_count, LANES), jnp.bfloat16),
            pltpu.VMEM((prefix + token_count, LANES), jnp.bfloat16),
            pltpu.VMEM((8, prefix), jnp.float32),
        ],
        compiler_params=pltpu.CompilerParams(vmem_limit_bytes=16 * 2**20),
        cost_estimate=pl.CostEstimate(
            flops=2 * 2 * token_count * fill_width * (prefix + token_count // 2),
            bytes_accessed=3000000,
            transcendentals=token_count * head_count * (prefix + token_count // 2),
        ),
        name="prefill",
    )(prefix_held, received, prefill_q[0], prefill_new_kv[0])

    decode_out = pl.pallas_call(
        functools.partial(unpack_kernel, cap, head_rows),
        out_shape=jax.ShapeDtypeStruct((row_count, q_width), jnp.bfloat16),
        in_specs=[smem_spec(), vmem_spec()],
        out_specs=vmem_spec(),
        scratch_shapes=[
            pltpu.VMEM((row_count * q_width // LANES, LANES), jnp.float32),
            pltpu.SMEM((decode_groups,), jnp.int32),
        ],
        compiler_params=small,
        name="unpack",
    )(groups, back)
    return (prefill_out[None], decode_out)


def solution(mesh):
    in_specs = (
        P(("rep", "pool"), None, None, None),
        P("rep", None),
        P("rep"),
        P(("rep", "pool"), None, None),
        P(("rep", "pool"), None, None),
        P(("rep", "pool"), None),
        P(("rep", "pool"), None),
        P(("rep", "pool"), None, None, None, None),
        P("rep", None),
        P("rep"),
    )
    out_specs = (P(("rep", "pool"), None, None), P(("rep", "pool"), None))
    return jax.shard_map(shards, mesh=mesh, in_specs=in_specs, out_specs=out_specs, check_vma=False)
```

```python
import functools

import jax
import jax.numpy as jnp
from jax import lax
from jax.experimental import pallas as pl
from jax.experimental.pallas import tpu as pltpu
from jax.sharding import PartitionSpec as P

PGRP = 8
DGRP = 4
PCAP = 2
LANES = 128
MASKED = -1e30
LOG2E = 1.4426950408889634


def up16(n):
    return -(-n // 16) * 16


def any_spec():
    return pl.BlockSpec(memory_space=pl.ANY)


def smem_spec():
    return pl.BlockSpec(memory_space=pltpu.SMEM)


def vmem_spec():
    return pl.BlockSpec(memory_space=pltpu.VMEM)


def pack_kernel(layout, groups, q, kv, out, rows_scr, stage, group_fill, sems):
    cap, head_rows, own_rows, own_start = layout
    decode_groups = out.shape[0]
    row_count = q.shape[0]
    head_total = q.shape[1] // LANES
    pair_count = kv.shape[1] // (2 * LANES * DGRP)
    device = lax.axis_index("pool")
    for a in range(decode_groups):
        group_fill[a] = 0
    for h in range(head_total):
        rows_scr[pl.ds(h, row_count, stride=head_total), :] = q[
            :, h * LANES : (h + 1) * LANES
        ].astype(jnp.float32)
    slot_axis = lax.broadcasted_iota(jnp.int32, (decode_groups * cap, row_count), 0)
    row_axis = lax.broadcasted_iota(jnp.int32, (decode_groups * cap, row_count), 1)
    slot_of_row = jnp.full((decode_groups * cap, row_count), -1, jnp.int32)
    homes = []
    for i in range(row_count):
        a = groups[device * row_count + i]
        c = group_fill[a]
        group_fill[a] = c + 1
        slot_of_row = jnp.where(row_axis == i, a * cap + c, slot_of_row)
        homes.append((a, c))
    pick = (slot_of_row == slot_axis).astype(jnp.bfloat16)
    own = jnp.dot(pick, kv[...], preferred_element_type=jnp.float32)
    blank = jnp.zeros((own_rows - pair_count * cap, LANES), jnp.float32)
    copies = []
    for m in range(DGRP):
        for i, (a, c) in enumerate(homes):
            first = i * head_total + m * head_rows
            stage[m, a, pl.ds(pl.multiple_of(c * head_rows, 16), head_rows), :] = rows_scr[
                first : first + head_rows, :
            ].astype(out.dtype)
        for a in range(decode_groups):
            for part in range(2):
                pieces = []
                for k in range(pair_count):
                    lane = ((m * pair_count + k) * 2 + part) * LANES
                    pieces.append(own[a * cap : (a + 1) * cap, lane : lane + LANES])
                if blank.shape[0]:
                    pieces.append(blank)
                place = own_start + part * own_rows
                stage[m, a, place : place + own_rows, :] = jnp.concatenate(
                    pieces, axis=0
                ).astype(out.dtype)
        copy = pltpu.make_async_copy(stage.at[m], out.at[:, m], sems.at[m])
        copy.start()
        copies.append(copy)
    for copy in copies:
        copy.wait()


def blocks_kernel(table, count, pool, *rest):
    outs, sems = rest[:PGRP], rest[PGRP]
    blocks_here = pool.shape[0]
    group_count, most_blocks = table.shape
    device = lax.axis_index("pool")
    first_block = device * blocks_here
    flying = []
    for g in range(group_count):

        def scan_table(j, carry):
            seen, chosen = carry
            entry = table[g, j]
            mine = (entry >= first_block) & (entry < first_block + blocks_here) & (j < count[g])
            chosen = tuple(
                jnp.where(mine & (seen == k), entry - first_block, chosen[k]) for k in range(PCAP)
            )
            return seen + mine.astype(jnp.int32), chosen

        start = (jnp.int32(0), tuple(jnp.int32(0) for _ in range(PCAP)))
        _, chosen = lax.fori_loop(0, most_blocks, scan_table, start, unroll=8)
        if g >= 2:
            for copy in flying.pop(0):
                copy.wait()
        copies = []
        for t in range(PGRP):
            for k in range(PCAP):
                copy = pltpu.make_async_copy(
                    pool.at[chosen[k], (device % PGRP) ^ t],
                    outs[t].at[g, k],
                    sems.at[((g % 2) * PGRP + t) * PCAP + k],
                )
                copy.start()
                copies.append(copy)
        flying.append(copies)
    for copies in flying:
        for copy in copies:
            copy.wait()


def regroup_kernel(group_count, *rest):
    held, outs, sems = rest[:PGRP], rest[PGRP : PGRP + group_count], rest[-1]
    mine = lax.axis_index("pool") // PGRP
    copies = []
    for x in range(group_count):
        for t in range(PGRP):
            copy = pltpu.make_async_copy(
                held[t].at[(mine + x) % group_count], outs[x].at[t], sems.at[x * PGRP + t]
            )
            copy.start()
            copies.append(copy)
    for copy in copies:
        copy.wait()


def plan_kernel(cap, step, owners, table, count, groups, lengths, slot_len, listed, prefix_held):
    device = lax.axis_index("pool")
    home_count = owners
    row_count = groups.shape[0] // home_count
    group_id = device // DGRP
    prefill_id = device // PGRP
    blocks_here = listed.shape[0]
    most_blocks = table.shape[1]
    chunk = min(cap, step)

    def one_owner(o, carry):
        prefix_held[o] = 0
        return carry

    lax.fori_loop(0, owners, one_owner, 0)
    pool_blocks = prefix_held.shape[0] // owners

    def one_entry(j, carry):
        o = table[prefill_id, j] // pool_blocks
        prefix_held[o] = prefix_held[o] + 1
        return carry

    lax.fori_loop(0, jnp.minimum(count[prefill_id], most_blocks), one_entry, 0)

    def one_home(s, filled):
        for c in range(cap):
            slot_len[s * cap + c] = 0
        here = jnp.int32(0)
        for i in range(row_count):
            row = s * row_count + i
            mine = groups[row] == group_id
            place = s * cap + jnp.minimum(here, cap - 1)
            slot_len[place] = jnp.where(mine, lengths[row], slot_len[place])
            here = here + mine.astype(jnp.int32)
        for b in range(cap // chunk):
            listed[1 + jnp.minimum(filled, blocks_here - 2)] = s * (cap // chunk) + b
            filled = filled + (here > b * chunk).astype(jnp.int32)
        return filled

    listed[0] = lax.fori_loop(0, home_count, one_home, jnp.int32(0))


def decode_kernel(layout, chunk, width, listed, slot_len, recv, cache, out, held, sems):
    cap, head_rows, own_rows, own_start = layout
    pair_count, positions = cache.shape[1], cache.shape[2]
    per_home = cap // chunk
    key_count = pair_count * positions
    query_heads = head_rows // pair_count
    live = listed[0]
    scale = LANES ** (-0.5) * LOG2E
    rows = chunk * head_rows
    slots = width * chunk

    def fetch(i):
        return pltpu.make_async_copy(
            cache.at[pl.ds(listed[1 + i] * chunk, chunk)],
            held.at[pl.ds(i * chunk, chunk)],
            sems.at[i],
        )

    def begin(i, carry):
        fetch(i).start()
        return carry

    lax.fori_loop(0, live, begin, 0)
    row_pair = lax.broadcasted_iota(jnp.int32, (head_rows, key_count), 0) // query_heads
    key_axis = lax.broadcasted_iota(jnp.int32, (head_rows, key_count), 1)
    pos = jnp.where(key_axis // positions == row_pair, key_axis % positions, positions)
    own_axis = lax.broadcasted_iota(jnp.int32, (rows, own_rows), 1)
    own_row = lax.broadcasted_iota(jnp.int32, (rows, own_rows), 0)
    own_want = ((own_row % head_rows) // query_heads) * cap + own_row // head_rows

    def several(t, carry):
        ids = [jnp.minimum(t * width + w, live - 1) for w in range(width)]
        for w in range(width):

            @pl.when(t * width + w < live)
            def _():
                fetch(t * width + w).wait()

        blocks = [listed[1 + i] for i in ids]
        homes = [b // per_home for b in blocks]
        firsts = [(b % per_home) * chunk for b in blocks]
        places = [pl.multiple_of(f * head_rows, 16) for f in firsts]
        q = jnp.concatenate(
            [recv[h, pl.ds(p, rows), :] for h, p in zip(homes, places)], axis=0
        )
        own_keys = jnp.stack([recv[h, own_start : own_start + own_rows, :] for h in homes])
        own_values = jnp.stack(
            [recv[h, own_start + own_rows : own_start + 2 * own_rows, :] for h in homes]
        )
        kv = held[pl.ds(t * slots, slots)]
        keys = kv[..., :LANES].reshape(slots, key_count, LANES)
        values = kv[..., LANES:].reshape(slots, key_count, LANES)
        scores = jnp.einsum(
            "jqd,jkd->jqk",
            q.reshape(slots, head_rows, LANES),
            keys,
            preferred_element_type=jnp.float32,
        )
        kept = jnp.stack(
            [pos < slot_len[blocks[w] * chunk + j] for w in range(width) for j in range(chunk)]
        )
        scores = jnp.where(kept, scores, MASKED)
        own_scores = jnp.einsum(
            "jqd,jkd->jqk",
            q.reshape(width, rows, LANES),
            own_keys,
            preferred_element_type=jnp.float32,
        )
        own_hit = jnp.stack([own_axis == own_want + f for f in firsts])
        own_score = jnp.sum(jnp.where(own_hit, own_scores, 0.0), axis=2, keepdims=True)
        own_score = own_score.reshape(slots, head_rows, 1)
        top = jnp.maximum(jnp.max(scores, axis=2, keepdims=True), own_score)
        weights = jnp.exp2((scores - top) * scale)
        own_weight = jnp.exp2((own_score - top) * scale)
        total = jnp.sum(weights, axis=2, keepdims=True) + own_weight
        mixed = jnp.einsum(
            "jqk,jkd->jqd",
            weights.astype(jnp.bfloat16),
            values,
            preferred_element_type=jnp.float32,
        )
        own_part = jnp.where(own_hit, own_weight.reshape(width, rows, 1), 0.0)
        mixed = mixed.reshape(width, rows, LANES) + jnp.einsum(
            "jqk,jkd->jqd",
            own_part.astype(jnp.bfloat16),
            own_values,
            preferred_element_type=jnp.float32,
        )
        mixed = mixed / total.reshape(width, rows, 1)
        for w in reversed(range(width)):
            out[homes[w], pl.ds(places[w], rows), :] = mixed[w].astype(out.dtype)
        return carry

    lax.fori_loop(0, (live + width - 1) // width, several, 0)


def prefill_kernel(group_count, tile, prefix_held, *rest):
    sources = rest[:group_count]
    q, new_kv, out, keys, values, bias = rest[group_count:]
    blk = sources[0].shape[2]
    prefix = group_count * PGRP * PCAP * blk
    token_count = new_kv.shape[0]
    scale = LANES ** (-0.5) * LOG2E
    device = lax.axis_index("pool")

    @pl.when(pl.program_id(0) == 0)
    def _():
        lane_block = lax.broadcasted_iota(jnp.int32, (8, prefix), 1) // blk
        hide = jnp.zeros((8, prefix), jnp.float32)
        for x in range(group_count):
            sender = (device // PGRP - x + group_count) % group_count
            for t in range(PGRP):
                owner = sender * PGRP + ((device % PGRP) ^ t)
                for k in range(PCAP):
                    ordinal = (x * PGRP + t) * PCAP + k
                    block = sources[x][t, k]
                    keys[ordinal * blk : (ordinal + 1) * blk, :] = block[:, :LANES]
                    values[ordinal * blk : (ordinal + 1) * blk, :] = block[:, LANES:]
                    gone = jnp.where(prefix_held[owner] > k, 0.0, MASKED)
                    hide = jnp.where(lane_block == ordinal, gone, hide)
        bias[...] = hide
        keys[prefix:, :] = new_kv[:, :LANES]
        values[prefix:, :] = new_kv[:, LANES:]

    for t in range(token_count // tile):
        width = prefix + (t + 1) * tile
        block = q[t * tile : (t + 1) * tile, :]
        scores = lax.dot_general(
            block, keys[:width, :], (((1,), (1,)), ((), ())), preferred_element_type=jnp.float32
        )
        causal = lax.broadcasted_iota(jnp.int32, (tile, tile), 0) >= lax.broadcasted_iota(
            jnp.int32, (tile, tile), 1
        )
        pieces = [scores[:, :prefix] + bias[0:1, :]]
        if t:
            pieces.append(scores[:, prefix : width - tile])
        pieces.append(jnp.where(causal, scores[:, width - tile :], MASKED))
        scores = jnp.concatenate(pieces, axis=1)
        top = jnp.max(scores, axis=1, keepdims=True)
        weights = jnp.exp2((scores - top) * scale)
        total = jnp.sum(weights, axis=1, keepdims=True)
        mixed = jnp.dot(
            weights.astype(jnp.bfloat16), values[:width, :], preferred_element_type=jnp.float32
        )
        out[t * tile : (t + 1) * tile, :] = (mixed / total).astype(out.dtype)


def unpack_kernel(cap, head_rows, groups, back, out, rows_scr, group_fill):
    device = lax.axis_index("pool")
    row_count = out.shape[0]
    head_total = out.shape[1] // LANES
    for a in range(back.shape[0] // DGRP):
        group_fill[a] = 0
    for i in range(row_count):
        a = groups[device * row_count + i]
        c = group_fill[a]
        group_fill[a] = c + 1
        for m in range(DGRP):
            first = i * head_total + m * head_rows
            rows_scr[first : first + head_rows, :] = back[
                a * DGRP + m, pl.ds(pl.multiple_of(c * head_rows, 16), head_rows), :
            ].astype(jnp.float32)
    for h in range(head_total):
        out[:, h * LANES : (h + 1) * LANES] = rows_scr[
            pl.ds(h, row_count, stride=head_total), :
        ].astype(out.dtype)


def shards(
    pool_kv,
    prefix_table,
    prefix_count,
    prefill_q,
    prefill_new_kv,
    decode_q,
    decode_new,
    decode_cache,
    decode_group,
    cached_len,
):
    devices = lax.axis_size("pool")
    blk = pool_kv.shape[2]
    row_count, q_width = decode_q.shape
    cap = decode_cache.shape[1] // devices
    decode_groups = devices // DGRP
    pair_count = decode_cache.shape[2]
    head_rows = q_width // LANES // DGRP
    own_rows = up16(pair_count * cap)
    own_start = cap * head_rows
    message_rows = own_start + 2 * own_rows
    layout = (cap, head_rows, own_rows, own_start)
    groups = decode_group.reshape(-1)
    prefill_groups = prefix_table.shape[0]
    big = pltpu.CompilerParams(vmem_limit_bytes=60 * 2**20)
    part = pltpu.CompilerParams(vmem_limit_bytes=52 * 2**20)
    small = pltpu.CompilerParams(vmem_limit_bytes=8 * 2**20)

    sending = pl.pallas_call(
        functools.partial(pack_kernel, layout),
        out_shape=jax.ShapeDtypeStruct((decode_groups, DGRP, message_rows, LANES), jnp.bfloat16),
        in_specs=[smem_spec(), vmem_spec(), vmem_spec()],
        out_specs=any_spec(),
        scratch_shapes=[
            pltpu.VMEM((row_count * q_width // LANES, LANES), jnp.float32),
            pltpu.VMEM((DGRP, decode_groups, message_rows, LANES), jnp.bfloat16),
            pltpu.SMEM((decode_groups,), jnp.int32),
            pltpu.SemaphoreType.DMA((DGRP,)),
        ],
        compiler_params=big,
        name="pack",
    )(groups, decode_q, decode_new)
    sending = sending.reshape(devices, message_rows, LANES)

    received = lax.all_to_all(sending, "pool", split_axis=0, concat_axis=0, tiled=True)

    share = jax.ShapeDtypeStruct((prefill_groups, PCAP, blk, 2 * LANES), jnp.bfloat16)
    shares = pl.pallas_call(
        blocks_kernel,
        out_shape=(share,) * PGRP,
        in_specs=[smem_spec(), smem_spec(), any_spec()],
        out_specs=(any_spec(),) * PGRP,
        scratch_shapes=[pltpu.SemaphoreType.DMA((2 * PGRP * PCAP,))],
        compiler_params=small,
        cost_estimate=pl.CostEstimate(flops=100000, bytes_accessed=1000000, transcendentals=0),
        name="blocks",
    )(prefix_table, prefix_count, pool_kv)
    shares = [shares[0]] + [
        lax.ppermute(shares[t], "pool", [(i, i ^ t) for i in range(devices)])
        for t in range(1, PGRP)
    ]
    bundle = jax.ShapeDtypeStruct((PGRP, PCAP, blk, 2 * LANES), jnp.bfloat16)
    bundles = pl.pallas_call(
        functools.partial(regroup_kernel, prefill_groups),
        out_shape=(bundle,) * prefill_groups,
        in_specs=[any_spec()] * PGRP,
        out_specs=(any_spec(),) * prefill_groups,
        scratch_shapes=[pltpu.SemaphoreType.DMA((prefill_groups * PGRP,))],
        compiler_params=small,
        cost_estimate=pl.CostEstimate(flops=100000, bytes_accessed=1000000, transcendentals=0),
        name="regroup",
    )(*shares)
    received, *bundles = lax.optimization_barrier((received, *bundles))
    bundles = [bundles[0]] + [
        lax.ppermute(
            bundles[x],
            "pool",
            [(i, (i + x * PGRP) % devices) for i in range(devices)],
        )
        for x in range(1, prefill_groups)
    ]

    chunk = min(cap, 4)
    width = 8
    block_count = devices * cap // chunk
    slot_len, listed, prefix_held = pl.pallas_call(
        functools.partial(plan_kernel, cap, chunk, devices),
        out_shape=(
            jax.ShapeDtypeStruct((devices * cap,), jnp.int32),
            jax.ShapeDtypeStruct((block_count + 2,), jnp.int32),
            jax.ShapeDtypeStruct((devices * pool_kv.shape[0],), jnp.int32),
        ),
        in_specs=[smem_spec()] * 4,
        out_specs=(smem_spec(),) * 3,
        compiler_params=small,
        cost_estimate=pl.CostEstimate(flops=1000000, bytes_accessed=4000000, transcendentals=0),
        name="plan",
    )(prefix_table, prefix_count, groups, cached_len)

    answers = pl.pallas_call(
        functools.partial(decode_kernel, layout, chunk, width),
        out_shape=jax.ShapeDtypeStruct((devices, cap * head_rows, LANES), jnp.bfloat16),
        in_specs=[smem_spec(), smem_spec(), vmem_spec(), any_spec()],
        out_specs=vmem_spec(),
        scratch_shapes=[
            pltpu.VMEM((block_count * chunk,) + decode_cache.shape[2:], jnp.bfloat16),
            pltpu.SemaphoreType.DMA((block_count,)),
        ],
        compiler_params=part,
        cost_estimate=pl.CostEstimate(
            flops=500000000, bytes_accessed=8000000, transcendentals=1000000
        ),
        name="decode",
    )(listed, slot_len, received, decode_cache[0])

    answers, *bundles = lax.optimization_barrier((answers, *bundles))
    back = lax.all_to_all(answers, "pool", split_axis=0, concat_axis=0, tiled=True)

    token_count, fill_width = prefill_q.shape[1:]
    prefix = devices * PCAP * blk
    head_count = fill_width // LANES
    prefix_held, _ = lax.optimization_barrier((prefix_held, answers))
    prefill_out = pl.pallas_call(
        functools.partial(prefill_kernel, prefill_groups, min(256, token_count)),
        grid=(head_count,),
        out_shape=jax.ShapeDtypeStruct((token_count, fill_width), jnp.bfloat16),
        in_specs=[smem_spec()]
        + [pl.BlockSpec(bundle.shape, lambda u: (0, 0, 0, 0))] * prefill_groups
        + [
            pl.BlockSpec((token_count, LANES), lambda u: (0, u)),
            pl.BlockSpec(prefill_new_kv.shape[1:], lambda u: (0, 0)),
        ],
        out_specs=pl.BlockSpec((token_count, LANES), lambda u: (0, u)),
        scratch_shapes=[
            pltpu.VMEM((prefix + token_count, LANES), jnp.bfloat16),
            pltpu.VMEM((prefix + token_count, LANES), jnp.bfloat16),
            pltpu.VMEM((8, prefix), jnp.float32),
        ],
        compiler_params=pltpu.CompilerParams(vmem_limit_bytes=16 * 2**20),
        cost_estimate=pl.CostEstimate(
            flops=2 * 2 * token_count * fill_width * (prefix + token_count // 2),
            bytes_accessed=3000000,
            transcendentals=token_count * head_count * (prefix + token_count // 2),
        ),
        name="prefill",
    )(prefix_held, *bundles, prefill_q[0], prefill_new_kv[0])

    decode_out = pl.pallas_call(
        functools.partial(unpack_kernel, cap, head_rows),
        out_shape=jax.ShapeDtypeStruct((row_count, q_width), jnp.bfloat16),
        in_specs=[smem_spec(), vmem_spec()],
        out_specs=vmem_spec(),
        scratch_shapes=[
            pltpu.VMEM((row_count * q_width // LANES, LANES), jnp.float32),
            pltpu.SMEM((decode_groups,), jnp.int32),
        ],
        compiler_params=small,
        name="unpack",
    )(groups, back)
    return (prefill_out[None], decode_out)


def solution(mesh):
    in_specs = (
        P(("rep", "pool"), None, None, None),
        P("rep", None),
        P("rep"),
        P(("rep", "pool"), None, None),
        P(("rep", "pool"), None, None),
        P(("rep", "pool"), None),
        P(("rep", "pool"), None),
        P(("rep", "pool"), None, None, None, None),
        P("rep", None),
        P("rep"),
    )
    out_specs = (P(("rep", "pool"), None, None), P(("rep", "pool"), None))
    return jax.shard_map(shards, mesh=mesh, in_specs=in_specs, out_specs=out_specs, check_vma=False)
```

```python
import functools

import jax
import jax.numpy as jnp
from jax import lax
from jax.experimental import pallas as pl
from jax.experimental.pallas import tpu as pltpu
from jax.sharding import PartitionSpec as P

PGRP = 8
DGRP = 4
PCAP = 2
PLANE = 4
LANES = 128
MASKED = -1e30
LOG2E = 1.4426950408889634


def up16(n):
    return -(-n // 16) * 16


def any_spec():
    return pl.BlockSpec(memory_space=pl.ANY)


def smem_spec():
    return pl.BlockSpec(memory_space=pltpu.SMEM)


def vmem_spec():
    return pl.BlockSpec(memory_space=pltpu.VMEM)


def pack_kernel(layout, groups, q, kv, out, rows_scr, stage, group_fill, sems):
    cap, head_rows, own_rows, own_start = layout
    decode_groups = out.shape[0]
    row_count = q.shape[0]
    head_total = q.shape[1] // LANES
    pair_count = kv.shape[1] // (2 * LANES * DGRP)
    device = lax.axis_index("pool")
    for a in range(decode_groups):
        group_fill[a] = 0
    for h in range(head_total):
        rows_scr[pl.ds(h, row_count, stride=head_total), :] = q[
            :, h * LANES : (h + 1) * LANES
        ].astype(jnp.float32)
    slot_axis = lax.broadcasted_iota(jnp.int32, (decode_groups * cap, row_count), 0)
    row_axis = lax.broadcasted_iota(jnp.int32, (decode_groups * cap, row_count), 1)
    slot_of_row = jnp.full((decode_groups * cap, row_count), -1, jnp.int32)
    homes = []
    for i in range(row_count):
        a = groups[device * row_count + i]
        c = group_fill[a]
        group_fill[a] = c + 1
        slot_of_row = jnp.where(row_axis == i, a * cap + c, slot_of_row)
        homes.append((a, c))
    pick = (slot_of_row == slot_axis).astype(jnp.bfloat16)
    own = jnp.dot(pick, kv[...], preferred_element_type=jnp.float32)
    blank = jnp.zeros((own_rows - pair_count * cap, LANES), jnp.float32)
    copies = []
    for m in range(DGRP):
        for i, (a, c) in enumerate(homes):
            first = i * head_total + m * head_rows
            stage[m, a, pl.ds(pl.multiple_of(c * head_rows, 16), head_rows), :] = rows_scr[
                first : first + head_rows, :
            ].astype(out.dtype)
        for a in range(decode_groups):
            for part in range(2):
                pieces = []
                for k in range(pair_count):
                    lane = ((m * pair_count + k) * 2 + part) * LANES
                    pieces.append(own[a * cap : (a + 1) * cap, lane : lane + LANES])
                if blank.shape[0]:
                    pieces.append(blank)
                place = own_start + part * own_rows
                stage[m, a, place : place + own_rows, :] = jnp.concatenate(
                    pieces, axis=0
                ).astype(out.dtype)
        copy = pltpu.make_async_copy(stage.at[m], out.at[:, m], sems.at[m])
        copy.start()
        copies.append(copy)
    for copy in copies:
        copy.wait()


def blocks_kernel(table, count, pool, *rest):
    outs, sems = rest[:PLANE], rest[PLANE]
    blocks_here = pool.shape[0]
    group_count, most_blocks = table.shape
    device = lax.axis_index("pool")
    first_block = device * blocks_here
    flying = []
    for g in range(group_count):

        def scan_table(j, carry):
            seen, chosen = carry
            entry = table[g, j]
            mine = (entry >= first_block) & (entry < first_block + blocks_here) & (j < count[g])
            chosen = tuple(
                jnp.where(mine & (seen == k), entry - first_block, chosen[k]) for k in range(PCAP)
            )
            return seen + mine.astype(jnp.int32), chosen

        start = (jnp.int32(0), tuple(jnp.int32(0) for _ in range(PCAP)))
        _, chosen = lax.fori_loop(0, most_blocks, scan_table, start, unroll=8)
        if g >= 2:
            for copy in flying.pop(0):
                copy.wait()
        copies = []
        for t in range(PGRP):
            for k in range(PCAP):
                copy = pltpu.make_async_copy(
                    pool.at[chosen[k], (device % PGRP) ^ t],
                    outs[t % PLANE].at[t // PLANE, g, k],
                    sems.at[((g % 2) * PGRP + t) * PCAP + k],
                )
                copy.start()
                copies.append(copy)
        flying.append(copies)
    for copies in flying:
        for copy in copies:
            copy.wait()


def forward_kernel(*rest):
    held, out, sems = rest[:PLANE], rest[PLANE], rest[PLANE + 1]
    copies = []
    for t in range(PLANE):
        copy = pltpu.make_async_copy(held[t].at[1], out.at[t], sems.at[t])
        copy.start()
        copies.append(copy)
    for copy in copies:
        copy.wait()


def regroup_kernel(group_count, *rest):
    held, crossed = rest[:PLANE], rest[PLANE]
    outs, sems = rest[PLANE + 1 : PLANE + 1 + group_count], rest[-1]
    mine = lax.axis_index("pool") // PGRP
    copies = []
    for x in range(group_count):
        g = (mine + x) % group_count
        for t in range(PLANE):
            for side, source in enumerate((held[t].at[0, g], crossed.at[t, g])):
                place = side * PLANE + t
                copy = pltpu.make_async_copy(source, outs[x].at[place], sems.at[x * PGRP + place])
                copy.start()
                copies.append(copy)
    for copy in copies:
        copy.wait()


def plan_kernel(cap, step, owners, table, count, groups, lengths, slot_len, listed, prefix_held):
    device = lax.axis_index("pool")
    home_count = owners
    row_count = groups.shape[0] // home_count
    group_id = device // DGRP
    prefill_id = device // PGRP
    blocks_here = listed.shape[0]
    most_blocks = table.shape[1]
    chunk = min(cap, step)

    def one_owner(o, carry):
        prefix_held[o] = 0
        return carry

    lax.fori_loop(0, owners, one_owner, 0)
    pool_blocks = prefix_held.shape[0] // owners

    def one_entry(j, carry):
        o = table[prefill_id, j] // pool_blocks
        prefix_held[o] = prefix_held[o] + 1
        return carry

    lax.fori_loop(0, jnp.minimum(count[prefill_id], most_blocks), one_entry, 0)

    def one_home(s, filled):
        for c in range(cap):
            slot_len[s * cap + c] = 0
        here = jnp.int32(0)
        for i in range(row_count):
            row = s * row_count + i
            mine = groups[row] == group_id
            place = s * cap + jnp.minimum(here, cap - 1)
            slot_len[place] = jnp.where(mine, lengths[row], slot_len[place])
            here = here + mine.astype(jnp.int32)
        for b in range(cap // chunk):
            listed[1 + jnp.minimum(filled, blocks_here - 2)] = s * (cap // chunk) + b
            filled = filled + (here > b * chunk).astype(jnp.int32)
        return filled

    listed[0] = lax.fori_loop(0, home_count, one_home, jnp.int32(0))


def decode_kernel(layout, chunk, width, listed, slot_len, recv, cache, out, held, sems):
    cap, head_rows, own_rows, own_start = layout
    pair_count, positions = cache.shape[1], cache.shape[2]
    per_home = cap // chunk
    key_count = pair_count * positions
    query_heads = head_rows // pair_count
    live = listed[0]
    scale = LANES ** (-0.5) * LOG2E
    rows = chunk * head_rows
    slots = width * chunk

    def fetch(i):
        return pltpu.make_async_copy(
            cache.at[pl.ds(listed[1 + i] * chunk, chunk)],
            held.at[pl.ds(i * chunk, chunk)],
            sems.at[i],
        )

    def begin(i, carry):
        fetch(i).start()
        return carry

    lax.fori_loop(0, live, begin, 0)
    row_pair = lax.broadcasted_iota(jnp.int32, (head_rows, key_count), 0) // query_heads
    key_axis = lax.broadcasted_iota(jnp.int32, (head_rows, key_count), 1)
    pos = jnp.where(key_axis // positions == row_pair, key_axis % positions, positions)
    own_axis = lax.broadcasted_iota(jnp.int32, (rows, own_rows), 1)
    own_row = lax.broadcasted_iota(jnp.int32, (rows, own_rows), 0)
    own_want = ((own_row % head_rows) // query_heads) * cap + own_row // head_rows

    def several(t, carry):
        ids = [jnp.minimum(t * width + w, live - 1) for w in range(width)]
        for w in range(width):

            @pl.when(t * width + w < live)
            def _():
                fetch(t * width + w).wait()

        blocks = [listed[1 + i] for i in ids]
        homes = [b // per_home for b in blocks]
        firsts = [(b % per_home) * chunk for b in blocks]
        places = [pl.multiple_of(f * head_rows, 16) for f in firsts]
        q = jnp.concatenate(
            [recv[h, pl.ds(p, rows), :] for h, p in zip(homes, places)], axis=0
        )
        own_keys = jnp.stack([recv[h, own_start : own_start + own_rows, :] for h in homes])
        own_values = jnp.stack(
            [recv[h, own_start + own_rows : own_start + 2 * own_rows, :] for h in homes]
        )
        kv = held[pl.ds(t * slots, slots)]
        keys = kv[..., :LANES].reshape(slots, key_count, LANES)
        values = kv[..., LANES:].reshape(slots, key_count, LANES)
        scores = jnp.einsum(
            "jqd,jkd->jqk",
            q.reshape(slots, head_rows, LANES),
            keys,
            preferred_element_type=jnp.float32,
        )
        kept = jnp.stack(
            [pos < slot_len[blocks[w] * chunk + j] for w in range(width) for j in range(chunk)]
        )
        scores = jnp.where(kept, scores, MASKED)
        own_scores = jnp.einsum(
            "jqd,jkd->jqk",
            q.reshape(width, rows, LANES),
            own_keys,
            preferred_element_type=jnp.float32,
        )
        own_hit = jnp.stack([own_axis == own_want + f for f in firsts])
        own_score = jnp.sum(jnp.where(own_hit, own_scores, 0.0), axis=2, keepdims=True)
        own_score = own_score.reshape(slots, head_rows, 1)
        top = jnp.maximum(jnp.max(scores, axis=2, keepdims=True), own_score)
        weights = jnp.exp2((scores - top) * scale)
        own_weight = jnp.exp2((own_score - top) * scale)
        total = jnp.sum(weights, axis=2, keepdims=True) + own_weight
        mixed = jnp.einsum(
            "jqk,jkd->jqd",
            weights.astype(jnp.bfloat16),
            values,
            preferred_element_type=jnp.float32,
        )
        own_part = jnp.where(own_hit, own_weight.reshape(width, rows, 1), 0.0)
        mixed = mixed.reshape(width, rows, LANES) + jnp.einsum(
            "jqk,jkd->jqd",
            own_part.astype(jnp.bfloat16),
            own_values,
            preferred_element_type=jnp.float32,
        )
        mixed = mixed / total.reshape(width, rows, 1)
        for w in reversed(range(width)):
            out[homes[w], pl.ds(places[w], rows), :] = mixed[w].astype(out.dtype)
        return carry

    lax.fori_loop(0, (live + width - 1) // width, several, 0)


def prefill_kernel(group_count, tile, prefix_held, *rest):
    sources = rest[:group_count]
    q, new_kv, out, keys, values, bias = rest[group_count:]
    blk = sources[0].shape[2]
    prefix = group_count * PGRP * PCAP * blk
    token_count = new_kv.shape[0]
    scale = LANES ** (-0.5) * LOG2E
    device = lax.axis_index("pool")

    @pl.when(pl.program_id(0) == 0)
    def _():
        lane_block = lax.broadcasted_iota(jnp.int32, (8, prefix), 1) // blk
        hide = jnp.zeros((8, prefix), jnp.float32)
        for x in range(group_count):
            sender = (device // PGRP - x + group_count) % group_count
            for t in range(PGRP):
                owner = sender * PGRP + ((device % PGRP) ^ t)
                for k in range(PCAP):
                    ordinal = (x * PGRP + t) * PCAP + k
                    block = sources[x][t, k]
                    keys[ordinal * blk : (ordinal + 1) * blk, :] = block[:, :LANES]
                    values[ordinal * blk : (ordinal + 1) * blk, :] = block[:, LANES:]
                    gone = jnp.where(prefix_held[owner] > k, 0.0, MASKED)
                    hide = jnp.where(lane_block == ordinal, gone, hide)
        bias[...] = hide
        keys[prefix:, :] = new_kv[:, :LANES]
        values[prefix:, :] = new_kv[:, LANES:]

    for t in range(token_count // tile):
        width = prefix + (t + 1) * tile
        block = q[t * tile : (t + 1) * tile, :]
        scores = lax.dot_general(
            block, keys[:width, :], (((1,), (1,)), ((), ())), preferred_element_type=jnp.float32
        )
        causal = lax.broadcasted_iota(jnp.int32, (tile, tile), 0) >= lax.broadcasted_iota(
            jnp.int32, (tile, tile), 1
        )
        pieces = [scores[:, :prefix] + bias[0:1, :]]
        if t:
            pieces.append(scores[:, prefix : width - tile])
        pieces.append(jnp.where(causal, scores[:, width - tile :], MASKED))
        scores = jnp.concatenate(pieces, axis=1)
        top = jnp.max(scores, axis=1, keepdims=True)
        weights = jnp.exp2((scores - top) * scale)
        total = jnp.sum(weights, axis=1, keepdims=True)
        mixed = jnp.dot(
            weights.astype(jnp.bfloat16), values[:width, :], preferred_element_type=jnp.float32
        )
        out[t * tile : (t + 1) * tile, :] = (mixed / total).astype(out.dtype)


def unpack_kernel(cap, head_rows, groups, back, out, rows_scr, group_fill):
    device = lax.axis_index("pool")
    row_count = out.shape[0]
    head_total = out.shape[1] // LANES
    for a in range(back.shape[0] // DGRP):
        group_fill[a] = 0
    for i in range(row_count):
        a = groups[device * row_count + i]
        c = group_fill[a]
        group_fill[a] = c + 1
        for m in range(DGRP):
            first = i * head_total + m * head_rows
            rows_scr[first : first + head_rows, :] = back[
                a * DGRP + m, pl.ds(pl.multiple_of(c * head_rows, 16), head_rows), :
            ].astype(jnp.float32)
    for h in range(head_total):
        out[:, h * LANES : (h + 1) * LANES] = rows_scr[
            pl.ds(h, row_count, stride=head_total), :
        ].astype(out.dtype)


def shards(
    pool_kv,
    prefix_table,
    prefix_count,
    prefill_q,
    prefill_new_kv,
    decode_q,
    decode_new,
    decode_cache,
    decode_group,
    cached_len,
):
    devices = lax.axis_size("pool")
    blk = pool_kv.shape[2]
    row_count, q_width = decode_q.shape
    cap = decode_cache.shape[1] // devices
    decode_groups = devices // DGRP
    pair_count = decode_cache.shape[2]
    head_rows = q_width // LANES // DGRP
    own_rows = up16(pair_count * cap)
    own_start = cap * head_rows
    message_rows = own_start + 2 * own_rows
    layout = (cap, head_rows, own_rows, own_start)
    groups = decode_group.reshape(-1)
    prefill_groups = prefix_table.shape[0]
    big = pltpu.CompilerParams(vmem_limit_bytes=60 * 2**20)
    part = pltpu.CompilerParams(vmem_limit_bytes=52 * 2**20)
    small = pltpu.CompilerParams(vmem_limit_bytes=8 * 2**20)

    sending = pl.pallas_call(
        functools.partial(pack_kernel, layout),
        out_shape=jax.ShapeDtypeStruct((decode_groups, DGRP, message_rows, LANES), jnp.bfloat16),
        in_specs=[smem_spec(), vmem_spec(), vmem_spec()],
        out_specs=any_spec(),
        scratch_shapes=[
            pltpu.VMEM((row_count * q_width // LANES, LANES), jnp.float32),
            pltpu.VMEM((DGRP, decode_groups, message_rows, LANES), jnp.bfloat16),
            pltpu.SMEM((decode_groups,), jnp.int32),
            pltpu.SemaphoreType.DMA((DGRP,)),
        ],
        compiler_params=big,
        name="pack",
    )(groups, decode_q, decode_new)
    sending = sending.reshape(devices, message_rows, LANES)

    received = lax.all_to_all(sending, "pool", split_axis=0, concat_axis=0, tiled=True)

    share = jax.ShapeDtypeStruct(
        (PGRP // PLANE, prefill_groups, PCAP, blk, 2 * LANES), jnp.bfloat16
    )
    shares = pl.pallas_call(
        blocks_kernel,
        out_shape=(share,) * PLANE,
        in_specs=[smem_spec(), smem_spec(), any_spec()],
        out_specs=(any_spec(),) * PLANE,
        scratch_shapes=[pltpu.SemaphoreType.DMA((2 * PGRP * PCAP,))],
        compiler_params=big,
        cost_estimate=pl.CostEstimate(flops=100000, bytes_accessed=1000000, transcendentals=0),
        name="blocks",
    )(prefix_table, prefix_count, pool_kv)
    shares = [shares[0]] + [
        lax.ppermute(shares[t], "pool", [(i, i ^ t) for i in range(devices)])
        for t in range(1, PLANE)
    ]
    far_half = pl.pallas_call(
        forward_kernel,
        out_shape=jax.ShapeDtypeStruct((PLANE,) + share.shape[1:], jnp.bfloat16),
        in_specs=[any_spec()] * PLANE,
        out_specs=any_spec(),
        scratch_shapes=[pltpu.SemaphoreType.DMA((PLANE,))],
        compiler_params=small,
        cost_estimate=pl.CostEstimate(flops=100000, bytes_accessed=1000000, transcendentals=0),
        name="forward",
    )(*shares)
    far_half = lax.ppermute(far_half, "pool", [(i, i ^ PLANE) for i in range(devices)])
    bundle = jax.ShapeDtypeStruct((PGRP, PCAP, blk, 2 * LANES), jnp.bfloat16)
    bundles = pl.pallas_call(
        functools.partial(regroup_kernel, prefill_groups),
        out_shape=(bundle,) * prefill_groups,
        in_specs=[any_spec()] * (PLANE + 1),
        out_specs=(any_spec(),) * prefill_groups,
        scratch_shapes=[pltpu.SemaphoreType.DMA((prefill_groups * PGRP,))],
        compiler_params=small,
        cost_estimate=pl.CostEstimate(flops=100000, bytes_accessed=1000000, transcendentals=0),
        name="regroup",
    )(*shares, far_half)

    chunk = min(cap, 4)
    width = 8
    block_count = devices * cap // chunk
    slot_len, listed, prefix_held = pl.pallas_call(
        functools.partial(plan_kernel, cap, chunk, devices),
        out_shape=(
            jax.ShapeDtypeStruct((devices * cap,), jnp.int32),
            jax.ShapeDtypeStruct((block_count + 2,), jnp.int32),
            jax.ShapeDtypeStruct((devices * pool_kv.shape[0],), jnp.int32),
        ),
        in_specs=[smem_spec()] * 4,
        out_specs=(smem_spec(),) * 3,
        compiler_params=small,
        cost_estimate=pl.CostEstimate(flops=1000000, bytes_accessed=4000000, transcendentals=0),
        name="plan",
    )(prefix_table, prefix_count, groups, cached_len)

    received, slot_len, listed, *bundles = lax.optimization_barrier(
        (received, slot_len, listed, *bundles)
    )
    bundles = [bundles[0]] + [
        lax.ppermute(
            bundles[x],
            "pool",
            [(i, (i + x * PGRP) % devices) for i in range(devices)],
        )
        for x in range(1, prefill_groups)
    ]

    answers = pl.pallas_call(
        functools.partial(decode_kernel, layout, chunk, width),
        out_shape=jax.ShapeDtypeStruct((devices, cap * head_rows, LANES), jnp.bfloat16),
        in_specs=[smem_spec(), smem_spec(), vmem_spec(), any_spec()],
        out_specs=vmem_spec(),
        scratch_shapes=[
            pltpu.VMEM((block_count * chunk,) + decode_cache.shape[2:], jnp.bfloat16),
            pltpu.SemaphoreType.DMA((block_count,)),
        ],
        compiler_params=part,
        cost_estimate=pl.CostEstimate(
            flops=500000000, bytes_accessed=8000000, transcendentals=1000000
        ),
        name="decode",
    )(listed, slot_len, received, decode_cache[0])

    answers, *bundles = lax.optimization_barrier((answers, *bundles))
    back = lax.all_to_all(answers, "pool", split_axis=0, concat_axis=0, tiled=True)

    token_count, fill_width = prefill_q.shape[1:]
    prefix = devices * PCAP * blk
    head_count = fill_width // LANES
    prefix_held, _ = lax.optimization_barrier((prefix_held, answers))
    prefill_out = pl.pallas_call(
        functools.partial(prefill_kernel, prefill_groups, min(256, token_count)),
        grid=(head_count,),
        out_shape=jax.ShapeDtypeStruct((token_count, fill_width), jnp.bfloat16),
        in_specs=[smem_spec()]
        + [pl.BlockSpec(bundle.shape, lambda u: (0, 0, 0, 0))] * prefill_groups
        + [
            pl.BlockSpec((token_count, LANES), lambda u: (0, u)),
            pl.BlockSpec(prefill_new_kv.shape[1:], lambda u: (0, 0)),
        ],
        out_specs=pl.BlockSpec((token_count, LANES), lambda u: (0, u)),
        scratch_shapes=[
            pltpu.VMEM((prefix + token_count, LANES), jnp.bfloat16),
            pltpu.VMEM((prefix + token_count, LANES), jnp.bfloat16),
            pltpu.VMEM((8, prefix), jnp.float32),
        ],
        compiler_params=pltpu.CompilerParams(vmem_limit_bytes=16 * 2**20),
        cost_estimate=pl.CostEstimate(
            flops=2 * 2 * token_count * fill_width * (prefix + token_count // 2),
            bytes_accessed=3000000,
            transcendentals=token_count * head_count * (prefix + token_count // 2),
        ),
        name="prefill",
    )(prefix_held, *bundles, prefill_q[0], prefill_new_kv[0])

    decode_out = pl.pallas_call(
        functools.partial(unpack_kernel, cap, head_rows),
        out_shape=jax.ShapeDtypeStruct((row_count, q_width), jnp.bfloat16),
        in_specs=[smem_spec(), vmem_spec()],
        out_specs=vmem_spec(),
        scratch_shapes=[
            pltpu.VMEM((row_count * q_width // LANES, LANES), jnp.float32),
            pltpu.SMEM((decode_groups,), jnp.int32),
        ],
        compiler_params=small,
        name="unpack",
    )(groups, back)
    return (prefill_out[None], decode_out)


def solution(mesh):
    in_specs = (
        P(("rep", "pool"), None, None, None),
        P("rep", None),
        P("rep"),
        P(("rep", "pool"), None, None),
        P(("rep", "pool"), None, None),
        P(("rep", "pool"), None),
        P(("rep", "pool"), None),
        P(("rep", "pool"), None, None, None, None),
        P("rep", None),
        P("rep"),
    )
    out_specs = (P(("rep", "pool"), None, None), P(("rep", "pool"), None))
    return jax.shard_map(shards, mesh=mesh, in_specs=in_specs, out_specs=out_specs, check_vma=False)
```

```python
import functools

import jax
import jax.numpy as jnp
from jax import lax
from jax.experimental import pallas as pl
from jax.experimental.pallas import tpu as pltpu
from jax.sharding import PartitionSpec as P

PGRP = 8
DGRP = 4
PCAP = 2
PLANE = 4
LANES = 128
MASKED = -1e30
LOG2E = 1.4426950408889634


def up16(n):
    return -(-n // 16) * 16


def any_spec():
    return pl.BlockSpec(memory_space=pl.ANY)


def smem_spec():
    return pl.BlockSpec(memory_space=pltpu.SMEM)


def in_hbm(x):
    return pltpu.with_memory_space_constraint(x, pltpu.HBM)


def vmem_spec():
    return pl.BlockSpec(memory_space=pltpu.VMEM)


def pack_kernel(layout, groups, q, kv, out, rows_scr, stage, group_fill, sems):
    cap, head_rows, own_rows, own_start = layout
    decode_groups = out.shape[0]
    row_count = q.shape[0]
    head_total = q.shape[1] // LANES
    pair_count = kv.shape[1] // (2 * LANES * DGRP)
    device = lax.axis_index("pool")
    for a in range(decode_groups):
        group_fill[a] = 0
    for h in range(head_total):
        rows_scr[pl.ds(h, row_count, stride=head_total), :] = q[
            :, h * LANES : (h + 1) * LANES
        ].astype(jnp.float32)
    slot_axis = lax.broadcasted_iota(jnp.int32, (decode_groups * cap, row_count), 0)
    row_axis = lax.broadcasted_iota(jnp.int32, (decode_groups * cap, row_count), 1)
    slot_of_row = jnp.full((decode_groups * cap, row_count), -1, jnp.int32)
    homes = []
    for i in range(row_count):
        a = groups[device * row_count + i]
        c = group_fill[a]
        group_fill[a] = c + 1
        slot_of_row = jnp.where(row_axis == i, a * cap + c, slot_of_row)
        homes.append((a, c))
    pick = (slot_of_row == slot_axis).astype(jnp.bfloat16)
    own = jnp.dot(pick, kv[...], preferred_element_type=jnp.float32)
    blank = jnp.zeros((own_rows - pair_count * cap, LANES), jnp.float32)
    copies = []
    for m in range(DGRP):
        for i, (a, c) in enumerate(homes):
            first = i * head_total + m * head_rows
            stage[m, a, pl.ds(pl.multiple_of(c * head_rows, 16), head_rows), :] = rows_scr[
                first : first + head_rows, :
            ].astype(out.dtype)
        for a in range(decode_groups):
            for part in range(2):
                pieces = []
                for k in range(pair_count):
                    lane = ((m * pair_count + k) * 2 + part) * LANES
                    pieces.append(own[a * cap : (a + 1) * cap, lane : lane + LANES])
                if blank.shape[0]:
                    pieces.append(blank)
                place = own_start + part * own_rows
                stage[m, a, place : place + own_rows, :] = jnp.concatenate(
                    pieces, axis=0
                ).astype(out.dtype)
        copy = pltpu.make_async_copy(stage.at[m], out.at[:, m], sems.at[m])
        copy.start()
        copies.append(copy)
    for copy in copies:
        copy.wait()


def blocks_kernel(table, count, pool, *rest):
    outs, sems = rest[:PLANE], rest[PLANE]
    blocks_here = pool.shape[0]
    group_count, most_blocks = table.shape
    device = lax.axis_index("pool")
    first_block = device * blocks_here
    flying = []
    for g in range(group_count):

        def scan_table(j, carry):
            seen, chosen = carry
            entry = table[g, j]
            mine = (entry >= first_block) & (entry < first_block + blocks_here) & (j < count[g])
            chosen = tuple(
                jnp.where(mine & (seen == k), entry - first_block, chosen[k]) for k in range(PCAP)
            )
            return seen + mine.astype(jnp.int32), chosen

        start = (jnp.int32(0), tuple(jnp.int32(0) for _ in range(PCAP)))
        _, chosen = lax.fori_loop(0, most_blocks, scan_table, start, unroll=8)
        if g >= 2:
            for copy in flying.pop(0):
                copy.wait()
        copies = []
        for t in range(PGRP):
            for k in range(PCAP):
                copy = pltpu.make_async_copy(
                    pool.at[chosen[k], (device % PGRP) ^ t],
                    outs[t % PLANE].at[t // PLANE, g, k],
                    sems.at[((g % 2) * PGRP + t) * PCAP + k],
                )
                copy.start()
                copies.append(copy)
        flying.append(copies)
    for copies in flying:
        for copy in copies:
            copy.wait()


def forward_kernel(*rest):
    held, out, sems = rest[:PLANE], rest[PLANE], rest[PLANE + 1]
    copies = []
    for t in range(PLANE):
        copy = pltpu.make_async_copy(held[t].at[1], out.at[t], sems.at[t])
        copy.start()
        copies.append(copy)
    for copy in copies:
        copy.wait()


def regroup_kernel(group_count, *rest):
    held, crossed = rest[:PLANE], rest[PLANE]
    outs, sems = rest[PLANE + 1 : PLANE + 1 + group_count], rest[-1]
    mine = lax.axis_index("pool") // PGRP
    copies = []
    for x in range(group_count):
        g = (mine + x) % group_count
        for t in range(PLANE):
            for side, source in enumerate((held[t].at[0, g], crossed.at[t, g])):
                place = side * PLANE + t
                copy = pltpu.make_async_copy(source, outs[x].at[place], sems.at[x * PGRP + place])
                copy.start()
                copies.append(copy)
    for copy in copies:
        copy.wait()


def plan_kernel(cap, step, owners, table, count, groups, lengths, slot_len, listed, prefix_held):
    device = lax.axis_index("pool")
    home_count = owners
    row_count = groups.shape[0] // home_count
    group_id = device // DGRP
    prefill_id = device // PGRP
    blocks_here = listed.shape[0]
    most_blocks = table.shape[1]
    chunk = min(cap, step)

    def one_owner(o, carry):
        prefix_held[o] = 0
        return carry

    lax.fori_loop(0, owners, one_owner, 0)
    pool_blocks = prefix_held.shape[0] // owners

    def one_entry(j, carry):
        o = table[prefill_id, j] // pool_blocks
        prefix_held[o] = prefix_held[o] + 1
        return carry

    lax.fori_loop(0, jnp.minimum(count[prefill_id], most_blocks), one_entry, 0)

    def one_home(s, filled):
        for c in range(cap):
            slot_len[s * cap + c] = 0
        here = jnp.int32(0)
        for i in range(row_count):
            row = s * row_count + i
            mine = groups[row] == group_id
            place = s * cap + jnp.minimum(here, cap - 1)
            slot_len[place] = jnp.where(mine, lengths[row], slot_len[place])
            here = here + mine.astype(jnp.int32)
        for b in range(cap // chunk):
            listed[1 + jnp.minimum(filled, blocks_here - 2)] = s * (cap // chunk) + b
            filled = filled + (here > b * chunk).astype(jnp.int32)
        return filled

    listed[0] = lax.fori_loop(0, home_count, one_home, jnp.int32(0))


def decode_kernel(layout, chunk, width, listed, slot_len, recv, cache, out, held, sems):
    cap, head_rows, own_rows, own_start = layout
    pair_count, positions = cache.shape[1], cache.shape[2]
    per_home = cap // chunk
    key_count = pair_count * positions
    query_heads = head_rows // pair_count
    live = listed[0]
    scale = LANES ** (-0.5) * LOG2E
    rows = chunk * head_rows
    slots = width * chunk

    def fetch(i):
        return pltpu.make_async_copy(
            cache.at[pl.ds(listed[1 + i] * chunk, chunk)],
            held.at[pl.ds(i * chunk, chunk)],
            sems.at[i],
        )

    def begin(i, carry):
        fetch(i).start()
        return carry

    lax.fori_loop(0, live, begin, 0)
    row_pair = lax.broadcasted_iota(jnp.int32, (head_rows, key_count), 0) // query_heads
    key_axis = lax.broadcasted_iota(jnp.int32, (head_rows, key_count), 1)
    pos = jnp.where(key_axis // positions == row_pair, key_axis % positions, positions)
    own_axis = lax.broadcasted_iota(jnp.int32, (rows, own_rows), 1)
    own_row = lax.broadcasted_iota(jnp.int32, (rows, own_rows), 0)
    own_want = ((own_row % head_rows) // query_heads) * cap + own_row // head_rows

    def several(t, carry):
        ids = [jnp.minimum(t * width + w, live - 1) for w in range(width)]
        for w in range(width):

            @pl.when(t * width + w < live)
            def _():
                fetch(t * width + w).wait()

        blocks = [listed[1 + i] for i in ids]
        homes = [b // per_home for b in blocks]
        firsts = [(b % per_home) * chunk for b in blocks]
        places = [pl.multiple_of(f * head_rows, 16) for f in firsts]
        q = jnp.concatenate(
            [recv[h, pl.ds(p, rows), :] for h, p in zip(homes, places)], axis=0
        )
        own_keys = jnp.stack([recv[h, own_start : own_start + own_rows, :] for h in homes])
        own_values = jnp.stack(
            [recv[h, own_start + own_rows : own_start + 2 * own_rows, :] for h in homes]
        )
        kv = held[pl.ds(t * slots, slots)]
        keys = kv[..., :LANES].reshape(slots, key_count, LANES)
        values = kv[..., LANES:].reshape(slots, key_count, LANES)
        scores = jnp.einsum(
            "jqd,jkd->jqk",
            q.reshape(slots, head_rows, LANES),
            keys,
            preferred_element_type=jnp.float32,
        )
        kept = jnp.stack(
            [pos < slot_len[blocks[w] * chunk + j] for w in range(width) for j in range(chunk)]
        )
        scores = jnp.where(kept, scores, MASKED)
        own_scores = jnp.einsum(
            "jqd,jkd->jqk",
            q.reshape(width, rows, LANES),
            own_keys,
            preferred_element_type=jnp.float32,
        )
        own_hit = jnp.stack([own_axis == own_want + f for f in firsts])
        own_score = jnp.sum(jnp.where(own_hit, own_scores, 0.0), axis=2, keepdims=True)
        own_score = own_score.reshape(slots, head_rows, 1)
        top = jnp.maximum(jnp.max(scores, axis=2, keepdims=True), own_score)
        weights = jnp.exp2((scores - top) * scale)
        own_weight = jnp.exp2((own_score - top) * scale)
        total = jnp.sum(weights, axis=2, keepdims=True) + own_weight
        mixed = jnp.einsum(
            "jqk,jkd->jqd",
            weights.astype(jnp.bfloat16),
            values,
            preferred_element_type=jnp.float32,
        )
        own_part = jnp.where(own_hit, own_weight.reshape(width, rows, 1), 0.0)
        mixed = mixed.reshape(width, rows, LANES) + jnp.einsum(
            "jqk,jkd->jqd",
            own_part.astype(jnp.bfloat16),
            own_values,
            preferred_element_type=jnp.float32,
        )
        mixed = mixed / total.reshape(width, rows, 1)
        for w in reversed(range(width)):
            out[homes[w], pl.ds(places[w], rows), :] = mixed[w].astype(out.dtype)
        return carry

    lax.fori_loop(0, (live + width - 1) // width, several, 0)


def prefill_kernel(group_count, tile, prefix_held, *rest):
    sources = rest[:group_count]
    q, new_kv, out, keys, values, bias = rest[group_count:]
    blk = sources[0].shape[2]
    prefix = group_count * PGRP * PCAP * blk
    token_count = new_kv.shape[0]
    scale = LANES ** (-0.5) * LOG2E
    device = lax.axis_index("pool")

    @pl.when(pl.program_id(0) == 0)
    def _():
        lane_block = lax.broadcasted_iota(jnp.int32, (8, prefix), 1) // blk
        hide = jnp.zeros((8, prefix), jnp.float32)
        for x in range(group_count):
            sender = (device // PGRP - x + group_count) % group_count
            for t in range(PGRP):
                owner = sender * PGRP + ((device % PGRP) ^ t)
                for k in range(PCAP):
                    ordinal = (x * PGRP + t) * PCAP + k
                    block = sources[x][t, k]
                    keys[ordinal * blk : (ordinal + 1) * blk, :] = block[:, :LANES]
                    values[ordinal * blk : (ordinal + 1) * blk, :] = block[:, LANES:]
                    gone = jnp.where(prefix_held[owner] > k, 0.0, MASKED)
                    hide = jnp.where(lane_block == ordinal, gone, hide)
        bias[...] = hide
        keys[prefix:, :] = new_kv[:, :LANES]
        values[prefix:, :] = new_kv[:, LANES:]

    for t in range(token_count // tile):
        width = prefix + (t + 1) * tile
        block = q[t * tile : (t + 1) * tile, :]
        scores = lax.dot_general(
            block, keys[:width, :], (((1,), (1,)), ((), ())), preferred_element_type=jnp.float32
        )
        causal = lax.broadcasted_iota(jnp.int32, (tile, tile), 0) >= lax.broadcasted_iota(
            jnp.int32, (tile, tile), 1
        )
        pieces = [scores[:, :prefix] + bias[0:1, :]]
        if t:
            pieces.append(scores[:, prefix : width - tile])
        pieces.append(jnp.where(causal, scores[:, width - tile :], MASKED))
        scores = jnp.concatenate(pieces, axis=1)
        top = jnp.max(scores, axis=1, keepdims=True)
        weights = jnp.exp2((scores - top) * scale)
        total = jnp.sum(weights, axis=1, keepdims=True)
        mixed = jnp.dot(
            weights.astype(jnp.bfloat16), values[:width, :], preferred_element_type=jnp.float32
        )
        out[t * tile : (t + 1) * tile, :] = (mixed / total).astype(out.dtype)


def unpack_kernel(cap, head_rows, groups, back, out, rows_scr, group_fill):
    device = lax.axis_index("pool")
    row_count = out.shape[0]
    head_total = out.shape[1] // LANES
    for a in range(back.shape[0] // DGRP):
        group_fill[a] = 0
    for i in range(row_count):
        a = groups[device * row_count + i]
        c = group_fill[a]
        group_fill[a] = c + 1
        for m in range(DGRP):
            first = i * head_total + m * head_rows
            rows_scr[first : first + head_rows, :] = back[
                a * DGRP + m, pl.ds(pl.multiple_of(c * head_rows, 16), head_rows), :
            ].astype(jnp.float32)
    for h in range(head_total):
        out[:, h * LANES : (h + 1) * LANES] = rows_scr[
            pl.ds(h, row_count, stride=head_total), :
        ].astype(out.dtype)


def shards(
    pool_kv,
    prefix_table,
    prefix_count,
    prefill_q,
    prefill_new_kv,
    decode_q,
    decode_new,
    decode_cache,
    decode_group,
    cached_len,
):
    devices = lax.axis_size("pool")
    blk = pool_kv.shape[2]
    row_count, q_width = decode_q.shape
    cap = decode_cache.shape[1] // devices
    decode_groups = devices // DGRP
    pair_count = decode_cache.shape[2]
    head_rows = q_width // LANES // DGRP
    own_rows = up16(pair_count * cap)
    own_start = cap * head_rows
    message_rows = own_start + 2 * own_rows
    layout = (cap, head_rows, own_rows, own_start)
    groups = decode_group.reshape(-1)
    prefill_groups = prefix_table.shape[0]
    big = pltpu.CompilerParams(vmem_limit_bytes=60 * 2**20)
    small = pltpu.CompilerParams(vmem_limit_bytes=8 * 2**20)

    sending = pl.pallas_call(
        functools.partial(pack_kernel, layout),
        out_shape=jax.ShapeDtypeStruct((decode_groups, DGRP, message_rows, LANES), jnp.bfloat16),
        in_specs=[smem_spec(), vmem_spec(), vmem_spec()],
        out_specs=any_spec(),
        scratch_shapes=[
            pltpu.VMEM((row_count * q_width // LANES, LANES), jnp.float32),
            pltpu.VMEM((DGRP, decode_groups, message_rows, LANES), jnp.bfloat16),
            pltpu.SMEM((decode_groups,), jnp.int32),
            pltpu.SemaphoreType.DMA((DGRP,)),
        ],
        compiler_params=big,
        name="pack",
    )(in_hbm(groups), in_hbm(decode_q), in_hbm(decode_new))
    sending = sending.reshape(devices, message_rows, LANES)

    received = lax.all_to_all(sending, "pool", split_axis=0, concat_axis=0, tiled=True)

    share = jax.ShapeDtypeStruct(
        (PGRP // PLANE, prefill_groups, PCAP, blk, 2 * LANES), jnp.bfloat16
    )
    shares = pl.pallas_call(
        blocks_kernel,
        out_shape=(share,) * PLANE,
        in_specs=[smem_spec(), smem_spec(), any_spec()],
        out_specs=(any_spec(),) * PLANE,
        scratch_shapes=[pltpu.SemaphoreType.DMA((2 * PGRP * PCAP,))],
        compiler_params=small,
        cost_estimate=pl.CostEstimate(flops=100000, bytes_accessed=1000000, transcendentals=0),
        name="blocks",
    )(in_hbm(prefix_table), in_hbm(prefix_count), in_hbm(pool_kv))
    shares = [shares[0]] + [
        lax.ppermute(shares[t], "pool", [(i, i ^ t) for i in range(devices)])
        for t in range(1, PLANE)
    ]
    far_half = pl.pallas_call(
        forward_kernel,
        out_shape=jax.ShapeDtypeStruct((PLANE,) + share.shape[1:], jnp.bfloat16),
        in_specs=[any_spec()] * PLANE,
        out_specs=any_spec(),
        scratch_shapes=[pltpu.SemaphoreType.DMA((PLANE,))],
        compiler_params=small,
        cost_estimate=pl.CostEstimate(flops=100000, bytes_accessed=1000000, transcendentals=0),
        name="forward",
    )(*shares)
    far_half = lax.ppermute(far_half, "pool", [(i, i ^ PLANE) for i in range(devices)])
    bundle = jax.ShapeDtypeStruct((PGRP, PCAP, blk, 2 * LANES), jnp.bfloat16)
    bundles = pl.pallas_call(
        functools.partial(regroup_kernel, prefill_groups),
        out_shape=(bundle,) * prefill_groups,
        in_specs=[any_spec()] * (PLANE + 1),
        out_specs=(any_spec(),) * prefill_groups,
        scratch_shapes=[pltpu.SemaphoreType.DMA((prefill_groups * PGRP,))],
        compiler_params=small,
        cost_estimate=pl.CostEstimate(flops=100000, bytes_accessed=1000000, transcendentals=0),
        name="regroup",
    )(*shares, far_half)

    chunk = min(cap, 4)
    width = 8
    block_count = devices * cap // chunk
    slot_len, listed, prefix_held = pl.pallas_call(
        functools.partial(plan_kernel, cap, chunk, devices),
        out_shape=(
            jax.ShapeDtypeStruct((devices * cap,), jnp.int32),
            jax.ShapeDtypeStruct((block_count + 2,), jnp.int32),
            jax.ShapeDtypeStruct((devices * pool_kv.shape[0],), jnp.int32),
        ),
        in_specs=[smem_spec()] * 4,
        out_specs=(smem_spec(),) * 3,
        compiler_params=small,
        cost_estimate=pl.CostEstimate(flops=1000000, bytes_accessed=4000000, transcendentals=0),
        name="plan",
    )(in_hbm(prefix_table), in_hbm(prefix_count), in_hbm(groups), in_hbm(cached_len))

    received, slot_len, listed, *bundles = lax.optimization_barrier(
        (received, slot_len, listed, *bundles)
    )
    bundles = [bundles[0]] + [
        lax.ppermute(
            bundles[x],
            "pool",
            [(i, (i + x * PGRP) % devices) for i in range(devices)],
        )
        for x in range(1, prefill_groups)
    ]

    answers = pl.pallas_call(
        functools.partial(decode_kernel, layout, chunk, width),
        out_shape=jax.ShapeDtypeStruct((devices, cap * head_rows, LANES), jnp.bfloat16),
        in_specs=[smem_spec(), smem_spec(), vmem_spec(), any_spec()],
        out_specs=vmem_spec(),
        scratch_shapes=[
            pltpu.VMEM((block_count * chunk,) + decode_cache.shape[2:], jnp.bfloat16),
            pltpu.SemaphoreType.DMA((block_count,)),
        ],
        compiler_params=pltpu.CompilerParams(vmem_limit_bytes=20 * 2**20),
        cost_estimate=pl.CostEstimate(
            flops=500000000, bytes_accessed=8000000, transcendentals=1000000
        ),
        name="decode",
    )(listed, slot_len, received, in_hbm(decode_cache[0]))

    answers, *bundles = lax.optimization_barrier((answers, *bundles))
    back = lax.all_to_all(answers, "pool", split_axis=0, concat_axis=0, tiled=True)

    token_count, fill_width = prefill_q.shape[1:]
    prefix = devices * PCAP * blk
    head_count = fill_width // LANES
    prefix_held, _ = lax.optimization_barrier((prefix_held, answers))
    prefill_out = pl.pallas_call(
        functools.partial(prefill_kernel, prefill_groups, min(256, token_count)),
        grid=(head_count,),
        out_shape=jax.ShapeDtypeStruct((token_count, fill_width), jnp.bfloat16),
        in_specs=[smem_spec()]
        + [pl.BlockSpec(bundle.shape, lambda u: (0, 0, 0, 0))] * prefill_groups
        + [
            pl.BlockSpec((token_count, LANES), lambda u: (0, u)),
            pl.BlockSpec(prefill_new_kv.shape[1:], lambda u: (0, 0)),
        ],
        out_specs=pl.BlockSpec((token_count, LANES), lambda u: (0, u)),
        scratch_shapes=[
            pltpu.VMEM((prefix + token_count, LANES), jnp.bfloat16),
            pltpu.VMEM((prefix + token_count, LANES), jnp.bfloat16),
            pltpu.VMEM((8, prefix), jnp.float32),
        ],
        compiler_params=pltpu.CompilerParams(vmem_limit_bytes=16 * 2**20),
        cost_estimate=pl.CostEstimate(
            flops=2 * 2 * token_count * fill_width * (prefix + token_count // 2),
            bytes_accessed=3000000,
            transcendentals=token_count * head_count * (prefix + token_count // 2),
        ),
        name="prefill",
    )(prefix_held, *bundles, prefill_q[0], prefill_new_kv[0])

    decode_out = pl.pallas_call(
        functools.partial(unpack_kernel, cap, head_rows),
        out_shape=jax.ShapeDtypeStruct((row_count, q_width), jnp.bfloat16),
        in_specs=[smem_spec(), vmem_spec()],
        out_specs=vmem_spec(),
        scratch_shapes=[
            pltpu.VMEM((row_count * q_width // LANES, LANES), jnp.float32),
            pltpu.SMEM((decode_groups,), jnp.int32),
        ],
        compiler_params=small,
        name="unpack",
    )(in_hbm(groups), back)
    return (prefill_out[None], decode_out)


def solution(mesh):
    in_specs = (
        P(("rep", "pool"), None, None, None),
        P("rep", None),
        P("rep"),
        P(("rep", "pool"), None, None),
        P(("rep", "pool"), None, None),
        P(("rep", "pool"), None),
        P(("rep", "pool"), None),
        P(("rep", "pool"), None, None, None, None),
        P("rep", None),
        P("rep"),
    )
    out_specs = (P(("rep", "pool"), None, None), P(("rep", "pool"), None))
    return jax.shard_map(shards, mesh=mesh, in_specs=in_specs, out_specs=out_specs, check_vma=False)
```

```python
import functools

import jax
import jax.numpy as jnp
from jax import lax
from jax.experimental import pallas as pl
from jax.experimental.pallas import tpu as pltpu
from jax.sharding import PartitionSpec as P

PGRP = 8
DGRP = 4
PCAP = 2
PLANE = 4
LANES = 128
MASKED = -1e30
LOG2E = 1.4426950408889634


def up16(n):
    return -(-n // 16) * 16


def any_spec():
    return pl.BlockSpec(memory_space=pl.ANY)


def smem_spec():
    return pl.BlockSpec(memory_space=pltpu.SMEM)


def in_hbm(x):
    return pltpu.with_memory_space_constraint(x, pltpu.HBM)


def vmem_spec():
    return pl.BlockSpec(memory_space=pltpu.VMEM)


def pack_kernel(layout, groups, q, kv, out, rows_scr, stage, group_fill, sems):
    cap, head_rows, own_rows, own_start = layout
    decode_groups = out.shape[0]
    row_count = q.shape[0]
    head_total = q.shape[1] // LANES
    pair_count = kv.shape[1] // (2 * LANES * DGRP)
    device = lax.axis_index("pool")
    for a in range(decode_groups):
        group_fill[a] = 0
    for h in range(head_total):
        rows_scr[pl.ds(h, row_count, stride=head_total), :] = q[
            :, h * LANES : (h + 1) * LANES
        ].astype(jnp.float32)
    slot_axis = lax.broadcasted_iota(jnp.int32, (decode_groups * cap, row_count), 0)
    row_axis = lax.broadcasted_iota(jnp.int32, (decode_groups * cap, row_count), 1)
    slot_of_row = jnp.full((decode_groups * cap, row_count), -1, jnp.int32)
    homes = []
    for i in range(row_count):
        a = groups[device * row_count + i]
        c = group_fill[a]
        group_fill[a] = c + 1
        slot_of_row = jnp.where(row_axis == i, a * cap + c, slot_of_row)
        homes.append((a, c))
    pick = (slot_of_row == slot_axis).astype(jnp.bfloat16)
    own = jnp.dot(pick, kv[...], preferred_element_type=jnp.float32)
    blank = jnp.zeros((own_rows - pair_count * cap, LANES), jnp.float32)
    copies = []
    for m in range(DGRP):
        for i, (a, c) in enumerate(homes):
            first = i * head_total + m * head_rows
            stage[m, a, pl.ds(pl.multiple_of(c * head_rows, 16), head_rows), :] = rows_scr[
                first : first + head_rows, :
            ].astype(out.dtype)
        for a in range(decode_groups):
            for part in range(2):
                pieces = []
                for k in range(pair_count):
                    lane = ((m * pair_count + k) * 2 + part) * LANES
                    pieces.append(own[a * cap : (a + 1) * cap, lane : lane + LANES])
                if blank.shape[0]:
                    pieces.append(blank)
                place = own_start + part * own_rows
                stage[m, a, place : place + own_rows, :] = jnp.concatenate(
                    pieces, axis=0
                ).astype(out.dtype)
        copy = pltpu.make_async_copy(stage.at[m], out.at[:, m], sems.at[m])
        copy.start()
        copies.append(copy)
    for copy in copies:
        copy.wait()


def blocks_kernel(table, count, pool, *rest):
    outs, sems = rest[:PLANE], rest[PLANE]
    blocks_here = pool.shape[0]
    group_count, most_blocks = table.shape
    device = lax.axis_index("pool")
    first_block = device * blocks_here
    flying = []
    for g in range(group_count):

        def scan_table(j, carry):
            seen, chosen = carry
            entry = table[g, j]
            mine = (entry >= first_block) & (entry < first_block + blocks_here) & (j < count[g])
            chosen = tuple(
                jnp.where(mine & (seen == k), entry - first_block, chosen[k]) for k in range(PCAP)
            )
            return seen + mine.astype(jnp.int32), chosen

        start = (jnp.int32(0), tuple(jnp.int32(0) for _ in range(PCAP)))
        _, chosen = lax.fori_loop(0, most_blocks, scan_table, start, unroll=8)
        if g >= 2:
            for copy in flying.pop(0):
                copy.wait()
        copies = []
        for half in range(PGRP // PLANE):
            for t in range(PLANE):
                for k in range(PCAP):
                    copy = pltpu.make_async_copy(
                        pool.at[chosen[k], half * PLANE + ((device % PLANE) ^ t)],
                        outs[t].at[half, g, k],
                        sems.at[((g % 2) * PGRP + half * PLANE + t) * PCAP + k],
                    )
                    copy.start()
                    copies.append(copy)
        flying.append(copies)
    for copies in flying:
        for copy in copies:
            copy.wait()


def partner(plane, step, planes):
    return plane ^ step if planes & (planes - 1) == 0 else (plane + step) % planes


def regroup_kernel(planes, *rest):
    held, outs, sems = rest[:PLANE], rest[PLANE:-1], rest[-1]
    mine = lax.axis_index("pool") // PLANE
    per_group = PGRP // PLANE
    copies = []
    for step in range(planes):
        there = partner(mine, step, planes)
        for t in range(PLANE):
            copy = pltpu.make_async_copy(
                held[t].at[there % per_group, there // per_group],
                outs[step].at[t],
                sems.at[step * PLANE + t],
            )
            copy.start()
            copies.append(copy)
    for copy in copies:
        copy.wait()


def plan_kernel(cap, step, owners, table, count, groups, lengths, slot_len, listed, prefix_held):
    device = lax.axis_index("pool")
    home_count = owners
    row_count = groups.shape[0] // home_count
    group_id = device // DGRP
    prefill_id = device // PGRP
    blocks_here = listed.shape[0]
    most_blocks = table.shape[1]
    chunk = min(cap, step)

    def one_owner(o, carry):
        prefix_held[o] = 0
        return carry

    lax.fori_loop(0, owners, one_owner, 0)
    pool_blocks = prefix_held.shape[0] // owners

    def one_entry(j, carry):
        o = table[prefill_id, j] // pool_blocks
        prefix_held[o] = prefix_held[o] + 1
        return carry

    lax.fori_loop(0, jnp.minimum(count[prefill_id], most_blocks), one_entry, 0)

    def one_home(s, filled):
        for c in range(cap):
            slot_len[s * cap + c] = 0
        here = jnp.int32(0)
        for i in range(row_count):
            row = s * row_count + i
            mine = groups[row] == group_id
            place = s * cap + jnp.minimum(here, cap - 1)
            slot_len[place] = jnp.where(mine, lengths[row], slot_len[place])
            here = here + mine.astype(jnp.int32)
        for b in range(cap // chunk):
            listed[1 + jnp.minimum(filled, blocks_here - 2)] = s * (cap // chunk) + b
            filled = filled + (here > b * chunk).astype(jnp.int32)
        return filled

    listed[0] = lax.fori_loop(0, home_count, one_home, jnp.int32(0))


def decode_kernel(layout, chunk, width, listed, slot_len, recv, cache, out, held, sems):
    cap, head_rows, own_rows, own_start = layout
    pair_count, positions = cache.shape[1], cache.shape[2]
    per_home = cap // chunk
    key_count = pair_count * positions
    query_heads = head_rows // pair_count
    live = listed[0]
    scale = LANES ** (-0.5) * LOG2E
    rows = chunk * head_rows
    slots = width * chunk

    def fetch(i):
        return pltpu.make_async_copy(
            cache.at[pl.ds(listed[1 + i] * chunk, chunk)],
            held.at[pl.ds(i * chunk, chunk)],
            sems.at[i],
        )

    def begin(i, carry):
        fetch(i).start()
        return carry

    lax.fori_loop(0, live, begin, 0)
    row_pair = lax.broadcasted_iota(jnp.int32, (head_rows, key_count), 0) // query_heads
    key_axis = lax.broadcasted_iota(jnp.int32, (head_rows, key_count), 1)
    pos = jnp.where(key_axis // positions == row_pair, key_axis % positions, positions)
    own_axis = lax.broadcasted_iota(jnp.int32, (rows, own_rows), 1)
    own_row = lax.broadcasted_iota(jnp.int32, (rows, own_rows), 0)
    own_want = ((own_row % head_rows) // query_heads) * cap + own_row // head_rows

    def several(t, carry):
        ids = [jnp.minimum(t * width + w, live - 1) for w in range(width)]
        for w in range(width):

            @pl.when(t * width + w < live)
            def _():
                fetch(t * width + w).wait()

        blocks = [listed[1 + i] for i in ids]
        homes = [b // per_home for b in blocks]
        firsts = [(b % per_home) * chunk for b in blocks]
        places = [pl.multiple_of(f * head_rows, 16) for f in firsts]
        q = jnp.concatenate(
            [recv[h, pl.ds(p, rows), :] for h, p in zip(homes, places)], axis=0
        )
        own_keys = jnp.stack([recv[h, own_start : own_start + own_rows, :] for h in homes])
        own_values = jnp.stack(
            [recv[h, own_start + own_rows : own_start + 2 * own_rows, :] for h in homes]
        )
        kv = held[pl.ds(t * slots, slots)]
        keys = kv[..., :LANES].reshape(slots, key_count, LANES)
        values = kv[..., LANES:].reshape(slots, key_count, LANES)
        scores = jnp.einsum(
            "jqd,jkd->jqk",
            q.reshape(slots, head_rows, LANES),
            keys,
            preferred_element_type=jnp.float32,
        )
        kept = jnp.stack(
            [pos < slot_len[blocks[w] * chunk + j] for w in range(width) for j in range(chunk)]
        )
        scores = jnp.where(kept, scores, MASKED)
        own_scores = jnp.einsum(
            "jqd,jkd->jqk",
            q.reshape(width, rows, LANES),
            own_keys,
            preferred_element_type=jnp.float32,
        )
        own_hit = jnp.stack([own_axis == own_want + f for f in firsts])
        own_score = jnp.sum(jnp.where(own_hit, own_scores, 0.0), axis=2, keepdims=True)
        own_score = own_score.reshape(slots, head_rows, 1)
        top = jnp.maximum(jnp.max(scores, axis=2, keepdims=True), own_score)
        weights = jnp.exp2((scores - top) * scale)
        own_weight = jnp.exp2((own_score - top) * scale)
        total = jnp.sum(weights, axis=2, keepdims=True) + own_weight
        mixed = jnp.einsum(
            "jqk,jkd->jqd",
            weights.astype(jnp.bfloat16),
            values,
            preferred_element_type=jnp.float32,
        )
        own_part = jnp.where(own_hit, own_weight.reshape(width, rows, 1), 0.0)
        mixed = mixed.reshape(width, rows, LANES) + jnp.einsum(
            "jqk,jkd->jqd",
            own_part.astype(jnp.bfloat16),
            own_values,
            preferred_element_type=jnp.float32,
        )
        mixed = mixed / total.reshape(width, rows, 1)
        for w in reversed(range(width)):
            out[homes[w], pl.ds(places[w], rows), :] = mixed[w].astype(out.dtype)
        return carry

    lax.fori_loop(0, (live + width - 1) // width, several, 0)


def prefill_kernel(planes, tile, prefix_held, *rest):
    sources = rest[:planes]
    q, new_kv, out, keys, values, bias = rest[planes:]
    blk = sources[0].shape[2]
    prefix = planes * PLANE * PCAP * blk
    token_count = new_kv.shape[0]
    scale = LANES ** (-0.5) * LOG2E
    device = lax.axis_index("pool")

    @pl.when(pl.program_id(0) == 0)
    def _():
        lane_block = lax.broadcasted_iota(jnp.int32, (8, prefix), 1) // blk
        hide = jnp.zeros((8, prefix), jnp.float32)
        for step in range(planes):
            sender = device // PLANE
            sender = sender ^ step if planes & (planes - 1) == 0 else (sender + planes - step) % planes
            for t in range(PLANE):
                owner = sender * PLANE + ((device % PLANE) ^ t)
                for k in range(PCAP):
                    ordinal = (step * PLANE + t) * PCAP + k
                    block = sources[step][t, k]
                    keys[ordinal * blk : (ordinal + 1) * blk, :] = block[:, :LANES]
                    values[ordinal * blk : (ordinal + 1) * blk, :] = block[:, LANES:]
                    gone = jnp.where(prefix_held[owner] > k, 0.0, MASKED)
                    hide = jnp.where(lane_block == ordinal, gone, hide)
        bias[...] = hide
        keys[prefix:, :] = new_kv[:, :LANES]
        values[prefix:, :] = new_kv[:, LANES:]

    for t in range(token_count // tile):
        width = prefix + (t + 1) * tile
        block = q[t * tile : (t + 1) * tile, :]
        scores = lax.dot_general(
            block, keys[:width, :], (((1,), (1,)), ((), ())), preferred_element_type=jnp.float32
        )
        causal = lax.broadcasted_iota(jnp.int32, (tile, tile), 0) >= lax.broadcasted_iota(
            jnp.int32, (tile, tile), 1
        )
        pieces = [scores[:, :prefix] + bias[0:1, :]]
        if t:
            pieces.append(scores[:, prefix : width - tile])
        pieces.append(jnp.where(causal, scores[:, width - tile :], MASKED))
        scores = jnp.concatenate(pieces, axis=1)
        top = jnp.max(scores, axis=1, keepdims=True)
        weights = jnp.exp2((scores - top) * scale)
        total = jnp.sum(weights, axis=1, keepdims=True)
        mixed = jnp.dot(
            weights.astype(jnp.bfloat16), values[:width, :], preferred_element_type=jnp.float32
        )
        out[t * tile : (t + 1) * tile, :] = (mixed / total).astype(out.dtype)


def unpack_kernel(cap, head_rows, groups, back, out, rows_scr, group_fill):
    device = lax.axis_index("pool")
    row_count = out.shape[0]
    head_total = out.shape[1] // LANES
    for a in range(back.shape[0] // DGRP):
        group_fill[a] = 0
    for i in range(row_count):
        a = groups[device * row_count + i]
        c = group_fill[a]
        group_fill[a] = c + 1
        for m in range(DGRP):
            first = i * head_total + m * head_rows
            rows_scr[first : first + head_rows, :] = back[
                a * DGRP + m, pl.ds(pl.multiple_of(c * head_rows, 16), head_rows), :
            ].astype(jnp.float32)
    for h in range(head_total):
        out[:, h * LANES : (h + 1) * LANES] = rows_scr[
            pl.ds(h, row_count, stride=head_total), :
        ].astype(out.dtype)


def shards(
    pool_kv,
    prefix_table,
    prefix_count,
    prefill_q,
    prefill_new_kv,
    decode_q,
    decode_new,
    decode_cache,
    decode_group,
    cached_len,
):
    devices = lax.axis_size("pool")
    blk = pool_kv.shape[2]
    row_count, q_width = decode_q.shape
    cap = decode_cache.shape[1] // devices
    decode_groups = devices // DGRP
    pair_count = decode_cache.shape[2]
    head_rows = q_width // LANES // DGRP
    own_rows = up16(pair_count * cap)
    own_start = cap * head_rows
    message_rows = own_start + 2 * own_rows
    layout = (cap, head_rows, own_rows, own_start)
    groups = decode_group.reshape(-1)
    prefill_groups = prefix_table.shape[0]
    big = pltpu.CompilerParams(vmem_limit_bytes=60 * 2**20)
    small = pltpu.CompilerParams(vmem_limit_bytes=8 * 2**20)

    sending = pl.pallas_call(
        functools.partial(pack_kernel, layout),
        out_shape=jax.ShapeDtypeStruct((decode_groups, DGRP, message_rows, LANES), jnp.bfloat16),
        in_specs=[smem_spec(), vmem_spec(), vmem_spec()],
        out_specs=any_spec(),
        scratch_shapes=[
            pltpu.VMEM((row_count * q_width // LANES, LANES), jnp.float32),
            pltpu.VMEM((DGRP, decode_groups, message_rows, LANES), jnp.bfloat16),
            pltpu.SMEM((decode_groups,), jnp.int32),
            pltpu.SemaphoreType.DMA((DGRP,)),
        ],
        compiler_params=big,
        name="pack",
    )(in_hbm(groups), in_hbm(decode_q), in_hbm(decode_new))
    sending = sending.reshape(devices, message_rows, LANES)

    received = lax.all_to_all(sending, "pool", split_axis=0, concat_axis=0, tiled=True)

    share = jax.ShapeDtypeStruct(
        (PGRP // PLANE, prefill_groups, PCAP, blk, 2 * LANES), jnp.bfloat16
    )
    shares = pl.pallas_call(
        blocks_kernel,
        out_shape=(share,) * PLANE,
        in_specs=[smem_spec(), smem_spec(), any_spec()],
        out_specs=(any_spec(),) * PLANE,
        scratch_shapes=[pltpu.SemaphoreType.DMA((2 * PGRP * PCAP,))],
        compiler_params=small,
        cost_estimate=pl.CostEstimate(flops=100000, bytes_accessed=1000000, transcendentals=0),
        name="blocks",
    )(in_hbm(prefix_table), in_hbm(prefix_count), in_hbm(pool_kv))
    shares = [shares[0]] + [
        lax.ppermute(shares[t], "pool", [(i, i ^ t) for i in range(devices)])
        for t in range(1, PLANE)
    ]
    chunk = min(cap, 4)
    width = 8
    block_count = devices * cap // chunk
    slot_len, listed, prefix_held = pl.pallas_call(
        functools.partial(plan_kernel, cap, chunk, devices),
        out_shape=(
            jax.ShapeDtypeStruct((devices * cap,), jnp.int32),
            jax.ShapeDtypeStruct((block_count + 2,), jnp.int32),
            jax.ShapeDtypeStruct((devices * pool_kv.shape[0],), jnp.int32),
        ),
        in_specs=[smem_spec()] * 4,
        out_specs=(smem_spec(),) * 3,
        compiler_params=small,
        cost_estimate=pl.CostEstimate(flops=1000000, bytes_accessed=4000000, transcendentals=0),
        name="plan",
    )(in_hbm(prefix_table), in_hbm(prefix_count), in_hbm(groups), in_hbm(cached_len))

    *shares, slot_len, listed = lax.optimization_barrier((*shares, slot_len, listed))
    planes = devices // PLANE
    bundle = jax.ShapeDtypeStruct((PLANE, PCAP, blk, 2 * LANES), jnp.bfloat16)
    bundles = pl.pallas_call(
        functools.partial(regroup_kernel, planes),
        out_shape=(bundle,) * planes,
        in_specs=[any_spec()] * PLANE,
        out_specs=(any_spec(),) * planes,
        scratch_shapes=[pltpu.SemaphoreType.DMA((planes * PLANE,))],
        compiler_params=small,
        cost_estimate=pl.CostEstimate(flops=100000, bytes_accessed=1000000, transcendentals=0),
        name="regroup",
    )(*shares)

    def along_line(step):
        pairs = [
            (i, partner(i // PLANE, step, planes) * PLANE + i % PLANE) for i in range(devices)
        ]
        return lax.ppermute(bundles[step], "pool", pairs)

    lines = [bundles[0], along_line(1)]

    lines += [along_line(step) for step in range(2, planes)]

    answers = pl.pallas_call(
        functools.partial(decode_kernel, layout, chunk, width),
        out_shape=jax.ShapeDtypeStruct((devices, cap * head_rows, LANES), jnp.bfloat16),
        in_specs=[smem_spec(), smem_spec(), vmem_spec(), any_spec()],
        out_specs=vmem_spec(),
        scratch_shapes=[
            pltpu.VMEM((block_count * chunk,) + decode_cache.shape[2:], jnp.bfloat16),
            pltpu.SemaphoreType.DMA((block_count,)),
        ],
        compiler_params=pltpu.CompilerParams(vmem_limit_bytes=20 * 2**20),
        cost_estimate=pl.CostEstimate(
            flops=500000000, bytes_accessed=8000000, transcendentals=1000000
        ),
        name="decode",
    )(listed, slot_len, received, in_hbm(decode_cache[0]))

    answers, *lines = lax.optimization_barrier((answers, *lines))
    back = lax.all_to_all(answers, "pool", split_axis=0, concat_axis=0, tiled=True)

    token_count, fill_width = prefill_q.shape[1:]
    prefix = devices * PCAP * blk
    head_count = fill_width // LANES
    prefix_held, _ = lax.optimization_barrier((prefix_held, answers))
    prefill_out = pl.pallas_call(
        functools.partial(prefill_kernel, planes, min(256, token_count)),
        grid=(head_count,),
        out_shape=jax.ShapeDtypeStruct((token_count, fill_width), jnp.bfloat16),
        in_specs=[smem_spec()]
        + [pl.BlockSpec(bundle.shape, lambda u: (0, 0, 0, 0))] * planes
        + [
            pl.BlockSpec((token_count, LANES), lambda u: (0, u)),
            pl.BlockSpec(prefill_new_kv.shape[1:], lambda u: (0, 0)),
        ],
        out_specs=pl.BlockSpec((token_count, LANES), lambda u: (0, u)),
        scratch_shapes=[
            pltpu.VMEM((prefix + token_count, LANES), jnp.bfloat16),
            pltpu.VMEM((prefix + token_count, LANES), jnp.bfloat16),
            pltpu.VMEM((8, prefix), jnp.float32),
        ],
        compiler_params=pltpu.CompilerParams(vmem_limit_bytes=16 * 2**20),
        cost_estimate=pl.CostEstimate(
            flops=2 * 2 * token_count * fill_width * (prefix + token_count // 2),
            bytes_accessed=3000000,
            transcendentals=token_count * head_count * (prefix + token_count // 2),
        ),
        name="prefill",
    )(prefix_held, *lines, prefill_q[0], prefill_new_kv[0])

    decode_out = pl.pallas_call(
        functools.partial(unpack_kernel, cap, head_rows),
        out_shape=jax.ShapeDtypeStruct((row_count, q_width), jnp.bfloat16),
        in_specs=[smem_spec(), vmem_spec()],
        out_specs=vmem_spec(),
        scratch_shapes=[
            pltpu.VMEM((row_count * q_width // LANES, LANES), jnp.float32),
            pltpu.SMEM((decode_groups,), jnp.int32),
        ],
        compiler_params=small,
        name="unpack",
    )(in_hbm(groups), back)
    return (prefill_out[None], decode_out)


def solution(mesh):
    in_specs = (
        P(("rep", "pool"), None, None, None),
        P("rep", None),
        P("rep"),
        P(("rep", "pool"), None, None),
        P(("rep", "pool"), None, None),
        P(("rep", "pool"), None),
        P(("rep", "pool"), None),
        P(("rep", "pool"), None, None, None, None),
        P("rep", None),
        P("rep"),
    )
    out_specs = (P(("rep", "pool"), None, None), P(("rep", "pool"), None))
    return jax.shard_map(shards, mesh=mesh, in_specs=in_specs, out_specs=out_specs, check_vma=False)
```

```python
import functools

import jax
import jax.numpy as jnp
from jax import lax
from jax.experimental import pallas as pl
from jax.experimental.pallas import tpu as pltpu
from jax.sharding import PartitionSpec as P

PGRP = 8
DGRP = 4
PCAP = 2
PLANE = 4
LANES = 128
MASKED = -1e30
LOG2E = 1.4426950408889634


def up16(n):
    return -(-n // 16) * 16


def any_spec():
    return pl.BlockSpec(memory_space=pl.ANY)


def smem_spec():
    return pl.BlockSpec(memory_space=pltpu.SMEM)


def in_hbm(x):
    return pltpu.with_memory_space_constraint(x, pltpu.HBM)


def vmem_spec():
    return pl.BlockSpec(memory_space=pltpu.VMEM)


def pack_kernel(layout, groups, q, kv, out, rows_scr, stage, group_fill, sems):
    cap, head_rows, own_rows, own_start = layout
    decode_groups = out.shape[0]
    row_count = q.shape[0]
    head_total = q.shape[1] // LANES
    pair_count = kv.shape[1] // (2 * LANES * DGRP)
    device = lax.axis_index("pool")
    for a in range(decode_groups):
        group_fill[a] = 0
    for h in range(head_total):
        rows_scr[pl.ds(h, row_count, stride=head_total), :] = q[
            :, h * LANES : (h + 1) * LANES
        ].astype(jnp.float32)
    slot_axis = lax.broadcasted_iota(jnp.int32, (decode_groups * cap, row_count), 0)
    row_axis = lax.broadcasted_iota(jnp.int32, (decode_groups * cap, row_count), 1)
    slot_of_row = jnp.full((decode_groups * cap, row_count), -1, jnp.int32)
    homes = []
    for i in range(row_count):
        a = groups[device * row_count + i]
        c = group_fill[a]
        group_fill[a] = c + 1
        slot_of_row = jnp.where(row_axis == i, a * cap + c, slot_of_row)
        homes.append((a, c))
    pick = (slot_of_row == slot_axis).astype(jnp.bfloat16)
    own = jnp.dot(pick, kv[...], preferred_element_type=jnp.float32)
    blank = jnp.zeros((own_rows - pair_count * cap, LANES), jnp.float32)
    copies = []
    for m in range(DGRP):
        for i, (a, c) in enumerate(homes):
            first = i * head_total + m * head_rows
            stage[m, a, pl.ds(pl.multiple_of(c * head_rows, 16), head_rows), :] = rows_scr[
                first : first + head_rows, :
            ].astype(out.dtype)
        for a in range(decode_groups):
            for part in range(2):
                pieces = []
                for k in range(pair_count):
                    lane = ((m * pair_count + k) * 2 + part) * LANES
                    pieces.append(own[a * cap : (a + 1) * cap, lane : lane + LANES])
                if blank.shape[0]:
                    pieces.append(blank)
                place = own_start + part * own_rows
                stage[m, a, place : place + own_rows, :] = jnp.concatenate(
                    pieces, axis=0
                ).astype(out.dtype)
        copy = pltpu.make_async_copy(stage.at[m], out.at[:, m], sems.at[m])
        copy.start()
        copies.append(copy)
    for copy in copies:
        copy.wait()


def blocks_kernel(table, count, pool, *rest):
    outs, sems = rest[:PLANE], rest[PLANE]
    blocks_here = pool.shape[0]
    group_count, most_blocks = table.shape
    device = lax.axis_index("pool")
    first_block = device * blocks_here
    flying = []
    for g in range(group_count):

        def scan_table(j, carry):
            seen, chosen = carry
            entry = table[g, j]
            mine = (entry >= first_block) & (entry < first_block + blocks_here) & (j < count[g])
            chosen = tuple(
                jnp.where(mine & (seen == k), entry - first_block, chosen[k]) for k in range(PCAP)
            )
            return seen + mine.astype(jnp.int32), chosen

        start = (jnp.int32(0), tuple(jnp.int32(0) for _ in range(PCAP)))
        _, chosen = lax.fori_loop(0, most_blocks, scan_table, start, unroll=8)
        if g >= 2:
            for copy in flying.pop(0):
                copy.wait()
        copies = []
        for half in range(PGRP // PLANE):
            for t in range(PLANE):
                for k in range(PCAP):
                    copy = pltpu.make_async_copy(
                        pool.at[chosen[k], half * PLANE + ((device % PLANE) ^ t)],
                        outs[t].at[half, g, k],
                        sems.at[((g % 2) * PGRP + half * PLANE + t) * PCAP + k],
                    )
                    copy.start()
                    copies.append(copy)
        flying.append(copies)
    for copies in flying:
        for copy in copies:
            copy.wait()


def partner(plane, step, planes):
    return plane ^ step if planes & (planes - 1) == 0 else (plane + step) % planes


def regroup_kernel(planes, *rest):
    held, outs, sems = rest[:PLANE], rest[PLANE:-1], rest[-1]
    mine = lax.axis_index("pool") // PLANE
    per_group = PGRP // PLANE
    copies = []
    for step in range(planes):
        there = partner(mine, step, planes)
        for t in range(PLANE):
            copy = pltpu.make_async_copy(
                held[t].at[there % per_group, there // per_group],
                outs[step].at[t],
                sems.at[step * PLANE + t],
            )
            copy.start()
            copies.append(copy)
    for copy in copies:
        copy.wait()


def plan_kernel(cap, step, owners, table, count, groups, lengths, slot_len, listed, prefix_held):
    device = lax.axis_index("pool")
    home_count = owners
    row_count = groups.shape[0] // home_count
    group_id = device // DGRP
    prefill_id = device // PGRP
    blocks_here = listed.shape[0]
    most_blocks = table.shape[1]
    chunk = min(cap, step)

    def one_owner(o, carry):
        prefix_held[o] = 0
        return carry

    lax.fori_loop(0, owners, one_owner, 0)
    pool_blocks = prefix_held.shape[0] // owners

    def one_entry(j, carry):
        o = table[prefill_id, j] // pool_blocks
        prefix_held[o] = prefix_held[o] + 1
        return carry

    lax.fori_loop(0, jnp.minimum(count[prefill_id], most_blocks), one_entry, 0)

    def one_home(s, filled):
        for c in range(cap):
            slot_len[s * cap + c] = 0
        here = jnp.int32(0)
        for i in range(row_count):
            row = s * row_count + i
            mine = groups[row] == group_id
            place = s * cap + jnp.minimum(here, cap - 1)
            slot_len[place] = jnp.where(mine, lengths[row], slot_len[place])
            here = here + mine.astype(jnp.int32)
        for b in range(cap // chunk):
            listed[1 + jnp.minimum(filled, blocks_here - 2)] = s * (cap // chunk) + b
            filled = filled + (here > b * chunk).astype(jnp.int32)
        return filled

    listed[0] = lax.fori_loop(0, home_count, one_home, jnp.int32(0))


def decode_kernel(layout, chunk, width, listed, slot_len, recv, cache, out, held, sems):
    cap, head_rows, own_rows, own_start = layout
    pair_count, positions = cache.shape[1], cache.shape[2]
    per_home = cap // chunk
    key_count = pair_count * positions
    query_heads = head_rows // pair_count
    live = listed[0]
    scale = LANES ** (-0.5) * LOG2E
    rows = chunk * head_rows
    slots = width * chunk

    def fetch(i):
        return pltpu.make_async_copy(
            cache.at[pl.ds(listed[1 + i] * chunk, chunk)],
            held.at[pl.ds(i * chunk, chunk)],
            sems.at[i],
        )

    def begin(i, carry):
        fetch(i).start()
        return carry

    lax.fori_loop(0, live, begin, 0)
    row_pair = lax.broadcasted_iota(jnp.int32, (head_rows, key_count), 0) // query_heads
    key_axis = lax.broadcasted_iota(jnp.int32, (head_rows, key_count), 1)
    pos = jnp.where(key_axis // positions == row_pair, key_axis % positions, positions)
    own_axis = lax.broadcasted_iota(jnp.int32, (rows, own_rows), 1)
    own_row = lax.broadcasted_iota(jnp.int32, (rows, own_rows), 0)
    own_want = ((own_row % head_rows) // query_heads) * cap + own_row // head_rows

    def several(t, carry):
        ids = [jnp.minimum(t * width + w, live - 1) for w in range(width)]
        for w in range(width):

            @pl.when(t * width + w < live)
            def _():
                fetch(t * width + w).wait()

        blocks = [listed[1 + i] for i in ids]
        homes = [b // per_home for b in blocks]
        firsts = [(b % per_home) * chunk for b in blocks]
        places = [pl.multiple_of(f * head_rows, 16) for f in firsts]
        q = jnp.concatenate(
            [recv[h, pl.ds(p, rows), :] for h, p in zip(homes, places)], axis=0
        )
        own_keys = jnp.stack([recv[h, own_start : own_start + own_rows, :] for h in homes])
        own_values = jnp.stack(
            [recv[h, own_start + own_rows : own_start + 2 * own_rows, :] for h in homes]
        )
        kv = held[pl.ds(t * slots, slots)]
        keys = kv[..., :LANES].reshape(slots, key_count, LANES)
        values = kv[..., LANES:].reshape(slots, key_count, LANES)
        scores = jnp.einsum(
            "jqd,jkd->jqk",
            q.reshape(slots, head_rows, LANES),
            keys,
            preferred_element_type=jnp.float32,
        )
        kept = jnp.stack(
            [pos < slot_len[blocks[w] * chunk + j] for w in range(width) for j in range(chunk)]
        )
        scores = jnp.where(kept, scores, MASKED)
        own_scores = jnp.einsum(
            "jqd,jkd->jqk",
            q.reshape(width, rows, LANES),
            own_keys,
            preferred_element_type=jnp.float32,
        )
        own_hit = jnp.stack([own_axis == own_want + f for f in firsts])
        own_score = jnp.sum(jnp.where(own_hit, own_scores, 0.0), axis=2, keepdims=True)
        own_score = own_score.reshape(slots, head_rows, 1)
        top = jnp.maximum(jnp.max(scores, axis=2, keepdims=True), own_score)
        weights = jnp.exp2((scores - top) * scale)
        own_weight = jnp.exp2((own_score - top) * scale)
        total = jnp.sum(weights, axis=2, keepdims=True) + own_weight
        mixed = jnp.einsum(
            "jqk,jkd->jqd",
            weights.astype(jnp.bfloat16),
            values,
            preferred_element_type=jnp.float32,
        )
        own_part = jnp.where(own_hit, own_weight.reshape(width, rows, 1), 0.0)
        mixed = mixed.reshape(width, rows, LANES) + jnp.einsum(
            "jqk,jkd->jqd",
            own_part.astype(jnp.bfloat16),
            own_values,
            preferred_element_type=jnp.float32,
        )
        mixed = mixed / total.reshape(width, rows, 1)
        for w in reversed(range(width)):
            out[homes[w], pl.ds(places[w], rows), :] = mixed[w].astype(out.dtype)
        return carry

    lax.fori_loop(0, (live + width - 1) // width, several, 0)


def prefill_kernel(planes, tile, prefix_held, *rest):
    sources = rest[:planes]
    q, new_kv, out, keys, values, bias = rest[planes:]
    blk = sources[0].shape[2]
    prefix = planes * PLANE * PCAP * blk
    token_count = new_kv.shape[0]
    scale = LANES ** (-0.5) * LOG2E
    device = lax.axis_index("pool")

    @pl.when(pl.program_id(0) == 0)
    def _():
        lane_block = lax.broadcasted_iota(jnp.int32, (8, prefix), 1) // blk
        hide = jnp.zeros((8, prefix), jnp.float32)
        for step in range(planes):
            sender = device // PLANE
            sender = sender ^ step if planes & (planes - 1) == 0 else (sender + planes - step) % planes
            for t in range(PLANE):
                owner = sender * PLANE + ((device % PLANE) ^ t)
                for k in range(PCAP):
                    ordinal = (step * PLANE + t) * PCAP + k
                    block = sources[step][t, k]
                    keys[ordinal * blk : (ordinal + 1) * blk, :] = block[:, :LANES]
                    values[ordinal * blk : (ordinal + 1) * blk, :] = block[:, LANES:]
                    gone = jnp.where(prefix_held[owner] > k, 0.0, MASKED)
                    hide = jnp.where(lane_block == ordinal, gone, hide)
        bias[...] = hide
        keys[prefix:, :] = new_kv[:, :LANES]
        values[prefix:, :] = new_kv[:, LANES:]

    for t in range(token_count // tile):
        width = prefix + (t + 1) * tile
        block = q[t * tile : (t + 1) * tile, :]
        scores = lax.dot_general(
            block, keys[:width, :], (((1,), (1,)), ((), ())), preferred_element_type=jnp.float32
        )
        causal = lax.broadcasted_iota(jnp.int32, (tile, tile), 0) >= lax.broadcasted_iota(
            jnp.int32, (tile, tile), 1
        )
        pieces = [scores[:, :prefix] + bias[0:1, :]]
        if t:
            pieces.append(scores[:, prefix : width - tile])
        pieces.append(jnp.where(causal, scores[:, width - tile :], MASKED))
        scores = jnp.concatenate(pieces, axis=1)
        top = jnp.max(scores, axis=1, keepdims=True)
        weights = jnp.exp2((scores - top) * scale)
        total = jnp.sum(weights, axis=1, keepdims=True)
        mixed = jnp.dot(
            weights.astype(jnp.bfloat16), values[:width, :], preferred_element_type=jnp.float32
        )
        out[t * tile : (t + 1) * tile, :] = (mixed / total).astype(out.dtype)


def unpack_kernel(cap, head_rows, groups, back, out, rows_scr, group_fill):
    device = lax.axis_index("pool")
    row_count = out.shape[0]
    head_total = out.shape[1] // LANES
    for a in range(back.shape[0] // DGRP):
        group_fill[a] = 0
    for i in range(row_count):
        a = groups[device * row_count + i]
        c = group_fill[a]
        group_fill[a] = c + 1
        for m in range(DGRP):
            first = i * head_total + m * head_rows
            rows_scr[first : first + head_rows, :] = back[
                a * DGRP + m, pl.ds(pl.multiple_of(c * head_rows, 16), head_rows), :
            ].astype(jnp.float32)
    for h in range(head_total):
        out[:, h * LANES : (h + 1) * LANES] = rows_scr[
            pl.ds(h, row_count, stride=head_total), :
        ].astype(out.dtype)


def shards(
    pool_kv,
    prefix_table,
    prefix_count,
    prefill_q,
    prefill_new_kv,
    decode_q,
    decode_new,
    decode_cache,
    decode_group,
    cached_len,
):
    devices = lax.axis_size("pool")
    blk = pool_kv.shape[2]
    row_count, q_width = decode_q.shape
    cap = decode_cache.shape[1] // devices
    decode_groups = devices // DGRP
    pair_count = decode_cache.shape[2]
    head_rows = q_width // LANES // DGRP
    own_rows = up16(pair_count * cap)
    own_start = cap * head_rows
    message_rows = own_start + 2 * own_rows
    layout = (cap, head_rows, own_rows, own_start)
    groups = decode_group.reshape(-1)
    prefill_groups = prefix_table.shape[0]
    big = pltpu.CompilerParams(vmem_limit_bytes=60 * 2**20)
    small = pltpu.CompilerParams(vmem_limit_bytes=8 * 2**20)

    sending = pl.pallas_call(
        functools.partial(pack_kernel, layout),
        out_shape=jax.ShapeDtypeStruct((decode_groups, DGRP, message_rows, LANES), jnp.bfloat16),
        in_specs=[smem_spec(), vmem_spec(), vmem_spec()],
        out_specs=any_spec(),
        scratch_shapes=[
            pltpu.VMEM((row_count * q_width // LANES, LANES), jnp.float32),
            pltpu.VMEM((DGRP, decode_groups, message_rows, LANES), jnp.bfloat16),
            pltpu.SMEM((decode_groups,), jnp.int32),
            pltpu.SemaphoreType.DMA((DGRP,)),
        ],
        compiler_params=big,
        name="pack",
    )(in_hbm(groups), in_hbm(decode_q), in_hbm(decode_new))
    sending = sending.reshape(devices, message_rows, LANES)

    received = lax.all_to_all(sending, "pool", split_axis=0, concat_axis=0, tiled=True)

    share = jax.ShapeDtypeStruct(
        (PGRP // PLANE, prefill_groups, PCAP, blk, 2 * LANES), jnp.bfloat16
    )
    shares = pl.pallas_call(
        blocks_kernel,
        out_shape=(share,) * PLANE,
        in_specs=[smem_spec(), smem_spec(), any_spec()],
        out_specs=(any_spec(),) * PLANE,
        scratch_shapes=[pltpu.SemaphoreType.DMA((2 * PGRP * PCAP,))],
        compiler_params=small,
        cost_estimate=pl.CostEstimate(flops=100000, bytes_accessed=1000000, transcendentals=0),
        name="blocks",
    )(in_hbm(prefix_table), in_hbm(prefix_count), in_hbm(pool_kv))
    shares = [shares[0]] + [
        lax.ppermute(shares[t], "pool", [(i, i ^ t) for i in range(devices)])
        for t in range(1, PLANE)
    ]
    chunk = min(cap, 4)
    width = 8
    block_count = devices * cap // chunk
    slot_len, listed, prefix_held = pl.pallas_call(
        functools.partial(plan_kernel, cap, chunk, devices),
        out_shape=(
            jax.ShapeDtypeStruct((devices * cap,), jnp.int32),
            jax.ShapeDtypeStruct((block_count + 2,), jnp.int32),
            jax.ShapeDtypeStruct((devices * pool_kv.shape[0],), jnp.int32),
        ),
        in_specs=[smem_spec()] * 4,
        out_specs=(smem_spec(),) * 3,
        compiler_params=small,
        cost_estimate=pl.CostEstimate(flops=1000000, bytes_accessed=4000000, transcendentals=0),
        name="plan",
    )(in_hbm(prefix_table), in_hbm(prefix_count), in_hbm(groups), in_hbm(cached_len))

    *shares, slot_len, listed = lax.optimization_barrier((*shares, slot_len, listed))
    planes = devices // PLANE
    bundle = jax.ShapeDtypeStruct((PLANE, PCAP, blk, 2 * LANES), jnp.bfloat16)
    bundles = pl.pallas_call(
        functools.partial(regroup_kernel, planes),
        out_shape=(bundle,) * planes,
        in_specs=[any_spec()] * PLANE,
        out_specs=(any_spec(),) * planes,
        scratch_shapes=[pltpu.SemaphoreType.DMA((planes * PLANE,))],
        compiler_params=small,
        cost_estimate=pl.CostEstimate(flops=100000, bytes_accessed=1000000, transcendentals=0),
        name="regroup",
    )(*shares)

    def along_line(step):
        pairs = [
            (i, partner(i // PLANE, step, planes) * PLANE + i % PLANE) for i in range(devices)
        ]
        return lax.ppermute(bundles[step], "pool", pairs)

    lines = [bundles[0], along_line(1)]

    received, slot_len, listed, *bundles = lax.optimization_barrier(
        (received, slot_len, listed, *bundles)
    )
    lines += [along_line(step) for step in range(2, planes)]

    answers = pl.pallas_call(
        functools.partial(decode_kernel, layout, chunk, width),
        out_shape=jax.ShapeDtypeStruct((devices, cap * head_rows, LANES), jnp.bfloat16),
        in_specs=[smem_spec(), smem_spec(), vmem_spec(), any_spec()],
        out_specs=vmem_spec(),
        scratch_shapes=[
            pltpu.VMEM((block_count * chunk,) + decode_cache.shape[2:], jnp.bfloat16),
            pltpu.SemaphoreType.DMA((block_count,)),
        ],
        compiler_params=pltpu.CompilerParams(vmem_limit_bytes=20 * 2**20),
        cost_estimate=pl.CostEstimate(
            flops=500000000, bytes_accessed=8000000, transcendentals=1000000
        ),
        name="decode",
    )(listed, slot_len, received, in_hbm(decode_cache[0]))

    answers, *lines = lax.optimization_barrier((answers, *lines))
    back = lax.all_to_all(answers, "pool", split_axis=0, concat_axis=0, tiled=True)

    token_count, fill_width = prefill_q.shape[1:]
    prefix = devices * PCAP * blk
    head_count = fill_width // LANES
    prefix_held, _ = lax.optimization_barrier((prefix_held, answers))
    prefill_out = pl.pallas_call(
        functools.partial(prefill_kernel, planes, min(256, token_count)),
        grid=(head_count,),
        out_shape=jax.ShapeDtypeStruct((token_count, fill_width), jnp.bfloat16),
        in_specs=[smem_spec()]
        + [pl.BlockSpec(bundle.shape, lambda u: (0, 0, 0, 0))] * planes
        + [
            pl.BlockSpec((token_count, LANES), lambda u: (0, u)),
            pl.BlockSpec(prefill_new_kv.shape[1:], lambda u: (0, 0)),
        ],
        out_specs=pl.BlockSpec((token_count, LANES), lambda u: (0, u)),
        scratch_shapes=[
            pltpu.VMEM((prefix + token_count, LANES), jnp.bfloat16),
            pltpu.VMEM((prefix + token_count, LANES), jnp.bfloat16),
            pltpu.VMEM((8, prefix), jnp.float32),
        ],
        compiler_params=pltpu.CompilerParams(vmem_limit_bytes=16 * 2**20),
        cost_estimate=pl.CostEstimate(
            flops=2 * 2 * token_count * fill_width * (prefix + token_count // 2),
            bytes_accessed=3000000,
            transcendentals=token_count * head_count * (prefix + token_count // 2),
        ),
        name="prefill",
    )(prefix_held, *lines, prefill_q[0], prefill_new_kv[0])

    decode_out = pl.pallas_call(
        functools.partial(unpack_kernel, cap, head_rows),
        out_shape=jax.ShapeDtypeStruct((row_count, q_width), jnp.bfloat16),
        in_specs=[smem_spec(), vmem_spec()],
        out_specs=vmem_spec(),
        scratch_shapes=[
            pltpu.VMEM((row_count * q_width // LANES, LANES), jnp.float32),
            pltpu.SMEM((decode_groups,), jnp.int32),
        ],
        compiler_params=small,
        name="unpack",
    )(in_hbm(groups), back)
    return (prefill_out[None], decode_out)


def solution(mesh):
    in_specs = (
        P(("rep", "pool"), None, None, None),
        P("rep", None),
        P("rep"),
        P(("rep", "pool"), None, None),
        P(("rep", "pool"), None, None),
        P(("rep", "pool"), None),
        P(("rep", "pool"), None),
        P(("rep", "pool"), None, None, None, None),
        P("rep", None),
        P("rep"),
    )
    out_specs = (P(("rep", "pool"), None, None), P(("rep", "pool"), None))
    return jax.shard_map(shards, mesh=mesh, in_specs=in_specs, out_specs=out_specs, check_vma=False)
```

```python
import functools

import jax
import jax.numpy as jnp
from jax import lax
from jax.experimental import pallas as pl
from jax.experimental.pallas import tpu as pltpu
from jax.sharding import PartitionSpec as P

PGRP = 8
DGRP = 4
PCAP = 2
PLANE = 4
LANES = 128
MASKED = -1e30
LOG2E = 1.4426950408889634


def up16(n):
    return -(-n // 16) * 16


def any_spec():
    return pl.BlockSpec(memory_space=pl.ANY)


def smem_spec():
    return pl.BlockSpec(memory_space=pltpu.SMEM)


def in_hbm(x):
    return pltpu.with_memory_space_constraint(x, pltpu.HBM)


def vmem_spec():
    return pl.BlockSpec(memory_space=pltpu.VMEM)


def pack_kernel(layout, groups, q, kv, out, rows_scr, stage, group_fill, sems):
    cap, head_rows, own_rows, own_start = layout
    decode_groups = out.shape[0]
    row_count = q.shape[0]
    head_total = q.shape[1] // LANES
    pair_count = kv.shape[1] // (2 * LANES * DGRP)
    device = lax.axis_index("pool")
    for a in range(decode_groups):
        group_fill[a] = 0
    for h in range(head_total):
        rows_scr[pl.ds(h, row_count, stride=head_total), :] = q[
            :, h * LANES : (h + 1) * LANES
        ].astype(jnp.float32)
    slot_axis = lax.broadcasted_iota(jnp.int32, (decode_groups * cap, row_count), 0)
    row_axis = lax.broadcasted_iota(jnp.int32, (decode_groups * cap, row_count), 1)
    slot_of_row = jnp.full((decode_groups * cap, row_count), -1, jnp.int32)
    homes = []
    for i in range(row_count):
        a = groups[device * row_count + i]
        c = group_fill[a]
        group_fill[a] = c + 1
        slot_of_row = jnp.where(row_axis == i, a * cap + c, slot_of_row)
        homes.append((a, c))
    pick = (slot_of_row == slot_axis).astype(jnp.bfloat16)
    own = jnp.dot(pick, kv[...], preferred_element_type=jnp.float32)
    blank = jnp.zeros((own_rows - pair_count * cap, LANES), jnp.float32)
    copies = []
    for m in range(DGRP):
        for i, (a, c) in enumerate(homes):
            first = i * head_total + m * head_rows
            stage[m, a, pl.ds(pl.multiple_of(c * head_rows, 16), head_rows), :] = rows_scr[
                first : first + head_rows, :
            ].astype(out.dtype)
        for a in range(decode_groups):
            for part in range(2):
                pieces = []
                for k in range(pair_count):
                    lane = ((m * pair_count + k) * 2 + part) * LANES
                    pieces.append(own[a * cap : (a + 1) * cap, lane : lane + LANES])
                if blank.shape[0]:
                    pieces.append(blank)
                place = own_start + part * own_rows
                stage[m, a, place : place + own_rows, :] = jnp.concatenate(
                    pieces, axis=0
                ).astype(out.dtype)
        copy = pltpu.make_async_copy(stage.at[m], out.at[:, m], sems.at[m])
        copy.start()
        copies.append(copy)
    for copy in copies:
        copy.wait()


def blocks_kernel(table, count, pool, *rest):
    outs, sems = rest[:PLANE], rest[PLANE]
    blocks_here = pool.shape[0]
    group_count, most_blocks = table.shape
    device = lax.axis_index("pool")
    first_block = device * blocks_here
    flying = []
    for g in range(group_count):

        def scan_table(j, carry):
            seen, chosen = carry
            entry = table[g, j]
            mine = (entry >= first_block) & (entry < first_block + blocks_here) & (j < count[g])
            chosen = tuple(
                jnp.where(mine & (seen == k), entry - first_block, chosen[k]) for k in range(PCAP)
            )
            return seen + mine.astype(jnp.int32), chosen

        start = (jnp.int32(0), tuple(jnp.int32(0) for _ in range(PCAP)))
        _, chosen = lax.fori_loop(0, most_blocks, scan_table, start, unroll=8)
        if g >= 2:
            for copy in flying.pop(0):
                copy.wait()
        copies = []
        for half in range(PGRP // PLANE):
            for t in range(PLANE):
                for k in range(PCAP):
                    copy = pltpu.make_async_copy(
                        pool.at[chosen[k], half * PLANE + ((device % PLANE) ^ t)],
                        outs[t].at[half, g, k],
                        sems.at[((g % 2) * PGRP + half * PLANE + t) * PCAP + k],
                    )
                    copy.start()
                    copies.append(copy)
        flying.append(copies)
    for copies in flying:
        for copy in copies:
            copy.wait()


def partner(plane, step, planes):
    return plane ^ step if planes & (planes - 1) == 0 else (plane + step) % planes


def regroup_kernel(planes, *rest):
    held, outs, sems = rest[:PLANE], rest[PLANE:-1], rest[-1]
    mine = lax.axis_index("pool") // PLANE
    per_group = PGRP // PLANE
    copies = []
    for step in range(planes):
        there = partner(mine, step, planes)
        for t in range(PLANE):
            copy = pltpu.make_async_copy(
                held[t].at[there % per_group, there // per_group],
                outs[step].at[t],
                sems.at[step * PLANE + t],
            )
            copy.start()
            copies.append(copy)
    for copy in copies:
        copy.wait()


def fetch_block(cache, listed, i, chunk, held, place, sem):
    return pltpu.make_async_copy(
        cache.at[pl.ds(listed[1 + i] * chunk, chunk)], held.at[pl.ds(place * chunk, chunk)], sem
    )


def plan_kernel(
    cap, step, owners, table, count, groups, lengths, cache, slot_len, listed, prefix_held, ahead, sems
):
    device = lax.axis_index("pool")
    home_count = owners
    row_count = groups.shape[0] // home_count
    group_id = device // DGRP
    prefill_id = device // PGRP
    blocks_here = listed.shape[0]
    most_blocks = table.shape[1]
    chunk = min(cap, step)

    def one_owner(o, carry):
        prefix_held[o] = 0
        return carry

    lax.fori_loop(0, owners, one_owner, 0)
    pool_blocks = prefix_held.shape[0] // owners

    def one_entry(j, carry):
        o = table[prefill_id, j] // pool_blocks
        prefix_held[o] = prefix_held[o] + 1
        return carry

    lax.fori_loop(0, jnp.minimum(count[prefill_id], most_blocks), one_entry, 0)

    def one_home(s, filled):
        for c in range(cap):
            slot_len[s * cap + c] = 0
        here = jnp.int32(0)
        for i in range(row_count):
            row = s * row_count + i
            mine = groups[row] == group_id
            place = s * cap + jnp.minimum(here, cap - 1)
            slot_len[place] = jnp.where(mine, lengths[row], slot_len[place])
            here = here + mine.astype(jnp.int32)
        for b in range(cap // chunk):
            listed[1 + jnp.minimum(filled, blocks_here - 2)] = s * (cap // chunk) + b
            filled = filled + (here > b * chunk).astype(jnp.int32)
        return filled

    live = lax.fori_loop(0, home_count, one_home, jnp.int32(0))
    listed[0] = live
    for i in range(ahead.shape[0] // chunk):
        pl.when(i < live)(fetch_block(cache, listed, i, chunk, ahead, i, sems.at[i]).start)
    for i in range(ahead.shape[0] // chunk):
        pl.when(i < live)(fetch_block(cache, listed, i, chunk, ahead, i, sems.at[i]).wait)


def decode_kernel(layout, chunk, width, listed, slot_len, recv, ahead, cache, out, held, sems):
    cap, head_rows, own_rows, own_start = layout
    pair_count, positions = cache.shape[1], cache.shape[2]
    per_home = cap // chunk
    key_count = pair_count * positions
    query_heads = head_rows // pair_count
    live = listed[0]
    scale = LANES ** (-0.5) * LOG2E
    rows = chunk * head_rows
    slots = width * chunk
    pair = 2 if chunk % 2 == 0 else 1

    def fetch(i):
        return fetch_block(cache, listed, i, chunk, held, i - width, sems.at[i - width])

    def begin(i, carry):
        fetch(i).start()
        return carry

    lax.fori_loop(width, live, begin, 0)
    row_pair = lax.broadcasted_iota(jnp.int32, (head_rows, key_count), 0) // query_heads
    key_axis = lax.broadcasted_iota(jnp.int32, (head_rows, key_count), 1)
    pos = jnp.where(key_axis // positions == row_pair, key_axis % positions, positions)
    own_axis = lax.broadcasted_iota(jnp.int32, (rows, own_rows), 1)
    own_row = lax.broadcasted_iota(jnp.int32, (rows, own_rows), 0)
    own_want = ((own_row % head_rows) // query_heads) * cap + own_row // head_rows

    def several(t, kv):
        ids = [jnp.minimum(t * width + w, live - 1) for w in range(width)]
        blocks = [listed[1 + i] for i in ids]
        homes = [b // per_home for b in blocks]
        firsts = [(b % per_home) * chunk for b in blocks]
        places = [pl.multiple_of(f * head_rows, 16) for f in firsts]
        q = jnp.concatenate(
            [recv[h, pl.ds(p, rows), :] for h, p in zip(homes, places)], axis=0
        )
        own_keys = jnp.stack([recv[h, own_start : own_start + own_rows, :] for h in homes])
        own_values = jnp.stack(
            [recv[h, own_start + own_rows : own_start + 2 * own_rows, :] for h in homes]
        )
        keys = kv[..., :LANES].reshape(slots, key_count, LANES)
        values = kv[..., LANES:].reshape(slots, key_count, LANES)
        scores = jnp.einsum(
            "jqd,jkd->jqk",
            q.reshape(slots // pair, pair * head_rows, LANES),
            keys.reshape(slots // pair, pair * key_count, LANES),
            preferred_element_type=jnp.float32,
        )
        if pair == 2:
            scores = jnp.stack(
                [scores[:, :head_rows, :key_count], scores[:, head_rows:, key_count:]], axis=1
            ).reshape(slots, head_rows, key_count)
        kept = jnp.stack(
            [pos < slot_len[blocks[w] * chunk + j] for w in range(width) for j in range(chunk)]
        )
        scores = jnp.where(kept, scores, MASKED)
        own_scores = jnp.einsum(
            "jqd,jkd->jqk",
            q.reshape(width, rows, LANES),
            own_keys,
            preferred_element_type=jnp.float32,
        )
        own_hit = jnp.stack([own_axis == own_want + f for f in firsts])
        own_score = jnp.sum(jnp.where(own_hit, own_scores, 0.0), axis=2, keepdims=True)
        own_score = own_score.reshape(slots, head_rows, 1)
        top = jnp.maximum(jnp.max(scores, axis=2, keepdims=True), own_score)
        weights = jnp.exp2((scores - top) * scale)
        own_weight = jnp.exp2((own_score - top) * scale)
        total = jnp.sum(weights, axis=2, keepdims=True) + own_weight
        weights = weights.astype(jnp.bfloat16)
        if pair == 2:
            weights = weights.reshape(slots // 2, 2, head_rows, key_count)
            nothing = jnp.zeros((slots // 2, head_rows, key_count), jnp.bfloat16)
            upper = jnp.concatenate([weights[:, 0], nothing], axis=2)
            lower = jnp.concatenate([nothing, weights[:, 1]], axis=2)
            weights = jnp.concatenate([upper, lower], axis=1)
        mixed = jnp.einsum(
            "jqk,jkd->jqd",
            weights,
            values.reshape(slots // pair, pair * key_count, LANES),
            preferred_element_type=jnp.float32,
        )
        own_part = jnp.where(own_hit, own_weight.reshape(width, rows, 1), 0.0)
        mixed = mixed.reshape(width, rows, LANES) + jnp.einsum(
            "jqk,jkd->jqd",
            own_part.astype(jnp.bfloat16),
            own_values,
            preferred_element_type=jnp.float32,
        )
        mixed = mixed / total.reshape(width, rows, 1)
        for w in reversed(range(width)):
            out[homes[w], pl.ds(places[w], rows), :] = mixed[w].astype(out.dtype)

    several(0, ahead[...])

    def later(t, carry):
        for w in range(width):
            pl.when(t * width + w < live)(fetch(t * width + w).wait)
        several(t, held[pl.ds((t - 1) * slots, slots)])
        return carry

    lax.fori_loop(1, (live + width - 1) // width, later, 0)


def prefill_kernel(planes, tile, prefix_held, *rest):
    sources = rest[:planes]
    q, new_kv, out, keys, values, bias = rest[planes:]
    blk = sources[0].shape[2]
    prefix = planes * PLANE * PCAP * blk
    token_count = new_kv.shape[0]
    scale = LANES ** (-0.5) * LOG2E
    device = lax.axis_index("pool")

    @pl.when(pl.program_id(0) == 0)
    def _():
        lane_block = lax.broadcasted_iota(jnp.int32, (8, prefix), 1) // blk
        hide = jnp.zeros((8, prefix), jnp.float32)
        for step in range(planes):
            sender = device // PLANE
            sender = sender ^ step if planes & (planes - 1) == 0 else (sender + planes - step) % planes
            for t in range(PLANE):
                owner = sender * PLANE + ((device % PLANE) ^ t)
                for k in range(PCAP):
                    ordinal = (step * PLANE + t) * PCAP + k
                    block = sources[step][t, k]
                    keys[ordinal * blk : (ordinal + 1) * blk, :] = block[:, :LANES]
                    values[ordinal * blk : (ordinal + 1) * blk, :] = block[:, LANES:]
                    gone = jnp.where(prefix_held[owner] > k, 0.0, MASKED)
                    hide = jnp.where(lane_block == ordinal, gone, hide)
        bias[...] = hide
        keys[prefix:, :] = new_kv[:, :LANES]
        values[prefix:, :] = new_kv[:, LANES:]

    for t in range(token_count // tile):
        width = prefix + (t + 1) * tile
        block = q[t * tile : (t + 1) * tile, :]
        scores = lax.dot_general(
            block, keys[:width, :], (((1,), (1,)), ((), ())), preferred_element_type=jnp.float32
        )
        causal = lax.broadcasted_iota(jnp.int32, (tile, tile), 0) >= lax.broadcasted_iota(
            jnp.int32, (tile, tile), 1
        )
        pieces = [scores[:, :prefix] + bias[0:1, :]]
        if t:
            pieces.append(scores[:, prefix : width - tile])
        pieces.append(jnp.where(causal, scores[:, width - tile :], MASKED))
        scores = jnp.concatenate(pieces, axis=1)
        top = jnp.max(scores, axis=1, keepdims=True)
        weights = jnp.exp2((scores - top) * scale)
        total = jnp.sum(weights, axis=1, keepdims=True)
        mixed = jnp.dot(
            weights.astype(jnp.bfloat16), values[:width, :], preferred_element_type=jnp.float32
        )
        out[t * tile : (t + 1) * tile, :] = (mixed / total).astype(out.dtype)


def unpack_kernel(cap, head_rows, groups, back, out, rows_scr, group_fill):
    device = lax.axis_index("pool")
    row_count = out.shape[0]
    head_total = out.shape[1] // LANES
    for a in range(back.shape[0] // DGRP):
        group_fill[a] = 0
    for i in range(row_count):
        a = groups[device * row_count + i]
        c = group_fill[a]
        group_fill[a] = c + 1
        for m in range(DGRP):
            first = i * head_total + m * head_rows
            rows_scr[first : first + head_rows, :] = back[
                a * DGRP + m, pl.ds(pl.multiple_of(c * head_rows, 16), head_rows), :
            ].astype(jnp.float32)
    for h in range(head_total):
        out[:, h * LANES : (h + 1) * LANES] = rows_scr[
            pl.ds(h, row_count, stride=head_total), :
        ].astype(out.dtype)


def shards(
    pool_kv,
    prefix_table,
    prefix_count,
    prefill_q,
    prefill_new_kv,
    decode_q,
    decode_new,
    decode_cache,
    decode_group,
    cached_len,
):
    devices = lax.axis_size("pool")
    blk = pool_kv.shape[2]
    row_count, q_width = decode_q.shape
    cap = decode_cache.shape[1] // devices
    decode_groups = devices // DGRP
    pair_count = decode_cache.shape[2]
    head_rows = q_width // LANES // DGRP
    own_rows = up16(pair_count * cap)
    own_start = cap * head_rows
    message_rows = own_start + 2 * own_rows
    layout = (cap, head_rows, own_rows, own_start)
    groups = decode_group.reshape(-1)
    prefill_groups = prefix_table.shape[0]
    big = pltpu.CompilerParams(vmem_limit_bytes=60 * 2**20)
    small = pltpu.CompilerParams(vmem_limit_bytes=8 * 2**20)

    sending = pl.pallas_call(
        functools.partial(pack_kernel, layout),
        out_shape=jax.ShapeDtypeStruct((decode_groups, DGRP, message_rows, LANES), jnp.bfloat16),
        in_specs=[smem_spec(), vmem_spec(), vmem_spec()],
        out_specs=any_spec(),
        scratch_shapes=[
            pltpu.VMEM((row_count * q_width // LANES, LANES), jnp.float32),
            pltpu.VMEM((DGRP, decode_groups, message_rows, LANES), jnp.bfloat16),
            pltpu.SMEM((decode_groups,), jnp.int32),
            pltpu.SemaphoreType.DMA((DGRP,)),
        ],
        compiler_params=big,
        name="pack",
    )(in_hbm(groups), in_hbm(decode_q), in_hbm(decode_new))
    sending = sending.reshape(devices, message_rows, LANES)

    received = lax.all_to_all(sending, "pool", split_axis=0, concat_axis=0, tiled=True)

    share = jax.ShapeDtypeStruct(
        (PGRP // PLANE, prefill_groups, PCAP, blk, 2 * LANES), jnp.bfloat16
    )
    shares = pl.pallas_call(
        blocks_kernel,
        out_shape=(share,) * PLANE,
        in_specs=[smem_spec(), smem_spec(), any_spec()],
        out_specs=(any_spec(),) * PLANE,
        scratch_shapes=[pltpu.SemaphoreType.DMA((2 * PGRP * PCAP,))],
        compiler_params=small,
        cost_estimate=pl.CostEstimate(flops=100000, bytes_accessed=1000000, transcendentals=0),
        name="blocks",
    )(in_hbm(prefix_table), in_hbm(prefix_count), in_hbm(pool_kv))
    shares = [shares[0]] + [
        lax.ppermute(shares[t], "pool", [(i, i ^ t) for i in range(devices)])
        for t in range(1, PLANE)
    ]
    chunk = min(cap, 4)
    width = 8
    block_count = devices * cap // chunk
    slot_len, listed, prefix_held, ahead = pl.pallas_call(
        functools.partial(plan_kernel, cap, chunk, devices),
        out_shape=(
            jax.ShapeDtypeStruct((devices * cap,), jnp.int32),
            jax.ShapeDtypeStruct((block_count + 2,), jnp.int32),
            jax.ShapeDtypeStruct((devices * pool_kv.shape[0],), jnp.int32),
            jax.ShapeDtypeStruct((width * chunk,) + decode_cache.shape[2:], jnp.bfloat16),
        ),
        in_specs=[smem_spec()] * 4 + [any_spec()],
        out_specs=(smem_spec(),) * 3 + (vmem_spec(),),
        scratch_shapes=[pltpu.SemaphoreType.DMA((width,))],
        compiler_params=small,
        cost_estimate=pl.CostEstimate(flops=1000000, bytes_accessed=4000000, transcendentals=0),
        name="plan",
    )(in_hbm(prefix_table), in_hbm(prefix_count), in_hbm(groups), in_hbm(cached_len), in_hbm(decode_cache[0]))

    *shares, slot_len, listed = lax.optimization_barrier((*shares, slot_len, listed))
    planes = devices // PLANE
    bundle = jax.ShapeDtypeStruct((PLANE, PCAP, blk, 2 * LANES), jnp.bfloat16)
    bundles = pl.pallas_call(
        functools.partial(regroup_kernel, planes),
        out_shape=(bundle,) * planes,
        in_specs=[any_spec()] * PLANE,
        out_specs=(any_spec(),) * planes,
        scratch_shapes=[pltpu.SemaphoreType.DMA((planes * PLANE,))],
        compiler_params=small,
        cost_estimate=pl.CostEstimate(flops=100000, bytes_accessed=1000000, transcendentals=0),
        name="regroup",
    )(*shares)

    def along_line(step):
        pairs = [
            (i, partner(i // PLANE, step, planes) * PLANE + i % PLANE) for i in range(devices)
        ]
        return lax.ppermute(bundles[step], "pool", pairs)

    lines = [bundles[0], along_line(1)]

    received, slot_len, listed, *bundles = lax.optimization_barrier(
        (received, slot_len, listed, *bundles)
    )
    lines += [along_line(step) for step in range(2, planes)]

    answers = pl.pallas_call(
        functools.partial(decode_kernel, layout, chunk, width),
        out_shape=jax.ShapeDtypeStruct((devices, cap * head_rows, LANES), jnp.bfloat16),
        in_specs=[smem_spec(), smem_spec(), vmem_spec(), vmem_spec(), any_spec()],
        out_specs=vmem_spec(),
        scratch_shapes=[
            pltpu.VMEM(((block_count - width) * chunk,) + decode_cache.shape[2:], jnp.bfloat16),
            pltpu.SemaphoreType.DMA((block_count - width,)),
        ],
        compiler_params=pltpu.CompilerParams(vmem_limit_bytes=20 * 2**20),
        cost_estimate=pl.CostEstimate(
            flops=500000000, bytes_accessed=8000000, transcendentals=1000000
        ),
        name="decode",
    )(listed, slot_len, received, ahead, in_hbm(decode_cache[0]))

    answers, *lines = lax.optimization_barrier((answers, *lines))
    back = lax.all_to_all(answers, "pool", split_axis=0, concat_axis=0, tiled=True)

    token_count, fill_width = prefill_q.shape[1:]
    prefix = devices * PCAP * blk
    head_count = fill_width // LANES
    prefix_held, _ = lax.optimization_barrier((prefix_held, answers))
    prefill_out = pl.pallas_call(
        functools.partial(prefill_kernel, planes, min(256, token_count)),
        grid=(head_count,),
        out_shape=jax.ShapeDtypeStruct((token_count, fill_width), jnp.bfloat16),
        in_specs=[smem_spec()]
        + [pl.BlockSpec(bundle.shape, lambda u: (0, 0, 0, 0))] * planes
        + [
            pl.BlockSpec((token_count, LANES), lambda u: (0, u)),
            pl.BlockSpec(prefill_new_kv.shape[1:], lambda u: (0, 0)),
        ],
        out_specs=pl.BlockSpec((token_count, LANES), lambda u: (0, u)),
        scratch_shapes=[
            pltpu.VMEM((prefix + token_count, LANES), jnp.bfloat16),
            pltpu.VMEM((prefix + token_count, LANES), jnp.bfloat16),
            pltpu.VMEM((8, prefix), jnp.float32),
        ],
        compiler_params=pltpu.CompilerParams(vmem_limit_bytes=16 * 2**20),
        cost_estimate=pl.CostEstimate(
            flops=2 * 2 * token_count * fill_width * (prefix + token_count // 2),
            bytes_accessed=3000000,
            transcendentals=token_count * head_count * (prefix + token_count // 2),
        ),
        name="prefill",
    )(prefix_held, *lines, in_hbm(prefill_q[0]), in_hbm(prefill_new_kv[0]))

    decode_out = pl.pallas_call(
        functools.partial(unpack_kernel, cap, head_rows),
        out_shape=jax.ShapeDtypeStruct((row_count, q_width), jnp.bfloat16),
        in_specs=[smem_spec(), vmem_spec()],
        out_specs=vmem_spec(),
        scratch_shapes=[
            pltpu.VMEM((row_count * q_width // LANES, LANES), jnp.float32),
            pltpu.SMEM((decode_groups,), jnp.int32),
        ],
        compiler_params=small,
        name="unpack",
    )(in_hbm(groups), back)
    return (prefill_out[None], decode_out)


def solution(mesh):
    in_specs = (
        P(("rep", "pool"), None, None, None),
        P("rep", None),
        P("rep"),
        P(("rep", "pool"), None, None),
        P(("rep", "pool"), None, None),
        P(("rep", "pool"), None),
        P(("rep", "pool"), None),
        P(("rep", "pool"), None, None, None, None),
        P("rep", None),
        P("rep"),
    )
    out_specs = (P(("rep", "pool"), None, None), P(("rep", "pool"), None))
    return jax.shard_map(shards, mesh=mesh, in_specs=in_specs, out_specs=out_specs, check_vma=False)
```

```python
import functools

import jax
import jax.numpy as jnp
from jax import lax
from jax.experimental import pallas as pl
from jax.experimental.pallas import tpu as pltpu
from jax.sharding import PartitionSpec as P

PGRP = 8
DGRP = 4
PCAP = 2
PLANE = 4
LANES = 128
MASKED = -1e30
LOG2E = 1.4426950408889634


def up16(n):
    return -(-n // 16) * 16


def any_spec():
    return pl.BlockSpec(memory_space=pl.ANY)


def smem_spec():
    return pl.BlockSpec(memory_space=pltpu.SMEM)


def in_hbm(x):
    return pltpu.with_memory_space_constraint(x, pltpu.HBM)


def vmem_spec():
    return pl.BlockSpec(memory_space=pltpu.VMEM)


def pack_kernel(layout, groups, q, kv, out, rows_scr, stage, group_fill, sems):
    cap, head_rows, own_rows, own_start = layout
    decode_groups = out.shape[0]
    row_count = q.shape[0]
    head_total = q.shape[1] // LANES
    pair_count = kv.shape[1] // (2 * LANES * DGRP)
    device = lax.axis_index("pool")
    for a in range(decode_groups):
        group_fill[a] = 0
    for h in range(head_total):
        rows_scr[pl.ds(h, row_count, stride=head_total), :] = q[
            :, h * LANES : (h + 1) * LANES
        ].astype(jnp.float32)
    slot_axis = lax.broadcasted_iota(jnp.int32, (decode_groups * cap, row_count), 0)
    row_axis = lax.broadcasted_iota(jnp.int32, (decode_groups * cap, row_count), 1)
    slot_of_row = jnp.full((decode_groups * cap, row_count), -1, jnp.int32)
    homes = []
    for i in range(row_count):
        a = groups[device * row_count + i]
        c = group_fill[a]
        group_fill[a] = c + 1
        slot_of_row = jnp.where(row_axis == i, a * cap + c, slot_of_row)
        homes.append((a, c))
    pick = (slot_of_row == slot_axis).astype(jnp.bfloat16)
    own = jnp.dot(pick, kv[...], preferred_element_type=jnp.float32)
    blank = jnp.zeros((own_rows - pair_count * cap, LANES), jnp.float32)
    copies = []
    for m in range(DGRP):
        for i, (a, c) in enumerate(homes):
            first = i * head_total + m * head_rows
            stage[m, a, pl.ds(pl.multiple_of(c * head_rows, 16), head_rows), :] = rows_scr[
                first : first + head_rows, :
            ].astype(out.dtype)
        for a in range(decode_groups):
            for part in range(2):
                pieces = []
                for k in range(pair_count):
                    lane = ((m * pair_count + k) * 2 + part) * LANES
                    pieces.append(own[a * cap : (a + 1) * cap, lane : lane + LANES])
                if blank.shape[0]:
                    pieces.append(blank)
                place = own_start + part * own_rows
                stage[m, a, place : place + own_rows, :] = jnp.concatenate(
                    pieces, axis=0
                ).astype(out.dtype)
        copy = pltpu.make_async_copy(stage.at[m], out.at[:, m], sems.at[m])
        copy.start()
        copies.append(copy)
    for copy in copies:
        copy.wait()


def blocks_kernel(table, count, pool, *rest):
    outs, sems = rest[:PLANE], rest[PLANE]
    blocks_here = pool.shape[0]
    group_count, most_blocks = table.shape
    device = lax.axis_index("pool")
    first_block = device * blocks_here
    flying = []
    for g in range(group_count):

        def scan_table(j, carry):
            seen, chosen = carry
            entry = table[g, j]
            mine = (entry >= first_block) & (entry < first_block + blocks_here) & (j < count[g])
            chosen = tuple(
                jnp.where(mine & (seen == k), entry - first_block, chosen[k]) for k in range(PCAP)
            )
            return seen + mine.astype(jnp.int32), chosen

        start = (jnp.int32(0), tuple(jnp.int32(0) for _ in range(PCAP)))
        _, chosen = lax.fori_loop(0, most_blocks, scan_table, start, unroll=8)
        if g >= 2:
            for copy in flying.pop(0):
                copy.wait()
        copies = []
        for half in range(PGRP // PLANE):
            for t in range(PLANE):
                for k in range(PCAP):
                    copy = pltpu.make_async_copy(
                        pool.at[chosen[k], half * PLANE + ((device % PLANE) ^ t)],
                        outs[t].at[half, g, k],
                        sems.at[((g % 2) * PGRP + half * PLANE + t) * PCAP + k],
                    )
                    copy.start()
                    copies.append(copy)
        flying.append(copies)
    for copies in flying:
        for copy in copies:
            copy.wait()


def partner(plane, step, planes):
    return plane ^ step if planes & (planes - 1) == 0 else (plane + step) % planes


def regroup_kernel(planes, *rest):
    held, outs, sems = rest[:PLANE], rest[PLANE:-1], rest[-1]
    mine = lax.axis_index("pool") // PLANE
    per_group = PGRP // PLANE
    copies = []
    for step in range(planes):
        there = partner(mine, step, planes)
        for t in range(PLANE):
            copy = pltpu.make_async_copy(
                held[t].at[there % per_group, there // per_group],
                outs[step].at[t],
                sems.at[step * PLANE + t],
            )
            copy.start()
            copies.append(copy)
    for copy in copies:
        copy.wait()


def fetch_block(cache, listed, i, chunk, held, place, sem):
    return pltpu.make_async_copy(
        cache.at[pl.ds(listed[1 + i] * chunk, chunk)], held.at[pl.ds(place * chunk, chunk)], sem
    )


def plan_kernel(
    cap, step, owners, table, count, groups, lengths, cache, slot_len, listed, prefix_held, ahead, sems
):
    device = lax.axis_index("pool")
    home_count = owners
    row_count = groups.shape[0] // home_count
    group_id = device // DGRP
    prefill_id = device // PGRP
    blocks_here = listed.shape[0]
    most_blocks = table.shape[1]
    chunk = min(cap, step)

    def one_owner(o, carry):
        prefix_held[o] = 0
        return carry

    lax.fori_loop(0, owners, one_owner, 0)
    pool_blocks = prefix_held.shape[0] // owners

    def one_entry(j, carry):
        o = table[prefill_id, j] // pool_blocks
        prefix_held[o] = prefix_held[o] + 1
        return carry

    lax.fori_loop(0, jnp.minimum(count[prefill_id], most_blocks), one_entry, 0)

    def one_home(s, filled):
        for c in range(cap):
            slot_len[s * cap + c] = 0
        here = jnp.int32(0)
        for i in range(row_count):
            row = s * row_count + i
            mine = groups[row] == group_id
            place = s * cap + jnp.minimum(here, cap - 1)
            slot_len[place] = jnp.where(mine, lengths[row], slot_len[place])
            here = here + mine.astype(jnp.int32)
        for b in range(cap // chunk):
            listed[1 + jnp.minimum(filled, blocks_here - 2)] = s * (cap // chunk) + b
            filled = filled + (here > b * chunk).astype(jnp.int32)
        return filled

    live = lax.fori_loop(0, home_count, one_home, jnp.int32(0))
    listed[0] = live
    for i in range(ahead.shape[0] // chunk):
        pl.when(i < live)(fetch_block(cache, listed, i, chunk, ahead, i, sems.at[i]).start)
    for i in range(ahead.shape[0] // chunk):
        pl.when(i < live)(fetch_block(cache, listed, i, chunk, ahead, i, sems.at[i]).wait)


def decode_kernel(layout, chunk, width, listed, slot_len, recv, ahead, cache, out, held, sems):
    cap, head_rows, own_rows, own_start = layout
    pair_count, positions = cache.shape[1], cache.shape[2]
    per_home = cap // chunk
    key_count = pair_count * positions
    query_heads = head_rows // pair_count
    live = listed[0]
    scale = LANES ** (-0.5) * LOG2E
    rows = chunk * head_rows
    slots = width * chunk
    pair = 2 if chunk % 2 == 0 else 1

    def fetch(i):
        return fetch_block(cache, listed, i, chunk, held, i - width, sems.at[i - width])

    def begin(i, carry):
        fetch(i).start()
        return carry

    lax.fori_loop(width, live, begin, 0)
    row_pair = lax.broadcasted_iota(jnp.int32, (head_rows, key_count), 0) // query_heads
    key_axis = lax.broadcasted_iota(jnp.int32, (head_rows, key_count), 1)
    pos = jnp.where(key_axis // positions == row_pair, key_axis % positions, positions)
    own_axis = lax.broadcasted_iota(jnp.int32, (rows, own_rows), 1)
    own_row = lax.broadcasted_iota(jnp.int32, (rows, own_rows), 0)
    own_want = ((own_row % head_rows) // query_heads) * cap + own_row // head_rows

    def several(t, kv):
        ids = [jnp.minimum(t * width + w, live - 1) for w in range(width)]
        blocks = [listed[1 + i] for i in ids]
        homes = [b // per_home for b in blocks]
        firsts = [(b % per_home) * chunk for b in blocks]
        places = [pl.multiple_of(f * head_rows, 16) for f in firsts]
        q = jnp.concatenate(
            [recv[h, pl.ds(p, rows), :] for h, p in zip(homes, places)], axis=0
        )
        own_keys = jnp.stack([recv[h, own_start : own_start + own_rows, :] for h in homes])
        own_values = jnp.stack(
            [recv[h, own_start + own_rows : own_start + 2 * own_rows, :] for h in homes]
        )
        keys = kv[..., :LANES].reshape(slots, key_count, LANES)
        values = kv[..., LANES:].reshape(slots, key_count, LANES)
        scores = jnp.einsum(
            "jqd,jkd->jqk",
            q.reshape(slots // pair, pair * head_rows, LANES),
            keys.reshape(slots // pair, pair * key_count, LANES),
            preferred_element_type=jnp.float32,
        )
        if pair == 2:
            scores = jnp.stack(
                [scores[:, :head_rows, :key_count], scores[:, head_rows:, key_count:]], axis=1
            ).reshape(slots, head_rows, key_count)
        kept = jnp.stack(
            [pos < slot_len[blocks[w] * chunk + j] for w in range(width) for j in range(chunk)]
        )
        scores = jnp.where(kept, scores, MASKED)
        own_scores = jnp.einsum(
            "jqd,jkd->jqk",
            q.reshape(width, rows, LANES),
            own_keys,
            preferred_element_type=jnp.float32,
        )
        own_hit = jnp.stack([own_axis == own_want + f for f in firsts])
        own_score = jnp.sum(jnp.where(own_hit, own_scores, 0.0), axis=2, keepdims=True)
        own_score = own_score.reshape(slots, head_rows, 1)
        top = jnp.maximum(jnp.max(scores, axis=2, keepdims=True), own_score)
        weights = jnp.exp2((scores - top) * scale)
        own_weight = jnp.exp2((own_score - top) * scale)
        total = jnp.sum(weights, axis=2, keepdims=True) + own_weight
        weights = weights.astype(jnp.bfloat16)
        if pair == 2:
            weights = weights.reshape(slots // 2, 2, head_rows, key_count)
            nothing = jnp.zeros((slots // 2, head_rows, key_count), jnp.bfloat16)
            upper = jnp.concatenate([weights[:, 0], nothing], axis=2)
            lower = jnp.concatenate([nothing, weights[:, 1]], axis=2)
            weights = jnp.concatenate([upper, lower], axis=1)
        mixed = jnp.einsum(
            "jqk,jkd->jqd",
            weights,
            values.reshape(slots // pair, pair * key_count, LANES),
            preferred_element_type=jnp.float32,
        )
        own_part = jnp.where(own_hit, own_weight.reshape(width, rows, 1), 0.0)
        mixed = mixed.reshape(width, rows, LANES) + jnp.einsum(
            "jqk,jkd->jqd",
            own_part.astype(jnp.bfloat16),
            own_values,
            preferred_element_type=jnp.float32,
        )
        mixed = mixed / total.reshape(width, rows, 1)
        for w in reversed(range(width)):
            out[homes[w], pl.ds(places[w], rows), :] = mixed[w].astype(out.dtype)

    several(0, ahead[...])

    def later(t, carry):
        for w in range(width):
            pl.when(t * width + w < live)(fetch(t * width + w).wait)
        several(t, held[pl.ds((t - 1) * slots, slots)])
        return carry

    lax.fori_loop(1, (live + width - 1) // width, later, 0)


def prefill_kernel(planes, tile, prefix_held, *rest):
    sources = rest[:planes]
    q, new_kv, out, keys, values, bias = rest[planes:]
    blk = sources[0].shape[2]
    prefix = planes * PLANE * PCAP * blk
    token_count = new_kv.shape[0]
    scale = LANES ** (-0.5) * LOG2E
    device = lax.axis_index("pool")

    @pl.when(pl.program_id(0) == 0)
    def _():
        lane_block = lax.broadcasted_iota(jnp.int32, (8, prefix), 1) // blk
        hide = jnp.zeros((8, prefix), jnp.float32)
        for step in range(planes):
            sender = device // PLANE
            sender = sender ^ step if planes & (planes - 1) == 0 else (sender + planes - step) % planes
            for t in range(PLANE):
                owner = sender * PLANE + ((device % PLANE) ^ t)
                for k in range(PCAP):
                    ordinal = (step * PLANE + t) * PCAP + k
                    block = sources[step][t, k]
                    keys[ordinal * blk : (ordinal + 1) * blk, :] = block[:, :LANES]
                    values[ordinal * blk : (ordinal + 1) * blk, :] = block[:, LANES:]
                    gone = jnp.where(prefix_held[owner] > k, 0.0, MASKED)
                    hide = jnp.where(lane_block == ordinal, gone, hide)
        bias[...] = hide
        keys[prefix:, :] = new_kv[:, :LANES]
        values[prefix:, :] = new_kv[:, LANES:]

    for t in range(token_count // tile):
        width = prefix + (t + 1) * tile
        block = q[t * tile : (t + 1) * tile, :]
        scores = lax.dot_general(
            block, keys[:width, :], (((1,), (1,)), ((), ())), preferred_element_type=jnp.float32
        )
        causal = lax.broadcasted_iota(jnp.int32, (tile, tile), 0) >= lax.broadcasted_iota(
            jnp.int32, (tile, tile), 1
        )
        pieces = [scores[:, :prefix] + bias[0:1, :]]
        if t:
            pieces.append(scores[:, prefix : width - tile])
        pieces.append(jnp.where(causal, scores[:, width - tile :], MASKED))
        scores = jnp.concatenate(pieces, axis=1)
        top = jnp.max(scores, axis=1, keepdims=True)
        weights = jnp.exp2((scores - top) * scale)
        total = jnp.sum(weights, axis=1, keepdims=True)
        mixed = jnp.dot(
            weights.astype(jnp.bfloat16), values[:width, :], preferred_element_type=jnp.float32
        )
        out[t * tile : (t + 1) * tile, :] = (mixed / total).astype(out.dtype)


def unpack_kernel(cap, head_rows, groups, back, out, rows_scr, group_fill):
    device = lax.axis_index("pool")
    row_count = out.shape[0]
    head_total = out.shape[1] // LANES
    for a in range(back.shape[0] // DGRP):
        group_fill[a] = 0
    for i in range(row_count):
        a = groups[device * row_count + i]
        c = group_fill[a]
        group_fill[a] = c + 1
        for m in range(DGRP):
            first = i * head_total + m * head_rows
            rows_scr[first : first + head_rows, :] = back[
                a * DGRP + m, pl.ds(pl.multiple_of(c * head_rows, 16), head_rows), :
            ].astype(jnp.float32)
    for h in range(head_total):
        out[:, h * LANES : (h + 1) * LANES] = rows_scr[
            pl.ds(h, row_count, stride=head_total), :
        ].astype(out.dtype)


def shards(
    pool_kv,
    prefix_table,
    prefix_count,
    prefill_q,
    prefill_new_kv,
    decode_q,
    decode_new,
    decode_cache,
    decode_group,
    cached_len,
):
    devices = lax.axis_size("pool")
    blk = pool_kv.shape[2]
    row_count, q_width = decode_q.shape
    cap = decode_cache.shape[1] // devices
    decode_groups = devices // DGRP
    pair_count = decode_cache.shape[2]
    head_rows = q_width // LANES // DGRP
    own_rows = up16(pair_count * cap)
    own_start = cap * head_rows
    message_rows = own_start + 2 * own_rows
    layout = (cap, head_rows, own_rows, own_start)
    groups = decode_group.reshape(-1)
    prefill_groups = prefix_table.shape[0]
    big = pltpu.CompilerParams(vmem_limit_bytes=60 * 2**20)
    small = pltpu.CompilerParams(vmem_limit_bytes=8 * 2**20)

    sending = pl.pallas_call(
        functools.partial(pack_kernel, layout),
        out_shape=jax.ShapeDtypeStruct((decode_groups, DGRP, message_rows, LANES), jnp.bfloat16),
        in_specs=[smem_spec(), vmem_spec(), vmem_spec()],
        out_specs=any_spec(),
        scratch_shapes=[
            pltpu.VMEM((row_count * q_width // LANES, LANES), jnp.float32),
            pltpu.VMEM((DGRP, decode_groups, message_rows, LANES), jnp.bfloat16),
            pltpu.SMEM((decode_groups,), jnp.int32),
            pltpu.SemaphoreType.DMA((DGRP,)),
        ],
        compiler_params=big,
        name="pack",
    )(in_hbm(groups), in_hbm(decode_q), in_hbm(decode_new))
    sending = sending.reshape(devices, message_rows, LANES)

    received = lax.all_to_all(sending, "pool", split_axis=0, concat_axis=0, tiled=True)

    share = jax.ShapeDtypeStruct(
        (PGRP // PLANE, prefill_groups, PCAP, blk, 2 * LANES), jnp.bfloat16
    )
    shares = pl.pallas_call(
        blocks_kernel,
        out_shape=(share,) * PLANE,
        in_specs=[smem_spec(), smem_spec(), any_spec()],
        out_specs=(any_spec(),) * PLANE,
        scratch_shapes=[pltpu.SemaphoreType.DMA((2 * PGRP * PCAP,))],
        compiler_params=small,
        cost_estimate=pl.CostEstimate(flops=100000, bytes_accessed=1000000, transcendentals=0),
        name="blocks",
    )(in_hbm(prefix_table), in_hbm(prefix_count), in_hbm(pool_kv))
    shares = [shares[0]] + [
        lax.ppermute(shares[t], "pool", [(i, i ^ t) for i in range(devices)])
        for t in range(1, PLANE)
    ]
    chunk = min(cap, 4)
    width = 8
    block_count = devices * cap // chunk
    slot_len, listed, prefix_held, ahead = pl.pallas_call(
        functools.partial(plan_kernel, cap, chunk, devices),
        out_shape=(
            jax.ShapeDtypeStruct((devices * cap,), jnp.int32),
            jax.ShapeDtypeStruct((block_count + 2,), jnp.int32),
            jax.ShapeDtypeStruct((devices * pool_kv.shape[0],), jnp.int32),
            jax.ShapeDtypeStruct((width * chunk,) + decode_cache.shape[2:], jnp.bfloat16),
        ),
        in_specs=[smem_spec()] * 4 + [any_spec()],
        out_specs=(smem_spec(),) * 3 + (vmem_spec(),),
        scratch_shapes=[pltpu.SemaphoreType.DMA((width,))],
        compiler_params=small,
        cost_estimate=pl.CostEstimate(flops=1000000, bytes_accessed=4000000, transcendentals=0),
        name="plan",
    )(in_hbm(prefix_table), in_hbm(prefix_count), in_hbm(groups), in_hbm(cached_len), in_hbm(decode_cache[0]))

    *shares, slot_len, listed = lax.optimization_barrier((*shares, slot_len, listed))
    planes = devices // PLANE
    bundle = jax.ShapeDtypeStruct((PLANE, PCAP, blk, 2 * LANES), jnp.bfloat16)
    bundles = pl.pallas_call(
        functools.partial(regroup_kernel, planes),
        out_shape=(bundle,) * planes,
        in_specs=[any_spec()] * PLANE,
        out_specs=(any_spec(),) * planes,
        scratch_shapes=[pltpu.SemaphoreType.DMA((planes * PLANE,))],
        compiler_params=small,
        cost_estimate=pl.CostEstimate(flops=100000, bytes_accessed=1000000, transcendentals=0),
        name="regroup",
    )(*shares)

    def along_line(step):
        pairs = [
            (i, partner(i // PLANE, step, planes) * PLANE + i % PLANE) for i in range(devices)
        ]
        return lax.ppermute(bundles[step], "pool", pairs)

    lines = [bundles[0], along_line(1)]

    lines += [along_line(step) for step in range(2, planes)]

    answers = pl.pallas_call(
        functools.partial(decode_kernel, layout, chunk, width),
        out_shape=jax.ShapeDtypeStruct((devices, cap * head_rows, LANES), jnp.bfloat16),
        in_specs=[smem_spec(), smem_spec(), vmem_spec(), vmem_spec(), any_spec()],
        out_specs=vmem_spec(),
        scratch_shapes=[
            pltpu.VMEM(((block_count - width) * chunk,) + decode_cache.shape[2:], jnp.bfloat16),
            pltpu.SemaphoreType.DMA((block_count - width,)),
        ],
        compiler_params=pltpu.CompilerParams(vmem_limit_bytes=20 * 2**20),
        cost_estimate=pl.CostEstimate(
            flops=500000000, bytes_accessed=8000000, transcendentals=1000000
        ),
        name="decode",
    )(listed, slot_len, received, ahead, in_hbm(decode_cache[0]))

    answers, *lines = lax.optimization_barrier((answers, *lines))
    back = lax.all_to_all(answers, "pool", split_axis=0, concat_axis=0, tiled=True)

    token_count, fill_width = prefill_q.shape[1:]
    prefix = devices * PCAP * blk
    head_count = fill_width // LANES
    prefix_held, _ = lax.optimization_barrier((prefix_held, answers))
    prefill_out = pl.pallas_call(
        functools.partial(prefill_kernel, planes, min(256, token_count)),
        grid=(head_count,),
        out_shape=jax.ShapeDtypeStruct((token_count, fill_width), jnp.bfloat16),
        in_specs=[smem_spec()]
        + [pl.BlockSpec(bundle.shape, lambda u: (0, 0, 0, 0))] * planes
        + [
            pl.BlockSpec((token_count, LANES), lambda u: (0, u)),
            pl.BlockSpec(prefill_new_kv.shape[1:], lambda u: (0, 0)),
        ],
        out_specs=pl.BlockSpec((token_count, LANES), lambda u: (0, u)),
        scratch_shapes=[
            pltpu.VMEM((prefix + token_count, LANES), jnp.bfloat16),
            pltpu.VMEM((prefix + token_count, LANES), jnp.bfloat16),
            pltpu.VMEM((8, prefix), jnp.float32),
        ],
        compiler_params=pltpu.CompilerParams(vmem_limit_bytes=16 * 2**20),
        cost_estimate=pl.CostEstimate(
            flops=2 * 2 * token_count * fill_width * (prefix + token_count // 2),
            bytes_accessed=3000000,
            transcendentals=token_count * head_count * (prefix + token_count // 2),
        ),
        name="prefill",
    )(prefix_held, *lines, in_hbm(prefill_q[0]), in_hbm(prefill_new_kv[0]))

    decode_out = pl.pallas_call(
        functools.partial(unpack_kernel, cap, head_rows),
        out_shape=jax.ShapeDtypeStruct((row_count, q_width), jnp.bfloat16),
        in_specs=[smem_spec(), vmem_spec()],
        out_specs=vmem_spec(),
        scratch_shapes=[
            pltpu.VMEM((row_count * q_width // LANES, LANES), jnp.float32),
            pltpu.SMEM((decode_groups,), jnp.int32),
        ],
        compiler_params=small,
        name="unpack",
    )(in_hbm(groups), back)
    return (prefill_out[None], decode_out)


def solution(mesh):
    in_specs = (
        P(("rep", "pool"), None, None, None),
        P("rep", None),
        P("rep"),
        P(("rep", "pool"), None, None),
        P(("rep", "pool"), None, None),
        P(("rep", "pool"), None),
        P(("rep", "pool"), None),
        P(("rep", "pool"), None, None, None, None),
        P("rep", None),
        P("rep"),
    )
    out_specs = (P(("rep", "pool"), None, None), P(("rep", "pool"), None))
    return jax.shard_map(shards, mesh=mesh, in_specs=in_specs, out_specs=out_specs, check_vma=False)
```

```python
import functools

import jax
import jax.numpy as jnp
from jax import lax
from jax.experimental import pallas as pl
from jax.experimental.pallas import tpu as pltpu
from jax.sharding import PartitionSpec as P

PGRP = 8
DGRP = 4
PCAP = 2
PLANE = 4
LANES = 128
MASKED = -1e30
LOG2E = 1.4426950408889634


def any_spec():
    return pl.BlockSpec(memory_space=pl.ANY)


def smem_spec():
    return pl.BlockSpec(memory_space=pltpu.SMEM)


def in_hbm(x):
    return pltpu.with_memory_space_constraint(x, pltpu.HBM)


def vmem_spec():
    return pl.BlockSpec(memory_space=pltpu.VMEM)


def pack_kernel(head_rows, groups, q, out, rows_scr, stage, group_fill, sems):
    decode_groups = out.shape[0]
    row_count = q.shape[0]
    head_total = q.shape[1] // LANES
    device = lax.axis_index("pool")
    for a in range(decode_groups):
        group_fill[a] = 0
    for h in range(head_total):
        rows_scr[pl.ds(h, row_count, stride=head_total), :] = q[
            :, h * LANES : (h + 1) * LANES
        ].astype(jnp.float32)
    homes = []
    for i in range(row_count):
        a = groups[device * row_count + i]
        c = group_fill[a]
        group_fill[a] = c + 1
        homes.append((a, c))
    copies = []
    for m in range(DGRP):
        for i, (a, c) in enumerate(homes):
            first = i * head_total + m * head_rows
            stage[m, a, pl.ds(pl.multiple_of(c * head_rows, 16), head_rows), :] = rows_scr[
                first : first + head_rows, :
            ].astype(out.dtype)
        copy = pltpu.make_async_copy(stage.at[m], out.at[:, m], sems.at[m])
        copy.start()
        copies.append(copy)
    for copy in copies:
        copy.wait()


def blocks_kernel(table, count, pool, *rest):
    outs, sems = rest[:PLANE], rest[PLANE]
    blocks_here = pool.shape[0]
    group_count, most_blocks = table.shape
    device = lax.axis_index("pool")
    first_block = device * blocks_here
    flying = []
    for g in range(group_count):

        def scan_table(j, carry):
            seen, chosen = carry
            entry = table[g, j]
            mine = (entry >= first_block) & (entry < first_block + blocks_here) & (j < count[g])
            chosen = tuple(
                jnp.where(mine & (seen == k), entry - first_block, chosen[k]) for k in range(PCAP)
            )
            return seen + mine.astype(jnp.int32), chosen

        start = (jnp.int32(0), tuple(jnp.int32(0) for _ in range(PCAP)))
        _, chosen = lax.fori_loop(0, most_blocks, scan_table, start, unroll=8)
        if g >= 2:
            for copy in flying.pop(0):
                copy.wait()
        copies = []
        for half in range(PGRP // PLANE):
            for t in range(PLANE):
                for k in range(PCAP):
                    copy = pltpu.make_async_copy(
                        pool.at[chosen[k], half * PLANE + ((device % PLANE) ^ t)],
                        outs[t].at[half, g, k],
                        sems.at[((g % 2) * PGRP + half * PLANE + t) * PCAP + k],
                    )
                    copy.start()
                    copies.append(copy)
        flying.append(copies)
    for copies in flying:
        for copy in copies:
            copy.wait()


def partner(plane, step, planes):
    return plane ^ step if planes & (planes - 1) == 0 else (plane + step) % planes


def regroup_kernel(planes, *rest):
    held, outs, sems = rest[:PLANE], rest[PLANE:-1], rest[-1]
    mine = lax.axis_index("pool") // PLANE
    per_group = PGRP // PLANE
    copies = []
    for step in range(planes):
        there = partner(mine, step, planes)
        for t in range(PLANE):
            copy = pltpu.make_async_copy(
                held[t].at[there % per_group, there // per_group],
                outs[step].at[t],
                sems.at[step * PLANE + t],
            )
            copy.start()
            copies.append(copy)
    for copy in copies:
        copy.wait()


def fetch_block(cache, listed, i, chunk, held, place, sem):
    return pltpu.make_async_copy(
        cache.at[pl.ds(listed[1 + i] * chunk, chunk)], held.at[pl.ds(place * chunk, chunk)], sem
    )


def plan_kernel(
    cap,
    step,
    owners,
    table,
    count,
    groups,
    lengths,
    cache,
    slot_len,
    listed,
    prefix_held,
    places,
    ahead,
    group_fill,
    sems,
):
    device = lax.axis_index("pool")
    home_count = owners
    row_count = groups.shape[0] // home_count
    for a in range(owners // DGRP):
        group_fill[a] = 0
    for i in range(row_count):
        a = groups[device * row_count + i]
        places[2 * i] = a
        places[2 * i + 1] = group_fill[a]
        group_fill[a] = group_fill[a] + 1
    group_id = device // DGRP
    prefill_id = device // PGRP
    blocks_here = listed.shape[0]
    most_blocks = table.shape[1]
    chunk = min(cap, step)

    def one_owner(o, carry):
        prefix_held[o] = 0
        return carry

    lax.fori_loop(0, owners, one_owner, 0)
    pool_blocks = prefix_held.shape[0] // owners

    def one_entry(j, carry):
        o = table[prefill_id, j] // pool_blocks
        prefix_held[o] = prefix_held[o] + 1
        return carry

    lax.fori_loop(0, jnp.minimum(count[prefill_id], most_blocks), one_entry, 0)

    def one_home(s, filled):
        for c in range(cap):
            slot_len[s * cap + c] = 0
        here = jnp.int32(0)
        for i in range(row_count):
            row = s * row_count + i
            mine = groups[row] == group_id
            place = s * cap + jnp.minimum(here, cap - 1)
            slot_len[place] = jnp.where(mine, lengths[row], slot_len[place])
            here = here + mine.astype(jnp.int32)
        for b in range(cap // chunk):
            listed[1 + jnp.minimum(filled, blocks_here - 2)] = s * (cap // chunk) + b
            filled = filled + (here > b * chunk).astype(jnp.int32)
        return filled

    live = lax.fori_loop(0, home_count, one_home, jnp.int32(0))
    listed[0] = live
    for i in range(ahead.shape[0] // chunk):
        pl.when(i < live)(fetch_block(cache, listed, i, chunk, ahead, i, sems.at[i]).start)
    for i in range(ahead.shape[0] // chunk):
        pl.when(i < live)(fetch_block(cache, listed, i, chunk, ahead, i, sems.at[i]).wait)


def decode_kernel(
    cap, head_rows, chunk, width, listed, slot_len, recv, ahead, cache, out, held, sems
):
    pair_count, positions = cache.shape[1], cache.shape[2]
    per_home = cap // chunk
    key_count = pair_count * positions
    query_heads = head_rows // pair_count
    live = listed[0]
    scale = LANES ** (-0.5) * LOG2E
    rows = chunk * head_rows
    slots = width * chunk
    pair = 2 if chunk % 2 == 0 else 1

    def fetch(i):
        return fetch_block(cache, listed, i, chunk, held, i - width, sems.at[i - width])

    def begin(i, carry):
        fetch(i).start()
        return carry

    lax.fori_loop(width, live, begin, 0)
    row_pair = lax.broadcasted_iota(jnp.int32, (head_rows, key_count), 0) // query_heads
    key_axis = lax.broadcasted_iota(jnp.int32, (head_rows, key_count), 1)
    pos = jnp.where(key_axis // positions == row_pair, key_axis % positions, positions)
    lane = lax.broadcasted_iota(jnp.int32, (head_rows, LANES), 1)

    def several(t, kv):
        ids = [jnp.minimum(t * width + w, live - 1) for w in range(width)]
        blocks = [listed[1 + i] for i in ids]
        homes = [b // per_home for b in blocks]
        firsts = [(b % per_home) * chunk for b in blocks]
        places = [pl.multiple_of(f * head_rows, 16) for f in firsts]
        q = jnp.concatenate(
            [recv[h, pl.ds(p, rows), :] for h, p in zip(homes, places)], axis=0
        )
        keys = kv[..., :LANES].reshape(slots, key_count, LANES)
        values = kv[..., LANES:].reshape(slots, key_count, LANES)
        scores = jnp.einsum(
            "jqd,jkd->jqk",
            q.reshape(slots // pair, pair * head_rows, LANES),
            keys.reshape(slots // pair, pair * key_count, LANES),
            preferred_element_type=jnp.float32,
        )
        if pair == 2:
            scores = jnp.stack(
                [scores[:, :head_rows, :key_count], scores[:, head_rows:, key_count:]], axis=1
            ).reshape(slots, head_rows, key_count)
        kept = jnp.stack(
            [pos < slot_len[blocks[w] * chunk + j] for w in range(width) for j in range(chunk)]
        )
        scores = jnp.where(kept, scores, MASKED)
        top = jnp.max(scores, axis=2, keepdims=True)
        weights = jnp.exp2((scores - top) * scale)
        total = jnp.sum(weights, axis=2, keepdims=True)
        weights = weights.astype(jnp.bfloat16)
        if pair == 2:
            weights = weights.reshape(slots // 2, 2, head_rows, key_count)
            nothing = jnp.zeros((slots // 2, head_rows, key_count), jnp.bfloat16)
            upper = jnp.concatenate([weights[:, 0], nothing], axis=2)
            lower = jnp.concatenate([nothing, weights[:, 1]], axis=2)
            weights = jnp.concatenate([upper, lower], axis=1)
        mixed = jnp.einsum(
            "jqk,jkd->jqd",
            weights,
            values.reshape(slots // pair, pair * key_count, LANES),
            preferred_element_type=jnp.float32,
        )
        mixed = mixed.reshape(slots, head_rows, LANES) / total
        mass = top * scale + jnp.log(total) * LOG2E
        high = mass.astype(jnp.bfloat16).astype(jnp.float32)
        middle = (mass - high).astype(jnp.bfloat16).astype(jnp.float32)
        low = mass - high - middle
        mixed = mixed.reshape(width, rows, LANES)
        for w in reversed(range(width)):
            out[homes[w], pl.ds(places[w], rows), :] = mixed[w].astype(out.dtype)
            masses = out[homes[w], cap * head_rows :, :].astype(jnp.float32)
            for j in range(chunk):
                at = w * chunk + j
                split = jnp.where(
                    lane % 3 == 0, high[at], jnp.where(lane % 3 == 1, middle[at], low[at])
                )
                masses = jnp.where(lane // 3 == firsts[w] + j, split, masses)
            out[homes[w], cap * head_rows :, :] = masses.astype(out.dtype)

    several(0, ahead[...])

    def later(t, carry):
        for w in range(width):
            pl.when(t * width + w < live)(fetch(t * width + w).wait)
        several(t, held[pl.ds((t - 1) * slots, slots)])
        return carry

    lax.fori_loop(1, (live + width - 1) // width, later, 0)


def prefill_kernel(planes, tile, prefix_held, *rest):
    sources = rest[:planes]
    q, new_kv, out, keys, values, bias = rest[planes:]
    blk = sources[0].shape[2]
    prefix = planes * PLANE * PCAP * blk
    token_count = new_kv.shape[0]
    scale = LANES ** (-0.5) * LOG2E
    device = lax.axis_index("pool")

    @pl.when(pl.program_id(0) == 0)
    def _():
        lane_block = lax.broadcasted_iota(jnp.int32, (8, prefix), 1) // blk
        hide = jnp.zeros((8, prefix), jnp.float32)
        for step in range(planes):
            sender = device // PLANE
            sender = sender ^ step if planes & (planes - 1) == 0 else (sender + planes - step) % planes
            for t in range(PLANE):
                owner = sender * PLANE + ((device % PLANE) ^ t)
                for k in range(PCAP):
                    ordinal = (step * PLANE + t) * PCAP + k
                    block = sources[step][t, k]
                    keys[ordinal * blk : (ordinal + 1) * blk, :] = block[:, :LANES]
                    values[ordinal * blk : (ordinal + 1) * blk, :] = block[:, LANES:]
                    gone = jnp.where(prefix_held[owner] > k, 0.0, MASKED)
                    hide = jnp.where(lane_block == ordinal, gone, hide)
        bias[...] = hide
        keys[prefix:, :] = new_kv[:, :LANES]
        values[prefix:, :] = new_kv[:, LANES:]

    for t in range(token_count // tile):
        width = prefix + (t + 1) * tile
        block = q[t * tile : (t + 1) * tile, :]
        scores = lax.dot_general(
            block, keys[:width, :], (((1,), (1,)), ((), ())), preferred_element_type=jnp.float32
        )
        causal = lax.broadcasted_iota(jnp.int32, (tile, tile), 0) >= lax.broadcasted_iota(
            jnp.int32, (tile, tile), 1
        )
        pieces = [scores[:, :prefix] + bias[0:1, :]]
        if t:
            pieces.append(scores[:, prefix : width - tile])
        pieces.append(jnp.where(causal, scores[:, width - tile :], MASKED))
        scores = jnp.concatenate(pieces, axis=1)
        top = jnp.max(scores, axis=1, keepdims=True)
        weights = jnp.exp2((scores - top) * scale)
        total = jnp.sum(weights, axis=1, keepdims=True)
        mixed = jnp.dot(
            weights.astype(jnp.bfloat16), values[:width, :], preferred_element_type=jnp.float32
        )
        out[t * tile : (t + 1) * tile, :] = (mixed / total).astype(out.dtype)


def own_kernel(q, kv, score, value, key):
    row_count = q.shape[0]
    head_total = q.shape[1] // LANES
    per_pair = head_total // (kv.shape[1] // (2 * LANES))
    for h in range(head_total):
        at = pl.ds(h, row_count, stride=head_total)
        lane = h // per_pair * 2 * LANES
        score[at, :] = q[:, h * LANES : (h + 1) * LANES].astype(jnp.float32)
        key[at, :] = kv[:, lane : lane + LANES].astype(jnp.float32)
        value[at, :] = kv[:, lane + LANES : lane + 2 * LANES].astype(jnp.float32)
    for i in range(row_count):
        at = slice(i * head_total, (i + 1) * head_total)
        product = jnp.sum(score[at, :] * key[at, :], axis=1, keepdims=True)
        score[at, :] = jnp.broadcast_to(product * (LANES ** (-0.5) * LOG2E), (head_total, LANES))


def unpack_kernel(cap, head_rows, places, back, score, value, out, rows_scr):
    row_count = out.shape[0]
    head_total = out.shape[1] // LANES
    lane = lax.broadcasted_iota(jnp.int32, (head_rows, LANES), 1) // 3
    for i in range(row_count):
        a, c = places[2 * i], places[2 * i + 1]
        for m in range(DGRP):
            at = slice(i * head_total + m * head_rows, i * head_total + (m + 1) * head_rows)
            cached = back[
                a * DGRP + m, pl.ds(pl.multiple_of(c * head_rows, 16), head_rows), :
            ].astype(jnp.float32)
            masses = back[a * DGRP + m, cap * head_rows :, :].astype(jnp.float32)
            mass = jnp.sum(jnp.where(lane == c, masses, 0.0), axis=1, keepdims=True)
            share = 1.0 / (1.0 + jnp.exp2(mass - score[at, :]))
            rows_scr[at, :] = cached + share * (value[at, :] - cached)
    for h in range(head_total):
        out[:, h * LANES : (h + 1) * LANES] = rows_scr[
            pl.ds(h, row_count, stride=head_total), :
        ].astype(out.dtype)


def shards(
    pool_kv,
    prefix_table,
    prefix_count,
    prefill_q,
    prefill_new_kv,
    decode_q,
    decode_new,
    decode_cache,
    decode_group,
    cached_len,
):
    devices = lax.axis_size("pool")
    blk = pool_kv.shape[2]
    row_count, q_width = decode_q.shape
    cap = decode_cache.shape[1] // devices
    decode_groups = devices // DGRP
    pair_count = decode_cache.shape[2]
    head_rows = q_width // LANES // DGRP
    message_rows = cap * head_rows
    groups = decode_group.reshape(-1)
    prefill_groups = prefix_table.shape[0]
    big = pltpu.CompilerParams(vmem_limit_bytes=60 * 2**20)
    small = pltpu.CompilerParams(vmem_limit_bytes=8 * 2**20)

    sending = pl.pallas_call(
        functools.partial(pack_kernel, head_rows),
        out_shape=jax.ShapeDtypeStruct((decode_groups, DGRP, message_rows, LANES), jnp.bfloat16),
        in_specs=[smem_spec(), vmem_spec()],
        out_specs=any_spec(),
        scratch_shapes=[
            pltpu.VMEM((row_count * q_width // LANES, LANES), jnp.float32),
            pltpu.VMEM((DGRP, decode_groups, message_rows, LANES), jnp.bfloat16),
            pltpu.SMEM((decode_groups,), jnp.int32),
            pltpu.SemaphoreType.DMA((DGRP,)),
        ],
        compiler_params=big,
        name="pack",
    )(in_hbm(groups), in_hbm(decode_q))
    sending = sending.reshape(devices, message_rows, LANES)

    received = lax.all_to_all(sending, "pool", split_axis=0, concat_axis=0, tiled=True)

    share = jax.ShapeDtypeStruct(
        (PGRP // PLANE, prefill_groups, PCAP, blk, 2 * LANES), jnp.bfloat16
    )
    shares = pl.pallas_call(
        blocks_kernel,
        out_shape=(share,) * PLANE,
        in_specs=[smem_spec(), smem_spec(), any_spec()],
        out_specs=(any_spec(),) * PLANE,
        scratch_shapes=[pltpu.SemaphoreType.DMA((2 * PGRP * PCAP,))],
        compiler_params=small,
        cost_estimate=pl.CostEstimate(flops=100000, bytes_accessed=1000000, transcendentals=0),
        name="blocks",
    )(in_hbm(prefix_table), in_hbm(prefix_count), in_hbm(pool_kv))
    shares = [shares[0]] + [
        lax.ppermute(shares[t], "pool", [(i, i ^ t) for i in range(devices)])
        for t in range(1, PLANE)
    ]
    chunk = min(cap, 4)
    width = 8
    block_count = devices * cap // chunk
    slot_len, listed, prefix_held, places, ahead = pl.pallas_call(
        functools.partial(plan_kernel, cap, chunk, devices),
        out_shape=(
            jax.ShapeDtypeStruct((devices * cap,), jnp.int32),
            jax.ShapeDtypeStruct((block_count + 2,), jnp.int32),
            jax.ShapeDtypeStruct((devices * pool_kv.shape[0],), jnp.int32),
            jax.ShapeDtypeStruct((2 * row_count,), jnp.int32),
            jax.ShapeDtypeStruct((width * chunk,) + decode_cache.shape[2:], jnp.bfloat16),
        ),
        in_specs=[smem_spec()] * 4 + [any_spec()],
        out_specs=(smem_spec(),) * 4 + (vmem_spec(),),
        scratch_shapes=[pltpu.SMEM((decode_groups,), jnp.int32), pltpu.SemaphoreType.DMA((width,))],
        compiler_params=small,
        cost_estimate=pl.CostEstimate(flops=1000000, bytes_accessed=4000000, transcendentals=0),
        name="plan",
    )(in_hbm(prefix_table), in_hbm(prefix_count), in_hbm(groups), in_hbm(cached_len), in_hbm(decode_cache[0]))

    *shares, slot_len, listed = lax.optimization_barrier((*shares, slot_len, listed))
    planes = devices // PLANE
    bundle = jax.ShapeDtypeStruct((PLANE, PCAP, blk, 2 * LANES), jnp.bfloat16)
    bundles = pl.pallas_call(
        functools.partial(regroup_kernel, planes),
        out_shape=(bundle,) * planes,
        in_specs=[any_spec()] * PLANE,
        out_specs=(any_spec(),) * planes,
        scratch_shapes=[pltpu.SemaphoreType.DMA((planes * PLANE,))],
        compiler_params=small,
        cost_estimate=pl.CostEstimate(flops=100000, bytes_accessed=1000000, transcendentals=0),
        name="regroup",
    )(*shares)

    def along_line(step):
        pairs = [
            (i, partner(i // PLANE, step, planes) * PLANE + i % PLANE) for i in range(devices)
        ]
        return lax.ppermute(bundles[step], "pool", pairs)

    lines = [bundles[0], along_line(1)]

    lines += [along_line(step) for step in range(2, planes)]

    answers = pl.pallas_call(
        functools.partial(decode_kernel, cap, head_rows, chunk, width),
        out_shape=jax.ShapeDtypeStruct((devices, (cap + 1) * head_rows, LANES), jnp.bfloat16),
        in_specs=[smem_spec(), smem_spec(), vmem_spec(), vmem_spec(), any_spec()],
        out_specs=vmem_spec(),
        scratch_shapes=[
            pltpu.VMEM(((block_count - width) * chunk,) + decode_cache.shape[2:], jnp.bfloat16),
            pltpu.SemaphoreType.DMA((block_count - width,)),
        ],
        compiler_params=pltpu.CompilerParams(vmem_limit_bytes=20 * 2**20),
        cost_estimate=pl.CostEstimate(
            flops=500000000, bytes_accessed=8000000, transcendentals=1000000
        ),
        name="decode",
    )(listed, slot_len, received, ahead, in_hbm(decode_cache[0]))

    answers, *lines = lax.optimization_barrier((answers, *lines))
    back = lax.all_to_all(answers, "pool", split_axis=0, concat_axis=0, tiled=True)

    token_count, fill_width = prefill_q.shape[1:]
    prefix = devices * PCAP * blk
    head_count = fill_width // LANES
    prefix_held, decode_q, decode_new, _ = lax.optimization_barrier(
        (prefix_held, decode_q, decode_new, answers)
    )
    expanded = jax.ShapeDtypeStruct((row_count * q_width // LANES, LANES), jnp.float32)
    own_score, own_value = pl.pallas_call(
        own_kernel,
        out_shape=(expanded, expanded),
        in_specs=[vmem_spec(), vmem_spec()],
        out_specs=(vmem_spec(), vmem_spec()),
        scratch_shapes=[pltpu.VMEM(expanded.shape, jnp.float32)],
        compiler_params=small,
        cost_estimate=pl.CostEstimate(flops=1000000, bytes_accessed=2000000, transcendentals=0),
        name="own",
    )(in_hbm(decode_q), in_hbm(decode_new))
    prefill_out = pl.pallas_call(
        functools.partial(prefill_kernel, planes, min(256, token_count)),
        grid=(head_count,),
        out_shape=jax.ShapeDtypeStruct((token_count, fill_width), jnp.bfloat16),
        in_specs=[smem_spec()]
        + [pl.BlockSpec(bundle.shape, lambda u: (0, 0, 0, 0))] * planes
        + [
            pl.BlockSpec((token_count, LANES), lambda u: (0, u)),
            pl.BlockSpec(prefill_new_kv.shape[1:], lambda u: (0, 0)),
        ],
        out_specs=pl.BlockSpec((token_count, LANES), lambda u: (0, u)),
        scratch_shapes=[
            pltpu.VMEM((prefix + token_count, LANES), jnp.bfloat16),
            pltpu.VMEM((prefix + token_count, LANES), jnp.bfloat16),
            pltpu.VMEM((8, prefix), jnp.float32),
        ],
        compiler_params=pltpu.CompilerParams(vmem_limit_bytes=16 * 2**20),
        cost_estimate=pl.CostEstimate(
            flops=2 * 2 * token_count * fill_width * (prefix + token_count // 2),
            bytes_accessed=3000000,
            transcendentals=token_count * head_count * (prefix + token_count // 2),
        ),
        name="prefill",
    )(prefix_held, *lines, in_hbm(prefill_q[0]), in_hbm(prefill_new_kv[0]))

    decode_out = pl.pallas_call(
        functools.partial(unpack_kernel, cap, head_rows),
        out_shape=jax.ShapeDtypeStruct((row_count, q_width), jnp.bfloat16),
        in_specs=[smem_spec()] + [vmem_spec()] * 3,
        out_specs=vmem_spec(),
        scratch_shapes=[pltpu.VMEM(expanded.shape, jnp.float32)],
        compiler_params=small,
        name="unpack",
    )(places, back, own_score, own_value)
    return (prefill_out[None], decode_out)


def solution(mesh):
    in_specs = (
        P(("rep", "pool"), None, None, None),
        P("rep", None),
        P("rep"),
        P(("rep", "pool"), None, None),
        P(("rep", "pool"), None, None),
        P(("rep", "pool"), None),
        P(("rep", "pool"), None),
        P(("rep", "pool"), None, None, None, None),
        P("rep", None),
        P("rep"),
    )
    out_specs = (P(("rep", "pool"), None, None), P(("rep", "pool"), None))
    return jax.shard_map(shards, mesh=mesh, in_specs=in_specs, out_specs=out_specs, check_vma=False)
```

```python
import functools

import jax
import jax.numpy as jnp
from jax import lax
from jax.experimental import pallas as pl
from jax.experimental.pallas import tpu as pltpu
from jax.sharding import PartitionSpec as P

PGRP = 8
DGRP = 4
PCAP = 2
PLANE = 4
LANES = 128
MASKED = -1e30
LOG2E = 1.4426950408889634


def any_spec():
    return pl.BlockSpec(memory_space=pl.ANY)


def smem_spec():
    return pl.BlockSpec(memory_space=pltpu.SMEM)


def in_hbm(x):
    return pltpu.with_memory_space_constraint(x, pltpu.HBM)


def vmem_spec():
    return pl.BlockSpec(memory_space=pltpu.VMEM)


def pack_kernel(head_rows, groups, q, out, rows_scr, stage, group_fill, sems):
    decode_groups = out.shape[0]
    row_count = q.shape[0]
    head_total = q.shape[1] // LANES
    device = lax.axis_index("pool")
    for a in range(decode_groups):
        group_fill[a] = 0
    for h in range(head_total):
        rows_scr[pl.ds(h, row_count, stride=head_total), :] = q[
            :, h * LANES : (h + 1) * LANES
        ].astype(jnp.float32)
    homes = []
    for i in range(row_count):
        a = groups[device * row_count + i]
        c = group_fill[a]
        group_fill[a] = c + 1
        homes.append((a, c))
    copies = []
    for m in range(DGRP):
        for i, (a, c) in enumerate(homes):
            first = i * head_total + m * head_rows
            stage[m, a, pl.ds(pl.multiple_of(c * head_rows, 16), head_rows), :] = rows_scr[
                first : first + head_rows, :
            ].astype(out.dtype)
        copy = pltpu.make_async_copy(stage.at[m], out.at[:, m], sems.at[m])
        copy.start()
        copies.append(copy)
    for copy in copies:
        copy.wait()


def blocks_kernel(table, count, pool, *rest):
    outs, sems = rest[:PLANE], rest[PLANE]
    blocks_here = pool.shape[0]
    group_count, most_blocks = table.shape
    device = lax.axis_index("pool")
    first_block = device * blocks_here
    flying = []
    for g in range(group_count):

        def scan_table(j, carry):
            seen, chosen = carry
            entry = table[g, j]
            mine = (entry >= first_block) & (entry < first_block + blocks_here) & (j < count[g])
            chosen = tuple(
                jnp.where(mine & (seen == k), entry - first_block, chosen[k]) for k in range(PCAP)
            )
            return seen + mine.astype(jnp.int32), chosen

        start = (jnp.int32(0), tuple(jnp.int32(0) for _ in range(PCAP)))
        _, chosen = lax.fori_loop(0, most_blocks, scan_table, start, unroll=8)
        if g >= 2:
            for copy in flying.pop(0):
                copy.wait()
        copies = []
        for t in range(PLANE):
            for k in range(PCAP):
                copy = pltpu.make_async_copy(
                    pool.at[chosen[k], :, (device % PLANE) ^ t],
                    outs[t].at[:, g, k],
                    sems.at[((g % 2) * PLANE + t) * PCAP + k],
                )
                copy.start()
                copies.append(copy)
        flying.append(copies)
    for copies in flying:
        for copy in copies:
            copy.wait()


def partner(plane, step, planes):
    return plane ^ step if planes & (planes - 1) == 0 else (plane + step) % planes


def regroup_kernel(planes, *rest):
    held, outs, sems = rest[:PLANE], rest[PLANE:-1], rest[-1]
    mine = lax.axis_index("pool") // PLANE
    per_group = PGRP // PLANE
    copies = []
    for step in range(planes):
        there = partner(mine, step, planes)
        for t in range(PLANE):
            copy = pltpu.make_async_copy(
                held[t].at[there % per_group, there // per_group],
                outs[step].at[t],
                sems.at[step * PLANE + t],
            )
            copy.start()
            copies.append(copy)
    for copy in copies:
        copy.wait()


def fetch_block(cache, listed, i, chunk, held, place, sem):
    return pltpu.make_async_copy(
        cache.at[pl.ds(listed[1 + i] * chunk, chunk)], held.at[pl.ds(place * chunk, chunk)], sem
    )


def plan_kernel(
    cap,
    step,
    owners,
    table,
    count,
    groups,
    lengths,
    cache,
    slot_len,
    listed,
    prefix_held,
    places,
    ahead,
    group_fill,
    found,
    sems,
):
    device = lax.axis_index("pool")
    home_count = owners
    row_count = groups.shape[0] // home_count
    group_id = device // DGRP
    prefill_id = device // PGRP
    blocks_here = listed.shape[0]
    most_blocks = table.shape[1]
    chunk = min(cap, step)

    def one_home(s, filled):
        here = jnp.int32(0)
        for i in range(row_count):
            row = s * row_count + i
            found[here] = lengths[row]
            here = here + (groups[row] == group_id).astype(jnp.int32)
        for c in range(cap):
            slot_len[s * cap + c] = jnp.where(c < here, found[c], 0)
        for b in range(cap // chunk):
            listed[1 + jnp.minimum(filled, blocks_here - 2)] = s * (cap // chunk) + b
            filled = filled + (here > b * chunk).astype(jnp.int32)
        return filled

    live = lax.fori_loop(0, home_count, one_home, jnp.int32(0))
    listed[0] = live
    for i in range(ahead.shape[0] // chunk):
        pl.when(i < live)(fetch_block(cache, listed, i, chunk, ahead, i, sems.at[i]).start)

    for a in range(owners // DGRP):
        group_fill[a] = 0
    for i in range(row_count):
        a = groups[device * row_count + i]
        c = group_fill[a]
        places[2 * i] = a
        places[2 * i + 1] = c
        group_fill[a] = c + 1

    def one_owner(o, carry):
        prefix_held[o] = 0
        return carry

    lax.fori_loop(0, owners, one_owner, 0, unroll=8)
    pool_blocks = prefix_held.shape[0] // owners

    def one_entry(j, carry):
        o = lax.div(table[prefill_id, j], pool_blocks)
        prefix_held[o] = prefix_held[o] + 1
        return carry

    lax.fori_loop(0, jnp.minimum(count[prefill_id], most_blocks), one_entry, 0)
    for i in range(ahead.shape[0] // chunk):
        pl.when(i < live)(fetch_block(cache, listed, i, chunk, ahead, i, sems.at[i]).wait)


def decode_kernel(
    cap, head_rows, chunk, width, listed, slot_len, recv, ahead, cache, out, held, sems
):
    pair_count, positions = cache.shape[1], cache.shape[2]
    per_home = cap // chunk
    key_count = pair_count * positions
    query_heads = head_rows // pair_count
    live = listed[0]
    scale = LANES ** (-0.5) * LOG2E
    rows = chunk * head_rows
    slots = width * chunk
    pair = 2 if chunk % 2 == 0 else 1

    def fetch(i):
        return fetch_block(cache, listed, i, chunk, held, i - width, sems.at[i - width])

    def begin(i, carry):
        fetch(i).start()
        return carry

    lax.fori_loop(width, live, begin, 0)
    row_pair = lax.broadcasted_iota(jnp.int32, (head_rows, key_count), 0) // query_heads
    key_axis = lax.broadcasted_iota(jnp.int32, (head_rows, key_count), 1)
    pos = jnp.where(key_axis // positions == row_pair, key_axis % positions, positions)
    half = head_rows // 2
    lane = lax.broadcasted_iota(jnp.int32, (half, LANES), 1)
    part, stat_slot = lane % (LANES // 2) % 3, lane % (LANES // 2) // 3

    def several(t, kv):
        ids = [jnp.minimum(t * width + w, live - 1) for w in range(width)]
        blocks = [listed[1 + i] for i in ids]
        homes = [b // per_home for b in blocks]
        firsts = [(b % per_home) * chunk for b in blocks]
        places = [pl.multiple_of(f * head_rows, 16) for f in firsts]
        q = jnp.concatenate(
            [recv[h, pl.ds(p, rows), :] for h, p in zip(homes, places)], axis=0
        )
        keys = kv[..., :LANES].reshape(slots, key_count, LANES)
        values = kv[..., LANES:].reshape(slots, key_count, LANES)
        scores = jnp.einsum(
            "jqd,jkd->jqk",
            q.reshape(slots // pair, pair * head_rows, LANES),
            keys.reshape(slots // pair, pair * key_count, LANES),
            preferred_element_type=jnp.float32,
        )
        if pair == 2:
            scores = jnp.stack(
                [scores[:, :head_rows, :key_count], scores[:, head_rows:, key_count:]], axis=1
            ).reshape(slots, head_rows, key_count)
        kept = jnp.stack(
            [pos < slot_len[blocks[w] * chunk + j] for w in range(width) for j in range(chunk)]
        )
        scores = jnp.where(kept, scores, MASKED)
        top = jnp.max(scores, axis=2, keepdims=True)
        weights = jnp.exp2((scores - top) * scale)
        total = jnp.sum(weights, axis=2, keepdims=True)
        weights = weights.astype(jnp.bfloat16)
        if pair == 2:
            weights = weights.reshape(slots // 2, 2, head_rows, key_count)
            nothing = jnp.zeros((slots // 2, head_rows, key_count), jnp.bfloat16)
            upper = jnp.concatenate([weights[:, 0], nothing], axis=2)
            lower = jnp.concatenate([nothing, weights[:, 1]], axis=2)
            weights = jnp.concatenate([upper, lower], axis=1)
        mixed = jnp.einsum(
            "jqk,jkd->jqd",
            weights,
            values.reshape(slots // pair, pair * key_count, LANES),
            preferred_element_type=jnp.float32,
        )
        mixed = mixed.reshape(slots, head_rows, LANES) / total
        mass = top * scale + jnp.log(total) * LOG2E
        high = mass.astype(jnp.bfloat16).astype(jnp.float32)
        middle = (mass - high).astype(jnp.bfloat16).astype(jnp.float32)
        low = mass - high - middle
        mixed = mixed.reshape(width, rows, LANES)
        for w in reversed(range(width)):
            out[homes[w], pl.ds(places[w], rows), :] = mixed[w].astype(out.dtype)
            masses = out[homes[w], cap * head_rows :, :].astype(jnp.float32)
            for j in range(chunk):
                at = w * chunk + j
                split = [
                    jnp.where(lane < LANES // 2, piece[at, :half], piece[at, half:])
                    for piece in (high, middle, low)
                ]
                split = jnp.where(part == 0, split[0], jnp.where(part == 1, split[1], split[2]))
                masses = jnp.where(stat_slot == firsts[w] + j, split, masses)
            out[homes[w], cap * head_rows :, :] = masses.astype(out.dtype)

    several(0, ahead[...])

    def later(t, carry):
        for w in range(width):
            pl.when(t * width + w < live)(fetch(t * width + w).wait)
        several(t, held[pl.ds((t - 1) * slots, slots)])
        return carry

    lax.fori_loop(1, (live + width - 1) // width, later, 0)


def prefill_kernel(planes, tile, prefix_held, *rest):
    sources = rest[:planes]
    q, new_kv, out, keys, values, bias = rest[planes:]
    blk = sources[0].shape[2]
    prefix = planes * PLANE * PCAP * blk
    token_count = new_kv.shape[0]
    scale = LANES ** (-0.5) * LOG2E
    device = lax.axis_index("pool")

    @pl.when(pl.program_id(0) == 0)
    def _():
        lane_block = lax.broadcasted_iota(jnp.int32, (8, prefix), 1) // blk
        hide = jnp.zeros((8, prefix), jnp.float32)
        for step in range(planes):
            sender = device // PLANE
            sender = sender ^ step if planes & (planes - 1) == 0 else (sender + planes - step) % planes
            for t in range(PLANE):
                owner = sender * PLANE + ((device % PLANE) ^ t)
                for k in range(PCAP):
                    ordinal = (step * PLANE + t) * PCAP + k
                    block = sources[step][t, k]
                    keys[ordinal * blk : (ordinal + 1) * blk, :] = block[:, :LANES]
                    values[ordinal * blk : (ordinal + 1) * blk, :] = block[:, LANES:]
                    gone = jnp.where(prefix_held[owner] > k, 0.0, MASKED)
                    hide = jnp.where(lane_block == ordinal, gone, hide)
        bias[...] = hide
        keys[prefix:, :] = new_kv[:, :LANES]
        values[prefix:, :] = new_kv[:, LANES:]

    for t in range(token_count // tile):
        width = prefix + (t + 1) * tile
        block = q[t * tile : (t + 1) * tile, :]
        scores = lax.dot_general(
            block, keys[:width, :], (((1,), (1,)), ((), ())), preferred_element_type=jnp.float32
        )
        causal = lax.broadcasted_iota(jnp.int32, (tile, tile), 0) >= lax.broadcasted_iota(
            jnp.int32, (tile, tile), 1
        )
        pieces = [scores[:, :prefix] + bias[0:1, :]]
        if t:
            pieces.append(scores[:, prefix : width - tile])
        pieces.append(jnp.where(causal, scores[:, width - tile :], MASKED))
        scores = jnp.concatenate(pieces, axis=1)
        top = jnp.max(scores, axis=1, keepdims=True)
        weights = jnp.exp2((scores - top) * scale)
        total = jnp.sum(weights, axis=1, keepdims=True)
        mixed = jnp.dot(
            weights.astype(jnp.bfloat16), values[:width, :], preferred_element_type=jnp.float32
        )
        out[t * tile : (t + 1) * tile, :] = (mixed / total).astype(out.dtype)


def own_kernel(q, kv, score, value, key):
    row_count = q.shape[0]
    head_total = q.shape[1] // LANES
    per_pair = head_total // (kv.shape[1] // (2 * LANES))
    for h in range(head_total):
        at = pl.ds(h, row_count, stride=head_total)
        lane = h // per_pair * 2 * LANES
        score[at, :] = q[:, h * LANES : (h + 1) * LANES].astype(jnp.float32)
        key[at, :] = kv[:, lane : lane + LANES].astype(jnp.float32)
        value[at, :] = kv[:, lane + LANES : lane + 2 * LANES].astype(jnp.float32)
    for i in range(row_count):
        at = slice(i * head_total, (i + 1) * head_total)
        product = jnp.sum(score[at, :] * key[at, :], axis=1, keepdims=True)
        score[at, :] = jnp.broadcast_to(product * (LANES ** (-0.5) * LOG2E), (head_total, LANES))


def unpack_kernel(cap, head_rows, places, back, score, value, out, rows_scr):
    row_count = out.shape[0]
    head_total = out.shape[1] // LANES
    lane = lax.broadcasted_iota(jnp.int32, (head_rows // 2, LANES), 1)
    stat_slot = lane % (LANES // 2) // 3
    for i in range(row_count):
        a, c = places[2 * i], places[2 * i + 1]
        for m in range(DGRP):
            at = slice(i * head_total + m * head_rows, i * head_total + (m + 1) * head_rows)
            cached = back[
                a * DGRP + m, pl.ds(pl.multiple_of(c * head_rows, 16), head_rows), :
            ].astype(jnp.float32)
            masses = back[a * DGRP + m, cap * head_rows :, :].astype(jnp.float32)
            masses = jnp.where(stat_slot == c, masses, 0.0)
            mass = jnp.concatenate(
                [
                    jnp.sum(jnp.where(lane < LANES // 2, masses, 0.0), axis=1, keepdims=True),
                    jnp.sum(jnp.where(lane < LANES // 2, 0.0, masses), axis=1, keepdims=True),
                ],
                axis=0,
            )
            share = 1.0 / (1.0 + jnp.exp2(mass - score[at, :]))
            rows_scr[at, :] = cached + share * (value[at, :] - cached)
    for h in range(head_total):
        out[:, h * LANES : (h + 1) * LANES] = rows_scr[
            pl.ds(h, row_count, stride=head_total), :
        ].astype(out.dtype)


def shards(
    pool_kv,
    prefix_table,
    prefix_count,
    prefill_q,
    prefill_new_kv,
    decode_q,
    decode_new,
    decode_cache,
    decode_group,
    cached_len,
):
    devices = lax.axis_size("pool")
    blk = pool_kv.shape[2]
    row_count, q_width = decode_q.shape
    cap = decode_cache.shape[1] // devices
    decode_groups = devices // DGRP
    pair_count = decode_cache.shape[2]
    head_rows = q_width // LANES // DGRP
    message_rows = cap * head_rows
    groups = decode_group.reshape(-1)
    prefill_groups = prefix_table.shape[0]
    big = pltpu.CompilerParams(vmem_limit_bytes=60 * 2**20)
    small = pltpu.CompilerParams(vmem_limit_bytes=8 * 2**20)

    sending = pl.pallas_call(
        functools.partial(pack_kernel, head_rows),
        out_shape=jax.ShapeDtypeStruct((decode_groups, DGRP, message_rows, LANES), jnp.bfloat16),
        in_specs=[smem_spec(), vmem_spec()],
        out_specs=any_spec(),
        scratch_shapes=[
            pltpu.VMEM((row_count * q_width // LANES, LANES), jnp.float32),
            pltpu.VMEM((DGRP, decode_groups, message_rows, LANES), jnp.bfloat16),
            pltpu.SMEM((decode_groups,), jnp.int32),
            pltpu.SemaphoreType.DMA((DGRP,)),
        ],
        compiler_params=big,
        name="pack",
    )(in_hbm(groups), in_hbm(decode_q))
    sending = sending.reshape(devices, message_rows, LANES)

    received = lax.all_to_all(sending, "pool", split_axis=0, concat_axis=0, tiled=True)

    share = jax.ShapeDtypeStruct(
        (PGRP // PLANE, prefill_groups, PCAP, blk, 2 * LANES), jnp.bfloat16
    )
    shares = pl.pallas_call(
        blocks_kernel,
        out_shape=(share,) * PLANE,
        in_specs=[smem_spec(), smem_spec(), any_spec()],
        out_specs=(any_spec(),) * PLANE,
        scratch_shapes=[pltpu.SemaphoreType.DMA((2 * PLANE * PCAP,))],
        compiler_params=small,
        cost_estimate=pl.CostEstimate(flops=100000, bytes_accessed=1000000, transcendentals=0),
        name="blocks",
    )(
        in_hbm(prefix_table),
        in_hbm(prefix_count),
        in_hbm(pool_kv.reshape((-1, PGRP // PLANE, PLANE) + pool_kv.shape[2:])),
    )
    shares = [shares[0]] + [
        lax.ppermute(shares[t], "pool", [(i, i ^ t) for i in range(devices)])
        for t in range(1, PLANE)
    ]
    chunk = min(cap, 4)
    width = 8
    block_count = devices * cap // chunk
    slot_len, listed, prefix_held, places, ahead = pl.pallas_call(
        functools.partial(plan_kernel, cap, chunk, devices),
        out_shape=(
            jax.ShapeDtypeStruct((devices * cap,), jnp.int32),
            jax.ShapeDtypeStruct((block_count + 2,), jnp.int32),
            jax.ShapeDtypeStruct((devices * pool_kv.shape[0],), jnp.int32),
            jax.ShapeDtypeStruct((2 * row_count,), jnp.int32),
            jax.ShapeDtypeStruct((width * chunk,) + decode_cache.shape[2:], jnp.bfloat16),
        ),
        in_specs=[smem_spec()] * 4 + [any_spec()],
        out_specs=(smem_spec(),) * 4 + (vmem_spec(),),
        scratch_shapes=[
            pltpu.SMEM((decode_groups,), jnp.int32),
            pltpu.SMEM((cap + 1,), jnp.int32),
            pltpu.SemaphoreType.DMA((width,)),
        ],
        compiler_params=small,
        cost_estimate=pl.CostEstimate(flops=1000000, bytes_accessed=4000000, transcendentals=0),
        name="plan",
    )(in_hbm(prefix_table), in_hbm(prefix_count), in_hbm(groups), in_hbm(cached_len), in_hbm(decode_cache[0]))

    *shares, slot_len, listed = lax.optimization_barrier((*shares, slot_len, listed))
    planes = devices // PLANE
    bundle = jax.ShapeDtypeStruct((PLANE, PCAP, blk, 2 * LANES), jnp.bfloat16)
    bundles = pl.pallas_call(
        functools.partial(regroup_kernel, planes),
        out_shape=(bundle,) * planes,
        in_specs=[any_spec()] * PLANE,
        out_specs=(any_spec(),) * planes,
        scratch_shapes=[pltpu.SemaphoreType.DMA((planes * PLANE,))],
        compiler_params=small,
        cost_estimate=pl.CostEstimate(flops=100000, bytes_accessed=1000000, transcendentals=0),
        name="regroup",
    )(*shares)

    def along_line(step):
        pairs = [
            (i, partner(i // PLANE, step, planes) * PLANE + i % PLANE) for i in range(devices)
        ]
        return lax.ppermute(bundles[step], "pool", pairs)


    far_first = {step: along_line(step) for step in reversed(range(1, planes))}
    lines = [bundles[0]] + [far_first[step] for step in range(1, planes)]

    answers = pl.pallas_call(
        functools.partial(decode_kernel, cap, head_rows, chunk, width),
        out_shape=jax.ShapeDtypeStruct(
            (devices, cap * head_rows + head_rows // 2, LANES), jnp.bfloat16
        ),
        in_specs=[smem_spec(), smem_spec(), vmem_spec(), vmem_spec(), any_spec()],
        out_specs=vmem_spec(),
        scratch_shapes=[
            pltpu.VMEM(((block_count - width) * chunk,) + decode_cache.shape[2:], jnp.bfloat16),
            pltpu.SemaphoreType.DMA((block_count - width,)),
        ],
        compiler_params=pltpu.CompilerParams(vmem_limit_bytes=20 * 2**20),
        cost_estimate=pl.CostEstimate(
            flops=500000000, bytes_accessed=8000000, transcendentals=1000000
        ),
        name="decode",
    )(listed, slot_len, received, ahead, in_hbm(decode_cache[0]))

    answers, *lines = lax.optimization_barrier((answers, *lines))
    back = lax.all_to_all(answers, "pool", split_axis=0, concat_axis=0, tiled=True)

    token_count, fill_width = prefill_q.shape[1:]
    prefix = devices * PCAP * blk
    head_count = fill_width // LANES
    prefix_held, decode_q, decode_new, _ = lax.optimization_barrier(
        (prefix_held, decode_q, decode_new, answers)
    )
    expanded = jax.ShapeDtypeStruct((row_count * q_width // LANES, LANES), jnp.float32)
    own_score, own_value = pl.pallas_call(
        own_kernel,
        out_shape=(expanded, expanded),
        in_specs=[vmem_spec(), vmem_spec()],
        out_specs=(vmem_spec(), vmem_spec()),
        scratch_shapes=[pltpu.VMEM(expanded.shape, jnp.float32)],
        compiler_params=small,
        cost_estimate=pl.CostEstimate(flops=1000000, bytes_accessed=2000000, transcendentals=0),
        name="own",
    )(in_hbm(decode_q), in_hbm(decode_new))
    prefill_out = pl.pallas_call(
        functools.partial(prefill_kernel, planes, min(256, token_count)),
        grid=(head_count,),
        out_shape=jax.ShapeDtypeStruct((token_count, fill_width), jnp.bfloat16),
        in_specs=[smem_spec()]
        + [pl.BlockSpec(bundle.shape, lambda u: (0, 0, 0, 0))] * planes
        + [
            pl.BlockSpec((token_count, LANES), lambda u: (0, u)),
            pl.BlockSpec(prefill_new_kv.shape[1:], lambda u: (0, 0)),
        ],
        out_specs=pl.BlockSpec((token_count, LANES), lambda u: (0, u)),
        scratch_shapes=[
            pltpu.VMEM((prefix + token_count, LANES), jnp.bfloat16),
            pltpu.VMEM((prefix + token_count, LANES), jnp.bfloat16),
            pltpu.VMEM((8, prefix), jnp.float32),
        ],
        compiler_params=pltpu.CompilerParams(vmem_limit_bytes=16 * 2**20),
        cost_estimate=pl.CostEstimate(
            flops=2 * 2 * token_count * fill_width * (prefix + token_count // 2),
            bytes_accessed=3000000,
            transcendentals=token_count * head_count * (prefix + token_count // 2),
        ),
        name="prefill",
    )(prefix_held, *lines, in_hbm(prefill_q[0]), in_hbm(prefill_new_kv[0]))

    decode_out = pl.pallas_call(
        functools.partial(unpack_kernel, cap, head_rows),
        out_shape=jax.ShapeDtypeStruct((row_count, q_width), jnp.bfloat16),
        in_specs=[smem_spec()] + [vmem_spec()] * 3,
        out_specs=vmem_spec(),
        scratch_shapes=[pltpu.VMEM(expanded.shape, jnp.float32)],
        compiler_params=small,
        name="unpack",
    )(places, back, own_score, own_value)
    return (prefill_out[None], decode_out)


def solution(mesh):
    in_specs = (
        P(("rep", "pool"), None, None, None),
        P("rep", None),
        P("rep"),
        P(("rep", "pool"), None, None),
        P(("rep", "pool"), None, None),
        P(("rep", "pool"), None),
        P(("rep", "pool"), None),
        P(("rep", "pool"), None, None, None, None),
        P("rep", None),
        P("rep"),
    )
    out_specs = (P(("rep", "pool"), None, None), P(("rep", "pool"), None))
    return jax.shard_map(shards, mesh=mesh, in_specs=in_specs, out_specs=out_specs, check_vma=False)
```

```python
import functools

import jax
import jax.numpy as jnp
from jax import lax
from jax.experimental import pallas as pl
from jax.experimental.pallas import tpu as pltpu
from jax.sharding import PartitionSpec as P

PGRP = 8
DGRP = 4
PCAP = 2
PLANE = 4
LANES = 128
MASKED = -1e30
LOG2E = 1.4426950408889634


def any_spec():
    return pl.BlockSpec(memory_space=pl.ANY)


def smem_spec():
    return pl.BlockSpec(memory_space=pltpu.SMEM)


def in_hbm(x):
    return pltpu.with_memory_space_constraint(x, pltpu.HBM)


def vmem_spec():
    return pl.BlockSpec(memory_space=pltpu.VMEM)


def pack_kernel(head_rows, groups, q, out, rows_scr, stage, group_fill, sems):
    decode_groups = out.shape[0]
    row_count = q.shape[0]
    head_total = q.shape[1] // LANES
    device = lax.axis_index("pool")
    for a in range(decode_groups):
        group_fill[a] = 0
    for h in range(head_total):
        rows_scr[pl.ds(h, row_count, stride=head_total), :] = q[
            :, h * LANES : (h + 1) * LANES
        ].astype(jnp.float32)
    homes = []
    for i in range(row_count):
        a = groups[device * row_count + i]
        c = group_fill[a]
        group_fill[a] = c + 1
        homes.append((a, c))
    copies = []
    for m in range(DGRP):
        for i, (a, c) in enumerate(homes):
            first = i * head_total + m * head_rows
            stage[m, a, pl.ds(pl.multiple_of(c * head_rows, 16), head_rows), :] = rows_scr[
                first : first + head_rows, :
            ].astype(out.dtype)
        copy = pltpu.make_async_copy(stage.at[m], out.at[:, m], sems.at[m])
        copy.start()
        copies.append(copy)
    for copy in copies:
        copy.wait()


def blocks_kernel(table, count, pool, *rest):
    outs, sems = rest[:PLANE], rest[PLANE]
    blocks_here = pool.shape[0]
    group_count, most_blocks = table.shape
    device = lax.axis_index("pool")
    first_block = device * blocks_here
    flying = []
    for g in range(group_count):

        def scan_table(j, carry):
            seen, chosen = carry
            entry = table[g, j]
            mine = (entry >= first_block) & (entry < first_block + blocks_here) & (j < count[g])
            chosen = tuple(
                jnp.where(mine & (seen == k), entry - first_block, chosen[k]) for k in range(PCAP)
            )
            return seen + mine.astype(jnp.int32), chosen

        start = (jnp.int32(0), tuple(jnp.int32(0) for _ in range(PCAP)))
        _, chosen = lax.fori_loop(0, most_blocks, scan_table, start, unroll=8)
        if g >= 2:
            for copy in flying.pop(0):
                copy.wait()
        copies = []
        for t in range(PLANE):
            for k in range(PCAP):
                copy = pltpu.make_async_copy(
                    pool.at[chosen[k], :, (device % PLANE) ^ t],
                    outs[t].at[:, g, k],
                    sems.at[((g % 2) * PLANE + t) * PCAP + k],
                )
                copy.start()
                copies.append(copy)
        flying.append(copies)
    for copies in flying:
        for copy in copies:
            copy.wait()


def partner(plane, step, planes):
    return plane ^ step if planes & (planes - 1) == 0 else (plane + step) % planes


def regroup_kernel(planes, *rest):
    held, outs, sems = rest[:PLANE], rest[PLANE:-1], rest[-1]
    mine = lax.axis_index("pool") // PLANE
    per_group = PGRP // PLANE
    copies = []
    for step in range(planes):
        there = partner(mine, step, planes)
        for t in range(PLANE):
            copy = pltpu.make_async_copy(
                held[t].at[there % per_group, there // per_group],
                outs[step].at[t],
                sems.at[step * PLANE + t],
            )
            copy.start()
            copies.append(copy)
    for copy in copies:
        copy.wait()


def fetch_block(cache, listed, i, chunk, held, place, sem):
    return pltpu.make_async_copy(
        cache.at[pl.ds(listed[1 + i] * chunk, chunk)], held.at[pl.ds(place * chunk, chunk)], sem
    )


def plan_kernel(
    cap,
    step,
    owners,
    table,
    count,
    groups,
    lengths,
    cache,
    slot_len,
    listed,
    prefix_held,
    places,
    ahead,
    group_fill,
    found,
    sems,
):
    device = lax.axis_index("pool")
    home_count = owners
    row_count = groups.shape[0] // home_count
    group_id = device // DGRP
    prefill_id = device // PGRP
    blocks_here = listed.shape[0]
    most_blocks = table.shape[1]
    chunk = min(cap, step)

    def one_home(s, filled):
        here = jnp.int32(0)
        for i in range(row_count):
            row = s * row_count + i
            found[here] = lengths[row]
            here = here + (groups[row] == group_id).astype(jnp.int32)
        for c in range(cap):
            slot_len[s * cap + c] = jnp.where(c < here, found[c], 0)
        for b in range(cap // chunk):
            listed[1 + jnp.minimum(filled, blocks_here - 2)] = s * (cap // chunk) + b
            filled = filled + (here > b * chunk).astype(jnp.int32)
        return filled

    live = lax.fori_loop(0, home_count, one_home, jnp.int32(0))
    listed[0] = live
    for i in range(ahead.shape[0] // chunk):
        pl.when(i < live)(fetch_block(cache, listed, i, chunk, ahead, i, sems.at[i]).start)

    for a in range(owners // DGRP):
        group_fill[a] = 0
    for i in range(row_count):
        a = groups[device * row_count + i]
        c = group_fill[a]
        places[2 * i] = a
        places[2 * i + 1] = c
        group_fill[a] = c + 1

    def one_owner(o, carry):
        prefix_held[o] = 0
        return carry

    lax.fori_loop(0, owners, one_owner, 0, unroll=8)
    pool_blocks = prefix_held.shape[0] // owners

    def one_entry(j, carry):
        o = lax.div(table[prefill_id, j], pool_blocks)
        prefix_held[o] = prefix_held[o] + 1
        return carry

    lax.fori_loop(0, jnp.minimum(count[prefill_id], most_blocks), one_entry, 0)
    for i in range(ahead.shape[0] // chunk):
        pl.when(i < live)(fetch_block(cache, listed, i, chunk, ahead, i, sems.at[i]).wait)


def decode_kernel(
    cap, head_rows, chunk, width, listed, slot_len, recv, ahead, cache, out, held, sems
):
    pair_count, positions = cache.shape[1], cache.shape[2]
    per_home = cap // chunk
    key_count = pair_count * positions
    query_heads = head_rows // pair_count
    live = listed[0]
    scale = LANES ** (-0.5) * LOG2E
    rows = chunk * head_rows
    slots = width * chunk
    pair = 2 if chunk % 2 == 0 else 1

    def fetch(i):
        return fetch_block(cache, listed, i, chunk, held, i - width, sems.at[i - width])

    def begin(i, carry):
        fetch(i).start()
        return carry

    lax.fori_loop(width, live, begin, 0)
    row_pair = lax.broadcasted_iota(jnp.int32, (head_rows, key_count), 0) // query_heads
    key_axis = lax.broadcasted_iota(jnp.int32, (head_rows, key_count), 1)
    pos = jnp.where(key_axis // positions == row_pair, key_axis % positions, positions)
    half = head_rows // 2
    lane = lax.broadcasted_iota(jnp.int32, (half, LANES), 1)
    part, stat_slot = lane % (LANES // 2) % 3, lane % (LANES // 2) // 3

    def several(t, kv):
        ids = [jnp.minimum(t * width + w, live - 1) for w in range(width)]
        blocks = [listed[1 + i] for i in ids]
        homes = [b // per_home for b in blocks]
        firsts = [(b % per_home) * chunk for b in blocks]
        places = [pl.multiple_of(f * head_rows, 16) for f in firsts]
        q = jnp.concatenate(
            [recv[h, pl.ds(p, rows), :] for h, p in zip(homes, places)], axis=0
        )
        keys = kv[..., :LANES].reshape(slots, key_count, LANES)
        values = kv[..., LANES:].reshape(slots, key_count, LANES)
        scores = jnp.einsum(
            "jqd,jkd->jqk",
            q.reshape(slots // pair, pair * head_rows, LANES),
            keys.reshape(slots // pair, pair * key_count, LANES),
            preferred_element_type=jnp.float32,
        )
        if pair == 2:
            scores = jnp.stack(
                [scores[:, :head_rows, :key_count], scores[:, head_rows:, key_count:]], axis=1
            ).reshape(slots, head_rows, key_count)
        kept = jnp.stack(
            [pos < slot_len[blocks[w] * chunk + j] for w in range(width) for j in range(chunk)]
        )
        scores = jnp.where(kept, scores, MASKED)
        top = jnp.max(scores, axis=2, keepdims=True)
        weights = jnp.exp2((scores - top) * scale)
        total = jnp.sum(weights, axis=2, keepdims=True)
        weights = weights.astype(jnp.bfloat16)
        if pair == 2:
            weights = weights.reshape(slots // 2, 2, head_rows, key_count)
            nothing = jnp.zeros((slots // 2, head_rows, key_count), jnp.bfloat16)
            upper = jnp.concatenate([weights[:, 0], nothing], axis=2)
            lower = jnp.concatenate([nothing, weights[:, 1]], axis=2)
            weights = jnp.concatenate([upper, lower], axis=1)
        mixed = jnp.einsum(
            "jqk,jkd->jqd",
            weights,
            values.reshape(slots // pair, pair * key_count, LANES),
            preferred_element_type=jnp.float32,
        )
        mixed = mixed.reshape(slots, head_rows, LANES) / total
        mass = top * scale + jnp.log(total) * LOG2E
        high = mass.astype(jnp.bfloat16).astype(jnp.float32)
        middle = (mass - high).astype(jnp.bfloat16).astype(jnp.float32)
        low = mass - high - middle
        mixed = mixed.reshape(width, rows, LANES)
        for w in reversed(range(width)):
            out[homes[w], pl.ds(places[w], rows), :] = mixed[w].astype(out.dtype)
            masses = out[homes[w], cap * head_rows :, :].astype(jnp.float32)
            for j in range(chunk):
                at = w * chunk + j
                split = [
                    jnp.where(lane < LANES // 2, piece[at, :half], piece[at, half:])
                    for piece in (high, middle, low)
                ]
                split = jnp.where(part == 0, split[0], jnp.where(part == 1, split[1], split[2]))
                masses = jnp.where(stat_slot == firsts[w] + j, split, masses)
            out[homes[w], cap * head_rows :, :] = masses.astype(out.dtype)

    several(0, ahead[...])

    def later(t, carry):
        for w in range(width):
            pl.when(t * width + w < live)(fetch(t * width + w).wait)
        several(t, held[pl.ds((t - 1) * slots, slots)])
        return carry

    lax.fori_loop(1, (live + width - 1) // width, later, 0)


def prefill_kernel(planes, tile, prefix_held, *rest):
    sources = rest[:planes]
    q, new_kv, out, keys, values, bias = rest[planes:]
    blk = sources[0].shape[2]
    prefix = planes * PLANE * PCAP * blk
    token_count = new_kv.shape[0]
    scale = LANES ** (-0.5) * LOG2E
    device = lax.axis_index("pool")

    @pl.when(pl.program_id(0) == 0)
    def _():
        lane_block = lax.broadcasted_iota(jnp.int32, (8, prefix), 1) // blk
        hide = jnp.zeros((8, prefix), jnp.float32)
        for step in range(planes):
            sender = device // PLANE
            sender = sender ^ step if planes & (planes - 1) == 0 else (sender + planes - step) % planes
            for t in range(PLANE):
                owner = sender * PLANE + ((device % PLANE) ^ t)
                for k in range(PCAP):
                    ordinal = (step * PLANE + t) * PCAP + k
                    block = sources[step][t, k]
                    keys[ordinal * blk : (ordinal + 1) * blk, :] = block[:, :LANES]
                    values[ordinal * blk : (ordinal + 1) * blk, :] = block[:, LANES:]
                    gone = jnp.where(prefix_held[owner] > k, 0.0, MASKED)
                    hide = jnp.where(lane_block == ordinal, gone, hide)
        bias[...] = hide
        keys[prefix:, :] = new_kv[:, :LANES]
        values[prefix:, :] = new_kv[:, LANES:]

    for t in range(token_count // tile):
        width = prefix + (t + 1) * tile
        block = q[t * tile : (t + 1) * tile, :]
        scores = lax.dot_general(
            block, keys[:width, :], (((1,), (1,)), ((), ())), preferred_element_type=jnp.float32
        )
        causal = lax.broadcasted_iota(jnp.int32, (tile, tile), 0) >= lax.broadcasted_iota(
            jnp.int32, (tile, tile), 1
        )
        pieces = [scores[:, :prefix] + bias[0:1, :]]
        if t:
            pieces.append(scores[:, prefix : width - tile])
        pieces.append(jnp.where(causal, scores[:, width - tile :], MASKED))
        scores = jnp.concatenate(pieces, axis=1)
        top = jnp.max(scores, axis=1, keepdims=True)
        weights = jnp.exp2((scores - top) * scale)
        total = jnp.sum(weights, axis=1, keepdims=True)
        mixed = jnp.dot(
            weights.astype(jnp.bfloat16), values[:width, :], preferred_element_type=jnp.float32
        )
        out[t * tile : (t + 1) * tile, :] = (mixed / total).astype(out.dtype)


def own_kernel(q, kv, score, value, key):
    row_count = q.shape[0]
    head_total = q.shape[1] // LANES
    per_pair = head_total // (kv.shape[1] // (2 * LANES))
    for h in range(head_total):
        at = pl.ds(h, row_count, stride=head_total)
        lane = h // per_pair * 2 * LANES
        score[at, :] = q[:, h * LANES : (h + 1) * LANES].astype(jnp.float32)
        key[at, :] = kv[:, lane : lane + LANES].astype(jnp.float32)
        value[at, :] = kv[:, lane + LANES : lane + 2 * LANES].astype(jnp.float32)
    for i in range(row_count):
        at = slice(i * head_total, (i + 1) * head_total)
        product = jnp.sum(score[at, :] * key[at, :], axis=1, keepdims=True)
        score[at, :] = jnp.broadcast_to(product * (LANES ** (-0.5) * LOG2E), (head_total, LANES))


def unpack_kernel(cap, head_rows, places, back, score, value, out, rows_scr):
    row_count = out.shape[0]
    head_total = out.shape[1] // LANES
    lane = lax.broadcasted_iota(jnp.int32, (head_rows // 2, LANES), 1)
    stat_slot = lane % (LANES // 2) // 3
    for i in range(row_count):
        a, c = places[2 * i], places[2 * i + 1]
        for m in range(DGRP):
            at = slice(i * head_total + m * head_rows, i * head_total + (m + 1) * head_rows)
            cached = back[
                a * DGRP + m, pl.ds(pl.multiple_of(c * head_rows, 16), head_rows), :
            ].astype(jnp.float32)
            masses = back[a * DGRP + m, cap * head_rows :, :].astype(jnp.float32)
            masses = jnp.where(stat_slot == c, masses, 0.0)
            mass = jnp.concatenate(
                [
                    jnp.sum(jnp.where(lane < LANES // 2, masses, 0.0), axis=1, keepdims=True),
                    jnp.sum(jnp.where(lane < LANES // 2, 0.0, masses), axis=1, keepdims=True),
                ],
                axis=0,
            )
            share = 1.0 / (1.0 + jnp.exp2(mass - score[at, :]))
            rows_scr[at, :] = cached + share * (value[at, :] - cached)
    for h in range(head_total):
        out[:, h * LANES : (h + 1) * LANES] = rows_scr[
            pl.ds(h, row_count, stride=head_total), :
        ].astype(out.dtype)


def shards(
    pool_kv,
    prefix_table,
    prefix_count,
    prefill_q,
    prefill_new_kv,
    decode_q,
    decode_new,
    decode_cache,
    decode_group,
    cached_len,
):
    devices = lax.axis_size("pool")
    blk = pool_kv.shape[2]
    row_count, q_width = decode_q.shape
    cap = decode_cache.shape[1] // devices
    decode_groups = devices // DGRP
    pair_count = decode_cache.shape[2]
    head_rows = q_width // LANES // DGRP
    message_rows = cap * head_rows
    groups = decode_group.reshape(-1)
    prefill_groups = prefix_table.shape[0]
    big = pltpu.CompilerParams(vmem_limit_bytes=60 * 2**20)
    small = pltpu.CompilerParams(vmem_limit_bytes=8 * 2**20)

    sending = pl.pallas_call(
        functools.partial(pack_kernel, head_rows),
        out_shape=jax.ShapeDtypeStruct((decode_groups, DGRP, message_rows, LANES), jnp.bfloat16),
        in_specs=[smem_spec(), vmem_spec()],
        out_specs=any_spec(),
        scratch_shapes=[
            pltpu.VMEM((row_count * q_width // LANES, LANES), jnp.float32),
            pltpu.VMEM((DGRP, decode_groups, message_rows, LANES), jnp.bfloat16),
            pltpu.SMEM((decode_groups,), jnp.int32),
            pltpu.SemaphoreType.DMA((DGRP,)),
        ],
        compiler_params=big,
        name="pack",
    )(in_hbm(groups), in_hbm(decode_q))
    sending = sending.reshape(devices, message_rows, LANES)

    received = lax.all_to_all(sending, "pool", split_axis=0, concat_axis=0, tiled=True)

    share = jax.ShapeDtypeStruct(
        (PGRP // PLANE, prefill_groups, PCAP, blk, 2 * LANES), jnp.bfloat16
    )
    shares = pl.pallas_call(
        blocks_kernel,
        out_shape=(share,) * PLANE,
        in_specs=[smem_spec(), smem_spec(), any_spec()],
        out_specs=(any_spec(),) * PLANE,
        scratch_shapes=[pltpu.SemaphoreType.DMA((2 * PLANE * PCAP,))],
        compiler_params=small,
        cost_estimate=pl.CostEstimate(flops=100000, bytes_accessed=1000000, transcendentals=0),
        name="blocks",
    )(
        in_hbm(prefix_table),
        in_hbm(prefix_count),
        in_hbm(pool_kv.reshape((-1, PGRP // PLANE, PLANE) + pool_kv.shape[2:])),
    )
    shares = [shares[0]] + [
        lax.ppermute(shares[t], "pool", [(i, i ^ t) for i in range(devices)])
        for t in range(1, PLANE)
    ]
    chunk = min(cap, 4)
    width = 8
    block_count = devices * cap // chunk
    slot_len, listed, prefix_held, places, ahead = pl.pallas_call(
        functools.partial(plan_kernel, cap, chunk, devices),
        out_shape=(
            jax.ShapeDtypeStruct((devices * cap,), jnp.int32),
            jax.ShapeDtypeStruct((block_count + 2,), jnp.int32),
            jax.ShapeDtypeStruct((devices * pool_kv.shape[0],), jnp.int32),
            jax.ShapeDtypeStruct((2 * row_count,), jnp.int32),
            jax.ShapeDtypeStruct((width * chunk,) + decode_cache.shape[2:], jnp.bfloat16),
        ),
        in_specs=[smem_spec()] * 4 + [any_spec()],
        out_specs=(smem_spec(),) * 4 + (vmem_spec(),),
        scratch_shapes=[
            pltpu.SMEM((decode_groups,), jnp.int32),
            pltpu.SMEM((cap + 1,), jnp.int32),
            pltpu.SemaphoreType.DMA((width,)),
        ],
        compiler_params=small,
        cost_estimate=pl.CostEstimate(flops=1000000, bytes_accessed=4000000, transcendentals=0),
        name="plan",
    )(in_hbm(prefix_table), in_hbm(prefix_count), in_hbm(groups), in_hbm(cached_len), in_hbm(decode_cache[0]))

    *shares, slot_len, listed = lax.optimization_barrier((*shares, slot_len, listed))
    planes = devices // PLANE
    bundle = jax.ShapeDtypeStruct((PLANE, PCAP, blk, 2 * LANES), jnp.bfloat16)
    bundles = pl.pallas_call(
        functools.partial(regroup_kernel, planes),
        out_shape=(bundle,) * planes,
        in_specs=[any_spec()] * PLANE,
        out_specs=(any_spec(),) * planes,
        scratch_shapes=[pltpu.SemaphoreType.DMA((planes * PLANE,))],
        compiler_params=small,
        cost_estimate=pl.CostEstimate(flops=100000, bytes_accessed=1000000, transcendentals=0),
        name="regroup",
    )(*shares)

    def along_line(step):
        pairs = [
            (i, partner(i // PLANE, step, planes) * PLANE + i % PLANE) for i in range(devices)
        ]
        return lax.ppermute(bundles[step], "pool", pairs)


    far_first = {step: along_line(step) for step in reversed(range(1, planes))}
    lines = [bundles[0]] + [far_first[step] for step in range(1, planes)]

    answers = pl.pallas_call(
        functools.partial(decode_kernel, cap, head_rows, chunk, width),
        out_shape=jax.ShapeDtypeStruct(
            (devices, cap * head_rows + head_rows // 2, LANES), jnp.bfloat16
        ),
        in_specs=[smem_spec(), smem_spec(), vmem_spec(), vmem_spec(), any_spec()],
        out_specs=vmem_spec(),
        scratch_shapes=[
            pltpu.VMEM(((block_count - width) * chunk,) + decode_cache.shape[2:], jnp.bfloat16),
            pltpu.SemaphoreType.DMA((block_count - width,)),
        ],
        compiler_params=pltpu.CompilerParams(vmem_limit_bytes=20 * 2**20),
        cost_estimate=pl.CostEstimate(
            flops=500000000, bytes_accessed=8000000, transcendentals=1000000
        ),
        name="decode",
    )(listed, slot_len, received, ahead, in_hbm(decode_cache[0]))

    back = lax.all_to_all(answers, "pool", split_axis=0, concat_axis=0, tiled=True)

    token_count, fill_width = prefill_q.shape[1:]
    prefix = devices * PCAP * blk
    head_count = fill_width // LANES
    prefix_held, decode_q, decode_new, _ = lax.optimization_barrier(
        (prefix_held, decode_q, decode_new, answers)
    )
    expanded = jax.ShapeDtypeStruct((row_count * q_width // LANES, LANES), jnp.float32)
    own_score, own_value = pl.pallas_call(
        own_kernel,
        out_shape=(expanded, expanded),
        in_specs=[vmem_spec(), vmem_spec()],
        out_specs=(vmem_spec(), vmem_spec()),
        scratch_shapes=[pltpu.VMEM(expanded.shape, jnp.float32)],
        compiler_params=small,
        cost_estimate=pl.CostEstimate(flops=1000000, bytes_accessed=2000000, transcendentals=0),
        name="own",
    )(in_hbm(decode_q), in_hbm(decode_new))
    prefill_out = pl.pallas_call(
        functools.partial(prefill_kernel, planes, min(256, token_count)),
        grid=(head_count,),
        out_shape=jax.ShapeDtypeStruct((token_count, fill_width), jnp.bfloat16),
        in_specs=[smem_spec()]
        + [pl.BlockSpec(bundle.shape, lambda u: (0, 0, 0, 0))] * planes
        + [
            pl.BlockSpec((token_count, LANES), lambda u: (0, u)),
            pl.BlockSpec(prefill_new_kv.shape[1:], lambda u: (0, 0)),
        ],
        out_specs=pl.BlockSpec((token_count, LANES), lambda u: (0, u)),
        scratch_shapes=[
            pltpu.VMEM((prefix + token_count, LANES), jnp.bfloat16),
            pltpu.VMEM((prefix + token_count, LANES), jnp.bfloat16),
            pltpu.VMEM((8, prefix), jnp.float32),
        ],
        compiler_params=pltpu.CompilerParams(vmem_limit_bytes=16 * 2**20),
        cost_estimate=pl.CostEstimate(
            flops=32 * token_count * fill_width * (prefix + token_count),
            bytes_accessed=3000000,
            transcendentals=token_count * head_count * (prefix + token_count // 2),
        ),
        name="prefill",
    )(prefix_held, *lines, in_hbm(prefill_q[0]), in_hbm(prefill_new_kv[0]))

    decode_out = pl.pallas_call(
        functools.partial(unpack_kernel, cap, head_rows),
        out_shape=jax.ShapeDtypeStruct((row_count, q_width), jnp.bfloat16),
        in_specs=[smem_spec()] + [vmem_spec()] * 3,
        out_specs=vmem_spec(),
        scratch_shapes=[pltpu.VMEM(expanded.shape, jnp.float32)],
        compiler_params=small,
        name="unpack",
    )(places, back, own_score, own_value)
    return (prefill_out[None], decode_out)


def solution(mesh):
    in_specs = (
        P(("rep", "pool"), None, None, None),
        P("rep", None),
        P("rep"),
        P(("rep", "pool"), None, None),
        P(("rep", "pool"), None, None),
        P(("rep", "pool"), None),
        P(("rep", "pool"), None),
        P(("rep", "pool"), None, None, None, None),
        P("rep", None),
        P("rep"),
    )
    out_specs = (P(("rep", "pool"), None, None), P(("rep", "pool"), None))
    return jax.shard_map(shards, mesh=mesh, in_specs=in_specs, out_specs=out_specs, check_vma=False)
```

```python
import functools

import jax
import jax.numpy as jnp
from jax import lax
from jax.experimental import pallas as pl
from jax.experimental.pallas import tpu as pltpu
from jax.sharding import PartitionSpec as P

PGRP = 8
DGRP = 4
PCAP = 2
PLANE = 4
LANES = 128
MASKED = -1e30
LOG2E = 1.4426950408889634


def any_spec():
    return pl.BlockSpec(memory_space=pl.ANY)


def smem_spec():
    return pl.BlockSpec(memory_space=pltpu.SMEM)


def in_hbm(x):
    return pltpu.with_memory_space_constraint(x, pltpu.HBM)


def vmem_spec():
    return pl.BlockSpec(memory_space=pltpu.VMEM)


def pack_kernel(head_rows, groups, table, count, q, pool, out, *rest):
    shares = rest[:PLANE]
    rows_scr, stage, group_fill, sems, block_sems = rest[PLANE:]
    flying = send_blocks(table, count, pool, shares, block_sems)
    decode_groups = out.shape[0]
    row_count = q.shape[0]
    head_total = q.shape[1] // LANES
    device = lax.axis_index("pool")
    for a in range(decode_groups):
        group_fill[a] = 0
    for h in range(head_total):
        rows_scr[pl.ds(h, row_count, stride=head_total), :] = q[
            :, h * LANES : (h + 1) * LANES
        ].astype(jnp.float32)
    homes = []
    for i in range(row_count):
        a = groups[device * row_count + i]
        c = group_fill[a]
        group_fill[a] = c + 1
        homes.append((a, c))
    copies = []
    for m in range(DGRP):
        for i, (a, c) in enumerate(homes):
            first = i * head_total + m * head_rows
            stage[m, a, pl.ds(pl.multiple_of(c * head_rows, 16), head_rows), :] = rows_scr[
                first : first + head_rows, :
            ].astype(out.dtype)
        copy = pltpu.make_async_copy(stage.at[m], out.at[:, m], sems.at[m])
        copy.start()
        copies.append(copy)
    for copy in copies + flying:
        copy.wait()


def send_blocks(table, count, pool, outs, sems):
    blocks_here = pool.shape[0]
    group_count, most_blocks = table.shape
    device = lax.axis_index("pool")
    first_block = device * blocks_here
    flying = []
    for g in range(group_count):

        def scan_table(j, carry):
            seen, chosen = carry
            entry = table[g, j]
            mine = (entry >= first_block) & (entry < first_block + blocks_here) & (j < count[g])
            chosen = tuple(
                jnp.where(mine & (seen == k), entry - first_block, chosen[k]) for k in range(PCAP)
            )
            return seen + mine.astype(jnp.int32), chosen

        start = (jnp.int32(0), tuple(jnp.int32(0) for _ in range(PCAP)))
        _, chosen = lax.fori_loop(0, most_blocks, scan_table, start, unroll=8)
        if g >= 2:
            for copy in flying.pop(0):
                copy.wait()
        copies = []
        for t in range(PLANE):
            for k in range(PCAP):
                copy = pltpu.make_async_copy(
                    pool.at[chosen[k], :, (device % PLANE) ^ t],
                    outs[t].at[:, g, k],
                    sems.at[((g % 2) * PLANE + t) * PCAP + k],
                )
                copy.start()
                copies.append(copy)
        flying.append(copies)
    return [copy for copies in flying for copy in copies]


def partner(plane, step, planes):
    return plane ^ step if planes & (planes - 1) == 0 else (plane + step) % planes


def regroup_kernel(planes, *rest):
    held, outs, sems = rest[:PLANE], rest[PLANE:-1], rest[-1]
    mine = lax.axis_index("pool") // PLANE
    per_group = PGRP // PLANE
    copies = []
    for step in range(planes):
        there = partner(mine, step, planes)
        for t in range(PLANE):
            copy = pltpu.make_async_copy(
                held[t].at[there % per_group, there // per_group],
                outs[step].at[t],
                sems.at[step * PLANE + t],
            )
            copy.start()
            copies.append(copy)
    for copy in copies:
        copy.wait()


def fetch_block(cache, listed, i, chunk, held, place, sem):
    return pltpu.make_async_copy(
        cache.at[pl.ds(listed[1 + i] * chunk, chunk)], held.at[pl.ds(place * chunk, chunk)], sem
    )


def plan_kernel(
    cap,
    step,
    owners,
    table,
    count,
    groups,
    lengths,
    cache,
    slot_len,
    listed,
    prefix_held,
    places,
    ahead,
    group_fill,
    found,
    sems,
):
    device = lax.axis_index("pool")
    home_count = owners
    row_count = groups.shape[0] // home_count
    group_id = device // DGRP
    prefill_id = device // PGRP
    blocks_here = listed.shape[0]
    most_blocks = table.shape[1]
    chunk = min(cap, step)

    def one_home(s, filled):
        here = jnp.int32(0)
        for i in range(row_count):
            row = s * row_count + i
            found[here] = lengths[row]
            here = here + (groups[row] == group_id).astype(jnp.int32)
        for c in range(cap):
            slot_len[s * cap + c] = jnp.where(c < here, found[c], 0)
        for b in range(cap // chunk):
            listed[1 + jnp.minimum(filled, blocks_here - 2)] = s * (cap // chunk) + b
            filled = filled + (here > b * chunk).astype(jnp.int32)
        return filled

    live = lax.fori_loop(0, home_count, one_home, jnp.int32(0))
    listed[0] = live
    for i in range(ahead.shape[0] // chunk):
        pl.when(i < live)(fetch_block(cache, listed, i, chunk, ahead, i, sems.at[i]).start)

    for a in range(owners // DGRP):
        group_fill[a] = 0
    for i in range(row_count):
        a = groups[device * row_count + i]
        c = group_fill[a]
        places[2 * i] = a
        places[2 * i + 1] = c
        group_fill[a] = c + 1

    def one_owner(o, carry):
        prefix_held[o] = 0
        return carry

    lax.fori_loop(0, owners, one_owner, 0, unroll=8)
    pool_blocks = prefix_held.shape[0] // owners

    def one_entry(j, carry):
        o = lax.div(table[prefill_id, j], pool_blocks)
        prefix_held[o] = prefix_held[o] + 1
        return carry

    lax.fori_loop(0, jnp.minimum(count[prefill_id], most_blocks), one_entry, 0)
    for i in range(ahead.shape[0] // chunk):
        pl.when(i < live)(fetch_block(cache, listed, i, chunk, ahead, i, sems.at[i]).wait)


def decode_kernel(
    cap, head_rows, chunk, width, listed, slot_len, recv, ahead, cache, out, held, sems
):
    pair_count, positions = cache.shape[1], cache.shape[2]
    per_home = cap // chunk
    key_count = pair_count * positions
    query_heads = head_rows // pair_count
    live = listed[0]
    scale = LANES ** (-0.5) * LOG2E
    rows = chunk * head_rows
    slots = width * chunk
    pair = 2 if chunk % 2 == 0 else 1

    def fetch(i):
        return fetch_block(cache, listed, i, chunk, held, i - width, sems.at[i - width])

    def begin(i, carry):
        fetch(i).start()
        return carry

    lax.fori_loop(width, live, begin, 0)
    row_pair = lax.broadcasted_iota(jnp.int32, (head_rows, key_count), 0) // query_heads
    key_axis = lax.broadcasted_iota(jnp.int32, (head_rows, key_count), 1)
    pos = jnp.where(key_axis // positions == row_pair, key_axis % positions, positions)
    half = head_rows // 2
    lane = lax.broadcasted_iota(jnp.int32, (half, LANES), 1)
    part, stat_slot = lane % (LANES // 2) % 3, lane % (LANES // 2) // 3

    def several(t, kv):
        ids = [jnp.minimum(t * width + w, live - 1) for w in range(width)]
        blocks = [listed[1 + i] for i in ids]
        homes = [b // per_home for b in blocks]
        firsts = [(b % per_home) * chunk for b in blocks]
        places = [pl.multiple_of(f * head_rows, 16) for f in firsts]
        q = jnp.concatenate(
            [recv[h, pl.ds(p, rows), :] for h, p in zip(homes, places)], axis=0
        )
        keys = kv[..., :LANES].reshape(slots, key_count, LANES)
        values = kv[..., LANES:].reshape(slots, key_count, LANES)
        scores = jnp.einsum(
            "jqd,jkd->jqk",
            q.reshape(slots // pair, pair * head_rows, LANES),
            keys.reshape(slots // pair, pair * key_count, LANES),
            preferred_element_type=jnp.float32,
        )
        if pair == 2:
            scores = jnp.stack(
                [scores[:, :head_rows, :key_count], scores[:, head_rows:, key_count:]], axis=1
            ).reshape(slots, head_rows, key_count)
        kept = jnp.stack(
            [pos < slot_len[blocks[w] * chunk + j] for w in range(width) for j in range(chunk)]
        )
        scores = jnp.where(kept, scores, MASKED)
        top = jnp.max(scores, axis=2, keepdims=True)
        weights = jnp.exp2((scores - top) * scale)
        total = jnp.sum(weights, axis=2, keepdims=True)
        weights = weights.astype(jnp.bfloat16)
        if pair == 2:
            weights = weights.reshape(slots // 2, 2, head_rows, key_count)
            nothing = jnp.zeros((slots // 2, head_rows, key_count), jnp.bfloat16)
            upper = jnp.concatenate([weights[:, 0], nothing], axis=2)
            lower = jnp.concatenate([nothing, weights[:, 1]], axis=2)
            weights = jnp.concatenate([upper, lower], axis=1)
        mixed = jnp.einsum(
            "jqk,jkd->jqd",
            weights,
            values.reshape(slots // pair, pair * key_count, LANES),
            preferred_element_type=jnp.float32,
        )
        mixed = mixed.reshape(slots, head_rows, LANES) / total
        mass = top * scale + jnp.log(total) * LOG2E
        high = mass.astype(jnp.bfloat16).astype(jnp.float32)
        middle = (mass - high).astype(jnp.bfloat16).astype(jnp.float32)
        low = mass - high - middle
        mixed = mixed.reshape(width, rows, LANES)
        for w in reversed(range(width)):
            out[homes[w], pl.ds(places[w], rows), :] = mixed[w].astype(out.dtype)
            masses = out[homes[w], cap * head_rows :, :].astype(jnp.float32)
            for j in range(chunk):
                at = w * chunk + j
                split = [
                    jnp.where(lane < LANES // 2, piece[at, :half], piece[at, half:])
                    for piece in (high, middle, low)
                ]
                split = jnp.where(part == 0, split[0], jnp.where(part == 1, split[1], split[2]))
                masses = jnp.where(stat_slot == firsts[w] + j, split, masses)
            out[homes[w], cap * head_rows :, :] = masses.astype(out.dtype)

    several(0, ahead[...])

    def later(t, carry):
        for w in range(width):
            pl.when(t * width + w < live)(fetch(t * width + w).wait)
        several(t, held[pl.ds((t - 1) * slots, slots)])
        return carry

    lax.fori_loop(1, (live + width - 1) // width, later, 0)


def prefill_kernel(planes, tile, prefix_held, *rest):
    sources = rest[:planes]
    q, new_kv, out, keys, values = rest[planes:]
    blk = sources[0].shape[2]
    prefix = planes * PLANE * PCAP * blk
    token_count = new_kv.shape[0]
    scale = LANES ** (-0.5) * LOG2E
    device = lax.axis_index("pool")

    @pl.when(pl.program_id(0) == 0)
    def _():
        first = jnp.broadcast_to(new_kv[0:1, :LANES], (blk, LANES))
        ones = jnp.ones((blk, LANES), values.dtype)
        for step in range(planes):
            sender = device // PLANE
            sender = sender ^ step if planes & (planes - 1) == 0 else (sender + planes - step) % planes
            for t in range(PLANE):
                owner = sender * PLANE + ((device % PLANE) ^ t)
                for k in range(PCAP):
                    ordinal = (step * PLANE + t) * PCAP + k
                    block = sources[step][t, k]
                    at = slice(ordinal * blk, (ordinal + 1) * blk)
                    here = prefix_held[owner] > k
                    keys[at, :] = jnp.where(here, block[:, :LANES], first)
                    values[at, :LANES] = jnp.where(here, block[:, LANES:], jnp.zeros_like(ones))
                    values[at, LANES:] = jnp.where(here, ones, jnp.zeros_like(ones))
        keys[prefix:, :] = new_kv[:, :LANES]
        values[prefix:, :LANES] = new_kv[:, LANES:]
        values[prefix:, LANES:] = jnp.ones((token_count, LANES), values.dtype)

    for t in range(token_count // tile):
        width = prefix + (t + 1) * tile
        block = q[t * tile : (t + 1) * tile, :]
        scores = lax.dot_general(
            block, keys[:width, :], (((1,), (1,)), ((), ())), preferred_element_type=jnp.float32
        )
        causal = lax.broadcasted_iota(jnp.int32, (tile, tile), 0) >= lax.broadcasted_iota(
            jnp.int32, (tile, tile), 1
        )
        scores = jnp.concatenate(
            [scores[:, : width - tile], jnp.where(causal, scores[:, width - tile :], MASKED)], axis=1
        )
        top = jnp.max(scores, axis=1, keepdims=True)
        weights = jnp.exp2((scores - top) * scale)
        mixed = jnp.dot(
            weights.astype(jnp.bfloat16), values[:width, :], preferred_element_type=jnp.float32
        )
        out[t * tile : (t + 1) * tile, :] = (mixed[:, :LANES] / mixed[:, LANES:]).astype(out.dtype)


def own_kernel(q, kv, score, value, key):
    row_count = q.shape[0]
    head_total = q.shape[1] // LANES
    per_pair = head_total // (kv.shape[1] // (2 * LANES))
    for h in range(head_total):
        at = pl.ds(h, row_count, stride=head_total)
        lane = h // per_pair * 2 * LANES
        score[at, :] = q[:, h * LANES : (h + 1) * LANES].astype(jnp.float32)
        key[at, :] = kv[:, lane : lane + LANES].astype(jnp.float32)
        value[at, :] = kv[:, lane + LANES : lane + 2 * LANES].astype(jnp.float32)
    for i in range(row_count):
        at = slice(i * head_total, (i + 1) * head_total)
        product = jnp.sum(score[at, :] * key[at, :], axis=1, keepdims=True)
        score[at, :] = jnp.broadcast_to(product * (LANES ** (-0.5) * LOG2E), (head_total, LANES))


def unpack_kernel(cap, head_rows, places, back, score, value, out, rows_scr):
    row_count = out.shape[0]
    head_total = out.shape[1] // LANES
    lane = lax.broadcasted_iota(jnp.int32, (head_rows // 2, LANES), 1)
    stat_slot = lane % (LANES // 2) // 3
    for i in range(row_count):
        a, c = places[2 * i], places[2 * i + 1]
        for m in range(DGRP):
            at = slice(i * head_total + m * head_rows, i * head_total + (m + 1) * head_rows)
            cached = back[
                a * DGRP + m, pl.ds(pl.multiple_of(c * head_rows, 16), head_rows), :
            ].astype(jnp.float32)
            masses = back[a * DGRP + m, cap * head_rows :, :].astype(jnp.float32)
            masses = jnp.where(stat_slot == c, masses, 0.0)
            mass = jnp.concatenate(
                [
                    jnp.sum(jnp.where(lane < LANES // 2, masses, 0.0), axis=1, keepdims=True),
                    jnp.sum(jnp.where(lane < LANES // 2, 0.0, masses), axis=1, keepdims=True),
                ],
                axis=0,
            )
            share = 1.0 / (1.0 + jnp.exp2(mass - score[at, :]))
            rows_scr[at, :] = cached + share * (value[at, :] - cached)
    for h in range(head_total):
        out[:, h * LANES : (h + 1) * LANES] = rows_scr[
            pl.ds(h, row_count, stride=head_total), :
        ].astype(out.dtype)


def shards(
    pool_kv,
    prefix_table,
    prefix_count,
    prefill_q,
    prefill_new_kv,
    decode_q,
    decode_new,
    decode_cache,
    decode_group,
    cached_len,
):
    devices = lax.axis_size("pool")
    blk = pool_kv.shape[2]
    row_count, q_width = decode_q.shape
    cap = decode_cache.shape[1] // devices
    decode_groups = devices // DGRP
    pair_count = decode_cache.shape[2]
    head_rows = q_width // LANES // DGRP
    message_rows = cap * head_rows
    groups = decode_group.reshape(-1)
    prefill_groups = prefix_table.shape[0]
    small = pltpu.CompilerParams(vmem_limit_bytes=8 * 2**20)

    share = jax.ShapeDtypeStruct(
        (PGRP // PLANE, prefill_groups, PCAP, blk, 2 * LANES), jnp.bfloat16
    )
    sending, *shares = pl.pallas_call(
        functools.partial(pack_kernel, head_rows),
        out_shape=(
            jax.ShapeDtypeStruct((decode_groups, DGRP, message_rows, LANES), jnp.bfloat16),
        )
        + (share,) * PLANE,
        in_specs=[smem_spec()] * 3 + [vmem_spec(), any_spec()],
        out_specs=(any_spec(),) * (1 + PLANE),
        scratch_shapes=[
            pltpu.VMEM((row_count * q_width // LANES, LANES), jnp.float32),
            pltpu.VMEM((DGRP, decode_groups, message_rows, LANES), jnp.bfloat16),
            pltpu.SMEM((decode_groups,), jnp.int32),
            pltpu.SemaphoreType.DMA((DGRP,)),
            pltpu.SemaphoreType.DMA((2 * PLANE * PCAP,)),
        ],
        compiler_params=small,
        name="pack",
    )(
        in_hbm(groups),
        in_hbm(prefix_table),
        in_hbm(prefix_count),
        in_hbm(decode_q),
        in_hbm(pool_kv.reshape((-1, PGRP // PLANE, PLANE) + pool_kv.shape[2:])),
    )
    sending = sending.reshape(devices, message_rows, LANES)

    received = lax.all_to_all(sending, "pool", split_axis=0, concat_axis=0, tiled=True)

    shares = [shares[0]] + [
        lax.ppermute(shares[t], "pool", [(i, i ^ t) for i in range(devices)])
        for t in range(1, PLANE)
    ]
    chunk = min(cap, 4)
    width = 8
    block_count = devices * cap // chunk
    slot_len, listed, prefix_held, places, ahead = pl.pallas_call(
        functools.partial(plan_kernel, cap, chunk, devices),
        out_shape=(
            jax.ShapeDtypeStruct((devices * cap,), jnp.int32),
            jax.ShapeDtypeStruct((block_count + 2,), jnp.int32),
            jax.ShapeDtypeStruct((devices * pool_kv.shape[0],), jnp.int32),
            jax.ShapeDtypeStruct((2 * row_count,), jnp.int32),
            jax.ShapeDtypeStruct((width * chunk,) + decode_cache.shape[2:], jnp.bfloat16),
        ),
        in_specs=[smem_spec()] * 4 + [any_spec()],
        out_specs=(smem_spec(),) * 4 + (vmem_spec(),),
        scratch_shapes=[
            pltpu.SMEM((decode_groups,), jnp.int32),
            pltpu.SMEM((cap + 1,), jnp.int32),
            pltpu.SemaphoreType.DMA((width,)),
        ],
        compiler_params=small,
        cost_estimate=pl.CostEstimate(flops=1000000, bytes_accessed=4000000, transcendentals=0),
        name="plan",
    )(in_hbm(prefix_table), in_hbm(prefix_count), in_hbm(groups), in_hbm(cached_len), in_hbm(decode_cache[0]))

    *shares, slot_len, listed = lax.optimization_barrier((*shares, slot_len, listed))
    planes = devices // PLANE
    bundle = jax.ShapeDtypeStruct((PLANE, PCAP, blk, 2 * LANES), jnp.bfloat16)
    bundles = pl.pallas_call(
        functools.partial(regroup_kernel, planes),
        out_shape=(bundle,) * planes,
        in_specs=[any_spec()] * PLANE,
        out_specs=(any_spec(),) * planes,
        scratch_shapes=[pltpu.SemaphoreType.DMA((planes * PLANE,))],
        compiler_params=small,
        cost_estimate=pl.CostEstimate(flops=100000, bytes_accessed=1000000, transcendentals=0),
        name="regroup",
    )(*shares)

    def along_line(step):
        pairs = [
            (i, partner(i // PLANE, step, planes) * PLANE + i % PLANE) for i in range(devices)
        ]
        return lax.ppermute(bundles[step], "pool", pairs)


    far_first = {step: along_line(step) for step in reversed(range(1, planes))}
    lines = [bundles[0]] + [far_first[step] for step in range(1, planes)]

    answers = pl.pallas_call(
        functools.partial(decode_kernel, cap, head_rows, chunk, width),
        out_shape=jax.ShapeDtypeStruct(
            (devices, cap * head_rows + head_rows // 2, LANES), jnp.bfloat16
        ),
        in_specs=[smem_spec(), smem_spec(), vmem_spec(), vmem_spec(), any_spec()],
        out_specs=vmem_spec(),
        scratch_shapes=[
            pltpu.VMEM(((block_count - width) * chunk,) + decode_cache.shape[2:], jnp.bfloat16),
            pltpu.SemaphoreType.DMA((block_count - width,)),
        ],
        compiler_params=pltpu.CompilerParams(vmem_limit_bytes=20 * 2**20),
        cost_estimate=pl.CostEstimate(
            flops=500000000, bytes_accessed=8000000, transcendentals=1000000
        ),
        name="decode",
    )(listed, slot_len, received, ahead, in_hbm(decode_cache[0]))

    back = lax.all_to_all(answers, "pool", split_axis=0, concat_axis=0, tiled=True)

    token_count, fill_width = prefill_q.shape[1:]
    prefix = devices * PCAP * blk
    head_count = fill_width // LANES
    prefix_held, decode_q, decode_new, _ = lax.optimization_barrier(
        (prefix_held, decode_q, decode_new, answers)
    )
    expanded = jax.ShapeDtypeStruct((row_count * q_width // LANES, LANES), jnp.float32)
    own_score, own_value = pl.pallas_call(
        own_kernel,
        out_shape=(expanded, expanded),
        in_specs=[vmem_spec(), vmem_spec()],
        out_specs=(vmem_spec(), vmem_spec()),
        scratch_shapes=[pltpu.VMEM(expanded.shape, jnp.float32)],
        compiler_params=small,
        cost_estimate=pl.CostEstimate(flops=1000000, bytes_accessed=2000000, transcendentals=0),
        name="own",
    )(in_hbm(decode_q), in_hbm(decode_new))
    prefill_out = pl.pallas_call(
        functools.partial(prefill_kernel, planes, min(256, token_count)),
        grid=(head_count,),
        out_shape=jax.ShapeDtypeStruct((token_count, fill_width), jnp.bfloat16),
        in_specs=[smem_spec()]
        + [pl.BlockSpec(bundle.shape, lambda u: (0, 0, 0, 0))] * planes
        + [
            pl.BlockSpec((token_count, LANES), lambda u: (0, u)),
            pl.BlockSpec(prefill_new_kv.shape[1:], lambda u: (0, 0)),
        ],
        out_specs=pl.BlockSpec((token_count, LANES), lambda u: (0, u)),
        scratch_shapes=[
            pltpu.VMEM((prefix + token_count, LANES), jnp.bfloat16),
            pltpu.VMEM((prefix + token_count, 2 * LANES), jnp.bfloat16),
        ],
        compiler_params=pltpu.CompilerParams(vmem_limit_bytes=16 * 2**20),
        cost_estimate=pl.CostEstimate(
            flops=32 * token_count * fill_width * (prefix + token_count),
            bytes_accessed=3000000,
            transcendentals=token_count * head_count * (prefix + token_count // 2),
        ),
        name="prefill",
    )(prefix_held, *lines, in_hbm(prefill_q[0]), in_hbm(prefill_new_kv[0]))

    decode_out = pl.pallas_call(
        functools.partial(unpack_kernel, cap, head_rows),
        out_shape=jax.ShapeDtypeStruct((row_count, q_width), jnp.bfloat16),
        in_specs=[smem_spec()] + [vmem_spec()] * 3,
        out_specs=vmem_spec(),
        scratch_shapes=[pltpu.VMEM(expanded.shape, jnp.float32)],
        compiler_params=small,
        name="unpack",
    )(places, back, own_score, own_value)
    return (prefill_out[None], decode_out)


def solution(mesh):
    in_specs = (
        P(("rep", "pool"), None, None, None),
        P("rep", None),
        P("rep"),
        P(("rep", "pool"), None, None),
        P(("rep", "pool"), None, None),
        P(("rep", "pool"), None),
        P(("rep", "pool"), None),
        P(("rep", "pool"), None, None, None, None),
        P("rep", None),
        P("rep"),
    )
    out_specs = (P(("rep", "pool"), None, None), P(("rep", "pool"), None))
    return jax.shard_map(shards, mesh=mesh, in_specs=in_specs, out_specs=out_specs, check_vma=False)
```

```python
import functools

import jax
import jax.numpy as jnp
from jax import lax
from jax.experimental import pallas as pl
from jax.experimental.pallas import tpu as pltpu
from jax.sharding import PartitionSpec as P

PGRP = 8
DGRP = 4
PCAP = 2
PLANE = 4
LANES = 128
MASKED = -1e30
LOG2E = 1.4426950408889634


def any_spec():
    return pl.BlockSpec(memory_space=pl.ANY)


def smem_spec():
    return pl.BlockSpec(memory_space=pltpu.SMEM)


def in_hbm(x):
    return pltpu.with_memory_space_constraint(x, pltpu.HBM)


def vmem_spec():
    return pl.BlockSpec(memory_space=pltpu.VMEM)


def pack_kernel(head_rows, groups, table, count, q_far, pool, out, *rest):
    shares = rest[:PLANE]
    q, rows_scr, stage, group_fill, sems, block_sems, q_sem = rest[PLANE:]
    q_copy = pltpu.make_async_copy(q_far, q, q_sem)
    q_copy.start()
    flying = send_blocks(table, count, pool, shares, block_sems)
    decode_groups = out.shape[0]
    row_count = q.shape[0]
    head_total = q.shape[1] // LANES
    device = lax.axis_index("pool")
    for a in range(decode_groups):
        group_fill[a] = 0
    homes = []
    for i in range(row_count):
        a = groups[device * row_count + i]
        c = group_fill[a]
        group_fill[a] = c + 1
        homes.append((a, c))
    q_copy.wait()
    for h in range(head_total):
        rows_scr[pl.ds(h, row_count, stride=head_total), :] = q[
            :, h * LANES : (h + 1) * LANES
        ].astype(jnp.float32)
    copies = []
    for m in range(DGRP):
        for i, (a, c) in enumerate(homes):
            first = i * head_total + m * head_rows
            stage[m, a, pl.ds(pl.multiple_of(c * head_rows, 16), head_rows), :] = rows_scr[
                first : first + head_rows, :
            ].astype(out.dtype)
        copy = pltpu.make_async_copy(stage.at[m], out.at[:, m], sems.at[m])
        copy.start()
        copies.append(copy)
    for copy in copies + flying:
        copy.wait()


def send_blocks(table, count, pool, outs, sems):
    blocks_here = pool.shape[0]
    group_count, most_blocks = table.shape
    device = lax.axis_index("pool")
    first_block = device * blocks_here
    flying = []
    for g in range(group_count):

        def scan_table(j, carry):
            seen, chosen = carry
            entry = table[g, j]
            mine = (entry >= first_block) & (entry < first_block + blocks_here) & (j < count[g])
            chosen = tuple(
                jnp.where(mine & (seen == k), entry - first_block, chosen[k]) for k in range(PCAP)
            )
            return seen + mine.astype(jnp.int32), chosen

        start = (jnp.int32(0), tuple(jnp.int32(0) for _ in range(PCAP)))
        _, chosen = lax.fori_loop(0, most_blocks, scan_table, start, unroll=8)
        if g >= 2:
            for copy in flying.pop(0):
                copy.wait()
        copies = []
        for t in range(PLANE):
            for k in range(PCAP):
                copy = pltpu.make_async_copy(
                    pool.at[chosen[k], :, (device % PLANE) ^ t],
                    outs[t].at[:, g, k],
                    sems.at[((g % 2) * PLANE + t) * PCAP + k],
                )
                copy.start()
                copies.append(copy)
        flying.append(copies)
    return [copy for copies in flying for copy in copies]


def partner(plane, step, planes):
    return plane ^ step if planes & (planes - 1) == 0 else (plane + step) % planes


def regroup_kernel(planes, *rest):
    held, outs, sems = rest[:PLANE], rest[PLANE:-1], rest[-1]
    mine = lax.axis_index("pool") // PLANE
    per_group = PGRP // PLANE
    copies = []
    for step in range(planes):
        there = partner(mine, step, planes)
        for t in range(PLANE):
            copy = pltpu.make_async_copy(
                held[t].at[there % per_group, there // per_group],
                outs[step].at[t],
                sems.at[step * PLANE + t],
            )
            copy.start()
            copies.append(copy)
    for copy in copies:
        copy.wait()


def fetch_block(cache, listed, i, chunk, held, place, sem):
    return pltpu.make_async_copy(
        cache.at[pl.ds(listed[1 + i] * chunk, chunk)], held.at[pl.ds(place * chunk, chunk)], sem
    )


def plan_kernel(
    cap,
    step,
    owners,
    table,
    count,
    groups,
    lengths,
    cache,
    slot_len,
    listed,
    prefix_held,
    places,
    ahead,
    group_fill,
    found,
    sems,
):
    device = lax.axis_index("pool")
    home_count = owners
    row_count = groups.shape[0] // home_count
    group_id = device // DGRP
    prefill_id = device // PGRP
    blocks_here = listed.shape[0]
    most_blocks = table.shape[1]
    chunk = min(cap, step)

    def one_home(s, filled):
        here = jnp.int32(0)
        for i in range(row_count):
            row = s * row_count + i
            found[here] = lengths[row]
            here = here + (groups[row] == group_id).astype(jnp.int32)
        for c in range(cap):
            slot_len[s * cap + c] = jnp.where(c < here, found[c], 0)
        for b in range(cap // chunk):
            listed[1 + jnp.minimum(filled, blocks_here - 2)] = s * (cap // chunk) + b
            filled = filled + (here > b * chunk).astype(jnp.int32)
        return filled

    live = lax.fori_loop(0, home_count, one_home, jnp.int32(0))
    listed[0] = live
    for i in range(ahead.shape[0] // chunk):
        pl.when(i < live)(fetch_block(cache, listed, i, chunk, ahead, i, sems.at[i]).start)

    for a in range(owners // DGRP):
        group_fill[a] = 0
    for i in range(row_count):
        a = groups[device * row_count + i]
        c = group_fill[a]
        places[2 * i] = a
        places[2 * i + 1] = c
        group_fill[a] = c + 1

    def one_owner(o, carry):
        prefix_held[o] = 0
        return carry

    lax.fori_loop(0, owners, one_owner, 0, unroll=8)
    pool_blocks = prefix_held.shape[0] // owners

    def one_entry(j, carry):
        o = lax.div(table[prefill_id, j], pool_blocks)
        prefix_held[o] = prefix_held[o] + 1
        return carry

    lax.fori_loop(0, jnp.minimum(count[prefill_id], most_blocks), one_entry, 0)
    for i in range(ahead.shape[0] // chunk):
        pl.when(i < live)(fetch_block(cache, listed, i, chunk, ahead, i, sems.at[i]).wait)


def decode_kernel(
    cap, head_rows, chunk, width, listed, slot_len, recv, ahead, cache, out, held, sems
):
    pair_count, positions = cache.shape[1], cache.shape[2]
    per_home = cap // chunk
    key_count = pair_count * positions
    query_heads = head_rows // pair_count
    live = listed[0]
    scale = LANES ** (-0.5) * LOG2E
    rows = chunk * head_rows
    slots = width * chunk
    pair = 2 if chunk % 2 == 0 else 1

    def fetch(i):
        return fetch_block(cache, listed, i, chunk, held, i - width, sems.at[i - width])

    def begin(i, carry):
        fetch(i).start()
        return carry

    lax.fori_loop(width, live, begin, 0)
    row_pair = lax.broadcasted_iota(jnp.int32, (head_rows, key_count), 0) // query_heads
    key_axis = lax.broadcasted_iota(jnp.int32, (head_rows, key_count), 1)
    pos = jnp.where(key_axis // positions == row_pair, key_axis % positions, positions)
    half = head_rows // 2
    lane = lax.broadcasted_iota(jnp.int32, (half, LANES), 1)
    part, stat_slot = lane % (LANES // 2) % 3, lane % (LANES // 2) // 3

    def several(t, kv):
        ids = [jnp.minimum(t * width + w, live - 1) for w in range(width)]
        blocks = [listed[1 + i] for i in ids]
        homes = [b // per_home for b in blocks]
        firsts = [(b % per_home) * chunk for b in blocks]
        places = [pl.multiple_of(f * head_rows, 16) for f in firsts]
        q = jnp.concatenate(
            [recv[h, pl.ds(p, rows), :] for h, p in zip(homes, places)], axis=0
        )
        keys = kv[..., :LANES].reshape(slots, key_count, LANES)
        values = kv[..., LANES:].reshape(slots, key_count, LANES)
        scores = jnp.einsum(
            "jqd,jkd->jqk",
            q.reshape(slots // pair, pair * head_rows, LANES),
            keys.reshape(slots // pair, pair * key_count, LANES),
            preferred_element_type=jnp.float32,
        )
        if pair == 2:
            scores = jnp.stack(
                [scores[:, :head_rows, :key_count], scores[:, head_rows:, key_count:]], axis=1
            ).reshape(slots, head_rows, key_count)
        kept = jnp.stack(
            [pos < slot_len[blocks[w] * chunk + j] for w in range(width) for j in range(chunk)]
        )
        scores = jnp.where(kept, scores, MASKED)
        top = jnp.max(scores, axis=2, keepdims=True)
        weights = jnp.exp2((scores - top) * scale)
        total = jnp.sum(weights, axis=2, keepdims=True)
        weights = weights.astype(jnp.bfloat16)
        if pair == 2:
            weights = weights.reshape(slots // 2, 2, head_rows, key_count)
            nothing = jnp.zeros((slots // 2, head_rows, key_count), jnp.bfloat16)
            upper = jnp.concatenate([weights[:, 0], nothing], axis=2)
            lower = jnp.concatenate([nothing, weights[:, 1]], axis=2)
            weights = jnp.concatenate([upper, lower], axis=1)
        mixed = jnp.einsum(
            "jqk,jkd->jqd",
            weights,
            values.reshape(slots // pair, pair * key_count, LANES),
            preferred_element_type=jnp.float32,
        )
        mixed = mixed.reshape(slots, head_rows, LANES) / total
        mass = top * scale + jnp.log(total) * LOG2E
        high = mass.astype(jnp.bfloat16).astype(jnp.float32)
        middle = (mass - high).astype(jnp.bfloat16).astype(jnp.float32)
        low = mass - high - middle
        mixed = mixed.reshape(width, rows, LANES)
        for w in reversed(range(width)):
            out[homes[w], pl.ds(places[w], rows), :] = mixed[w].astype(out.dtype)
            masses = out[homes[w], cap * head_rows :, :].astype(jnp.float32)
            for j in range(chunk):
                at = w * chunk + j
                split = [
                    jnp.where(lane < LANES // 2, piece[at, :half], piece[at, half:])
                    for piece in (high, middle, low)
                ]
                split = jnp.where(part == 0, split[0], jnp.where(part == 1, split[1], split[2]))
                masses = jnp.where(stat_slot == firsts[w] + j, split, masses)
            out[homes[w], cap * head_rows :, :] = masses.astype(out.dtype)

    several(0, ahead[...])

    def later(t, carry):
        for w in range(width):
            pl.when(t * width + w < live)(fetch(t * width + w).wait)
        several(t, held[pl.ds((t - 1) * slots, slots)])
        return carry

    lax.fori_loop(1, (live + width - 1) // width, later, 0)


def prefill_kernel(planes, tile, prefix_held, *rest):
    sources = rest[:planes]
    q, new_kv, out, keys, values, bias = rest[planes:]
    blk = sources[0].shape[2]
    prefix = planes * PLANE * PCAP * blk
    token_count = new_kv.shape[0]
    scale = LANES ** (-0.5) * LOG2E
    device = lax.axis_index("pool")

    @pl.when(pl.program_id(0) == 0)
    def _():
        lane_block = lax.broadcasted_iota(jnp.int32, (8, prefix), 1) // blk
        hide = jnp.zeros((8, prefix), jnp.float32)
        for step in range(planes):
            sender = device // PLANE
            sender = sender ^ step if planes & (planes - 1) == 0 else (sender + planes - step) % planes
            for t in range(PLANE):
                owner = sender * PLANE + ((device % PLANE) ^ t)
                for k in range(PCAP):
                    ordinal = (step * PLANE + t) * PCAP + k
                    block = sources[step][t, k]
                    keys[ordinal * blk : (ordinal + 1) * blk, :] = block[:, :LANES]
                    values[ordinal * blk : (ordinal + 1) * blk, :] = block[:, LANES:]
                    gone = jnp.where(prefix_held[owner] > k, 0.0, MASKED)
                    hide = jnp.where(lane_block == ordinal, gone, hide)
        bias[...] = hide
        keys[prefix:, :] = new_kv[:, :LANES]
        values[prefix:, :] = new_kv[:, LANES:]

    for t in range(token_count // tile):
        width = prefix + (t + 1) * tile
        block = q[t * tile : (t + 1) * tile, :]
        scores = lax.dot_general(
            block, keys[:width, :], (((1,), (1,)), ((), ())), preferred_element_type=jnp.float32
        )
        causal = lax.broadcasted_iota(jnp.int32, (tile, tile), 0) >= lax.broadcasted_iota(
            jnp.int32, (tile, tile), 1
        )
        pieces = [scores[:, :prefix] + bias[0:1, :]]
        if t:
            pieces.append(scores[:, prefix : width - tile])
        pieces.append(jnp.where(causal, scores[:, width - tile :], MASKED))
        scores = jnp.concatenate(pieces, axis=1)
        top = jnp.max(scores, axis=1, keepdims=True)
        weights = jnp.exp2((scores - top) * scale)
        total = jnp.sum(weights, axis=1, keepdims=True)
        mixed = jnp.dot(
            weights.astype(jnp.bfloat16), values[:width, :], preferred_element_type=jnp.float32
        )
        out[t * tile : (t + 1) * tile, :] = (mixed / total).astype(out.dtype)


def own_kernel(q, kv, score, value):
    row_count = q.shape[0]
    head_total = q.shape[1] // LANES
    pair_count = kv.shape[1] // (2 * LANES)
    per_pair = head_total // pair_count
    for k in range(pair_count):
        lane = k * 2 * LANES
        key = kv[:, lane : lane + LANES].astype(jnp.float32) * (LANES ** (-0.5) * LOG2E)
        held = kv[:, lane + LANES : lane + 2 * LANES].astype(jnp.float32)
        for h in range(k * per_pair, (k + 1) * per_pair):
            at = pl.ds(h, row_count, stride=head_total)
            query = q[:, h * LANES : (h + 1) * LANES].astype(jnp.float32)
            product = jnp.sum(query * key, axis=1, keepdims=True)
            score[at, :] = jnp.broadcast_to(product, (row_count, LANES))
            value[at, :] = held


def unpack_kernel(cap, head_rows, places, back, score, value, out, rows_scr):
    row_count = out.shape[0]
    head_total = out.shape[1] // LANES
    lane = lax.broadcasted_iota(jnp.int32, (head_rows // 2, LANES), 1)
    stat_slot = lane % (LANES // 2) // 3
    for i in range(row_count):
        a, c = places[2 * i], places[2 * i + 1]
        for m in range(DGRP):
            at = slice(i * head_total + m * head_rows, i * head_total + (m + 1) * head_rows)
            cached = back[
                a * DGRP + m, pl.ds(pl.multiple_of(c * head_rows, 16), head_rows), :
            ].astype(jnp.float32)
            masses = back[a * DGRP + m, cap * head_rows :, :].astype(jnp.float32)
            masses = jnp.where(stat_slot == c, masses, 0.0)
            mass = jnp.concatenate(
                [
                    jnp.sum(jnp.where(lane < LANES // 2, masses, 0.0), axis=1, keepdims=True),
                    jnp.sum(jnp.where(lane < LANES // 2, 0.0, masses), axis=1, keepdims=True),
                ],
                axis=0,
            )
            share = 1.0 / (1.0 + jnp.exp2(mass - score[at, :]))
            rows_scr[at, :] = cached + share * (value[at, :] - cached)
    for h in range(head_total):
        out[:, h * LANES : (h + 1) * LANES] = rows_scr[
            pl.ds(h, row_count, stride=head_total), :
        ].astype(out.dtype)


def shards(
    pool_kv,
    prefix_table,
    prefix_count,
    prefill_q,
    prefill_new_kv,
    decode_q,
    decode_new,
    decode_cache,
    decode_group,
    cached_len,
):
    devices = lax.axis_size("pool")
    blk = pool_kv.shape[2]
    row_count, q_width = decode_q.shape
    cap = decode_cache.shape[1] // devices
    decode_groups = devices // DGRP
    pair_count = decode_cache.shape[2]
    head_rows = q_width // LANES // DGRP
    message_rows = cap * head_rows
    groups = decode_group.reshape(-1)
    prefill_groups = prefix_table.shape[0]
    small = pltpu.CompilerParams(vmem_limit_bytes=8 * 2**20)

    share = jax.ShapeDtypeStruct(
        (PGRP // PLANE, prefill_groups, PCAP, blk, 2 * LANES), jnp.bfloat16
    )
    sending, *shares = pl.pallas_call(
        functools.partial(pack_kernel, head_rows),
        out_shape=(
            jax.ShapeDtypeStruct((decode_groups, DGRP, message_rows, LANES), jnp.bfloat16),
        )
        + (share,) * PLANE,
        in_specs=[smem_spec()] * 3 + [any_spec(), any_spec()],
        out_specs=(any_spec(),) * (1 + PLANE),
        scratch_shapes=[
            pltpu.VMEM((row_count, q_width), jnp.bfloat16),
            pltpu.VMEM((row_count * q_width // LANES, LANES), jnp.float32),
            pltpu.VMEM((DGRP, decode_groups, message_rows, LANES), jnp.bfloat16),
            pltpu.SMEM((decode_groups,), jnp.int32),
            pltpu.SemaphoreType.DMA((DGRP,)),
            pltpu.SemaphoreType.DMA((2 * PLANE * PCAP,)),
            pltpu.SemaphoreType.DMA,
        ],
        compiler_params=small,
        name="pack",
    )(
        in_hbm(groups),
        in_hbm(prefix_table),
        in_hbm(prefix_count),
        in_hbm(decode_q),
        in_hbm(pool_kv.reshape((-1, PGRP // PLANE, PLANE) + pool_kv.shape[2:])),
    )
    sending = sending.reshape(devices, message_rows, LANES)

    received = lax.all_to_all(sending, "pool", split_axis=0, concat_axis=0, tiled=True)

    shares = [shares[0]] + [
        lax.ppermute(shares[t], "pool", [(i, i ^ t) for i in range(devices)])
        for t in range(1, PLANE)
    ]
    chunk = min(cap, 4)
    width = 8
    block_count = devices * cap // chunk
    slot_len, listed, prefix_held, places, ahead = pl.pallas_call(
        functools.partial(plan_kernel, cap, chunk, devices),
        out_shape=(
            jax.ShapeDtypeStruct((devices * cap,), jnp.int32),
            jax.ShapeDtypeStruct((block_count + 2,), jnp.int32),
            jax.ShapeDtypeStruct((devices * pool_kv.shape[0],), jnp.int32),
            jax.ShapeDtypeStruct((2 * row_count,), jnp.int32),
            jax.ShapeDtypeStruct((width * chunk,) + decode_cache.shape[2:], jnp.bfloat16),
        ),
        in_specs=[smem_spec()] * 4 + [any_spec()],
        out_specs=(smem_spec(),) * 4 + (vmem_spec(),),
        scratch_shapes=[
            pltpu.SMEM((decode_groups,), jnp.int32),
            pltpu.SMEM((cap + 1,), jnp.int32),
            pltpu.SemaphoreType.DMA((width,)),
        ],
        compiler_params=small,
        cost_estimate=pl.CostEstimate(flops=1000000, bytes_accessed=4000000, transcendentals=0),
        name="plan",
    )(in_hbm(prefix_table), in_hbm(prefix_count), in_hbm(groups), in_hbm(cached_len), in_hbm(decode_cache[0]))

    *shares, slot_len, listed = lax.optimization_barrier((*shares, slot_len, listed))
    planes = devices // PLANE
    bundle = jax.ShapeDtypeStruct((PLANE, PCAP, blk, 2 * LANES), jnp.bfloat16)
    bundles = pl.pallas_call(
        functools.partial(regroup_kernel, planes),
        out_shape=(bundle,) * planes,
        in_specs=[any_spec()] * PLANE,
        out_specs=(any_spec(),) * planes,
        scratch_shapes=[pltpu.SemaphoreType.DMA((planes * PLANE,))],
        compiler_params=small,
        cost_estimate=pl.CostEstimate(flops=100000, bytes_accessed=1000000, transcendentals=0),
        name="regroup",
    )(*shares)

    def along_line(step):
        pairs = [
            (i, partner(i // PLANE, step, planes) * PLANE + i % PLANE) for i in range(devices)
        ]
        return lax.ppermute(bundles[step], "pool", pairs)


    far_first = {step: along_line(step) for step in reversed(range(1, planes))}
    lines = [bundles[0]] + [far_first[step] for step in range(1, planes)]

    answers = pl.pallas_call(
        functools.partial(decode_kernel, cap, head_rows, chunk, width),
        out_shape=jax.ShapeDtypeStruct(
            (devices, cap * head_rows + head_rows // 2, LANES), jnp.bfloat16
        ),
        in_specs=[smem_spec(), smem_spec(), vmem_spec(), vmem_spec(), any_spec()],
        out_specs=vmem_spec(),
        scratch_shapes=[
            pltpu.VMEM(((block_count - width) * chunk,) + decode_cache.shape[2:], jnp.bfloat16),
            pltpu.SemaphoreType.DMA((block_count - width,)),
        ],
        compiler_params=pltpu.CompilerParams(vmem_limit_bytes=20 * 2**20),
        cost_estimate=pl.CostEstimate(
            flops=500000000, bytes_accessed=8000000, transcendentals=1000000
        ),
        name="decode",
    )(listed, slot_len, received, ahead, in_hbm(decode_cache[0]))

    back = lax.all_to_all(answers, "pool", split_axis=0, concat_axis=0, tiled=True)

    token_count, fill_width = prefill_q.shape[1:]
    prefix = devices * PCAP * blk
    head_count = fill_width // LANES
    prefix_held, decode_q, decode_new, _ = lax.optimization_barrier(
        (prefix_held, decode_q, decode_new, answers)
    )
    expanded = jax.ShapeDtypeStruct((row_count * q_width // LANES, LANES), jnp.float32)
    own_score, own_value = pl.pallas_call(
        own_kernel,
        out_shape=(expanded, expanded),
        in_specs=[vmem_spec(), vmem_spec()],
        out_specs=(vmem_spec(), vmem_spec()),
        compiler_params=small,
        cost_estimate=pl.CostEstimate(flops=1000000, bytes_accessed=2000000, transcendentals=0),
        name="own",
    )(in_hbm(decode_q), in_hbm(decode_new))
    prefill_out = pl.pallas_call(
        functools.partial(prefill_kernel, planes, min(256, token_count)),
        grid=(head_count,),
        out_shape=jax.ShapeDtypeStruct((token_count, fill_width), jnp.bfloat16),
        in_specs=[smem_spec()]
        + [pl.BlockSpec(bundle.shape, lambda u: (0, 0, 0, 0))] * planes
        + [
            pl.BlockSpec((token_count, LANES), lambda u: (0, u)),
            pl.BlockSpec(prefill_new_kv.shape[1:], lambda u: (0, 0)),
        ],
        out_specs=pl.BlockSpec((token_count, LANES), lambda u: (0, u)),
        scratch_shapes=[
            pltpu.VMEM((prefix + token_count, LANES), jnp.bfloat16),
            pltpu.VMEM((prefix + token_count, LANES), jnp.bfloat16),
            pltpu.VMEM((8, prefix), jnp.float32),
        ],
        compiler_params=pltpu.CompilerParams(vmem_limit_bytes=16 * 2**20),
        cost_estimate=pl.CostEstimate(
            flops=32 * token_count * fill_width * (prefix + token_count),
            bytes_accessed=3000000,
            transcendentals=token_count * head_count * (prefix + token_count // 2),
        ),
        name="prefill",
    )(prefix_held, *lines, in_hbm(prefill_q[0]), in_hbm(prefill_new_kv[0]))

    decode_out = pl.pallas_call(
        functools.partial(unpack_kernel, cap, head_rows),
        out_shape=jax.ShapeDtypeStruct((row_count, q_width), jnp.bfloat16),
        in_specs=[smem_spec()] + [vmem_spec()] * 3,
        out_specs=vmem_spec(),
        scratch_shapes=[pltpu.VMEM(expanded.shape, jnp.float32)],
        compiler_params=small,
        name="unpack",
    )(places, back, own_score, own_value)
    return (prefill_out[None], decode_out)


def solution(mesh):
    in_specs = (
        P(("rep", "pool"), None, None, None),
        P("rep", None),
        P("rep"),
        P(("rep", "pool"), None, None),
        P(("rep", "pool"), None, None),
        P(("rep", "pool"), None),
        P(("rep", "pool"), None),
        P(("rep", "pool"), None, None, None, None),
        P("rep", None),
        P("rep"),
    )
    out_specs = (P(("rep", "pool"), None, None), P(("rep", "pool"), None))
    return jax.shard_map(shards, mesh=mesh, in_specs=in_specs, out_specs=out_specs, check_vma=False)
```

```python
import functools

import jax
import jax.numpy as jnp
from jax import lax
from jax.experimental import pallas as pl
from jax.experimental.pallas import tpu as pltpu
from jax.sharding import PartitionSpec as P

PGRP = 8
DGRP = 4
PCAP = 2
PLANE = 4
LANES = 128
MASKED = -1e30
LOG2E = 1.4426950408889634


def any_spec():
    return pl.BlockSpec(memory_space=pl.ANY)


def smem_spec():
    return pl.BlockSpec(memory_space=pltpu.SMEM)


def in_hbm(x):
    return pltpu.with_memory_space_constraint(x, pltpu.HBM)


def vmem_spec():
    return pl.BlockSpec(memory_space=pltpu.VMEM)


def pack_kernel(head_rows, groups, table, count, q_far, pool, out, *rest):
    shares = rest[:PLANE]
    q, rows_scr, stage, group_fill, sems, block_sems, q_sem = rest[PLANE:]
    q_copy = pltpu.make_async_copy(q_far, q, q_sem)
    q_copy.start()
    flying = send_blocks(table, count, pool, shares, block_sems)
    decode_groups = out.shape[0]
    row_count = q.shape[0]
    head_total = q.shape[1] // LANES
    device = lax.axis_index("pool")
    for a in range(decode_groups):
        group_fill[a] = 0
    homes = []
    for i in range(row_count):
        a = groups[device * row_count + i]
        c = group_fill[a]
        group_fill[a] = c + 1
        homes.append((a, c))
    q_copy.wait()
    copies = []
    for m in range(DGRP):
        for h in range(m * head_rows, (m + 1) * head_rows):
            rows_scr[pl.ds(h, row_count, stride=head_total), :] = q[
                :, h * LANES : (h + 1) * LANES
            ].astype(jnp.float32)
        for i, (a, c) in enumerate(homes):
            first = i * head_total + m * head_rows
            stage[m, a, pl.ds(pl.multiple_of(c * head_rows, 16), head_rows), :] = rows_scr[
                first : first + head_rows, :
            ].astype(out.dtype)
        copy = pltpu.make_async_copy(stage.at[m], out.at[:, m], sems.at[m])
        copy.start()
        copies.append(copy)
    for copy in copies + flying:
        copy.wait()


def send_blocks(table, count, pool, outs, sems):
    blocks_here = pool.shape[0]
    group_count, most_blocks = table.shape
    device = lax.axis_index("pool")
    first_block = device * blocks_here
    flying = []
    for g in range(group_count):

        def scan_table(j, carry):
            seen, chosen = carry
            entry = table[g, j]
            mine = (entry >= first_block) & (entry < first_block + blocks_here) & (j < count[g])
            chosen = tuple(
                jnp.where(mine & (seen == k), entry - first_block, chosen[k]) for k in range(PCAP)
            )
            return seen + mine.astype(jnp.int32), chosen

        start = (jnp.int32(0), tuple(jnp.int32(0) for _ in range(PCAP)))
        _, chosen = lax.fori_loop(0, most_blocks, scan_table, start, unroll=8)
        if g >= 2:
            for copy in flying.pop(0):
                copy.wait()
        copies = []
        for t in range(PLANE):
            for k in range(PCAP):
                copy = pltpu.make_async_copy(
                    pool.at[chosen[k], :, (device % PLANE) ^ t],
                    outs[t].at[:, g, k],
                    sems.at[((g % 2) * PLANE + t) * PCAP + k],
                )
                copy.start()
                copies.append(copy)
        flying.append(copies)
    return [copy for copies in flying for copy in copies]


def partner(plane, step, planes):
    return plane ^ step if planes & (planes - 1) == 0 else (plane + step) % planes


def regroup_kernel(planes, *rest):
    held, outs, sems = rest[:PLANE], rest[PLANE:-1], rest[-1]
    mine = lax.axis_index("pool") // PLANE
    per_group = PGRP // PLANE
    copies = []
    for step in range(planes):
        there = partner(mine, step, planes)
        for t in range(PLANE):
            copy = pltpu.make_async_copy(
                held[t].at[there % per_group, there // per_group],
                outs[step].at[t],
                sems.at[step * PLANE + t],
            )
            copy.start()
            copies.append(copy)
    for copy in copies:
        copy.wait()


def fetch_block(cache, listed, i, chunk, held, place, sem):
    return pltpu.make_async_copy(
        cache.at[pl.ds(listed[1 + i] * chunk, chunk)], held.at[pl.ds(place * chunk, chunk)], sem
    )


def plan_kernel(
    cap,
    step,
    owners,
    table,
    count,
    groups,
    lengths,
    cache,
    slot_len,
    listed,
    prefix_held,
    places,
    ahead,
    group_fill,
    found,
    sems,
):
    device = lax.axis_index("pool")
    home_count = owners
    row_count = groups.shape[0] // home_count
    group_id = device // DGRP
    prefill_id = device // PGRP
    blocks_here = listed.shape[0]
    most_blocks = table.shape[1]
    chunk = min(cap, step)

    def one_home(s, filled):
        here = jnp.int32(0)
        for i in range(row_count):
            row = s * row_count + i
            found[here] = lengths[row]
            here = here + (groups[row] == group_id).astype(jnp.int32)
        for c in range(cap):
            slot_len[s * cap + c] = jnp.where(c < here, found[c], 0)
        for b in range(cap // chunk):
            listed[1 + jnp.minimum(filled, blocks_here - 2)] = s * (cap // chunk) + b
            filled = filled + (here > b * chunk).astype(jnp.int32)
        return filled

    live = lax.fori_loop(0, home_count, one_home, jnp.int32(0))
    listed[0] = live
    for i in range(ahead.shape[0] // chunk):
        pl.when(i < live)(fetch_block(cache, listed, i, chunk, ahead, i, sems.at[i]).start)

    for a in range(owners // DGRP):
        group_fill[a] = 0
    for i in range(row_count):
        a = groups[device * row_count + i]
        c = group_fill[a]
        places[2 * i] = a
        places[2 * i + 1] = c
        group_fill[a] = c + 1

    def one_owner(o, carry):
        prefix_held[o] = 0
        return carry

    lax.fori_loop(0, owners, one_owner, 0, unroll=8)
    pool_blocks = prefix_held.shape[0] // owners

    def one_entry(j, carry):
        o = lax.div(table[prefill_id, j], pool_blocks)
        prefix_held[o] = prefix_held[o] + 1
        return carry

    lax.fori_loop(0, jnp.minimum(count[prefill_id], most_blocks), one_entry, 0)
    for i in range(ahead.shape[0] // chunk):
        pl.when(i < live)(fetch_block(cache, listed, i, chunk, ahead, i, sems.at[i]).wait)


def decode_kernel(
    cap, head_rows, chunk, width, listed, slot_len, recv, ahead, cache, out, held, sems
):
    pair_count, positions = cache.shape[1], cache.shape[2]
    per_home = cap // chunk
    key_count = pair_count * positions
    query_heads = head_rows // pair_count
    live = listed[0]
    scale = LANES ** (-0.5) * LOG2E
    rows = chunk * head_rows
    slots = width * chunk
    pair = 2 if chunk % 2 == 0 else 1

    def fetch(i):
        return fetch_block(cache, listed, i, chunk, held, i - width, sems.at[i - width])

    def begin(i, carry):
        fetch(i).start()
        return carry

    lax.fori_loop(width, live, begin, 0)
    row_pair = lax.broadcasted_iota(jnp.int32, (head_rows, key_count), 0) // query_heads
    key_axis = lax.broadcasted_iota(jnp.int32, (head_rows, key_count), 1)
    pos = jnp.where(key_axis // positions == row_pair, key_axis % positions, positions)
    half = head_rows // 2
    lane = lax.broadcasted_iota(jnp.int32, (half, LANES), 1)
    part, stat_slot = lane % (LANES // 2) % 3, lane % (LANES // 2) // 3

    def several(t, kv):
        ids = [jnp.minimum(t * width + w, live - 1) for w in range(width)]
        blocks = [listed[1 + i] for i in ids]
        homes = [b // per_home for b in blocks]
        firsts = [(b % per_home) * chunk for b in blocks]
        places = [pl.multiple_of(f * head_rows, 16) for f in firsts]
        q = jnp.concatenate(
            [recv[h, pl.ds(p, rows), :] for h, p in zip(homes, places)], axis=0
        )
        keys = kv[..., :LANES].reshape(slots, key_count, LANES)
        values = kv[..., LANES:].reshape(slots, key_count, LANES)
        scores = jnp.einsum(
            "jqd,jkd->jqk",
            q.reshape(slots // pair, pair * head_rows, LANES),
            keys.reshape(slots // pair, pair * key_count, LANES),
            preferred_element_type=jnp.float32,
        )
        if pair == 2:
            scores = jnp.stack(
                [scores[:, :head_rows, :key_count], scores[:, head_rows:, key_count:]], axis=1
            ).reshape(slots, head_rows, key_count)
        kept = jnp.stack(
            [pos < slot_len[blocks[w] * chunk + j] for w in range(width) for j in range(chunk)]
        )
        scores = jnp.where(kept, scores, MASKED)
        top = jnp.max(scores, axis=2, keepdims=True)
        weights = jnp.exp2((scores - top) * scale)
        total = jnp.sum(weights, axis=2, keepdims=True)
        weights = weights.astype(jnp.bfloat16)
        if pair == 2:
            weights = weights.reshape(slots // 2, 2, head_rows, key_count)
            nothing = jnp.zeros((slots // 2, head_rows, key_count), jnp.bfloat16)
            upper = jnp.concatenate([weights[:, 0], nothing], axis=2)
            lower = jnp.concatenate([nothing, weights[:, 1]], axis=2)
            weights = jnp.concatenate([upper, lower], axis=1)
        mixed = jnp.einsum(
            "jqk,jkd->jqd",
            weights,
            values.reshape(slots // pair, pair * key_count, LANES),
            preferred_element_type=jnp.float32,
        )
        mixed = mixed.reshape(slots, head_rows, LANES) / total
        mass = top * scale + jnp.log(total) * LOG2E
        high = mass.astype(jnp.bfloat16).astype(jnp.float32)
        middle = (mass - high).astype(jnp.bfloat16).astype(jnp.float32)
        low = mass - high - middle
        mixed = mixed.reshape(width, rows, LANES)
        for w in reversed(range(width)):
            out[homes[w], pl.ds(places[w], rows), :] = mixed[w].astype(out.dtype)
            masses = out[homes[w], cap * head_rows :, :].astype(jnp.float32)
            for j in range(chunk):
                at = w * chunk + j
                split = [
                    jnp.where(lane < LANES // 2, piece[at, :half], piece[at, half:])
                    for piece in (high, middle, low)
                ]
                split = jnp.where(part == 0, split[0], jnp.where(part == 1, split[1], split[2]))
                masses = jnp.where(stat_slot == firsts[w] + j, split, masses)
            out[homes[w], cap * head_rows :, :] = masses.astype(out.dtype)

    several(0, ahead[...])

    def later(t, carry):
        for w in range(width):
            pl.when(t * width + w < live)(fetch(t * width + w).wait)
        several(t, held[pl.ds((t - 1) * slots, slots)])
        return carry

    lax.fori_loop(1, (live + width - 1) // width, later, 0)


def prefill_kernel(planes, tile, prefix_held, *rest):
    sources = rest[:planes]
    q, new_kv, out, keys, values, bias = rest[planes:]
    blk = sources[0].shape[2]
    prefix = planes * PLANE * PCAP * blk
    token_count = new_kv.shape[0]
    scale = LANES ** (-0.5) * LOG2E
    device = lax.axis_index("pool")

    @pl.when(pl.program_id(0) == 0)
    def _():
        lane_block = lax.broadcasted_iota(jnp.int32, (8, prefix), 1) // blk
        hide = jnp.zeros((8, prefix), jnp.float32)
        for step in range(planes):
            sender = device // PLANE
            sender = sender ^ step if planes & (planes - 1) == 0 else (sender + planes - step) % planes
            for t in range(PLANE):
                owner = sender * PLANE + ((device % PLANE) ^ t)
                for k in range(PCAP):
                    ordinal = (step * PLANE + t) * PCAP + k
                    block = sources[step][t, k]
                    keys[ordinal * blk : (ordinal + 1) * blk, :] = block[:, :LANES]
                    values[ordinal * blk : (ordinal + 1) * blk, :] = block[:, LANES:]
                    gone = jnp.where(prefix_held[owner] > k, 0.0, MASKED)
                    hide = jnp.where(lane_block == ordinal, gone, hide)
        bias[...] = hide
        keys[prefix:, :] = new_kv[:, :LANES]
        values[prefix:, :] = new_kv[:, LANES:]

    for t in range(token_count // tile):
        width = prefix + (t + 1) * tile
        block = q[t * tile : (t + 1) * tile, :]
        scores = lax.dot_general(
            block, keys[:width, :], (((1,), (1,)), ((), ())), preferred_element_type=jnp.float32
        )
        causal = lax.broadcasted_iota(jnp.int32, (tile, tile), 0) >= lax.broadcasted_iota(
            jnp.int32, (tile, tile), 1
        )
        pieces = [scores[:, :prefix] + bias[0:1, :]]
        if t:
            pieces.append(scores[:, prefix : width - tile])
        pieces.append(jnp.where(causal, scores[:, width - tile :], MASKED))
        scores = jnp.concatenate(pieces, axis=1)
        top = jnp.max(scores, axis=1, keepdims=True)
        weights = jnp.exp2((scores - top) * scale)
        total = jnp.sum(weights, axis=1, keepdims=True)
        mixed = jnp.dot(
            weights.astype(jnp.bfloat16), values[:width, :], preferred_element_type=jnp.float32
        )
        out[t * tile : (t + 1) * tile, :] = (mixed / total).astype(out.dtype)


def own_kernel(q, kv, score, value):
    row_count = q.shape[0]
    head_total = q.shape[1] // LANES
    pair_count = kv.shape[1] // (2 * LANES)
    per_pair = head_total // pair_count
    for k in range(pair_count):
        lane = k * 2 * LANES
        key = kv[:, lane : lane + LANES].astype(jnp.float32) * (LANES ** (-0.5) * LOG2E)
        held = kv[:, lane + LANES : lane + 2 * LANES].astype(jnp.float32)
        for h in range(k * per_pair, (k + 1) * per_pair):
            at = pl.ds(h, row_count, stride=head_total)
            query = q[:, h * LANES : (h + 1) * LANES].astype(jnp.float32)
            product = jnp.sum(query * key, axis=1, keepdims=True)
            score[at, :] = jnp.broadcast_to(product, (row_count, LANES))
            value[at, :] = held


def unpack_kernel(cap, head_rows, places, back, score, value, out, rows_scr, stage, sems):
    row_count = out.shape[0]
    head_total = out.shape[1] // LANES
    lane = lax.broadcasted_iota(jnp.int32, (head_rows // 2, LANES), 1)
    stat_slot = lane % (LANES // 2) // 3
    copies = []
    for m in range(DGRP):
        for i in range(row_count):
            a, c = places[2 * i], places[2 * i + 1]
            at = slice(i * head_total + m * head_rows, i * head_total + (m + 1) * head_rows)
            cached = back[
                a * DGRP + m, pl.ds(pl.multiple_of(c * head_rows, 16), head_rows), :
            ].astype(jnp.float32)
            masses = back[a * DGRP + m, cap * head_rows :, :].astype(jnp.float32)
            masses = jnp.where(stat_slot == c, masses, 0.0)
            mass = jnp.concatenate(
                [
                    jnp.sum(jnp.where(lane < LANES // 2, masses, 0.0), axis=1, keepdims=True),
                    jnp.sum(jnp.where(lane < LANES // 2, 0.0, masses), axis=1, keepdims=True),
                ],
                axis=0,
            )
            share = 1.0 / (1.0 + jnp.exp2(mass - score[at, :]))
            rows_scr[at, :] = cached + share * (value[at, :] - cached)
        for h in range(m * head_rows, (m + 1) * head_rows):
            stage[:, h * LANES : (h + 1) * LANES] = rows_scr[
                pl.ds(h, row_count, stride=head_total), :
            ].astype(out.dtype)
        lanes = pl.ds(m * head_rows * LANES, head_rows * LANES)
        copy = pltpu.make_async_copy(stage.at[:, lanes], out.at[:, lanes], sems.at[m])
        copy.start()
        copies.append(copy)
    for copy in copies:
        copy.wait()


def shards(
    pool_kv,
    prefix_table,
    prefix_count,
    prefill_q,
    prefill_new_kv,
    decode_q,
    decode_new,
    decode_cache,
    decode_group,
    cached_len,
):
    devices = lax.axis_size("pool")
    blk = pool_kv.shape[2]
    row_count, q_width = decode_q.shape
    cap = decode_cache.shape[1] // devices
    decode_groups = devices // DGRP
    pair_count = decode_cache.shape[2]
    head_rows = q_width // LANES // DGRP
    message_rows = cap * head_rows
    groups = decode_group.reshape(-1)
    prefill_groups = prefix_table.shape[0]
    small = pltpu.CompilerParams(vmem_limit_bytes=8 * 2**20)

    share = jax.ShapeDtypeStruct(
        (PGRP // PLANE, prefill_groups, PCAP, blk, 2 * LANES), jnp.bfloat16
    )
    sending, *shares = pl.pallas_call(
        functools.partial(pack_kernel, head_rows),
        out_shape=(
            jax.ShapeDtypeStruct((decode_groups, DGRP, message_rows, LANES), jnp.bfloat16),
        )
        + (share,) * PLANE,
        in_specs=[smem_spec()] * 3 + [any_spec(), any_spec()],
        out_specs=(any_spec(),) * (1 + PLANE),
        scratch_shapes=[
            pltpu.VMEM((row_count, q_width), jnp.bfloat16),
            pltpu.VMEM((row_count * q_width // LANES, LANES), jnp.float32),
            pltpu.VMEM((DGRP, decode_groups, message_rows, LANES), jnp.bfloat16),
            pltpu.SMEM((decode_groups,), jnp.int32),
            pltpu.SemaphoreType.DMA((DGRP,)),
            pltpu.SemaphoreType.DMA((2 * PLANE * PCAP,)),
            pltpu.SemaphoreType.DMA,
        ],
        compiler_params=small,
        name="pack",
    )(
        in_hbm(groups),
        in_hbm(prefix_table),
        in_hbm(prefix_count),
        in_hbm(decode_q),
        in_hbm(pool_kv.reshape((-1, PGRP // PLANE, PLANE) + pool_kv.shape[2:])),
    )
    sending = sending.reshape(devices, message_rows, LANES)

    received = lax.all_to_all(sending, "pool", split_axis=0, concat_axis=0, tiled=True)

    shares = [shares[0]] + [
        lax.ppermute(shares[t], "pool", [(i, i ^ t) for i in range(devices)])
        for t in range(1, PLANE)
    ]
    chunk = min(cap, 4)
    width = 8
    block_count = devices * cap // chunk
    slot_len, listed, prefix_held, places, ahead = pl.pallas_call(
        functools.partial(plan_kernel, cap, chunk, devices),
        out_shape=(
            jax.ShapeDtypeStruct((devices * cap,), jnp.int32),
            jax.ShapeDtypeStruct((block_count + 2,), jnp.int32),
            jax.ShapeDtypeStruct((devices * pool_kv.shape[0],), jnp.int32),
            jax.ShapeDtypeStruct((2 * row_count,), jnp.int32),
            jax.ShapeDtypeStruct((width * chunk,) + decode_cache.shape[2:], jnp.bfloat16),
        ),
        in_specs=[smem_spec()] * 4 + [any_spec()],
        out_specs=(smem_spec(),) * 4 + (vmem_spec(),),
        scratch_shapes=[
            pltpu.SMEM((decode_groups,), jnp.int32),
            pltpu.SMEM((cap + 1,), jnp.int32),
            pltpu.SemaphoreType.DMA((width,)),
        ],
        compiler_params=small,
        cost_estimate=pl.CostEstimate(flops=1000000, bytes_accessed=4000000, transcendentals=0),
        name="plan",
    )(in_hbm(prefix_table), in_hbm(prefix_count), in_hbm(groups), in_hbm(cached_len), in_hbm(decode_cache[0]))

    *shares, slot_len, listed = lax.optimization_barrier((*shares, slot_len, listed))
    planes = devices // PLANE
    bundle = jax.ShapeDtypeStruct((PLANE, PCAP, blk, 2 * LANES), jnp.bfloat16)
    bundles = pl.pallas_call(
        functools.partial(regroup_kernel, planes),
        out_shape=(bundle,) * planes,
        in_specs=[any_spec()] * PLANE,
        out_specs=(any_spec(),) * planes,
        scratch_shapes=[pltpu.SemaphoreType.DMA((planes * PLANE,))],
        compiler_params=small,
        cost_estimate=pl.CostEstimate(flops=100000, bytes_accessed=1000000, transcendentals=0),
        name="regroup",
    )(*shares)

    def along_line(step):
        pairs = [
            (i, partner(i // PLANE, step, planes) * PLANE + i % PLANE) for i in range(devices)
        ]
        return lax.ppermute(bundles[step], "pool", pairs)


    far_first = {step: along_line(step) for step in reversed(range(1, planes))}
    lines = [bundles[0]] + [far_first[step] for step in range(1, planes)]

    answers = pl.pallas_call(
        functools.partial(decode_kernel, cap, head_rows, chunk, width),
        out_shape=jax.ShapeDtypeStruct(
            (devices, cap * head_rows + head_rows // 2, LANES), jnp.bfloat16
        ),
        in_specs=[smem_spec(), smem_spec(), vmem_spec(), vmem_spec(), any_spec()],
        out_specs=vmem_spec(),
        scratch_shapes=[
            pltpu.VMEM(((block_count - width) * chunk,) + decode_cache.shape[2:], jnp.bfloat16),
            pltpu.SemaphoreType.DMA((block_count - width,)),
        ],
        compiler_params=pltpu.CompilerParams(vmem_limit_bytes=20 * 2**20),
        cost_estimate=pl.CostEstimate(
            flops=500000000, bytes_accessed=8000000, transcendentals=1000000
        ),
        name="decode",
    )(listed, slot_len, received, ahead, in_hbm(decode_cache[0]))

    back = lax.all_to_all(answers, "pool", split_axis=0, concat_axis=0, tiled=True)

    token_count, fill_width = prefill_q.shape[1:]
    prefix = devices * PCAP * blk
    head_count = fill_width // LANES
    prefix_held, decode_q, decode_new, _ = lax.optimization_barrier(
        (prefix_held, decode_q, decode_new, answers)
    )
    expanded = jax.ShapeDtypeStruct((row_count * q_width // LANES, LANES), jnp.float32)
    own_score, own_value = pl.pallas_call(
        own_kernel,
        out_shape=(expanded, expanded),
        in_specs=[vmem_spec(), vmem_spec()],
        out_specs=(vmem_spec(), vmem_spec()),
        compiler_params=small,
        cost_estimate=pl.CostEstimate(flops=1000000, bytes_accessed=2000000, transcendentals=0),
        name="own",
    )(in_hbm(decode_q), in_hbm(decode_new))
    prefill_out = pl.pallas_call(
        functools.partial(prefill_kernel, planes, min(256, token_count)),
        grid=(head_count,),
        out_shape=jax.ShapeDtypeStruct((token_count, fill_width), jnp.bfloat16),
        in_specs=[smem_spec()]
        + [pl.BlockSpec(bundle.shape, lambda u: (0, 0, 0, 0))] * planes
        + [
            pl.BlockSpec((token_count, LANES), lambda u: (0, u)),
            pl.BlockSpec(prefill_new_kv.shape[1:], lambda u: (0, 0)),
        ],
        out_specs=pl.BlockSpec((token_count, LANES), lambda u: (0, u)),
        scratch_shapes=[
            pltpu.VMEM((prefix + token_count, LANES), jnp.bfloat16),
            pltpu.VMEM((prefix + token_count, LANES), jnp.bfloat16),
            pltpu.VMEM((8, prefix), jnp.float32),
        ],
        compiler_params=pltpu.CompilerParams(vmem_limit_bytes=16 * 2**20),
        cost_estimate=pl.CostEstimate(
            flops=32 * token_count * fill_width * (prefix + token_count),
            bytes_accessed=3000000,
            transcendentals=token_count * head_count * (prefix + token_count // 2),
        ),
        name="prefill",
    )(prefix_held, *lines, in_hbm(prefill_q[0]), in_hbm(prefill_new_kv[0]))

    decode_out = pl.pallas_call(
        functools.partial(unpack_kernel, cap, head_rows),
        out_shape=jax.ShapeDtypeStruct((row_count, q_width), jnp.bfloat16),
        in_specs=[smem_spec()] + [vmem_spec()] * 3,
        out_specs=any_spec(),
        scratch_shapes=[
            pltpu.VMEM(expanded.shape, jnp.float32),
            pltpu.VMEM((row_count, q_width), jnp.bfloat16),
            pltpu.SemaphoreType.DMA((DGRP,)),
        ],
        compiler_params=small,
        name="unpack",
    )(places, back, own_score, own_value)
    return (prefill_out[None], decode_out)


def solution(mesh):
    in_specs = (
        P(("rep", "pool"), None, None, None),
        P("rep", None),
        P("rep"),
        P(("rep", "pool"), None, None),
        P(("rep", "pool"), None, None),
        P(("rep", "pool"), None),
        P(("rep", "pool"), None),
        P(("rep", "pool"), None, None, None, None),
        P("rep", None),
        P("rep"),
    )
    out_specs = (P(("rep", "pool"), None, None), P(("rep", "pool"), None))
    return jax.shard_map(shards, mesh=mesh, in_specs=in_specs, out_specs=out_specs, check_vma=False)
```

```python
import functools

import jax
import jax.numpy as jnp
from jax import lax
from jax.experimental import pallas as pl
from jax.experimental.pallas import tpu as pltpu
from jax.sharding import PartitionSpec as P

PGRP = 8
DGRP = 4
PCAP = 2
PLANE = 4
LANES = 128
MASKED = -1e30
LOG2E = 1.4426950408889634


def any_spec():
    return pl.BlockSpec(memory_space=pl.ANY)


def smem_spec():
    return pl.BlockSpec(memory_space=pltpu.SMEM)


def in_hbm(x):
    return pltpu.with_memory_space_constraint(x, pltpu.HBM)


def vmem_spec():
    return pl.BlockSpec(memory_space=pltpu.VMEM)


def pack_kernel(head_rows, *rest):
    far, (pool, out), shares, near = rest[:4], rest[4:6], rest[6 : 6 + PLANE], rest[6 + PLANE :]
    table, count, groups, q, rows_scr, stage, group_fill, sems, block_sems, near_sems = near
    fetches = [
        pltpu.make_async_copy(there, here, near_sems.at[n])
        for n, (there, here) in enumerate(zip(far, (table, count, groups, q)))
    ]
    for fetch in fetches:
        fetch.start()
    for fetch in fetches[:3]:
        fetch.wait()
    flying = send_blocks(table, count, pool, shares, block_sems)
    decode_groups = out.shape[0]
    row_count = q.shape[0]
    head_total = q.shape[1] // LANES
    device = lax.axis_index("pool")
    for a in range(decode_groups):
        group_fill[a] = 0
    homes = []
    for i in range(row_count):
        a = groups[device * row_count + i]
        c = group_fill[a]
        group_fill[a] = c + 1
        homes.append((a, c))
    fetches[3].wait()
    copies = []
    for m in range(DGRP):
        for h in range(m * head_rows, (m + 1) * head_rows):
            rows_scr[pl.ds(h, row_count, stride=head_total), :] = q[
                :, h * LANES : (h + 1) * LANES
            ].astype(jnp.float32)
        for i, (a, c) in enumerate(homes):
            first = i * head_total + m * head_rows
            stage[m, a, pl.ds(pl.multiple_of(c * head_rows, 16), head_rows), :] = rows_scr[
                first : first + head_rows, :
            ].astype(out.dtype)
        copy = pltpu.make_async_copy(stage.at[m], out.at[:, m], sems.at[m])
        copy.start()
        copies.append(copy)
    for copy in copies + flying:
        copy.wait()


def send_blocks(table, count, pool, outs, sems):
    blocks_here = pool.shape[0]
    group_count, most_blocks = table.shape
    device = lax.axis_index("pool")
    first_block = device * blocks_here
    flying = []
    for g in range(group_count):

        def scan_table(j, carry):
            seen, chosen = carry
            entry = table[g, j]
            mine = (entry >= first_block) & (entry < first_block + blocks_here) & (j < count[g])
            chosen = tuple(
                jnp.where(mine & (seen == k), entry - first_block, chosen[k]) for k in range(PCAP)
            )
            return seen + mine.astype(jnp.int32), chosen

        start = (jnp.int32(0), tuple(jnp.int32(0) for _ in range(PCAP)))
        _, chosen = lax.fori_loop(0, most_blocks, scan_table, start, unroll=8)
        if g >= 2:
            for copy in flying.pop(0):
                copy.wait()
        copies = []
        for t in range(PLANE):
            for k in range(PCAP):
                copy = pltpu.make_async_copy(
                    pool.at[chosen[k], :, (device % PLANE) ^ t],
                    outs[t].at[:, g, k],
                    sems.at[((g % 2) * PLANE + t) * PCAP + k],
                )
                copy.start()
                copies.append(copy)
        flying.append(copies)
    return [copy for copies in flying for copy in copies]


def partner(plane, step, planes):
    return plane ^ step if planes & (planes - 1) == 0 else (plane + step) % planes


def regroup_kernel(planes, *rest):
    held, outs, sems = rest[:PLANE], rest[PLANE:-1], rest[-1]
    mine = lax.axis_index("pool") // PLANE
    per_group = PGRP // PLANE
    copies = []
    for step in range(planes):
        there = partner(mine, step, planes)
        for t in range(PLANE):
            copy = pltpu.make_async_copy(
                held[t].at[there % per_group, there // per_group],
                outs[step].at[t],
                sems.at[step * PLANE + t],
            )
            copy.start()
            copies.append(copy)
    for copy in copies:
        copy.wait()


def fetch_block(cache, listed, i, chunk, held, place, sem):
    return pltpu.make_async_copy(
        cache.at[pl.ds(listed[1 + i] * chunk, chunk)], held.at[pl.ds(place * chunk, chunk)], sem
    )


def plan_kernel(
    cap,
    step,
    owners,
    table,
    count,
    groups,
    lengths,
    cache,
    slot_len,
    listed,
    prefix_held,
    places,
    ahead,
    group_fill,
    found,
    sems,
):
    device = lax.axis_index("pool")
    home_count = owners
    row_count = groups.shape[0] // home_count
    group_id = device // DGRP
    prefill_id = device // PGRP
    blocks_here = listed.shape[0]
    most_blocks = table.shape[1]
    chunk = min(cap, step)

    def one_home(s, filled):
        here = jnp.int32(0)
        for i in range(row_count):
            row = s * row_count + i
            found[here] = lengths[row]
            here = here + (groups[row] == group_id).astype(jnp.int32)
        for c in range(cap):
            slot_len[s * cap + c] = jnp.where(c < here, found[c], 0)
        for b in range(cap // chunk):
            listed[1 + jnp.minimum(filled, blocks_here - 2)] = s * (cap // chunk) + b
            filled = filled + (here > b * chunk).astype(jnp.int32)
        return filled

    live = lax.fori_loop(0, home_count, one_home, jnp.int32(0))
    listed[0] = live
    for i in range(ahead.shape[0] // chunk):
        pl.when(i < live)(fetch_block(cache, listed, i, chunk, ahead, i, sems.at[i]).start)

    for a in range(owners // DGRP):
        group_fill[a] = 0
    for i in range(row_count):
        a = groups[device * row_count + i]
        c = group_fill[a]
        places[2 * i] = a
        places[2 * i + 1] = c
        group_fill[a] = c + 1

    def one_owner(o, carry):
        prefix_held[o] = 0
        return carry

    lax.fori_loop(0, owners, one_owner, 0, unroll=8)
    pool_blocks = prefix_held.shape[0] // owners

    def one_entry(j, carry):
        o = lax.div(table[prefill_id, j], pool_blocks)
        prefix_held[o] = prefix_held[o] + 1
        return carry

    lax.fori_loop(0, jnp.minimum(count[prefill_id], most_blocks), one_entry, 0)
    for i in range(ahead.shape[0] // chunk):
        pl.when(i < live)(fetch_block(cache, listed, i, chunk, ahead, i, sems.at[i]).wait)


def decode_kernel(
    cap, head_rows, chunk, width, listed, slot_len, recv, ahead, cache, out, held, sems
):
    pair_count, positions = cache.shape[1], cache.shape[2]
    per_home = cap // chunk
    key_count = pair_count * positions
    query_heads = head_rows // pair_count
    live = listed[0]
    scale = LANES ** (-0.5) * LOG2E
    rows = chunk * head_rows
    slots = width * chunk
    early = ahead.shape[0] // chunk
    pair = 2 if chunk % 2 == 0 else 1

    def fetch(i):
        return fetch_block(cache, listed, i, chunk, held, i - early, sems.at[i - early])

    def begin(i, carry):
        fetch(i).start()
        return carry

    lax.fori_loop(early, live, begin, 0)
    row_pair = lax.broadcasted_iota(jnp.int32, (head_rows, key_count), 0) // query_heads
    key_axis = lax.broadcasted_iota(jnp.int32, (head_rows, key_count), 1)
    pos = jnp.where(key_axis // positions == row_pair, key_axis % positions, positions)
    half = head_rows // 2
    lane = lax.broadcasted_iota(jnp.int32, (half, LANES), 1)
    part, stat_slot = lane % (LANES // 2) % 3, lane % (LANES // 2) // 3

    def several(t, kv):
        ids = [jnp.minimum(t * width + w, live - 1) for w in range(width)]
        blocks = [listed[1 + i] for i in ids]
        homes = [b // per_home for b in blocks]
        firsts = [(b % per_home) * chunk for b in blocks]
        places = [pl.multiple_of(f * head_rows, 16) for f in firsts]
        q = jnp.concatenate(
            [recv[h, pl.ds(p, rows), :] for h, p in zip(homes, places)], axis=0
        )
        keys = kv[..., :LANES].reshape(slots, key_count, LANES)
        values = kv[..., LANES:].reshape(slots, key_count, LANES)
        scores = jnp.einsum(
            "jqd,jkd->jqk",
            q.reshape(slots // pair, pair * head_rows, LANES),
            keys.reshape(slots // pair, pair * key_count, LANES),
            preferred_element_type=jnp.float32,
        )
        if pair == 2:
            scores = jnp.stack(
                [scores[:, :head_rows, :key_count], scores[:, head_rows:, key_count:]], axis=1
            ).reshape(slots, head_rows, key_count)
        kept = jnp.stack(
            [pos < slot_len[blocks[w] * chunk + j] for w in range(width) for j in range(chunk)]
        )
        scores = jnp.where(kept, scores, MASKED)
        top = jnp.max(scores, axis=2, keepdims=True)
        weights = jnp.exp2((scores - top) * scale)
        total = jnp.sum(weights, axis=2, keepdims=True)
        weights = weights.astype(jnp.bfloat16)
        if pair == 2:
            weights = weights.reshape(slots // 2, 2, head_rows, key_count)
            nothing = jnp.zeros((slots // 2, head_rows, key_count), jnp.bfloat16)
            upper = jnp.concatenate([weights[:, 0], nothing], axis=2)
            lower = jnp.concatenate([nothing, weights[:, 1]], axis=2)
            weights = jnp.concatenate([upper, lower], axis=1)
        mixed = jnp.einsum(
            "jqk,jkd->jqd",
            weights,
            values.reshape(slots // pair, pair * key_count, LANES),
            preferred_element_type=jnp.float32,
        )
        mixed = mixed.reshape(slots, head_rows, LANES) / total
        mass = top * scale + jnp.log(total) * LOG2E
        high = mass.astype(jnp.bfloat16).astype(jnp.float32)
        middle = (mass - high).astype(jnp.bfloat16).astype(jnp.float32)
        low = mass - high - middle
        mixed = mixed.reshape(width, rows, LANES)
        for w in reversed(range(width)):
            out[homes[w], pl.ds(places[w], rows), :] = mixed[w].astype(out.dtype)
            masses = out[homes[w], cap * head_rows :, :].astype(jnp.float32)
            for j in range(chunk):
                at = w * chunk + j
                split = [
                    jnp.where(lane < LANES // 2, piece[at, :half], piece[at, half:])
                    for piece in (high, middle, low)
                ]
                split = jnp.where(part == 0, split[0], jnp.where(part == 1, split[1], split[2]))
                masses = jnp.where(stat_slot == firsts[w] + j, split, masses)
            out[homes[w], cap * head_rows :, :] = masses.astype(out.dtype)

    several(0, ahead[:slots])

    @pl.when(width < live)
    def _():
        for i in range(early, 2 * width):
            pl.when(i < live)(fetch(i).wait)
        rest = held[: 2 * slots - early * chunk]
        several(1, jnp.concatenate([ahead[slots:], rest], axis=0))

    def later(t, carry):
        for w in range(width):
            pl.when(t * width + w < live)(fetch(t * width + w).wait)
        several(t, held[pl.ds(t * slots - early * chunk, slots)])
        return carry

    lax.fori_loop(2, (live + width - 1) // width, later, 0)


def prefill_kernel(planes, tile, prefix_held, *rest):
    sources = rest[:planes]
    q, new_kv, out, keys, values, bias = rest[planes:]
    blk = sources[0].shape[2]
    prefix = planes * PLANE * PCAP * blk
    token_count = new_kv.shape[0]
    scale = LANES ** (-0.5) * LOG2E
    device = lax.axis_index("pool")

    @pl.when(pl.program_id(0) == 0)
    def _():
        lane_block = lax.broadcasted_iota(jnp.int32, (8, prefix), 1) // blk
        hide = jnp.zeros((8, prefix), jnp.float32)
        for step in range(planes):
            sender = device // PLANE
            sender = sender ^ step if planes & (planes - 1) == 0 else (sender + planes - step) % planes
            for t in range(PLANE):
                owner = sender * PLANE + ((device % PLANE) ^ t)
                for k in range(PCAP):
                    ordinal = (step * PLANE + t) * PCAP + k
                    block = sources[step][t, k]
                    keys[ordinal * blk : (ordinal + 1) * blk, :] = block[:, :LANES]
                    values[ordinal * blk : (ordinal + 1) * blk, :] = block[:, LANES:]
                    gone = jnp.where(prefix_held[owner] > k, 0.0, MASKED)
                    hide = jnp.where(lane_block == ordinal, gone, hide)
        bias[...] = hide
        keys[prefix:, :] = new_kv[:, :LANES]
        values[prefix:, :] = new_kv[:, LANES:]

    for t in range(token_count // tile):
        width = prefix + (t + 1) * tile
        block = q[t * tile : (t + 1) * tile, :]
        scores = lax.dot_general(
            block, keys[:width, :], (((1,), (1,)), ((), ())), preferred_element_type=jnp.float32
        )
        causal = lax.broadcasted_iota(jnp.int32, (tile, tile), 0) >= lax.broadcasted_iota(
            jnp.int32, (tile, tile), 1
        )
        pieces = [scores[:, :prefix] + bias[0:1, :]]
        if t:
            pieces.append(scores[:, prefix : width - tile])
        pieces.append(jnp.where(causal, scores[:, width - tile :], MASKED))
        scores = jnp.concatenate(pieces, axis=1)
        top = jnp.max(scores, axis=1, keepdims=True)
        weights = jnp.exp2((scores - top) * scale)
        total = jnp.sum(weights, axis=1, keepdims=True)
        mixed = jnp.dot(
            weights.astype(jnp.bfloat16), values[:width, :], preferred_element_type=jnp.float32
        )
        out[t * tile : (t + 1) * tile, :] = (mixed / total).astype(out.dtype)


def own_kernel(q, kv, score, value):
    row_count = q.shape[0]
    head_total = q.shape[1] // LANES
    pair_count = kv.shape[1] // (2 * LANES)
    per_pair = head_total // pair_count
    for k in range(pair_count):
        lane = k * 2 * LANES
        key = kv[:, lane : lane + LANES].astype(jnp.float32) * (LANES ** (-0.5) * LOG2E)
        held = kv[:, lane + LANES : lane + 2 * LANES].astype(jnp.float32)
        for h in range(k * per_pair, (k + 1) * per_pair):
            at = pl.ds(h, row_count, stride=head_total)
            query = q[:, h * LANES : (h + 1) * LANES].astype(jnp.float32)
            product = jnp.sum(query * key, axis=1, keepdims=True)
            score[at, :] = jnp.broadcast_to(product, (row_count, LANES))
            value[at, :] = held


def unpack_kernel(cap, head_rows, places, back, score, value, out, rows_scr, stage, sems):
    row_count = out.shape[0]
    head_total = out.shape[1] // LANES
    lane = lax.broadcasted_iota(jnp.int32, (head_rows // 2, LANES), 1)
    stat_slot = lane % (LANES // 2) // 3
    copies = []
    for m in range(DGRP):
        for i in range(row_count):
            a, c = places[2 * i], places[2 * i + 1]
            at = slice(i * head_total + m * head_rows, i * head_total + (m + 1) * head_rows)
            cached = back[
                a * DGRP + m, pl.ds(pl.multiple_of(c * head_rows, 16), head_rows), :
            ].astype(jnp.float32)
            masses = back[a * DGRP + m, cap * head_rows :, :].astype(jnp.float32)
            masses = jnp.where(stat_slot == c, masses, 0.0)
            mass = jnp.concatenate(
                [
                    jnp.sum(jnp.where(lane < LANES // 2, masses, 0.0), axis=1, keepdims=True),
                    jnp.sum(jnp.where(lane < LANES // 2, 0.0, masses), axis=1, keepdims=True),
                ],
                axis=0,
            )
            share = 1.0 / (1.0 + jnp.exp2(mass - score[at, :]))
            rows_scr[at, :] = cached + share * (value[at, :] - cached)
        for h in range(m * head_rows, (m + 1) * head_rows):
            stage[:, h * LANES : (h + 1) * LANES] = rows_scr[
                pl.ds(h, row_count, stride=head_total), :
            ].astype(out.dtype)
        lanes = pl.ds(m * head_rows * LANES, head_rows * LANES)
        copy = pltpu.make_async_copy(stage.at[:, lanes], out.at[:, lanes], sems.at[m])
        copy.start()
        copies.append(copy)
    for copy in copies:
        copy.wait()


def shards(
    pool_kv,
    prefix_table,
    prefix_count,
    prefill_q,
    prefill_new_kv,
    decode_q,
    decode_new,
    decode_cache,
    decode_group,
    cached_len,
):
    devices = lax.axis_size("pool")
    blk = pool_kv.shape[2]
    row_count, q_width = decode_q.shape
    cap = decode_cache.shape[1] // devices
    decode_groups = devices // DGRP
    pair_count = decode_cache.shape[2]
    head_rows = q_width // LANES // DGRP
    message_rows = cap * head_rows
    groups = decode_group.reshape(-1)
    prefill_groups = prefix_table.shape[0]
    small = pltpu.CompilerParams(vmem_limit_bytes=8 * 2**20)

    share = jax.ShapeDtypeStruct(
        (PGRP // PLANE, prefill_groups, PCAP, blk, 2 * LANES), jnp.bfloat16
    )
    sending, *shares = pl.pallas_call(
        functools.partial(pack_kernel, head_rows),
        out_shape=(
            jax.ShapeDtypeStruct((decode_groups, DGRP, message_rows, LANES), jnp.bfloat16),
        )
        + (share,) * PLANE,
        in_specs=[any_spec()] * 5,
        out_specs=(any_spec(),) * (1 + PLANE),
        scratch_shapes=[
            pltpu.SMEM(prefix_table.shape, jnp.int32),
            pltpu.SMEM(prefix_count.shape, jnp.int32),
            pltpu.SMEM(groups.shape, jnp.int32),
            pltpu.VMEM((row_count, q_width), jnp.bfloat16),
            pltpu.VMEM((row_count * q_width // LANES, LANES), jnp.float32),
            pltpu.VMEM((DGRP, decode_groups, message_rows, LANES), jnp.bfloat16),
            pltpu.SMEM((decode_groups,), jnp.int32),
            pltpu.SemaphoreType.DMA((DGRP,)),
            pltpu.SemaphoreType.DMA((2 * PLANE * PCAP,)),
            pltpu.SemaphoreType.DMA((4,)),
        ],
        compiler_params=small,
        name="pack",
    )(
        in_hbm(prefix_table),
        in_hbm(prefix_count),
        in_hbm(groups),
        in_hbm(decode_q),
        in_hbm(pool_kv.reshape((-1, PGRP // PLANE, PLANE) + pool_kv.shape[2:])),
    )
    sending = sending.reshape(devices, message_rows, LANES)

    received = lax.all_to_all(sending, "pool", split_axis=0, concat_axis=0, tiled=True)

    shares = [shares[0]] + [
        lax.ppermute(shares[t], "pool", [(i, i ^ t) for i in range(devices)])
        for t in range(1, PLANE)
    ]
    chunk = min(cap, 4)
    width = 8
    early = width + width // 2
    block_count = devices * cap // chunk
    slot_len, listed, prefix_held, places, ahead = pl.pallas_call(
        functools.partial(plan_kernel, cap, chunk, devices),
        out_shape=(
            jax.ShapeDtypeStruct((devices * cap,), jnp.int32),
            jax.ShapeDtypeStruct((block_count + 2,), jnp.int32),
            jax.ShapeDtypeStruct((devices * pool_kv.shape[0],), jnp.int32),
            jax.ShapeDtypeStruct((2 * row_count,), jnp.int32),
            jax.ShapeDtypeStruct((early * chunk,) + decode_cache.shape[2:], jnp.bfloat16),
        ),
        in_specs=[smem_spec()] * 4 + [any_spec()],
        out_specs=(smem_spec(),) * 4 + (vmem_spec(),),
        scratch_shapes=[
            pltpu.SMEM((decode_groups,), jnp.int32),
            pltpu.SMEM((cap + 1,), jnp.int32),
            pltpu.SemaphoreType.DMA((early,)),
        ],
        compiler_params=small,
        cost_estimate=pl.CostEstimate(flops=1000000, bytes_accessed=4000000, transcendentals=0),
        name="plan",
    )(in_hbm(prefix_table), in_hbm(prefix_count), in_hbm(groups), in_hbm(cached_len), in_hbm(decode_cache[0]))

    *shares, slot_len, listed = lax.optimization_barrier((*shares, slot_len, listed))
    planes = devices // PLANE
    bundle = jax.ShapeDtypeStruct((PLANE, PCAP, blk, 2 * LANES), jnp.bfloat16)
    bundles = pl.pallas_call(
        functools.partial(regroup_kernel, planes),
        out_shape=(bundle,) * planes,
        in_specs=[any_spec()] * PLANE,
        out_specs=(any_spec(),) * planes,
        scratch_shapes=[pltpu.SemaphoreType.DMA((planes * PLANE,))],
        compiler_params=small,
        cost_estimate=pl.CostEstimate(flops=100000, bytes_accessed=1000000, transcendentals=0),
        name="regroup",
    )(*shares)

    def along_line(step):
        pairs = [
            (i, partner(i // PLANE, step, planes) * PLANE + i % PLANE) for i in range(devices)
        ]
        return lax.ppermute(bundles[step], "pool", pairs)


    far_first = {step: along_line(step) for step in reversed(range(1, planes))}
    lines = [bundles[0]] + [far_first[step] for step in range(1, planes)]

    answers = pl.pallas_call(
        functools.partial(decode_kernel, cap, head_rows, chunk, width),
        out_shape=pltpu.HBM((devices, cap * head_rows + head_rows // 2, LANES), jnp.bfloat16),
        in_specs=[smem_spec(), smem_spec(), vmem_spec(), vmem_spec(), any_spec()],
        out_specs=vmem_spec(),
        scratch_shapes=[
            pltpu.VMEM(((block_count - early) * chunk,) + decode_cache.shape[2:], jnp.bfloat16),
            pltpu.SemaphoreType.DMA((block_count - early,)),
        ],
        compiler_params=pltpu.CompilerParams(vmem_limit_bytes=20 * 2**20),
        cost_estimate=pl.CostEstimate(
            flops=500000000, bytes_accessed=8000000, transcendentals=1000000
        ),
        name="decode",
    )(listed, slot_len, received, ahead, in_hbm(decode_cache[0]))

    back = lax.all_to_all(answers, "pool", split_axis=0, concat_axis=0, tiled=True)

    token_count, fill_width = prefill_q.shape[1:]
    prefix = devices * PCAP * blk
    head_count = fill_width // LANES
    prefix_held, decode_q, decode_new, _ = lax.optimization_barrier(
        (prefix_held, decode_q, decode_new, answers)
    )
    expanded = jax.ShapeDtypeStruct((row_count * q_width // LANES, LANES), jnp.float32)
    own_score, own_value = pl.pallas_call(
        own_kernel,
        out_shape=(expanded, expanded),
        in_specs=[vmem_spec(), vmem_spec()],
        out_specs=(vmem_spec(), vmem_spec()),
        compiler_params=small,
        cost_estimate=pl.CostEstimate(flops=1000000, bytes_accessed=2000000, transcendentals=0),
        name="own",
    )(in_hbm(decode_q), in_hbm(decode_new))
    prefill_out = pl.pallas_call(
        functools.partial(prefill_kernel, planes, min(256, token_count)),
        grid=(head_count,),
        out_shape=jax.ShapeDtypeStruct((token_count, fill_width), jnp.bfloat16),
        in_specs=[smem_spec()]
        + [pl.BlockSpec(bundle.shape, lambda u: (0, 0, 0, 0))] * planes
        + [
            pl.BlockSpec((token_count, LANES), lambda u: (0, u)),
            pl.BlockSpec(prefill_new_kv.shape[1:], lambda u: (0, 0)),
        ],
        out_specs=pl.BlockSpec((token_count, LANES), lambda u: (0, u)),
        scratch_shapes=[
            pltpu.VMEM((prefix + token_count, LANES), jnp.bfloat16),
            pltpu.VMEM((prefix + token_count, LANES), jnp.bfloat16),
            pltpu.VMEM((8, prefix), jnp.float32),
        ],
        compiler_params=pltpu.CompilerParams(vmem_limit_bytes=16 * 2**20),
        cost_estimate=pl.CostEstimate(
            flops=32 * token_count * fill_width * (prefix + token_count),
            bytes_accessed=3000000,
            transcendentals=token_count * head_count * (prefix + token_count // 2),
        ),
        name="prefill",
    )(prefix_held, *lines, in_hbm(prefill_q[0]), in_hbm(prefill_new_kv[0]))

    decode_out = pl.pallas_call(
        functools.partial(unpack_kernel, cap, head_rows),
        out_shape=jax.ShapeDtypeStruct((row_count, q_width), jnp.bfloat16),
        in_specs=[smem_spec()] + [vmem_spec()] * 3,
        out_specs=any_spec(),
        scratch_shapes=[
            pltpu.VMEM(expanded.shape, jnp.float32),
            pltpu.VMEM((row_count, q_width), jnp.bfloat16),
            pltpu.SemaphoreType.DMA((DGRP,)),
        ],
        compiler_params=small,
        name="unpack",
    )(places, back, own_score, own_value)
    return (prefill_out[None], decode_out)


def solution(mesh):
    in_specs = (
        P(("rep", "pool"), None, None, None),
        P("rep", None),
        P("rep"),
        P(("rep", "pool"), None, None),
        P(("rep", "pool"), None, None),
        P(("rep", "pool"), None),
        P(("rep", "pool"), None),
        P(("rep", "pool"), None, None, None, None),
        P("rep", None),
        P("rep"),
    )
    out_specs = (P(("rep", "pool"), None, None), P(("rep", "pool"), None))
    return jax.shard_map(shards, mesh=mesh, in_specs=in_specs, out_specs=out_specs, check_vma=False)
```

```python
import functools

import jax
import jax.numpy as jnp
from jax import lax
from jax.experimental import pallas as pl
from jax.experimental.pallas import tpu as pltpu
from jax.sharding import PartitionSpec as P

PGRP = 8
DGRP = 4
PCAP = 2
PLANE = 4
LANES = 128
MASKED = -1e30
LOG2E = 1.4426950408889634


def any_spec():
    return pl.BlockSpec(memory_space=pl.ANY)


def smem_spec():
    return pl.BlockSpec(memory_space=pltpu.SMEM)


def in_hbm(x):
    return pltpu.with_memory_space_constraint(x, pltpu.HBM)


def vmem_spec():
    return pl.BlockSpec(memory_space=pltpu.VMEM)


def pack_kernel(head_rows, *rest):
    far, (pool, out), shares, near = rest[:4], rest[4:6], rest[6 : 6 + PLANE], rest[6 + PLANE :]
    table, count, groups, q, rows_scr, stage, group_fill, sems, block_sems, near_sems = near
    fetches = [
        pltpu.make_async_copy(there, here, near_sems.at[n])
        for n, (there, here) in enumerate(zip(far, (table, count, groups, q)))
    ]
    for fetch in fetches:
        fetch.start()
    for fetch in fetches[:3]:
        fetch.wait()
    flying = send_blocks(table, count, pool, shares, block_sems)
    decode_groups = out.shape[0]
    row_count = q.shape[0]
    head_total = q.shape[1] // LANES
    device = lax.axis_index("pool")
    for a in range(decode_groups):
        group_fill[a] = 0
    homes = []
    for i in range(row_count):
        a = groups[device * row_count + i]
        c = group_fill[a]
        group_fill[a] = c + 1
        homes.append((a, c))
    fetches[3].wait()
    copies = []
    for m in range(DGRP):
        for h in range(m * head_rows, (m + 1) * head_rows):
            rows_scr[pl.ds(h, row_count, stride=head_total), :] = q[
                :, h * LANES : (h + 1) * LANES
            ].astype(jnp.float32)
        for i, (a, c) in enumerate(homes):
            first = i * head_total + m * head_rows
            stage[m, a, pl.ds(pl.multiple_of(c * head_rows, 16), head_rows), :] = rows_scr[
                first : first + head_rows, :
            ].astype(out.dtype)
        copy = pltpu.make_async_copy(stage.at[m], out.at[:, m], sems.at[m])
        copy.start()
        copies.append(copy)
    for copy in copies + flying:
        copy.wait()


def send_blocks(table, count, pool, outs, sems):
    blocks_here = pool.shape[0]
    group_count, most_blocks = table.shape
    device = lax.axis_index("pool")
    first_block = device * blocks_here
    flying = []
    for g in range(group_count):

        def scan_table(j, carry):
            seen, chosen = carry
            entry = table[g, j]
            mine = (entry >= first_block) & (entry < first_block + blocks_here) & (j < count[g])
            chosen = tuple(
                jnp.where(mine & (seen == k), entry - first_block, chosen[k]) for k in range(PCAP)
            )
            return seen + mine.astype(jnp.int32), chosen

        start = (jnp.int32(0), tuple(jnp.int32(0) for _ in range(PCAP)))
        _, chosen = lax.fori_loop(0, most_blocks, scan_table, start, unroll=8)
        if g >= 2:
            for copy in flying.pop(0):
                copy.wait()
        copies = []
        for t in range(PLANE):
            for k in range(PCAP):
                copy = pltpu.make_async_copy(
                    pool.at[chosen[k], :, (device % PLANE) ^ t],
                    outs[t].at[:, g, k],
                    sems.at[((g % 2) * PLANE + t) * PCAP + k],
                )
                copy.start()
                copies.append(copy)
        flying.append(copies)
    return [copy for copies in flying for copy in copies]


def partner(plane, step, planes):
    return plane ^ step if planes & (planes - 1) == 0 else (plane + step) % planes


def regroup_kernel(planes, *rest):
    held, outs, sems = rest[:PLANE], rest[PLANE:-1], rest[-1]
    mine = lax.axis_index("pool") // PLANE
    per_group = PGRP // PLANE
    copies = []
    for step in range(planes):
        there = partner(mine, step, planes)
        for t in range(PLANE):
            copy = pltpu.make_async_copy(
                held[t].at[there % per_group, there // per_group],
                outs[step].at[t],
                sems.at[step * PLANE + t],
            )
            copy.start()
            copies.append(copy)
    for copy in copies:
        copy.wait()


def fetch_block(cache, listed, i, chunk, held, place, sem):
    return pltpu.make_async_copy(
        cache.at[pl.ds(listed[1 + i] * chunk, chunk)], held.at[pl.ds(place * chunk, chunk)], sem
    )


def plan_kernel(
    cap,
    step,
    owners,
    table,
    count,
    groups,
    lengths,
    cache,
    slot_len,
    listed,
    prefix_held,
    places,
    ahead,
    group_fill,
    found,
    sems,
):
    device = lax.axis_index("pool")
    home_count = owners
    row_count = groups.shape[0] // home_count
    group_id = device // DGRP
    prefill_id = device // PGRP
    blocks_here = listed.shape[0]
    most_blocks = table.shape[1]
    chunk = min(cap, step)

    def one_home(s, filled):
        here = jnp.int32(0)
        for i in range(row_count):
            row = s * row_count + i
            found[here] = lengths[row]
            here = here + (groups[row] == group_id).astype(jnp.int32)
        for c in range(cap):
            slot_len[s * cap + c] = jnp.where(c < here, found[c], 0)
        for b in range(cap // chunk):
            listed[1 + jnp.minimum(filled, blocks_here - 2)] = s * (cap // chunk) + b
            filled = filled + (here > b * chunk).astype(jnp.int32)
        return filled

    live = lax.fori_loop(0, home_count, one_home, jnp.int32(0))
    listed[0] = live
    for i in range(ahead.shape[0] // chunk):
        pl.when(i < live)(fetch_block(cache, listed, i, chunk, ahead, i, sems.at[i]).start)

    for a in range(owners // DGRP):
        group_fill[a] = 0
    for i in range(row_count):
        a = groups[device * row_count + i]
        c = group_fill[a]
        places[2 * i] = a
        places[2 * i + 1] = c
        group_fill[a] = c + 1

    def one_owner(o, carry):
        prefix_held[o] = 0
        return carry

    lax.fori_loop(0, owners, one_owner, 0, unroll=8)
    pool_blocks = prefix_held.shape[0] // owners

    def one_entry(j, carry):
        o = lax.div(table[prefill_id, j], pool_blocks)
        prefix_held[o] = prefix_held[o] + 1
        return carry

    lax.fori_loop(0, jnp.minimum(count[prefill_id], most_blocks), one_entry, 0)
    for i in range(ahead.shape[0] // chunk):
        pl.when(i < live)(fetch_block(cache, listed, i, chunk, ahead, i, sems.at[i]).wait)


def decode_kernel(
    cap, head_rows, chunk, width, listed, slot_len, recv, ahead, cache, out, held, sems
):
    pair_count, positions = cache.shape[1], cache.shape[2]
    per_home = cap // chunk
    key_count = pair_count * positions
    query_heads = head_rows // pair_count
    live = listed[0]
    scale = LANES ** (-0.5) * LOG2E
    rows = chunk * head_rows
    later_width = width + width // 2
    pair = 2 if chunk % 2 == 0 else 1

    def fetch(i):
        return fetch_block(cache, listed, i, chunk, held, i - width, sems.at[i - width])

    def begin(i, carry):
        fetch(i).start()
        return carry

    lax.fori_loop(width, live, begin, 0)
    row_pair = lax.broadcasted_iota(jnp.int32, (head_rows, key_count), 0) // query_heads
    key_axis = lax.broadcasted_iota(jnp.int32, (head_rows, key_count), 1)
    pos = jnp.where(key_axis // positions == row_pair, key_axis % positions, positions)
    half = head_rows // 2
    lane = lax.broadcasted_iota(jnp.int32, (half, LANES), 1)
    part, stat_slot = lane % (LANES // 2) % 3, lane % (LANES // 2) // 3

    def several(base, width, kv):
        slots = width * chunk
        ids = [jnp.minimum(base + w, live - 1) for w in range(width)]
        blocks = [listed[1 + i] for i in ids]
        homes = [b // per_home for b in blocks]
        firsts = [(b % per_home) * chunk for b in blocks]
        places = [pl.multiple_of(f * head_rows, 16) for f in firsts]
        q = jnp.concatenate(
            [recv[h, pl.ds(p, rows), :] for h, p in zip(homes, places)], axis=0
        )
        keys = kv[..., :LANES].reshape(slots, key_count, LANES)
        values = kv[..., LANES:].reshape(slots, key_count, LANES)
        scores = jnp.einsum(
            "jqd,jkd->jqk",
            q.reshape(slots // pair, pair * head_rows, LANES),
            keys.reshape(slots // pair, pair * key_count, LANES),
            preferred_element_type=jnp.float32,
        )
        if pair == 2:
            scores = jnp.stack(
                [scores[:, :head_rows, :key_count], scores[:, head_rows:, key_count:]], axis=1
            ).reshape(slots, head_rows, key_count)
        kept = jnp.stack(
            [pos < slot_len[blocks[w] * chunk + j] for w in range(width) for j in range(chunk)]
        )
        scores = jnp.where(kept, scores, MASKED)
        top = jnp.max(scores, axis=2, keepdims=True)
        weights = jnp.exp2((scores - top) * scale)
        total = jnp.sum(weights, axis=2, keepdims=True)
        weights = weights.astype(jnp.bfloat16)
        if pair == 2:
            weights = weights.reshape(slots // 2, 2, head_rows, key_count)
            nothing = jnp.zeros((slots // 2, head_rows, key_count), jnp.bfloat16)
            upper = jnp.concatenate([weights[:, 0], nothing], axis=2)
            lower = jnp.concatenate([nothing, weights[:, 1]], axis=2)
            weights = jnp.concatenate([upper, lower], axis=1)
        mixed = jnp.einsum(
            "jqk,jkd->jqd",
            weights,
            values.reshape(slots // pair, pair * key_count, LANES),
            preferred_element_type=jnp.float32,
        )
        mixed = mixed.reshape(slots, head_rows, LANES) / total
        mass = top * scale + jnp.log(total) * LOG2E
        high = mass.astype(jnp.bfloat16).astype(jnp.float32)
        middle = (mass - high).astype(jnp.bfloat16).astype(jnp.float32)
        low = mass - high - middle
        mixed = mixed.reshape(width, rows, LANES)
        for w in reversed(range(width)):
            out[homes[w], pl.ds(places[w], rows), :] = mixed[w].astype(out.dtype)
            masses = out[homes[w], cap * head_rows :, :].astype(jnp.float32)
            for j in range(chunk):
                at = w * chunk + j
                split = [
                    jnp.where(lane < LANES // 2, piece[at, :half], piece[at, half:])
                    for piece in (high, middle, low)
                ]
                split = jnp.where(part == 0, split[0], jnp.where(part == 1, split[1], split[2]))
                masses = jnp.where(stat_slot == firsts[w] + j, split, masses)
            out[homes[w], cap * head_rows :, :] = masses.astype(out.dtype)

    several(0, width, ahead[...])

    def later(t, carry):
        base = width + t * later_width
        for w in range(later_width):
            pl.when(base + w < live)(fetch(base + w).wait)
        place = t * later_width * chunk
        several(base, later_width, held[pl.ds(place, later_width * chunk)])
        return carry

    lax.fori_loop(0, (live - width + later_width - 1) // later_width, later, 0)


def prefill_kernel(planes, tile, prefix_held, *rest):
    sources = rest[:planes]
    q, new_kv, out, keys, values, bias = rest[planes:]
    blk = sources[0].shape[2]
    prefix = planes * PLANE * PCAP * blk
    token_count = new_kv.shape[0]
    scale = LANES ** (-0.5) * LOG2E
    device = lax.axis_index("pool")

    @pl.when(pl.program_id(0) == 0)
    def _():
        lane_block = lax.broadcasted_iota(jnp.int32, (8, prefix), 1) // blk
        hide = jnp.zeros((8, prefix), jnp.float32)
        for step in range(planes):
            sender = device // PLANE
            sender = sender ^ step if planes & (planes - 1) == 0 else (sender + planes - step) % planes
            for t in range(PLANE):
                owner = sender * PLANE + ((device % PLANE) ^ t)
                for k in range(PCAP):
                    ordinal = (step * PLANE + t) * PCAP + k
                    block = sources[step][t, k]
                    keys[ordinal * blk : (ordinal + 1) * blk, :] = block[:, :LANES]
                    values[ordinal * blk : (ordinal + 1) * blk, :] = block[:, LANES:]
                    gone = jnp.where(prefix_held[owner] > k, 0.0, MASKED)
                    hide = jnp.where(lane_block == ordinal, gone, hide)
        bias[...] = hide
        keys[prefix:, :] = new_kv[:, :LANES]
        values[prefix:, :] = new_kv[:, LANES:]

    for t in range(token_count // tile):
        width = prefix + (t + 1) * tile
        block = q[t * tile : (t + 1) * tile, :]
        scores = lax.dot_general(
            block, keys[:width, :], (((1,), (1,)), ((), ())), preferred_element_type=jnp.float32
        )
        causal = lax.broadcasted_iota(jnp.int32, (tile, tile), 0) >= lax.broadcasted_iota(
            jnp.int32, (tile, tile), 1
        )
        pieces = [scores[:, :prefix] + bias[0:1, :]]
        if t:
            pieces.append(scores[:, prefix : width - tile])
        pieces.append(jnp.where(causal, scores[:, width - tile :], MASKED))
        scores = jnp.concatenate(pieces, axis=1)
        top = jnp.max(scores, axis=1, keepdims=True)
        weights = jnp.exp2((scores - top) * scale)
        total = jnp.sum(weights, axis=1, keepdims=True)
        mixed = jnp.dot(
            weights.astype(jnp.bfloat16), values[:width, :], preferred_element_type=jnp.float32
        )
        out[t * tile : (t + 1) * tile, :] = (mixed / total).astype(out.dtype)


def own_kernel(q, kv, score, value):
    row_count = q.shape[0]
    head_total = q.shape[1] // LANES
    pair_count = kv.shape[1] // (2 * LANES)
    per_pair = head_total // pair_count
    for k in range(pair_count):
        lane = k * 2 * LANES
        key = kv[:, lane : lane + LANES].astype(jnp.float32) * (LANES ** (-0.5) * LOG2E)
        held = kv[:, lane + LANES : lane + 2 * LANES].astype(jnp.float32)
        for h in range(k * per_pair, (k + 1) * per_pair):
            at = pl.ds(h, row_count, stride=head_total)
            query = q[:, h * LANES : (h + 1) * LANES].astype(jnp.float32)
            product = jnp.sum(query * key, axis=1, keepdims=True)
            score[at, :] = jnp.broadcast_to(product, (row_count, LANES))
            value[at, :] = held


def unpack_kernel(cap, head_rows, places, back, score, value, out, rows_scr, stage, sems):
    row_count = out.shape[0]
    head_total = out.shape[1] // LANES
    lane = lax.broadcasted_iota(jnp.int32, (head_rows // 2, LANES), 1)
    stat_slot = lane % (LANES // 2) // 3
    copies = []
    for m in range(DGRP):
        for i in range(row_count):
            a, c = places[2 * i], places[2 * i + 1]
            at = slice(i * head_total + m * head_rows, i * head_total + (m + 1) * head_rows)
            cached = back[
                a * DGRP + m, pl.ds(pl.multiple_of(c * head_rows, 16), head_rows), :
            ].astype(jnp.float32)
            masses = back[a * DGRP + m, cap * head_rows :, :].astype(jnp.float32)
            masses = jnp.where(stat_slot == c, masses, 0.0)
            mass = jnp.concatenate(
                [
                    jnp.sum(jnp.where(lane < LANES // 2, masses, 0.0), axis=1, keepdims=True),
                    jnp.sum(jnp.where(lane < LANES // 2, 0.0, masses), axis=1, keepdims=True),
                ],
                axis=0,
            )
            share = 1.0 / (1.0 + jnp.exp2(mass - score[at, :]))
            rows_scr[at, :] = cached + share * (value[at, :] - cached)
        for h in range(m * head_rows, (m + 1) * head_rows):
            stage[:, h * LANES : (h + 1) * LANES] = rows_scr[
                pl.ds(h, row_count, stride=head_total), :
            ].astype(out.dtype)
        lanes = pl.ds(m * head_rows * LANES, head_rows * LANES)
        copy = pltpu.make_async_copy(stage.at[:, lanes], out.at[:, lanes], sems.at[m])
        copy.start()
        copies.append(copy)
    for copy in copies:
        copy.wait()


def shards(
    pool_kv,
    prefix_table,
    prefix_count,
    prefill_q,
    prefill_new_kv,
    decode_q,
    decode_new,
    decode_cache,
    decode_group,
    cached_len,
):
    devices = lax.axis_size("pool")
    blk = pool_kv.shape[2]
    row_count, q_width = decode_q.shape
    cap = decode_cache.shape[1] // devices
    decode_groups = devices // DGRP
    pair_count = decode_cache.shape[2]
    head_rows = q_width // LANES // DGRP
    message_rows = cap * head_rows
    groups = decode_group.reshape(-1)
    prefill_groups = prefix_table.shape[0]
    small = pltpu.CompilerParams(vmem_limit_bytes=8 * 2**20)

    share = jax.ShapeDtypeStruct(
        (PGRP // PLANE, prefill_groups, PCAP, blk, 2 * LANES), jnp.bfloat16
    )
    sending, *shares = pl.pallas_call(
        functools.partial(pack_kernel, head_rows),
        out_shape=(
            jax.ShapeDtypeStruct((decode_groups, DGRP, message_rows, LANES), jnp.bfloat16),
        )
        + (share,) * PLANE,
        in_specs=[any_spec()] * 5,
        out_specs=(any_spec(),) * (1 + PLANE),
        scratch_shapes=[
            pltpu.SMEM(prefix_table.shape, jnp.int32),
            pltpu.SMEM(prefix_count.shape, jnp.int32),
            pltpu.SMEM(groups.shape, jnp.int32),
            pltpu.VMEM((row_count, q_width), jnp.bfloat16),
            pltpu.VMEM((row_count * q_width // LANES, LANES), jnp.float32),
            pltpu.VMEM((DGRP, decode_groups, message_rows, LANES), jnp.bfloat16),
            pltpu.SMEM((decode_groups,), jnp.int32),
            pltpu.SemaphoreType.DMA((DGRP,)),
            pltpu.SemaphoreType.DMA((2 * PLANE * PCAP,)),
            pltpu.SemaphoreType.DMA((4,)),
        ],
        compiler_params=small,
        name="pack",
    )(
        in_hbm(prefix_table),
        in_hbm(prefix_count),
        in_hbm(groups),
        in_hbm(decode_q),
        in_hbm(pool_kv.reshape((-1, PGRP // PLANE, PLANE) + pool_kv.shape[2:])),
    )
    sending = sending.reshape(devices, message_rows, LANES)

    received = lax.all_to_all(sending, "pool", split_axis=0, concat_axis=0, tiled=True)

    shares = [shares[0]] + [
        lax.ppermute(shares[t], "pool", [(i, i ^ t) for i in range(devices)])
        for t in range(1, PLANE)
    ]
    chunk = min(cap, 4)
    width = 8
    block_count = devices * cap // chunk
    later_width = width + width // 2
    later_blocks = -(-(block_count - width) // later_width) * later_width
    slot_len, listed, prefix_held, places, ahead = pl.pallas_call(
        functools.partial(plan_kernel, cap, chunk, devices),
        out_shape=(
            jax.ShapeDtypeStruct((devices * cap,), jnp.int32),
            jax.ShapeDtypeStruct((width + later_blocks + 2,), jnp.int32),
            jax.ShapeDtypeStruct((devices * pool_kv.shape[0],), jnp.int32),
            jax.ShapeDtypeStruct((2 * row_count,), jnp.int32),
            jax.ShapeDtypeStruct((width * chunk,) + decode_cache.shape[2:], jnp.bfloat16),
        ),
        in_specs=[smem_spec()] * 4 + [any_spec()],
        out_specs=(smem_spec(),) * 4 + (vmem_spec(),),
        scratch_shapes=[
            pltpu.SMEM((decode_groups,), jnp.int32),
            pltpu.SMEM((cap + 1,), jnp.int32),
            pltpu.SemaphoreType.DMA((width,)),
        ],
        compiler_params=small,
        cost_estimate=pl.CostEstimate(flops=1000000, bytes_accessed=4000000, transcendentals=0),
        name="plan",
    )(in_hbm(prefix_table), in_hbm(prefix_count), in_hbm(groups), in_hbm(cached_len), in_hbm(decode_cache[0]))

    *shares, slot_len, listed = lax.optimization_barrier((*shares, slot_len, listed))
    planes = devices // PLANE
    bundle = jax.ShapeDtypeStruct((PLANE, PCAP, blk, 2 * LANES), jnp.bfloat16)
    bundles = pl.pallas_call(
        functools.partial(regroup_kernel, planes),
        out_shape=(bundle,) * planes,
        in_specs=[any_spec()] * PLANE,
        out_specs=(any_spec(),) * planes,
        scratch_shapes=[pltpu.SemaphoreType.DMA((planes * PLANE,))],
        compiler_params=small,
        cost_estimate=pl.CostEstimate(flops=100000, bytes_accessed=1000000, transcendentals=0),
        name="regroup",
    )(*shares)

    def along_line(step):
        pairs = [
            (i, partner(i // PLANE, step, planes) * PLANE + i % PLANE) for i in range(devices)
        ]
        return lax.ppermute(bundles[step], "pool", pairs)


    far_first = {step: along_line(step) for step in reversed(range(1, planes))}
    lines = [bundles[0]] + [far_first[step] for step in range(1, planes)]

    answers = pl.pallas_call(
        functools.partial(decode_kernel, cap, head_rows, chunk, width),
        out_shape=jax.ShapeDtypeStruct(
            (devices, cap * head_rows + head_rows // 2, LANES), jnp.bfloat16
        ),
        in_specs=[smem_spec(), smem_spec(), vmem_spec(), vmem_spec(), any_spec()],
        out_specs=vmem_spec(),
        scratch_shapes=[
            pltpu.VMEM((later_blocks * chunk,) + decode_cache.shape[2:], jnp.bfloat16),
            pltpu.SemaphoreType.DMA((later_blocks,)),
        ],
        compiler_params=pltpu.CompilerParams(vmem_limit_bytes=20 * 2**20),
        cost_estimate=pl.CostEstimate(
            flops=500000000, bytes_accessed=8000000, transcendentals=1000000
        ),
        name="decode",
    )(listed, slot_len, received, ahead, in_hbm(decode_cache[0]))

    back = lax.all_to_all(answers, "pool", split_axis=0, concat_axis=0, tiled=True)

    token_count, fill_width = prefill_q.shape[1:]
    prefix = devices * PCAP * blk
    head_count = fill_width // LANES
    prefix_held, decode_q, decode_new, _ = lax.optimization_barrier(
        (prefix_held, decode_q, decode_new, answers)
    )
    expanded = jax.ShapeDtypeStruct((row_count * q_width // LANES, LANES), jnp.float32)
    own_score, own_value = pl.pallas_call(
        own_kernel,
        out_shape=(expanded, expanded),
        in_specs=[vmem_spec(), vmem_spec()],
        out_specs=(vmem_spec(), vmem_spec()),
        compiler_params=small,
        cost_estimate=pl.CostEstimate(flops=1000000, bytes_accessed=2000000, transcendentals=0),
        name="own",
    )(in_hbm(decode_q), in_hbm(decode_new))
    prefill_out = pl.pallas_call(
        functools.partial(prefill_kernel, planes, min(256, token_count)),
        grid=(head_count,),
        out_shape=jax.ShapeDtypeStruct((token_count, fill_width), jnp.bfloat16),
        in_specs=[smem_spec()]
        + [pl.BlockSpec(bundle.shape, lambda u: (0, 0, 0, 0))] * planes
        + [
            pl.BlockSpec((token_count, LANES), lambda u: (0, u)),
            pl.BlockSpec(prefill_new_kv.shape[1:], lambda u: (0, 0)),
        ],
        out_specs=pl.BlockSpec((token_count, LANES), lambda u: (0, u)),
        scratch_shapes=[
            pltpu.VMEM((prefix + token_count, LANES), jnp.bfloat16),
            pltpu.VMEM((prefix + token_count, LANES), jnp.bfloat16),
            pltpu.VMEM((8, prefix), jnp.float32),
        ],
        compiler_params=pltpu.CompilerParams(vmem_limit_bytes=16 * 2**20),
        cost_estimate=pl.CostEstimate(
            flops=32 * token_count * fill_width * (prefix + token_count),
            bytes_accessed=3000000,
            transcendentals=token_count * head_count * (prefix + token_count // 2),
        ),
        name="prefill",
    )(prefix_held, *lines, in_hbm(prefill_q[0]), in_hbm(prefill_new_kv[0]))

    decode_out = pl.pallas_call(
        functools.partial(unpack_kernel, cap, head_rows),
        out_shape=jax.ShapeDtypeStruct((row_count, q_width), jnp.bfloat16),
        in_specs=[smem_spec()] + [vmem_spec()] * 3,
        out_specs=any_spec(),
        scratch_shapes=[
            pltpu.VMEM(expanded.shape, jnp.float32),
            pltpu.VMEM((row_count, q_width), jnp.bfloat16),
            pltpu.SemaphoreType.DMA((DGRP,)),
        ],
        compiler_params=small,
        name="unpack",
    )(places, back, own_score, own_value)
    return (prefill_out[None], decode_out)


def solution(mesh):
    in_specs = (
        P(("rep", "pool"), None, None, None),
        P("rep", None),
        P("rep"),
        P(("rep", "pool"), None, None),
        P(("rep", "pool"), None, None),
        P(("rep", "pool"), None),
        P(("rep", "pool"), None),
        P(("rep", "pool"), None, None, None, None),
        P("rep", None),
        P("rep"),
    )
    out_specs = (P(("rep", "pool"), None, None), P(("rep", "pool"), None))
    return jax.shard_map(shards, mesh=mesh, in_specs=in_specs, out_specs=out_specs, check_vma=False)
```

```python
import functools

import jax
import jax.numpy as jnp
from jax import lax
from jax.experimental import pallas as pl
from jax.experimental.pallas import tpu as pltpu
from jax.sharding import PartitionSpec as P

PGRP = 8
DGRP = 4
PCAP = 2
PLANE = 4
LANES = 128
MASKED = -1e30
LOG2E = 1.4426950408889634


def any_spec():
    return pl.BlockSpec(memory_space=pl.ANY)


def smem_spec():
    return pl.BlockSpec(memory_space=pltpu.SMEM)


def in_hbm(x):
    return pltpu.with_memory_space_constraint(x, pltpu.HBM)


def vmem_spec():
    return pl.BlockSpec(memory_space=pltpu.VMEM)


def pack_kernel(head_rows, *rest):
    far, (pool, out), shares, near = rest[:4], rest[4:6], rest[6 : 6 + PLANE], rest[6 + PLANE :]
    table, count, groups, q, rows_scr, stage, group_fill, sems, block_sems, near_sems = near
    fetches = [
        pltpu.make_async_copy(there, here, near_sems.at[n])
        for n, (there, here) in enumerate(zip(far, (table, count, groups, q)))
    ]
    for fetch in fetches:
        fetch.start()
    for fetch in fetches[:3]:
        fetch.wait()
    flying = send_blocks(table, count, pool, shares, block_sems)
    decode_groups = out.shape[0]
    row_count = q.shape[0]
    head_total = q.shape[1] // LANES
    device = lax.axis_index("pool")
    for a in range(decode_groups):
        group_fill[a] = 0
    homes = []
    for i in range(row_count):
        a = groups[device * row_count + i]
        c = group_fill[a]
        group_fill[a] = c + 1
        homes.append((a, c))
    fetches[3].wait()
    copies = []
    for m in range(DGRP):
        for h in range(m * head_rows, (m + 1) * head_rows):
            rows_scr[pl.ds(h, row_count, stride=head_total), :] = q[
                :, h * LANES : (h + 1) * LANES
            ].astype(jnp.float32)
        for i, (a, c) in enumerate(homes):
            first = i * head_total + m * head_rows
            stage[m, a, pl.ds(pl.multiple_of(c * head_rows, 16), head_rows), :] = rows_scr[
                first : first + head_rows, :
            ].astype(out.dtype)
        copy = pltpu.make_async_copy(stage.at[m], out.at[:, m], sems.at[m])
        copy.start()
        copies.append(copy)
    for copy in copies + flying:
        copy.wait()


def send_blocks(table, count, pool, outs, sems):
    blocks_here = pool.shape[0]
    group_count, most_blocks = table.shape
    device = lax.axis_index("pool")
    first_block = device * blocks_here
    flying = []
    for g in range(group_count):

        def scan_table(j, carry):
            seen, chosen = carry
            entry = table[g, j]
            mine = (entry >= first_block) & (entry < first_block + blocks_here) & (j < count[g])
            chosen = tuple(
                jnp.where(mine & (seen == k), entry - first_block, chosen[k]) for k in range(PCAP)
            )
            return seen + mine.astype(jnp.int32), chosen

        start = (jnp.int32(0), tuple(jnp.int32(0) for _ in range(PCAP)))
        _, chosen = lax.fori_loop(0, most_blocks, scan_table, start, unroll=8)
        if g >= 2:
            for copy in flying.pop(0):
                copy.wait()
        copies = []
        for t in range(PLANE):
            for k in range(PCAP):
                copy = pltpu.make_async_copy(
                    pool.at[chosen[k], :, (device % PLANE) ^ t],
                    outs[t].at[:, g, k],
                    sems.at[((g % 2) * PLANE + t) * PCAP + k],
                )
                copy.start()
                copies.append(copy)
        flying.append(copies)
    return [copy for copies in flying for copy in copies]


def partner(plane, step, planes):
    return plane ^ step if planes & (planes - 1) == 0 else (plane + step) % planes


def regroup_kernel(planes, *rest):
    held, outs, sems = rest[:PLANE], rest[PLANE:-1], rest[-1]
    mine = lax.axis_index("pool") // PLANE
    per_group = PGRP // PLANE
    copies = []
    for step in range(planes):
        there = partner(mine, step, planes)
        for t in range(PLANE):
            copy = pltpu.make_async_copy(
                held[t].at[there % per_group, there // per_group],
                outs[step].at[t],
                sems.at[step * PLANE + t],
            )
            copy.start()
            copies.append(copy)
    for copy in copies:
        copy.wait()


def fetch_block(cache, listed, i, chunk, held, place, sem):
    return pltpu.make_async_copy(
        cache.at[pl.ds(listed[1 + i] * chunk, chunk)], held.at[pl.ds(place * chunk, chunk)], sem
    )


def plan_kernel(
    cap,
    step,
    owners,
    table,
    count,
    groups,
    lengths,
    cache,
    slot_len,
    listed,
    prefix_held,
    places,
    ahead,
    group_fill,
    found,
    sems,
):
    device = lax.axis_index("pool")
    home_count = owners
    row_count = groups.shape[0] // home_count
    group_id = device // DGRP
    prefill_id = device // PGRP
    blocks_here = listed.shape[0]
    most_blocks = table.shape[1]
    chunk = min(cap, step)

    def one_home(s, filled):
        here = jnp.int32(0)
        for i in range(row_count):
            row = s * row_count + i
            found[here] = lengths[row]
            here = here + (groups[row] == group_id).astype(jnp.int32)
        for c in range(cap):
            slot_len[s * cap + c] = jnp.where(c < here, found[c], 0)
        for b in range(cap // chunk):
            listed[1 + jnp.minimum(filled, blocks_here - 2)] = s * (cap // chunk) + b
            filled = filled + (here > b * chunk).astype(jnp.int32)
        return filled

    live = lax.fori_loop(0, home_count, one_home, jnp.int32(0))
    listed[0] = live
    for i in range(ahead.shape[0] // chunk):
        pl.when(i < live)(fetch_block(cache, listed, i, chunk, ahead, i, sems.at[i]).start)

    for a in range(owners // DGRP):
        group_fill[a] = 0
    for i in range(row_count):
        a = groups[device * row_count + i]
        c = group_fill[a]
        places[2 * i] = a
        places[2 * i + 1] = c
        group_fill[a] = c + 1

    def one_owner(o, carry):
        prefix_held[o] = 0
        return carry

    lax.fori_loop(0, owners, one_owner, 0, unroll=8)
    pool_blocks = prefix_held.shape[0] // owners

    def one_entry(j, carry):
        o = lax.div(table[prefill_id, j], pool_blocks)
        prefix_held[o] = prefix_held[o] + 1
        return carry

    lax.fori_loop(0, jnp.minimum(count[prefill_id], most_blocks), one_entry, 0)
    for i in range(ahead.shape[0] // chunk):
        pl.when(i < live)(fetch_block(cache, listed, i, chunk, ahead, i, sems.at[i]).wait)


def decode_kernel(
    cap, head_rows, chunk, width, listed, slot_len, recv, ahead, cache, out, held, sems
):
    pair_count, positions = cache.shape[1], cache.shape[2]
    per_home = cap // chunk
    key_count = pair_count * positions
    query_heads = head_rows // pair_count
    live = listed[0]
    scale = LANES ** (-0.5) * LOG2E
    rows = chunk * head_rows
    slots = width * chunk
    pair = 2 if chunk % 2 == 0 else 1

    def fetch(i):
        return fetch_block(cache, listed, i, chunk, held, i - width, sems.at[i - width])

    def begin(i, carry):
        fetch(i).start()
        return carry

    lax.fori_loop(width, live, begin, 0)
    row_pair = lax.broadcasted_iota(jnp.int32, (head_rows, key_count), 0) // query_heads
    key_axis = lax.broadcasted_iota(jnp.int32, (head_rows, key_count), 1)
    pos = jnp.where(key_axis // positions == row_pair, key_axis % positions, positions)
    half = head_rows // 2
    lane = lax.broadcasted_iota(jnp.int32, (half, LANES), 1)
    part, stat_slot = lane % (LANES // 2) % 3, lane % (LANES // 2) // 3

    def several(t, kv):
        ids = [jnp.minimum(t * width + w, live - 1) for w in range(width)]
        blocks = [listed[1 + i] for i in ids]
        homes = [b // per_home for b in blocks]
        firsts = [(b % per_home) * chunk for b in blocks]
        places = [pl.multiple_of(f * head_rows, 16) for f in firsts]
        q = jnp.concatenate(
            [recv[h, pl.ds(p, rows), :] for h, p in zip(homes, places)], axis=0
        )
        keys = kv[..., :LANES].reshape(slots, key_count, LANES)
        values = kv[..., LANES:].reshape(slots, key_count, LANES)
        scores = jnp.einsum(
            "jqd,jkd->jqk",
            q.reshape(slots // pair, pair * head_rows, LANES),
            keys.reshape(slots // pair, pair * key_count, LANES),
            preferred_element_type=jnp.float32,
        )
        if pair == 2:
            scores = jnp.stack(
                [scores[:, :head_rows, :key_count], scores[:, head_rows:, key_count:]], axis=1
            ).reshape(slots, head_rows, key_count)
        kept = jnp.stack(
            [pos < slot_len[blocks[w] * chunk + j] for w in range(width) for j in range(chunk)]
        )
        scores = jnp.where(kept, scores, MASKED)
        top = jnp.max(scores, axis=2, keepdims=True)
        weights = jnp.exp2((scores - top) * scale)
        total = jnp.sum(weights, axis=2, keepdims=True)
        weights = weights.astype(jnp.bfloat16)
        if pair == 2:
            weights = weights.reshape(slots // 2, 2, head_rows, key_count)
            nothing = jnp.zeros((slots // 2, head_rows, key_count), jnp.bfloat16)
            upper = jnp.concatenate([weights[:, 0], nothing], axis=2)
            lower = jnp.concatenate([nothing, weights[:, 1]], axis=2)
            weights = jnp.concatenate([upper, lower], axis=1)
        mixed = jnp.einsum(
            "jqk,jkd->jqd",
            weights,
            values.reshape(slots // pair, pair * key_count, LANES),
            preferred_element_type=jnp.float32,
        )
        mixed = mixed.reshape(slots, head_rows, LANES) / total
        mass = top * scale + jnp.log(total) * LOG2E
        high = mass.astype(jnp.bfloat16).astype(jnp.float32)
        middle = (mass - high).astype(jnp.bfloat16).astype(jnp.float32)
        low = mass - high - middle
        mixed = mixed.reshape(width, rows, LANES)
        for w in reversed(range(width)):
            out[homes[w], pl.ds(places[w], rows), :] = mixed[w].astype(out.dtype)
            masses = out[homes[w], cap * head_rows :, :].astype(jnp.float32)
            for j in range(chunk):
                at = w * chunk + j
                split = [
                    jnp.where(lane < LANES // 2, piece[at, :half], piece[at, half:])
                    for piece in (high, middle, low)
                ]
                split = jnp.where(part == 0, split[0], jnp.where(part == 1, split[1], split[2]))
                masses = jnp.where(stat_slot == firsts[w] + j, split, masses)
            out[homes[w], cap * head_rows :, :] = masses.astype(out.dtype)

    several(0, ahead[...])

    def later(t, carry):
        for w in range(width):
            pl.when(t * width + w < live)(fetch(t * width + w).wait)
        several(t, held[pl.ds((t - 1) * slots, slots)])
        return carry

    lax.fori_loop(1, (live + width - 1) // width, later, 0)


def prefill_kernel(planes, tile, prefix_held, *rest):
    sources = rest[:planes]
    q, new_kv, out, keys, values, bias = rest[planes:]
    blk = sources[0].shape[2]
    prefix = planes * PLANE * PCAP * blk
    token_count = new_kv.shape[0]
    scale = LANES ** (-0.5) * LOG2E
    device = lax.axis_index("pool")

    @pl.when(pl.program_id(0) == 0)
    def _():
        lane_block = lax.broadcasted_iota(jnp.int32, (8, prefix), 1) // blk
        hide = jnp.zeros((8, prefix), jnp.float32)
        for step in range(planes):
            sender = device // PLANE
            sender = sender ^ step if planes & (planes - 1) == 0 else (sender + planes - step) % planes
            for t in range(PLANE):
                owner = sender * PLANE + ((device % PLANE) ^ t)
                for k in range(PCAP):
                    ordinal = (step * PLANE + t) * PCAP + k
                    block = sources[step][t, k]
                    keys[ordinal * blk : (ordinal + 1) * blk, :] = block[:, :LANES]
                    values[ordinal * blk : (ordinal + 1) * blk, :] = block[:, LANES:]
                    gone = jnp.where(prefix_held[owner] > k, 0.0, MASKED)
                    hide = jnp.where(lane_block == ordinal, gone, hide)
        bias[...] = hide
        keys[prefix:, :] = new_kv[:, :LANES]
        values[prefix:, :] = new_kv[:, LANES:]

    for t in range(token_count // tile):
        width = prefix + (t + 1) * tile
        block = q[t * tile : (t + 1) * tile, :]
        scores = lax.dot_general(
            block, keys[:width, :], (((1,), (1,)), ((), ())), preferred_element_type=jnp.float32
        )
        causal = lax.broadcasted_iota(jnp.int32, (tile, tile), 0) >= lax.broadcasted_iota(
            jnp.int32, (tile, tile), 1
        )
        pieces = [scores[:, :prefix] + bias[0:1, :]]
        if t:
            pieces.append(scores[:, prefix : width - tile])
        pieces.append(jnp.where(causal, scores[:, width - tile :], MASKED))
        scores = jnp.concatenate(pieces, axis=1)
        top = jnp.max(scores, axis=1, keepdims=True)
        weights = jnp.exp2((scores - top) * scale)
        total = jnp.sum(weights, axis=1, keepdims=True)
        mixed = jnp.dot(
            weights.astype(jnp.bfloat16), values[:width, :], preferred_element_type=jnp.float32
        )
        out[t * tile : (t + 1) * tile, :] = (mixed / total).astype(out.dtype)


def own_kernel(q, kv, score, value):
    row_count = q.shape[0]
    head_total = q.shape[1] // LANES
    pair_count = kv.shape[1] // (2 * LANES)
    per_pair = head_total // pair_count
    for k in range(pair_count):
        lane = k * 2 * LANES
        key = kv[:, lane : lane + LANES].astype(jnp.float32) * (LANES ** (-0.5) * LOG2E)
        held = kv[:, lane + LANES : lane + 2 * LANES].astype(jnp.float32)
        for h in range(k * per_pair, (k + 1) * per_pair):
            at = pl.ds(h, row_count, stride=head_total)
            query = q[:, h * LANES : (h + 1) * LANES].astype(jnp.float32)
            product = jnp.sum(query * key, axis=1, keepdims=True)
            score[at, :] = jnp.broadcast_to(product, (row_count, LANES))
            value[at, :] = held


def unpack_kernel(cap, head_rows, places, back, score, value, out, rows_scr, stage, sems):
    row_count = out.shape[0]
    head_total = out.shape[1] // LANES
    lane = lax.broadcasted_iota(jnp.int32, (head_rows // 2, LANES), 1)
    stat_slot = lane % (LANES // 2) // 3
    copies = []
    for m in range(DGRP):
        for i in range(row_count):
            a, c = places[2 * i], places[2 * i + 1]
            at = slice(i * head_total + m * head_rows, i * head_total + (m + 1) * head_rows)
            cached = back[
                a * DGRP + m, pl.ds(pl.multiple_of(c * head_rows, 16), head_rows), :
            ].astype(jnp.float32)
            masses = back[a * DGRP + m, cap * head_rows :, :].astype(jnp.float32)
            masses = jnp.where(stat_slot == c, masses, 0.0)
            mass = jnp.concatenate(
                [
                    jnp.sum(jnp.where(lane < LANES // 2, masses, 0.0), axis=1, keepdims=True),
                    jnp.sum(jnp.where(lane < LANES // 2, 0.0, masses), axis=1, keepdims=True),
                ],
                axis=0,
            )
            share = 1.0 / (1.0 + jnp.exp2(mass - score[at, :]))
            rows_scr[at, :] = cached + share * (value[at, :] - cached)
        for h in range(m * head_rows, (m + 1) * head_rows):
            stage[:, h * LANES : (h + 1) * LANES] = rows_scr[
                pl.ds(h, row_count, stride=head_total), :
            ].astype(out.dtype)
        lanes = pl.ds(m * head_rows * LANES, head_rows * LANES)
        copy = pltpu.make_async_copy(stage.at[:, lanes], out.at[:, lanes], sems.at[m])
        copy.start()
        copies.append(copy)
    for copy in copies:
        copy.wait()


def shards(
    pool_kv,
    prefix_table,
    prefix_count,
    prefill_q,
    prefill_new_kv,
    decode_q,
    decode_new,
    decode_cache,
    decode_group,
    cached_len,
):
    devices = lax.axis_size("pool")
    blk = pool_kv.shape[2]
    row_count, q_width = decode_q.shape
    cap = decode_cache.shape[1] // devices
    decode_groups = devices // DGRP
    pair_count = decode_cache.shape[2]
    head_rows = q_width // LANES // DGRP
    message_rows = cap * head_rows
    groups = decode_group.reshape(-1)
    prefill_groups = prefix_table.shape[0]
    small = pltpu.CompilerParams(vmem_limit_bytes=8 * 2**20)

    share = jax.ShapeDtypeStruct(
        (PGRP // PLANE, prefill_groups, PCAP, blk, 2 * LANES), jnp.bfloat16
    )
    sending, *shares = pl.pallas_call(
        functools.partial(pack_kernel, head_rows),
        out_shape=(
            jax.ShapeDtypeStruct((decode_groups, DGRP, message_rows, LANES), jnp.bfloat16),
        )
        + (share,) * PLANE,
        in_specs=[any_spec()] * 5,
        out_specs=(any_spec(),) * (1 + PLANE),
        scratch_shapes=[
            pltpu.SMEM(prefix_table.shape, jnp.int32),
            pltpu.SMEM(prefix_count.shape, jnp.int32),
            pltpu.SMEM(groups.shape, jnp.int32),
            pltpu.VMEM((row_count, q_width), jnp.bfloat16),
            pltpu.VMEM((row_count * q_width // LANES, LANES), jnp.float32),
            pltpu.VMEM((DGRP, decode_groups, message_rows, LANES), jnp.bfloat16),
            pltpu.SMEM((decode_groups,), jnp.int32),
            pltpu.SemaphoreType.DMA((DGRP,)),
            pltpu.SemaphoreType.DMA((2 * PLANE * PCAP,)),
            pltpu.SemaphoreType.DMA((4,)),
        ],
        compiler_params=small,
        name="pack",
    )(
        in_hbm(prefix_table),
        in_hbm(prefix_count),
        in_hbm(groups),
        in_hbm(decode_q),
        in_hbm(pool_kv.reshape((-1, PGRP // PLANE, PLANE) + pool_kv.shape[2:])),
    )
    sending = sending.reshape(devices, message_rows, LANES)

    received = lax.all_to_all(sending, "pool", split_axis=0, concat_axis=0, tiled=True)

    shares = [shares[0]] + [
        lax.ppermute(shares[t], "pool", [(i, i ^ t) for i in range(devices)])
        for t in range(1, PLANE)
    ]
    chunk = min(cap, 4)
    width = 8
    block_count = devices * cap // chunk
    slot_len, listed, prefix_held, places, ahead = pl.pallas_call(
        functools.partial(plan_kernel, cap, chunk, devices),
        out_shape=(
            jax.ShapeDtypeStruct((devices * cap,), jnp.int32),
            jax.ShapeDtypeStruct((block_count + 2,), jnp.int32),
            jax.ShapeDtypeStruct((devices * pool_kv.shape[0],), jnp.int32),
            jax.ShapeDtypeStruct((2 * row_count,), jnp.int32),
            jax.ShapeDtypeStruct((width * chunk,) + decode_cache.shape[2:], jnp.bfloat16),
        ),
        in_specs=[smem_spec()] * 4 + [any_spec()],
        out_specs=(smem_spec(),) * 4 + (vmem_spec(),),
        scratch_shapes=[
            pltpu.SMEM((decode_groups,), jnp.int32),
            pltpu.SMEM((cap + 1,), jnp.int32),
            pltpu.SemaphoreType.DMA((width,)),
        ],
        compiler_params=small,
        cost_estimate=pl.CostEstimate(flops=1000000, bytes_accessed=4000000, transcendentals=0),
        name="plan",
    )(in_hbm(prefix_table), in_hbm(prefix_count), in_hbm(groups), in_hbm(cached_len), in_hbm(decode_cache[0]))

    *shares, slot_len, listed = lax.optimization_barrier((*shares, slot_len, listed))
    planes = devices // PLANE
    bundle = jax.ShapeDtypeStruct((PLANE, PCAP, blk, 2 * LANES), jnp.bfloat16)
    bundles = pl.pallas_call(
        functools.partial(regroup_kernel, planes),
        out_shape=(bundle,) * planes,
        in_specs=[any_spec()] * PLANE,
        out_specs=(any_spec(),) * planes,
        scratch_shapes=[pltpu.SemaphoreType.DMA((planes * PLANE,))],
        compiler_params=small,
        cost_estimate=pl.CostEstimate(flops=100000, bytes_accessed=1000000, transcendentals=0),
        name="regroup",
    )(*shares)

    def along_line(step):
        pairs = [
            (i, partner(i // PLANE, step, planes) * PLANE + i % PLANE) for i in range(devices)
        ]
        return lax.ppermute(bundles[step], "pool", pairs)


    far_first = {step: along_line(step) for step in reversed(range(1, planes))}
    lines = [bundles[0]] + [far_first[step] for step in range(1, planes)]

    answers = pl.pallas_call(
        functools.partial(decode_kernel, cap, head_rows, chunk, width),
        out_shape=jax.ShapeDtypeStruct(
            (devices, cap * head_rows + head_rows // 2, LANES), jnp.bfloat16
        ),
        in_specs=[smem_spec(), smem_spec(), vmem_spec(), vmem_spec(), any_spec()],
        out_specs=vmem_spec(),
        scratch_shapes=[
            pltpu.VMEM(((block_count - width) * chunk,) + decode_cache.shape[2:], jnp.bfloat16),
            pltpu.SemaphoreType.DMA((block_count - width,)),
        ],
        compiler_params=pltpu.CompilerParams(vmem_limit_bytes=20 * 2**20),
        cost_estimate=pl.CostEstimate(
            flops=500000000, bytes_accessed=8000000, transcendentals=1000000
        ),
        name="decode",
    )(listed, slot_len, received, ahead, in_hbm(decode_cache[0]))

    back = lax.all_to_all(answers, "pool", split_axis=0, concat_axis=0, tiled=True)

    token_count, fill_width = prefill_q.shape[1:]
    prefix = devices * PCAP * blk
    head_count = fill_width // LANES
    prefix_held, decode_q, decode_new, _ = lax.optimization_barrier(
        (prefix_held, decode_q, decode_new, answers)
    )
    expanded = jax.ShapeDtypeStruct((row_count * q_width // LANES, LANES), jnp.float32)
    own_score, own_value = pl.pallas_call(
        own_kernel,
        out_shape=(expanded, expanded),
        in_specs=[vmem_spec(), vmem_spec()],
        out_specs=(vmem_spec(), vmem_spec()),
        compiler_params=small,
        cost_estimate=pl.CostEstimate(flops=1000000, bytes_accessed=2000000, transcendentals=0),
        name="own",
    )(in_hbm(decode_q), in_hbm(decode_new))
    prefill_out = pl.pallas_call(
        functools.partial(prefill_kernel, planes, min(256, token_count)),
        grid=(head_count,),
        out_shape=jax.ShapeDtypeStruct((token_count, fill_width), jnp.bfloat16),
        in_specs=[smem_spec()]
        + [pl.BlockSpec(bundle.shape, lambda u: (0, 0, 0, 0))] * planes
        + [
            pl.BlockSpec((token_count, LANES), lambda u: (0, u)),
            pl.BlockSpec(prefill_new_kv.shape[1:], lambda u: (0, 0)),
        ],
        out_specs=pl.BlockSpec((token_count, LANES), lambda u: (0, u)),
        scratch_shapes=[
            pltpu.VMEM((prefix + token_count, LANES), jnp.bfloat16),
            pltpu.VMEM((prefix + token_count, LANES), jnp.bfloat16),
            pltpu.VMEM((8, prefix), jnp.float32),
        ],
        compiler_params=pltpu.CompilerParams(vmem_limit_bytes=16 * 2**20),
        cost_estimate=pl.CostEstimate(
            flops=32 * token_count * fill_width * (prefix + token_count),
            bytes_accessed=3000000,
            transcendentals=token_count * head_count * (prefix + token_count // 2),
        ),
        name="prefill",
    )(prefix_held, *lines, in_hbm(prefill_q[0]), in_hbm(prefill_new_kv[0]))

    decode_out = pl.pallas_call(
        functools.partial(unpack_kernel, cap, head_rows),
        out_shape=jax.ShapeDtypeStruct((row_count, q_width), jnp.bfloat16),
        in_specs=[smem_spec()] + [vmem_spec()] * 3,
        out_specs=any_spec(),
        scratch_shapes=[
            pltpu.VMEM(expanded.shape, jnp.float32),
            pltpu.VMEM((row_count, q_width), jnp.bfloat16),
            pltpu.SemaphoreType.DMA((DGRP,)),
        ],
        compiler_params=small,
        name="unpack",
    )(places, back, own_score, own_value)
    return (prefill_out[None], decode_out)


def solution(mesh):
    in_specs = (
        P(("rep", "pool"), None, None, None),
        P("rep", None),
        P("rep"),
        P(("rep", "pool"), None, None),
        P(("rep", "pool"), None, None),
        P(("rep", "pool"), None),
        P(("rep", "pool"), None),
        P(("rep", "pool"), None, None, None, None),
        P("rep", None),
        P("rep"),
    )
    out_specs = (P(("rep", "pool"), None, None), P(("rep", "pool"), None))
    return jax.shard_map(shards, mesh=mesh, in_specs=in_specs, out_specs=out_specs, check_vma=False)
```
